32 devices in a mesh: dp: 16 (over z, x, core), mp: 2 (over y).
Axes of the slice: x: 2, y: 2, z: 4, core: 2. Of those that a mesh axis runs over, the one named last changes fastest.
Arguments:
- gradients: bfloat16 [16, 34816, 128], P('dp', 'mp'), may hold values from -8 to 8
- weights: float32 [34816, 128], P('mp'), may hold values from -40 to 40
- first_moment: float32 [2, 17408, 128], P('mp', 'dp'), may hold values from -240 to 240
- second_moment: float32 [2, 17408, 128], P('mp', 'dp'), may hold values from 0.3 to 3
- owner_list: int32 [2, 17408], P('mp'), may hold values from 0 to 15, as said below
- norm_grads: bfloat16 [16, 2, 1024], P('dp'), may hold values from -6 to 6
- norm_state: float32 [3, 2, 1024], replicated, may hold values from -1.6 to 3, as said below
Outputs:
- new_weights: float32 [34816, 128], P('mp')
- new_first: float32 [2, 17408, 128], P('mp', 'dp')
- new_second: float32 [2, 17408, 128], P('mp', 'dp')
- new_norm_state: float32 [3, 2, 1024], replicated
- trust_ratios: float32 [7], replicated
The draws below stay inside these ranges and needn't reach their ends.
Inputs may be any that keep to these rules, and one draw needn't show every extreme that they name: `owner_list`: in every mp shard each dp index owns exactly 1088 of the 17408 blocks. `norm_state`: gains near 1, second moments positive.
All inputs are finite; a program needn't handle non-finite values.
Results may differ from the reference program's by a relative error of at most 0.0003.
Values sent between devices are 32-bit elements; how exact they have to be, the bound alone decides.
No kernel may reach another device: no remote copies, remote signals or barrier semaphores. Data moves between devices by JAX's collectives and lax.ppermute only.
A program may use at most 64 MiB of HBM per device.

```python
import math
import jax
import jax.numpy as jnp
from jax import lax

D = 1024
LANE = 128
QBLK = 4096
KBLK = 1024
VBLK = 4096
NBLK = 17408
BPD = 1088
N_DP = 16
N_MP = 2


def draw_gradients(key, part):
    shape = (N_DP, N_MP * NBLK, LANE)
    key_own = jax.random.fold_in(key, 0)
    own_part = jax.random.truncated_normal(key_own, -4.0, 4.0, shape, jnp.float32)
    return own_part.astype(jnp.bfloat16)


def draw_weights(key, part):
    shape = (N_MP * NBLK, LANE)
    key_value, key_rows, key_lanes = jax.random.split(key, 3)
    lane_scale = jnp.exp(jax.random.uniform(key_lanes, (1, LANE), jnp.float32, -0.6, 0.6))
    row_scale = jnp.exp(jax.random.uniform(key_rows, (shape[0], 1), jnp.float32, -1.15, 1.15))
    values = jax.random.truncated_normal(key_value, -4.0, 4.0, shape, jnp.float32)
    return values * row_scale * lane_scale


def draw_first_moment(key, part):
    shape = (N_MP, NBLK, LANE)
    owner_pos = (jnp.arange(NBLK, dtype=jnp.int32) // BPD).astype(jnp.float32) / max(N_DP - 1, 1)
    shard_pos = jnp.arange(N_MP, dtype=jnp.int32).astype(jnp.float32) / max(N_MP - 1, 1)
    rise = jnp.log(10.0)
    values = jax.random.truncated_normal(key, -4.0, 4.0, shape, jnp.float32)
    scale = jnp.exp(rise * owner_pos)[None, :, None] * jnp.exp(jnp.log(2.0) * shard_pos)[:, None, None]
    return values * scale


def draw_owner_list(key, part):
    shard_keys = jax.random.split(key, N_MP)
    shuffled = jax.vmap(lambda shard_key: jax.random.permutation(shard_key, NBLK))(shard_keys)
    return (shuffled // BPD).astype(jnp.int32)


def draw_norm_state(key, part):
    key_gain, key_first, key_second = jax.random.split(key, 3)
    gain_rows = 1.0 + 0.1 * jax.random.truncated_normal(key_gain, -4.0, 4.0, (2, D), jnp.float32)
    first_rows = 0.4 * jax.random.truncated_normal(key_first, -4.0, 4.0, (2, D), jnp.float32)
    second_rows = jnp.exp(jax.random.uniform(key_second, (2, D), jnp.float32, jnp.log(0.3), jnp.log(3.0)))
    return jnp.stack([gain_rows, first_rows, second_rows])


def block_scale(own_key, dims, cuts, smallest, top_value):
    def one(dim, blocks):
        heights = jax.random.uniform(jax.random.fold_in(jax.random.fold_in(own_key, 6), dim), (blocks,), jnp.float32, smallest / len(cuts), top_value / len(cuts))
        return jnp.repeat(jnp.exp(heights), dims[dim] // blocks).reshape((-1,) + (1,) * (len(dims) - dim - 1))

    loudness = one(*cuts[0])
    for cut in cuts[1:]:
        loudness = loudness * one(*cut)
    return loudness


def centred(own_key, dims, deviation, reach, cuts=(), held_as=jnp.bfloat16):
    gain = block_scale(own_key, dims, cuts, -0.22, 0.18) if cuts else 1.0
    entries = jax.random.normal(own_key, dims, jnp.float32) * deviation * gain
    return jnp.minimum(jnp.maximum(entries, -reach), reach).astype(held_as)


def setup_inputs(seed: int = 0) -> dict:
    streams_of = jax.random.split(jax.random.key(seed), 8)
    return {
        "gradients": draw_gradients(jax.random.fold_in(streams_of[7], 71), 0),
        "weights": draw_weights(jax.random.fold_in(streams_of[7], 71), 0),
        "first_moment": draw_first_moment(jax.random.fold_in(streams_of[7], 71), 0),
        "second_moment": jnp.clip(jnp.exp(math.log(3.0) - 2.3025851 * jax.random.uniform(streams_of[3], (N_MP, NBLK, LANE), jnp.float32) ** block_scale(streams_of[3], (N_MP, NBLK, LANE), ((0, 2), (1, 16)), -0.2, 0.2)), 0.3, 3.0),
        "owner_list": draw_owner_list(jax.random.fold_in(streams_of[7], 71), 0),
        "norm_grads": centred(streams_of[5], (N_DP, 2, D), 1.0, 6.0, ((0, 16),)),
        "norm_state": draw_norm_state(jax.random.fold_in(streams_of[7], 71), 0),
    }


beta_one = 0.9
beta_two = 0.99
bias_one = 1.0 - 0.9 ** 4
bias_two = 1.0 - 0.99 ** 4
epsilon = 1e-06
learning = 0.02
decay_rate = 0.01
matrices = 5

def block_matrix():
    position = jnp.arange(NBLK, dtype=jnp.int32)
    bounds = (QBLK, QBLK + KBLK, QBLK + KBLK + VBLK, 2 * QBLK + KBLK + VBLK)
    result = jnp.zeros((NBLK,), jnp.int32)
    for boundary in bounds:
        result = result + (position >= boundary).astype(jnp.int32)
    return result

def adam_step(gradient, moment_one, moment_two, weight):
    moment_one = beta_one * moment_one + (1.0 - beta_one) * gradient
    moment_two = beta_two * moment_two + (1.0 - beta_two) * gradient * gradient
    update = moment_one / bias_one / (jnp.sqrt(moment_two / bias_two) + epsilon) + decay_rate * weight
    return (moment_one, moment_two, update)

def member_table(matrix_of):
    return (matrix_of[:, None] == jnp.arange(matrices, dtype=jnp.int32)[None, :]).astype(jnp.float32)

def reference(gradients, weights, first_moment, second_moment, owner_list, norm_grads, norm_state):

    def add_replica(replica, running):
        return running + lax.dynamic_index_in_dim(gradients, replica, 0, keepdims=False).astype(jnp.float32)
    summed = lax.fori_loop(0, N_DP, add_replica, jnp.zeros(gradients.shape[1:], jnp.float32))
    matrix_of = block_matrix()
    stats = jnp.zeros((2, matrices), jnp.float32)
    pieces = []
    for shard_index in range(N_MP):
        owner_order = jnp.argsort(owner_list[shard_index], stable=True).astype(jnp.int32)
        gradient = summed[shard_index * NBLK:(shard_index + 1) * NBLK][owner_order]
        weight = weights[shard_index * NBLK:(shard_index + 1) * NBLK][owner_order]
        moment_one, moment_two, update = adam_step(gradient, first_moment[shard_index], second_moment[shard_index], weight)
        member = member_table(matrix_of[owner_order])
        squares = jnp.stack([lax.optimization_barrier(jnp.sum(weight * weight, axis=1)), lax.optimization_barrier(jnp.sum(update * update, axis=1))])
        stats = stats + jnp.dot(squares, member, precision=lax.Precision.HIGHEST)
        pieces.append((owner_order, weight, update, moment_one, moment_two, member))
    ratios = jnp.sqrt(stats[0]) / (jnp.sqrt(stats[1]) + epsilon)
    shards = []
    firsts = []
    seconds = []
    for owner_order, weight, update, moment_one, moment_two, member in pieces:
        row_rates = jnp.dot(member, ratios, precision=lax.Precision.HIGHEST)
        fresh_rows = weight - learning * row_rates[:, None] * update
        shards.append(jnp.zeros((NBLK, LANE), jnp.float32).at[owner_order].set(fresh_rows))
        firsts.append(moment_one)
        seconds.append(moment_two)
    norm_sum = lax.optimization_barrier(jnp.sum(norm_grads.astype(jnp.float32), axis=0))
    gain_rows = norm_state[0]
    norm_one, norm_two, norm_update = adam_step(norm_sum, norm_state[1], norm_state[2], gain_rows)
    norm_ratio = jnp.sqrt(lax.optimization_barrier(jnp.sum(gain_rows * gain_rows, axis=1))) / (jnp.sqrt(lax.optimization_barrier(jnp.sum(norm_update * norm_update, axis=1))) + epsilon)
    new_gains = gain_rows - learning * norm_ratio[:, None] * norm_update
    new_norm_state = jnp.stack([new_gains, norm_one, norm_two])
    trust_ratios = jnp.concatenate([ratios, norm_ratio])
    return (jnp.concatenate(shards, axis=0), jnp.stack(firsts), jnp.stack(seconds), new_norm_state, trust_ratios)
```

```python
import functools

import jax
import jax.numpy as jnp
from jax import lax
from jax.experimental import pallas as pl
from jax.experimental.pallas import tpu as pltpu
from jax.sharding import PartitionSpec as P

D = 1024
NTAB = 8
NKEYS = 256
KDIM = 128
LANE = 128
VROW_DEV = 512

beta_one = 0.9
beta_two = 0.99
bias_one = 1.0 - 0.9**4
bias_two = 1.0 - 0.99**4
epsilon = 1e-06
learning = 0.02
decay_rate = 0.01
matrices = 5
MIB = 1 << 20


def matrix_bounds(narrow):
    query_blocks = D * D // (LANE * narrow)
    key_blocks = NTAB * NKEYS * KDIM // (LANE * narrow)
    value_blocks = VROW_DEV * D // LANE
    return (
        query_blocks,
        query_blocks + key_blocks,
        query_blocks + key_blocks + value_blocks,
        2 * query_blocks + key_blocks + value_blocks,
    )


class Plan:
    def __init__(self, replicas, narrow, blocks):
        self.replicas, self.narrow, self.blocks = replicas, narrow, blocks
        chips = replicas // 2
        self.nz = 4 if chips % 4 == 0 else chips
        self.nx = chips // self.nz
        self.slots = chips
        self.own = blocks // replicas
        self.rows_a = int(self.own * 0.6 / 8 + 0.5) * 8
        self.rows_b = self.own - self.rows_a
        self.half = self.slots * self.own
        self.lists = -(-blocks // (8 * LANE)) * 8
        self.bounds = matrix_bounds(narrow)
        self.size_b = self.nx * self.rows_b
        self.size_a = self.nz * self.rows_a

    def index(self, z, x, c):
        return (z * self.nx + x) * 2 + c

    def send(self, value, axis, pairs):
        every = []
        for z in range(self.nz):
            for x in range(self.nx):
                for c in range(2):
                    here = {"z": z, "x": x, "c": c}
                    for source, target in pairs:
                        if here[axis] == source:
                            there = dict(here)
                            there[axis] = target
                            every.append((self.index(z, x, c), self.index(**there)))
        return lax.ppermute(value, "dp", every)

    def swap(self, value):
        return self.send(value, "c", [(0, 1), (1, 0)])


def line_reduce(plan, axis, count, blocks):
    if count == 1:
        return [blocks[0]]
    if count == 2:
        return [blocks[0], plan.send(blocks[1], axis, [(0, 1), (1, 0)])]
    up, down = blocks[count - 1], blocks[1]
    for step in range(1, count):
        from_low = plan.send(up, axis, [(i, i + 1) for i in range(count - 1) if i <= step - 1])
        from_high = plan.send(down, axis, [(i, i - 1) for i in range(1, count) if i >= count - step])
        if step < count - 1:
            up = blocks[count - 1 - step] + from_low
            down = blocks[step + 1] + from_high
    return [blocks[0], from_low, from_high]


def line_gather(plan, axis, count, value):
    if count == 1:
        return [value]
    if count == 2:
        return [value, plan.send(value, axis, [(0, 1), (1, 0)])]
    low, high = [value], [value]
    for step in range(1, count):
        low.append(plan.send(low[-1], axis, [(i, i + 1) for i in range(count - 1) if i >= step - 1]))
        high.append(plan.send(high[-1], axis, [(i, i - 1) for i in range(1, count) if i <= count - step]))
    return [value] + [high[r] + low[count - r] for r in range(1, count)]


def place_kernel(plan, place_ref, owner_ref, grads_ref, *refs):
    count_b, count_a = plan.nz, plan.nx
    out_refs, refs = refs[: 1 + count_b + count_a], refs[1 + count_b + count_a :]
    position_ref, raw, moved, position, sem_in, sem_position, sem_out = refs
    fetch = pltpu.make_async_copy(grads_ref, raw, sem_in)
    fetch.start()
    lists = plan.lists
    owners = owner_ref[...]
    my_z, my_x, my_c = place_ref[0], place_ref[1], place_ref[2]
    lane_in = lax.broadcasted_iota(jnp.int32, (LANE, LANE), 0)
    lane_out = lax.broadcasted_iota(jnp.int32, (LANE, LANE), 1)
    before = (lane_in < lane_out).astype(jnp.bfloat16)
    every = jnp.ones((LANE, LANE), jnp.bfloat16)
    row_out = lax.broadcasted_iota(jnp.int32, (lists, lists), 0)
    row_in = lax.broadcasted_iota(jnp.int32, (lists, lists), 1)
    above = (row_in < row_out).astype(jnp.bfloat16)
    result = jnp.zeros((lists, LANE), jnp.int32)
    for z in range(plan.nz):
        for x in range(plan.nx):
            for c in range(2):
                mine = owners == plan.index(z, x, c)
                flags = mine.astype(jnp.float32).astype(jnp.bfloat16)
                inner = jnp.dot(flags, before, preferred_element_type=jnp.float32)
                totals = jnp.dot(flags, every, preferred_element_type=jnp.float32)
                outer = jnp.dot(above, totals.astype(jnp.bfloat16), preferred_element_type=jnp.float32)
                rank = (inner + outer).astype(jnp.int32)
                far_z = lax.rem(z - my_z + plan.nz, plan.nz)
                far_x = lax.rem(x - my_x + plan.nx, plan.nx)
                start = jnp.where(my_c == c, plan.half, 0)
                start_b = start + (far_z * plan.nx + far_x) * plan.rows_b - plan.rows_a
                start_a = start + plan.slots * plan.rows_b + (far_x * plan.nz + far_z) * plan.rows_a
                spot = rank + jnp.where(rank < plan.rows_a, start_a, start_b)
                result = jnp.where(mine, spot, result)
    position_ref[...] = result
    to_scalar = pltpu.make_async_copy(position_ref, position, sem_position)
    to_scalar.start()
    to_scalar.wait()
    fetch.wait()

    @pl.loop(0, plan.blocks // 64)
    def _(step):
        base = step * 64
        line = step // 2
        column = (step % 2) * 64
        for part in range(4):
            rows = raw[pl.ds(pl.multiple_of(base + part * 16, 16), 16), :].astype(jnp.float32)
            for u in range(16):
                moved[pl.ds(position[line, column + part * 16 + u], 1), :] = rows[u : u + 1, :]

    copies = []
    starts = [0] + [plan.half + i * plan.size_b for i in range(count_b)]
    starts += [plan.half + plan.slots * plan.rows_b + i * plan.size_a for i in range(count_a)]
    for i, (start, out) in enumerate(zip(starts, out_refs)):
        copies.append(pltpu.make_async_copy(moved.at[pl.ds(start, out.shape[0])], out, sem_out.at[i]))
    for copy in copies:
        copy.start()
    for copy in copies:
        copy.wait()


def place(plan, my_place, owners, grads):
    shapes = [(plan.half, LANE)] + [(plan.size_b, LANE)] * plan.nz + [(plan.size_a, LANE)] * plan.nx
    outs = pl.pallas_call(
        functools.partial(place_kernel, plan),
        out_shape=[jax.ShapeDtypeStruct(s, jnp.float32) for s in shapes]
        + [jax.ShapeDtypeStruct((plan.lists, LANE), jnp.int32)],
        in_specs=[
            pl.BlockSpec(memory_space=pltpu.SMEM),
            pl.BlockSpec(memory_space=pltpu.VMEM),
            pl.BlockSpec(memory_space=pl.ANY),
        ],
        out_specs=[pl.BlockSpec(memory_space=pl.ANY)] * len(shapes) + [pl.BlockSpec(memory_space=pltpu.VMEM)],
        scratch_shapes=[
            pltpu.VMEM((plan.blocks, LANE), jnp.bfloat16),
            pltpu.VMEM((plan.blocks, LANE), jnp.float32),
            pltpu.SMEM((plan.lists, LANE), jnp.int32),
            pltpu.SemaphoreType.DMA,
            pltpu.SemaphoreType.DMA,
            pltpu.SemaphoreType.DMA((len(shapes),)),
        ],
        compiler_params=pltpu.CompilerParams(vmem_limit_bytes=40 * MIB),
        name="place_gradients",
    )(my_place, owners, grads)
    sibling, blocks, position = outs[0], outs[1:-1], outs[-1]
    return sibling, blocks[: plan.nz], blocks[plan.nz :], position


def owned_kernel(plan, position_ref, weights_ref, owned_ref, natural_ref, held, listed, order, sem_in, sem_order):
    fetch = pltpu.make_async_copy(weights_ref, held, sem_in)
    fetch.start()
    high_rows = listed.shape[0]
    start_b = plan.half
    start_a = plan.half + plan.slots * plan.rows_b
    sub_high = lax.broadcasted_iota(jnp.int32, (high_rows, LANE), 0)
    lanes = lax.broadcasted_iota(jnp.int32, (high_rows, LANE), 1).astype(jnp.float32)
    sub_low = lax.broadcasted_iota(jnp.int32, (LANE, LANE), 0)
    zero = jnp.zeros((high_rows, LANE), jnp.float32)

    def add(line, sums):
        spot = position_ref[pl.ds(line, 1), :]
        valid = line * LANE + lax.broadcasted_iota(jnp.int32, (1, LANE), 1) < plan.blocks
        in_a = (spot >= start_a) & (spot < start_a + plan.rows_a) & valid
        in_b = (spot >= start_b) & (spot < start_b + plan.rows_b) & valid
        rank = jnp.where(in_a, spot - start_a, jnp.where(in_b, spot - start_b + plan.rows_a, -1))
        high = rank >> 7
        low = rank & 127
        at_high = (sub_high == high).astype(jnp.float32)
        at_low = (sub_low == low).astype(jnp.float32).astype(jnp.bfloat16)
        left = jnp.concatenate([at_high, at_high * lanes], 0).astype(jnp.bfloat16)
        hits = lax.dot_general(left, at_low, (((1,), (1,)), ((), ())), preferred_element_type=jnp.float32)
        return (
            sums[0] + hits[:high_rows] * (line * LANE).astype(jnp.float32),
            sums[1] + hits[high_rows:],
        )

    sums = lax.fori_loop(0, plan.lists, add, (zero, zero), unroll=2)
    listed[...] = (sums[0] + sums[1]).astype(jnp.int32)
    to_scalar = pltpu.make_async_copy(listed, order, sem_order)
    to_scalar.start()
    to_scalar.wait()
    fetch.wait()

    @pl.loop(0, plan.own // 8)
    def _(step):
        base = pl.multiple_of(step * 8, 8)
        line = base // LANE
        column = base % LANE
        for u in range(8):
            block = order[line, column + u]
            owned_ref[pl.ds(base + u, 1), :] = held[pl.ds(block, 1), :]
            natural_ref[pl.ds(base + u, 1), :] = jnp.full((1, LANE), block, jnp.int32)


def owned(plan, position, weights):
    high_rows = -(-plan.own // (8 * LANE)) * 8
    return pl.pallas_call(
        functools.partial(owned_kernel, plan),
        out_shape=[
            jax.ShapeDtypeStruct((plan.own, LANE), jnp.float32),
            jax.ShapeDtypeStruct((plan.own, LANE), jnp.int32),
        ],
        in_specs=[pl.BlockSpec(memory_space=pltpu.VMEM), pl.BlockSpec(memory_space=pl.ANY)],
        out_specs=[pl.BlockSpec(memory_space=pltpu.VMEM)] * 2,
        scratch_shapes=[
            pltpu.VMEM((plan.blocks, LANE), jnp.float32),
            pltpu.VMEM((high_rows, LANE), jnp.int32),
            pltpu.SMEM((high_rows, LANE), jnp.int32),
            pltpu.SemaphoreType.DMA,
            pltpu.SemaphoreType.DMA,
        ],
        compiler_params=pltpu.CompilerParams(vmem_limit_bytes=24 * MIB),
        name="owned_weights",
    )(position, weights)


def update_kernel(plan, terms_a, terms_b, *refs):
    parts_a, parts_b, refs = refs[:terms_a], refs[terms_a : terms_a + terms_b], refs[terms_a + terms_b :]
    first_ref, second_ref, weight_ref, natural_ref = refs[:4]
    new_first_ref, new_second_ref, step_a_ref, step_b_ref, stats_ref = refs[4:]
    weight_sums = [jnp.zeros((8, LANE), jnp.float32)] * matrices
    step_sums = [jnp.zeros((8, LANE), jnp.float32)] * matrices
    for parts, start, rows, step_ref in (
        (parts_a, 0, plan.rows_a, step_a_ref),
        (parts_b, plan.rows_a, plan.rows_b, step_b_ref),
    ):
        gradient = parts[0][:rows, :]
        for part in parts[1:]:
            gradient = gradient + part[:rows, :]
        here = pl.ds(start, rows)
        moment_one = beta_one * first_ref[here, :] + (1.0 - beta_one) * gradient
        moment_two = beta_two * second_ref[here, :] + (1.0 - beta_two) * gradient * gradient
        new_first_ref[here, :] = moment_one
        new_second_ref[here, :] = moment_two
        step = moment_one / bias_one / (jnp.sqrt(moment_two / bias_two) + epsilon)
        step_ref[...] = step
        weight = weight_ref[here, :]
        direction = step + decay_rate * weight
        natural = natural_ref[here, :]
        limits = (0,) + plan.bounds + (plan.blocks,)
        weight_square = weight * weight
        direction_square = direction * direction
        for k in range(matrices):
            inside = (natural >= limits[k]) & (natural < limits[k + 1])
            for sums, squares in ((weight_sums, weight_square), (step_sums, direction_square)):
                kept = jnp.where(inside, squares, 0.0).reshape(rows // 8, 8, LANE)
                sums[k] = sums[k] + jnp.sum(kept, axis=0)
    for k in range(8):
        for base, sums in ((0, weight_sums), (8, step_sums)):
            row = jnp.sum(sums[k], axis=0, keepdims=True) if k < matrices else jnp.zeros((1, LANE), jnp.float32)
            stats_ref[base + k : base + k + 1, :] = row


def update(plan, parts_a, parts_b, first, second, weight, natural):
    vmem = pl.BlockSpec(memory_space=pltpu.VMEM)
    shapes = [(plan.own, LANE), (plan.own, LANE), (plan.rows_a, LANE), (plan.rows_b, LANE), (16, LANE)]
    return pl.pallas_call(
        functools.partial(update_kernel, plan, len(parts_a), len(parts_b)),
        out_shape=[jax.ShapeDtypeStruct(s, jnp.float32) for s in shapes],
        in_specs=[vmem] * (len(parts_a) + len(parts_b) + 4),
        out_specs=[vmem] * len(shapes),
        compiler_params=pltpu.CompilerParams(vmem_limit_bytes=32 * MIB),
        name="moments",
    )(*parts_a, *parts_b, first, second, weight, natural)


def finish_kernel(plan, tile, starts, position_ref, rates_ref, weights_ref, *refs):
    pieces, refs = refs[: len(starts)], refs[len(starts) :]
    out_ref, held, sems = refs
    now = pl.program_id(0)

    @pl.when(now == 0)
    def _():
        copies = [
            pltpu.make_async_copy(piece, held.at[pl.ds(start, piece.shape[0])], sems.at[i])
            for i, (piece, start) in enumerate(zip(pieces, starts))
        ]
        for copy in copies:
            copy.start()
        for copy in copies:
            copy.wait()

    matrix = jnp.int32(0)
    for bound in plan.bounds:
        matrix = matrix + (now * tile >= bound).astype(jnp.int32)
    rate = rates_ref[matrix]
    lines = tile // LANE

    @pl.loop(0, tile // 64)
    def _(step):
        line = now * lines + step // 2
        column = (step % 2) * 64
        for group in range(8):
            rows = [held[pl.ds(position_ref[line, column + group * 8 + u], 1), :] for u in range(8)]
            here = pl.ds(pl.multiple_of(step * 64 + group * 8, 8), 8)
            weight = weights_ref[here, :]
            direction = jnp.concatenate(rows, 0) + decay_rate * weight
            out_ref[here, :] = weight - rate * direction


def finish(plan, position, rates, weights, pieces, starts):
    tile = LANE
    while tile < 1024 and all(b % (2 * tile) == 0 for b in plan.bounds + (plan.blocks,)):
        tile *= 2
    smem = pl.BlockSpec(memory_space=pltpu.SMEM)
    return pl.pallas_call(
        functools.partial(finish_kernel, plan, tile, starts),
        grid=(plan.blocks // tile,),
        out_shape=jax.ShapeDtypeStruct((plan.blocks, LANE), jnp.float32),
        in_specs=[smem, smem, pl.BlockSpec((tile, LANE), lambda i: (i, 0))]
        + [pl.BlockSpec(memory_space=pl.ANY)] * len(pieces),
        out_specs=pl.BlockSpec((tile, LANE), lambda i: (i, 0)),
        scratch_shapes=[
            pltpu.VMEM((plan.blocks, LANE), jnp.float32),
            pltpu.SemaphoreType.DMA((len(pieces),)),
        ],
        compiler_params=pltpu.CompilerParams(vmem_limit_bytes=24 * MIB),
        name="new_weights",
    )(position, rates, weights, *pieces)


def adam_step(gradient, moment_one, moment_two, weight):
    moment_one = beta_one * moment_one + (1.0 - beta_one) * gradient
    moment_two = beta_two * moment_two + (1.0 - beta_two) * gradient * gradient
    step = moment_one / bias_one / (jnp.sqrt(moment_two / bias_two) + epsilon) + decay_rate * weight
    return (moment_one, moment_two, step)


def local(gradients, weights, first_moment, second_moment, owner_list, norm_grads, norm_state):
    plan = Plan(lax.axis_size("dp"), lax.axis_size("mp"), weights.shape[0])
    me = lax.axis_index("dp").astype(jnp.int32)
    my_place = jnp.stack([me // (2 * plan.nx), (me // 2) % plan.nx, me % 2]).astype(jnp.int32)
    owners = jnp.pad(owner_list[0], (0, plan.lists * LANE - plan.blocks), constant_values=-1)
    owners = owners.reshape(plan.lists, LANE)
    sibling, blocks_b, blocks_a, position = place(plan, my_place, owners, gradients[0])

    other = plan.swap(sibling)
    size_b, size_a = plan.size_b, plan.size_a
    after_b = plan.slots * plan.rows_b
    blocks_b = [b + other[i * size_b : (i + 1) * size_b] for i, b in enumerate(blocks_b)]
    blocks_a = [b + other[after_b + i * size_a : after_b + (i + 1) * size_a] for i, b in enumerate(blocks_a)]
    terms = line_reduce(plan, "x", plan.nx, blocks_a)
    summed_a = sum(terms[1:], terms[0])
    rows_a, rows_b = plan.rows_a, plan.rows_b
    parts_a = line_reduce(plan, "z", plan.nz, [summed_a[i * rows_a : (i + 1) * rows_a] for i in range(plan.nz)])
    terms = line_reduce(plan, "z", plan.nz, blocks_b)
    summed_b = sum(terms[1:], terms[0])
    parts_b = line_reduce(plan, "x", plan.nx, [summed_b[i * rows_b : (i + 1) * rows_b] for i in range(plan.nx)])

    weight_own, natural = owned(plan, position, weights)
    new_first, new_second, step_a, step_b, stats = update(
        plan, parts_a, parts_b, first_moment[0], second_moment[0], weight_own, natural
    )

    small = jnp.concatenate([stats, norm_grads[0].astype(jnp.float32).reshape(-1, LANE)])
    small = small + plan.swap(small)
    for axis, count in (("x", plan.nx), ("z", plan.nz)):
        hop = 1
        while hop < count:
            small = small + plan.send(small, axis, [(i, i ^ hop) for i in range(count)])
            hop *= 2
    stats, norm_sum = small[:16], small[16:].reshape(norm_grads.shape[1:])
    hop = 1
    while hop < plan.narrow:
        stats = stats + lax.ppermute(stats, "mp", [(i, i ^ hop) for i in range(plan.narrow)])
        hop *= 2
    squares = jnp.sum(stats, axis=1)
    ratios = jnp.sqrt(squares[:matrices]) / (jnp.sqrt(squares[8 : 8 + matrices]) + epsilon)

    near_a = jnp.concatenate(line_gather(plan, "z", plan.nz, step_a))
    pieces_a = line_gather(plan, "x", plan.nx, near_a)
    near_b = jnp.concatenate(line_gather(plan, "x", plan.nx, step_b))
    pieces_b = line_gather(plan, "z", plan.nz, near_b)
    mine = pieces_b + pieces_a
    pieces = [plan.swap(piece) for piece in mine] + mine
    offsets = [i * size_b for i in range(plan.nz)] + [after_b + i * size_a for i in range(plan.nx)]
    starts = offsets + [plan.half + offset for offset in offsets]
    new_weights = finish(plan, position, learning * ratios, weights, pieces, starts)

    gain_rows = norm_state[0]
    norm_one, norm_two, norm_update = adam_step(norm_sum, norm_state[1], norm_state[2], gain_rows)
    norm_ratio = jnp.sqrt(jnp.sum(gain_rows * gain_rows, axis=1)) / (
        jnp.sqrt(jnp.sum(norm_update * norm_update, axis=1)) + epsilon
    )
    new_gains = gain_rows - learning * norm_ratio[:, None] * norm_update
    new_state = jnp.stack([new_gains, norm_one, norm_two])
    trust_ratios = jnp.concatenate([ratios, norm_ratio])
    return (new_weights, new_first[None], new_second[None], new_state, trust_ratios)


def solution(mesh):
    in_specs = (
        P("dp", "mp", None),
        P("mp", None),
        P("mp", "dp", None),
        P("mp", "dp", None),
        P("mp", None),
        P("dp", None, None),
        P(),
    )
    out_specs = (P("mp", None), P("mp", "dp", None), P("mp", "dp", None), P(), P())
    return jax.shard_map(local, mesh=mesh, in_specs=in_specs, out_specs=out_specs, check_vma=False)
```

```python
import functools

import jax
import jax.numpy as jnp
from jax import lax
from jax.experimental import pallas as pl
from jax.experimental.pallas import tpu as pltpu
from jax.sharding import PartitionSpec as P

D = 1024
NTAB = 8
NKEYS = 256
KDIM = 128
LANE = 128
VROW_DEV = 512

beta_one = 0.9
beta_two = 0.99
bias_one = 1.0 - 0.9**4
bias_two = 1.0 - 0.99**4
epsilon = 1e-06
learning = 0.02
decay_rate = 0.01
matrices = 5
MIB = 1 << 20


def matrix_bounds(narrow):
    query_blocks = D * D // (LANE * narrow)
    key_blocks = NTAB * NKEYS * KDIM // (LANE * narrow)
    value_blocks = VROW_DEV * D // LANE
    return (
        query_blocks,
        query_blocks + key_blocks,
        query_blocks + key_blocks + value_blocks,
        2 * query_blocks + key_blocks + value_blocks,
    )


class Plan:
    def __init__(self, replicas, narrow, blocks):
        self.replicas, self.narrow, self.blocks = replicas, narrow, blocks
        chips = replicas // 2
        self.nz = 4 if chips % 4 == 0 else chips
        self.nx = chips // self.nz
        self.slots = chips
        self.own = blocks // replicas
        self.rows_a = int(self.own * 0.6 / 8 + 0.5) * 8
        self.rows_b = self.own - self.rows_a
        self.tail = 8
        self.norm_rows = 2 * D // LANE
        self.norm_each = -(-self.norm_rows // replicas)
        self.block_b = self.rows_b + self.tail
        self.after_b = self.slots * self.block_b
        self.half = self.after_b + self.slots * self.rows_a
        self.lists = -(-blocks // (8 * LANE)) * 8
        self.bounds = matrix_bounds(narrow)
        self.size_b = self.nx * self.block_b
        self.size_a = self.nz * self.rows_a

    def index(self, z, x, c):
        return (z * self.nx + x) * 2 + c

    def send(self, value, axis, pairs, keep=()):
        every = []
        for z in range(self.nz):
            for x in range(self.nx):
                for c in range(2):
                    here = {"z": z, "x": x, "c": c}
                    for source, target in pairs:
                        if here[axis] == source and all(least <= here[a] <= most for a, least, most in keep):
                            there = dict(here)
                            there[axis] = target
                            every.append((self.index(z, x, c), self.index(**there)))
        return lax.ppermute(value, "dp", every)

    def swap(self, value, keep=()):
        return self.send(value, "c", [(0, 1), (1, 0)], keep)


def line_reduce(plan, axis, count, blocks):
    if count == 1:
        return [blocks[0]]
    if count == 2:
        return [blocks[0], plan.send(blocks[1], axis, [(0, 1), (1, 0)])]
    up, down = blocks[count - 1], blocks[1]
    for step in range(1, count):
        from_low = plan.send(up, axis, [(i, i + 1) for i in range(count - 1) if i <= step - 1])
        from_high = plan.send(down, axis, [(i, i - 1) for i in range(1, count) if i >= count - step])
        if step < count - 1:
            up = blocks[count - 1 - step] + from_low
            down = blocks[step + 1] + from_high
    return [blocks[0], from_low, from_high]


def line_gather(plan, axis, count, value, keep=()):
    found = [(value, 0, keep)]
    if count == 2:
        found.append((plan.send(value, axis, [(0, 1), (1, 0)], keep), 1, keep))
    elif count > 2:
        low = high = value
        for step in range(1, count):
            low = plan.send(low, axis, [(i, i + 1) for i in range(count - 1) if i >= step - 1], keep)
            high = plan.send(high, axis, [(i, i - 1) for i in range(1, count) if i <= count - step], keep)
            found.append((low, count - step, keep + ((axis, step, count - 1),)))
            found.append((high, step, keep + ((axis, 0, count - 1 - step),)))
    return found


def merged(found, count):
    return [sum(value for value, source, _ in found[1:] if source == r) if r else found[0][0] for r in range(count)]


def place_kernel(plan, place_ref, owner_ref, norm_ref, grads_ref, *refs):
    count_b, count_a = plan.nz, plan.nx
    out_refs, refs = refs[: 2 + count_b + count_a], refs[2 + count_b + count_a :]
    position_ref, raw, moved, position, sem_in, sem_position, sem_out = refs
    fetch = pltpu.make_async_copy(grads_ref, raw, sem_in)
    fetch.start()
    lists = plan.lists
    owners = owner_ref[...]
    my_z, my_x, my_c = place_ref[0], place_ref[1], place_ref[2]
    lane_in = lax.broadcasted_iota(jnp.int32, (LANE, LANE), 0)
    lane_out = lax.broadcasted_iota(jnp.int32, (LANE, LANE), 1)
    before = (lane_in < lane_out).astype(jnp.bfloat16)
    every = jnp.ones((LANE, LANE), jnp.bfloat16)
    row_out = lax.broadcasted_iota(jnp.int32, (lists, lists), 0)
    row_in = lax.broadcasted_iota(jnp.int32, (lists, lists), 1)
    above = (row_in < row_out).astype(jnp.bfloat16)
    result = jnp.zeros((lists, LANE), jnp.int32)
    for z in range(plan.nz):
        for x in range(plan.nx):
            for c in range(2):
                mine = owners == plan.index(z, x, c)
                flags = mine.astype(jnp.float32).astype(jnp.bfloat16)
                inner = jnp.dot(flags, before, preferred_element_type=jnp.float32)
                totals = jnp.dot(flags, every, preferred_element_type=jnp.float32)
                outer = jnp.dot(above, totals.astype(jnp.bfloat16), preferred_element_type=jnp.float32)
                rank = (inner + outer).astype(jnp.int32)
                far_z = lax.rem(z - my_z + plan.nz, plan.nz)
                far_x = lax.rem(x - my_x + plan.nx, plan.nx)
                start = jnp.where(my_c == c, plan.half, 0)
                start_b = start + (far_z * plan.nx + far_x) * plan.block_b - plan.rows_a
                start_a = start + plan.after_b + (far_x * plan.nz + far_z) * plan.rows_a
                first_norm = plan.index(z, x, c) * plan.norm_each
                tail = [jnp.zeros((plan.tail, LANE), jnp.float32)]
                for row in range(min(first_norm + plan.norm_each, plan.norm_rows) - 1, first_norm - 1, -1):
                    part = norm_ref[row * LANE // D : row * LANE // D + 1, row * LANE % D : row * LANE % D + LANE]
                    tail.insert(0, part.astype(jnp.float32))
                tail = jnp.concatenate(tail, 0)[: plan.tail]
                moved[pl.ds(pl.multiple_of(start_b + plan.own, 8), plan.tail), :] = tail
                spot = rank + jnp.where(rank < plan.rows_a, start_a, start_b)
                result = jnp.where(mine, spot, result)
    position_ref[...] = result
    to_scalar = pltpu.make_async_copy(position_ref, position, sem_position)
    to_scalar.start()
    to_scalar.wait()
    fetch.wait()

    @pl.loop(0, plan.blocks // LANE)
    def _(line):
        for part in range(0, LANE, 16):
            rows = raw[pl.ds(pl.multiple_of(line * LANE + part, 16), 16), :].astype(jnp.float32)
            for u in range(16):
                moved[pl.ds(position[line, part + u], 1), :] = rows[u : u + 1, :]

    copies = []
    starts = [0, plan.after_b] + [plan.half + i * plan.size_b for i in range(count_b)]
    starts += [plan.half + plan.after_b + i * plan.size_a for i in range(count_a)]
    for i, (start, out) in enumerate(zip(starts, out_refs)):
        copies.append(pltpu.make_async_copy(moved.at[pl.ds(start, out.shape[0])], out, sem_out.at[i]))
    for copy in copies:
        copy.start()
    for copy in copies:
        copy.wait()


def place(plan, my_place, owners, norm_grads, grads):
    shapes = [(plan.after_b, LANE), (plan.half - plan.after_b, LANE)]
    shapes += [(plan.size_b, LANE)] * plan.nz + [(plan.size_a, LANE)] * plan.nx
    outs = pl.pallas_call(
        functools.partial(place_kernel, plan),
        out_shape=[jax.ShapeDtypeStruct(s, jnp.float32) for s in shapes]
        + [jax.ShapeDtypeStruct((plan.lists, LANE), jnp.int32)],
        in_specs=[
            pl.BlockSpec(memory_space=pltpu.SMEM),
            pl.BlockSpec(memory_space=pltpu.VMEM),
            pl.BlockSpec(memory_space=pltpu.VMEM),
            pl.BlockSpec(memory_space=pl.ANY),
        ],
        out_specs=[pl.BlockSpec(memory_space=pl.ANY)] * len(shapes) + [pl.BlockSpec(memory_space=pltpu.VMEM)],
        scratch_shapes=[
            pltpu.VMEM((plan.blocks, LANE), jnp.bfloat16),
            pltpu.VMEM((2 * plan.half, LANE), jnp.float32),
            pltpu.SMEM((plan.lists, LANE), jnp.int32),
            pltpu.SemaphoreType.DMA,
            pltpu.SemaphoreType.DMA,
            pltpu.SemaphoreType.DMA((len(shapes),)),
        ],
        compiler_params=pltpu.CompilerParams(vmem_limit_bytes=58 * MIB),
        name="place_gradients",
    )(my_place, owners, norm_grads, grads)
    siblings, blocks, position = outs[:2], outs[2:-1], outs[-1]
    return siblings, blocks[: plan.nz], blocks[plan.nz :], position


def owned_kernel(plan, position_ref, weights_ref, owned_ref, natural_ref, held, listed, order, sem_in, sem_order):
    fetch = pltpu.make_async_copy(weights_ref, held, sem_in)
    fetch.start()
    high_rows = listed.shape[0]
    start_b = plan.half
    start_a = plan.half + plan.after_b
    sub_high = lax.broadcasted_iota(jnp.int32, (high_rows, LANE), 0)
    lanes = lax.broadcasted_iota(jnp.int32, (high_rows, LANE), 1).astype(jnp.float32)
    sub_low = lax.broadcasted_iota(jnp.int32, (LANE, LANE), 0)
    zero = jnp.zeros((high_rows, LANE), jnp.float32)

    def add(line, sums):
        spot = position_ref[pl.ds(line, 1), :]
        valid = line * LANE + lax.broadcasted_iota(jnp.int32, (1, LANE), 1) < plan.blocks
        in_a = (spot >= start_a) & (spot < start_a + plan.rows_a) & valid
        in_b = (spot >= start_b) & (spot < start_b + plan.rows_b) & valid
        rank = jnp.where(in_a, spot - start_a, jnp.where(in_b, spot - start_b + plan.rows_a, -1))
        high = rank >> 7
        low = rank & 127
        at_high = (sub_high == high).astype(jnp.float32)
        at_low = (sub_low == low).astype(jnp.float32).astype(jnp.bfloat16)
        left = jnp.concatenate([at_high, at_high * lanes], 0).astype(jnp.bfloat16)
        hits = lax.dot_general(left, at_low, (((1,), (1,)), ((), ())), preferred_element_type=jnp.float32)
        return (
            sums[0] + hits[:high_rows] * (line * LANE).astype(jnp.float32),
            sums[1] + hits[high_rows:],
        )

    sums = lax.fori_loop(0, plan.lists, add, (zero, zero), unroll=2)
    listed[...] = (sums[0] + sums[1]).astype(jnp.int32)
    to_scalar = pltpu.make_async_copy(listed, order, sem_order)
    to_scalar.start()
    to_scalar.wait()
    fetch.wait()

    def pick(line, count):
        for u in range(count):
            block = order[line, u]
            row = pl.ds(line * LANE + u, 1)
            owned_ref[row, :] = held[pl.ds(block, 1), :]
            natural_ref[row, :] = jnp.full((1, LANE), block, jnp.int32)

    @pl.loop(0, plan.own // LANE)
    def _(line):
        pick(line, LANE)

    if plan.own % LANE:
        pick(plan.own // LANE, plan.own % LANE)


def owned(plan, position, weights):
    high_rows = -(-plan.own // (8 * LANE)) * 8
    return pl.pallas_call(
        functools.partial(owned_kernel, plan),
        out_shape=[
            jax.ShapeDtypeStruct((plan.own, LANE), jnp.float32),
            jax.ShapeDtypeStruct((plan.own, LANE), jnp.int32),
        ],
        in_specs=[pl.BlockSpec(memory_space=pltpu.VMEM), pl.BlockSpec(memory_space=pl.ANY)],
        out_specs=[pl.BlockSpec(memory_space=pltpu.VMEM)] * 2,
        scratch_shapes=[
            pltpu.VMEM((plan.blocks, LANE), jnp.float32),
            pltpu.VMEM((high_rows, LANE), jnp.int32),
            pltpu.SMEM((high_rows, LANE), jnp.int32),
            pltpu.SemaphoreType.DMA,
            pltpu.SemaphoreType.DMA,
        ],
        compiler_params=pltpu.CompilerParams(vmem_limit_bytes=58 * MIB),
        cost_estimate=pl.CostEstimate(flops=0, bytes_accessed=20 * MIB, transcendentals=0),
        name="owned_weights",
    )(position, weights)


def update_kernel(plan, terms_a, terms_b, *refs):
    parts_a, parts_b, refs = refs[:terms_a], refs[terms_a : terms_a + terms_b], refs[terms_a + terms_b :]
    first_ref, second_ref, weight_ref, natural_ref = refs[:4]
    new_first_ref, new_second_ref, step_a_ref, step_b_ref, tail_ref, stats_ref = refs[4:]
    weight_sums = [jnp.zeros((8, LANE), jnp.float32)] * matrices
    step_sums = [jnp.zeros((8, LANE), jnp.float32)] * matrices
    for parts, start, rows, step_ref in (
        (parts_a, 0, plan.rows_a, step_a_ref),
        (parts_b, plan.rows_a, plan.rows_b, step_b_ref),
    ):
        gradient = parts[0][:rows, :]
        for part in parts[1:]:
            gradient = gradient + part[:rows, :]
        if step_ref is step_b_ref:
            tail = parts[0][rows : rows + plan.tail, :]
            for part in parts[1:]:
                tail = tail + part[rows : rows + plan.tail, :]
            tail_ref[...] = tail
        here = pl.ds(start, rows)
        moment_one = beta_one * first_ref[here, :] + (1.0 - beta_one) * gradient
        moment_two = beta_two * second_ref[here, :] + (1.0 - beta_two) * gradient * gradient
        new_first_ref[here, :] = moment_one
        new_second_ref[here, :] = moment_two
        step = moment_one / bias_one / (jnp.sqrt(moment_two / bias_two) + epsilon)
        step_ref[...] = step
        weight = weight_ref[here, :]
        direction = step + decay_rate * weight
        natural = natural_ref[here, :]
        limits = (0,) + plan.bounds + (plan.blocks,)
        weight_square = weight * weight
        direction_square = direction * direction
        for k in range(matrices):
            inside = (natural >= limits[k]) & (natural < limits[k + 1])
            for sums, squares in ((weight_sums, weight_square), (step_sums, direction_square)):
                kept = jnp.where(inside, squares, 0.0).reshape(rows // 8, 8, LANE)
                sums[k] = sums[k] + jnp.sum(kept, axis=0)
    lane = lax.broadcasted_iota(jnp.int32, (8, LANE), 1)
    rank = lax.broadcasted_iota(jnp.int32, (8, LANE), 0)
    stats = jnp.zeros((8, LANE), jnp.float32)
    for k in range(matrices):
        for column, sums in enumerate((weight_sums, step_sums)):
            stats = jnp.where((rank == k) & (lane == column), jnp.sum(sums[k]), stats)
    stats_ref[...] = stats


def update(plan, parts_a, parts_b, first, second, weight, natural):
    vmem = pl.BlockSpec(memory_space=pltpu.VMEM)
    shapes = [(plan.own, LANE), (plan.own, LANE), (plan.rows_a, LANE), (plan.rows_b, LANE), (plan.tail, LANE)]
    shapes.append((8, LANE))
    return pl.pallas_call(
        functools.partial(update_kernel, plan, len(parts_a), len(parts_b)),
        out_shape=[jax.ShapeDtypeStruct(s, jnp.float32) for s in shapes],
        in_specs=[vmem] * (len(parts_a) + len(parts_b) + 4),
        out_specs=[vmem] * len(shapes),
        compiler_params=pltpu.CompilerParams(vmem_limit_bytes=32 * MIB),
        name="moments",
    )(*parts_a, *parts_b, first, second, weight, natural)


def fetch_pieces(place_ref, copies, keeps):
    here = {"z": place_ref[0], "x": place_ref[1], "c": place_ref[2]}
    for act in (lambda copy: copy.start(), lambda copy: copy.wait()):
        for copy, keep in zip(copies, keeps):
            valid = None
            for axis, least, most in keep:
                inside = (here[axis] >= least) & (here[axis] <= most)
                valid = inside if valid is None else valid & inside
            if valid is None:
                act(copy)
            else:

                @pl.when(valid)
                def _(copy=copy, act=act):
                    act(copy)


def tails_kernel(plan, sources, place_ref, *refs):
    pieces, refs = refs[: len(sources)], refs[len(sources) :]
    norm_ref, ratio_ref, held, sems = refs
    copies, keeps = [], []
    for piece, (far_c, far_z, keep) in zip(pieces, sources):
        for far_x in range(plan.nx):
            z = lax.rem(place_ref[0] + far_z, plan.nz)
            x = lax.rem(place_ref[1] + far_x, plan.nx)
            d = plan.index(z, x, lax.rem(place_ref[2] + far_c, 2))
            rows = pl.ds(far_x * plan.block_b + plan.rows_b, plan.tail)
            copies.append(pltpu.make_async_copy(piece.at[rows], held.at[d], sems.at[len(copies)]))
            keeps.append(keep)
    fetch_pieces(place_ref, copies, keeps)
    total = held[0]
    for d in range(1, plan.replicas):
        total = total + held[d]
    for row in range(plan.norm_rows):
        norm_ref[row : row + 1, :] = held[row // plan.norm_each, pl.ds(row % plan.norm_each, 1), :]
    for k in range(matrices):
        row = plan.norm_each + k
        weight_square, direction_square = total[row : row + 1, 0:1], total[row : row + 1, 1:2]
        ratio = jnp.sqrt(weight_square) / (jnp.sqrt(direction_square) + epsilon)
        ratio_ref[k : k + 1, :] = jnp.broadcast_to(ratio, (1, LANE))


def tails(plan, my_place, pieces, sources):
    vmem = pl.BlockSpec(memory_space=pltpu.VMEM)
    return pl.pallas_call(
        functools.partial(tails_kernel, plan, sources),
        out_shape=[
            jax.ShapeDtypeStruct((plan.norm_rows, LANE), jnp.float32),
            jax.ShapeDtypeStruct((matrices, LANE), jnp.float32),
        ],
        in_specs=[pl.BlockSpec(memory_space=pltpu.SMEM)] + [pl.BlockSpec(memory_space=pl.ANY)] * len(pieces),
        out_specs=[vmem, vmem],
        scratch_shapes=[
            pltpu.VMEM((plan.replicas, plan.tail, LANE), jnp.float32),
            pltpu.SemaphoreType.DMA((len(pieces) * plan.nx,)),
        ],
        name="tails",
    )(my_place, *pieces)


def finish_kernel(plan, tile, sources, place_ref, position_ref, rates_ref, weights_ref, *refs):
    pieces, refs = refs[: len(sources)], refs[len(sources) :]
    out_ref, held, sems = refs
    now = pl.program_id(0)

    @pl.when(now == 0)
    def _():
        copies = [
            pltpu.make_async_copy(piece, held.at[pl.ds(start, piece.shape[0])], sems.at[i])
            for i, (piece, (start, _)) in enumerate(zip(pieces, sources))
        ]
        fetch_pieces(place_ref, copies, [keep for _, keep in sources])

    matrix = jnp.int32(0)
    for bound in plan.bounds:
        matrix = matrix + (now * tile >= bound).astype(jnp.int32)
    rate = rates_ref[matrix]
    lines = tile // LANE

    @pl.loop(0, lines)
    def _(line):
        for group in range(0, LANE, 8):
            rows = [held[pl.ds(position_ref[now * lines + line, group + u], 1), :] for u in range(8)]
            here = pl.ds(pl.multiple_of(line * LANE + group, 8), 8)
            weight = weights_ref[here, :]
            direction = jnp.concatenate(rows, 0) + decay_rate * weight
            out_ref[here, :] = weight - rate * direction


def finish(plan, my_place, position, rates, weights, pieces, sources):
    tile = LANE
    while tile < 1024 and all(b % (2 * tile) == 0 for b in plan.bounds + (plan.blocks,)):
        tile *= 2
    smem = pl.BlockSpec(memory_space=pltpu.SMEM)
    return pl.pallas_call(
        functools.partial(finish_kernel, plan, tile, sources),
        grid=(plan.blocks // tile,),
        out_shape=jax.ShapeDtypeStruct((plan.blocks, LANE), jnp.float32),
        in_specs=[smem, smem, smem, pl.BlockSpec((tile, LANE), lambda i: (i, 0))]
        + [pl.BlockSpec(memory_space=pl.ANY)] * len(pieces),
        out_specs=pl.BlockSpec((tile, LANE), lambda i: (i, 0)),
        scratch_shapes=[
            pltpu.VMEM((2 * plan.half, LANE), jnp.float32),
            pltpu.SemaphoreType.DMA((len(pieces),)),
        ],
        compiler_params=pltpu.CompilerParams(vmem_limit_bytes=58 * MIB),
        name="new_weights",
    )(my_place, position, rates, weights, *pieces)


def adam_step(gradient, moment_one, moment_two, weight):
    moment_one = beta_one * moment_one + (1.0 - beta_one) * gradient
    moment_two = beta_two * moment_two + (1.0 - beta_two) * gradient * gradient
    step = moment_one / bias_one / (jnp.sqrt(moment_two / bias_two) + epsilon) + decay_rate * weight
    return (moment_one, moment_two, step)


def local(gradients, weights, first_moment, second_moment, owner_list, norm_grads, norm_state):
    plan = Plan(lax.axis_size("dp"), lax.axis_size("mp"), weights.shape[0])
    me = lax.axis_index("dp").astype(jnp.int32)
    my_place = jnp.stack([me // (2 * plan.nx), (me // 2) % plan.nx, me % 2]).astype(jnp.int32)
    owners = jnp.pad(owner_list[0], (0, plan.lists * LANE - plan.blocks), constant_values=-1)
    owners = owners.reshape(plan.lists, LANE)
    siblings, blocks_b, blocks_a, position = place(plan, my_place, owners, norm_grads[0], gradients[0])

    other_b, other_a = plan.swap(siblings[0]), plan.swap(siblings[1])
    size_b, rows_a, block_b = plan.size_b, plan.rows_a, plan.block_b
    blocks_b = [b + other_b[i * size_b : (i + 1) * size_b] for i, b in enumerate(blocks_b)]
    terms = line_reduce(plan, "z", plan.nz, blocks_b)
    summed_b = sum(terms[1:], terms[0])
    parts_b = line_reduce(plan, "x", plan.nx, [summed_b[i * block_b : (i + 1) * block_b] for i in range(plan.nx)])
    near_a = []
    for z in range(plan.nz):
        blocks = []
        for x in range(plan.nx):
            far = (x * plan.nz + z) * rows_a
            blocks.append(blocks_a[x][z * rows_a : (z + 1) * rows_a] + other_a[far : far + rows_a])
        terms = line_reduce(plan, "x", plan.nx, blocks)
        near_a.append(sum(terms[1:], terms[0]))
    parts_a = line_reduce(plan, "z", plan.nz, near_a)

    weight_own, natural = owned(plan, position, weights)
    new_first, new_second, step_a, step_b, tail, stats = update(
        plan, parts_a, parts_b, first_moment[0], second_moment[0], weight_own, natural
    )

    hop = 1
    while hop < plan.narrow:
        stats = stats + lax.ppermute(stats, "mp", [(i, i ^ hop) for i in range(plan.narrow)])
        hop *= 2
    tail = jnp.concatenate([tail[: plan.norm_each], stats[: plan.tail - plan.norm_each]])
    step_b = jnp.concatenate([step_b, tail])
    near_b = jnp.concatenate(merged(line_gather(plan, "x", plan.nx, step_b), plan.nx))
    pieces, sources, tail_pieces, tail_sources = [], [], [], []
    for value, far_z, keep in line_gather(plan, "z", plan.nz, near_b):
        for far_c, piece in ((0, value), (1, plan.swap(value, keep))):
            pieces.append(piece)
            sources.append(((1 - far_c) * plan.half + far_z * plan.size_b, keep))
            tail_pieces.append(piece)
            tail_sources.append((far_c, far_z, keep))
    for block, far_z, keep_z in line_gather(plan, "z", plan.nz, step_a):
        for value, far_x, keep in line_gather(plan, "x", plan.nx, block, keep_z):
            for far_c, piece in ((0, value), (1, plan.swap(value, keep))):
                pieces.append(piece)
                start = plan.after_b + (far_x * plan.nz + far_z) * rows_a
                sources.append(((1 - far_c) * plan.half + start, keep))
    norm_sum, ratios = tails(plan, my_place, tail_pieces, tail_sources)
    norm_sum, ratios = norm_sum.reshape(norm_grads.shape[1:]), ratios[:, 0]
    new_weights = finish(plan, my_place, position, learning * ratios, weights, pieces, sources)

    gain_rows = norm_state[0]
    norm_one, norm_two, norm_update = adam_step(norm_sum, norm_state[1], norm_state[2], gain_rows)
    norm_ratio = jnp.sqrt(jnp.sum(gain_rows * gain_rows, axis=1)) / (
        jnp.sqrt(jnp.sum(norm_update * norm_update, axis=1)) + epsilon
    )
    new_gains = gain_rows - learning * norm_ratio[:, None] * norm_update
    new_state = jnp.stack([new_gains, norm_one, norm_two])
    trust_ratios = jnp.concatenate([ratios, norm_ratio])
    return (new_weights, new_first[None], new_second[None], new_state, trust_ratios)


def solution(mesh):
    in_specs = (
        P("dp", "mp", None),
        P("mp", None),
        P("mp", "dp", None),
        P("mp", "dp", None),
        P("mp", None),
        P("dp", None, None),
        P(),
    )
    out_specs = (P("mp", None), P("mp", "dp", None), P("mp", "dp", None), P(), P())
    return jax.shard_map(local, mesh=mesh, in_specs=in_specs, out_specs=out_specs, check_vma=False)
```

```python
import functools

import jax
import jax.numpy as jnp
from jax import lax
from jax.experimental import pallas as pl
from jax.experimental.pallas import tpu as pltpu
from jax.sharding import PartitionSpec as P

D = 1024
NTAB = 8
NKEYS = 256
KDIM = 128
LANE = 128
VROW_DEV = 512

beta_one = 0.9
beta_two = 0.99
bias_one = 1.0 - 0.9**4
bias_two = 1.0 - 0.99**4
epsilon = 1e-06
learning = 0.02
decay_rate = 0.01
matrices = 5
MIB = 1 << 20


def matrix_bounds(narrow):
    query_blocks = D * D // (LANE * narrow)
    key_blocks = NTAB * NKEYS * KDIM // (LANE * narrow)
    value_blocks = VROW_DEV * D // LANE
    return (
        query_blocks,
        query_blocks + key_blocks,
        query_blocks + key_blocks + value_blocks,
        2 * query_blocks + key_blocks + value_blocks,
    )


class Plan:
    def __init__(self, replicas, narrow, blocks):
        self.replicas, self.narrow, self.blocks = replicas, narrow, blocks
        chips = replicas // 2
        self.nz = 4 if chips % 4 == 0 else chips
        self.nx = chips // self.nz
        assert self.nz in (1, 2, 4) and self.nx in (1, 2, 4)
        self.own = blocks // replicas
        self.tail = 8
        self.norm_rows = 2 * D // LANE
        self.norm_each = -(-self.norm_rows // replicas)
        self.block = self.own + self.tail
        self.group = self.nx * self.block
        self.half = self.nz * self.group
        self.lists = -(-blocks // (8 * LANE)) * 8
        self.bounds = matrix_bounds(narrow)

    def index(self, z, x, c):
        return (z * self.nx + x) * 2 + c

    def start(self, far_z, far_x, far_c):
        return (1 - far_c) * self.half + far_z * self.group + far_x * self.block

    def send(self, value, axis, pairs):
        every = []
        for z in range(self.nz):
            for x in range(self.nx):
                for c in range(2):
                    here = {"z": z, "x": x, "c": c}
                    for source, target in pairs:
                        if here[axis] == source:
                            every.append((self.index(z, x, c), self.index(**{**here, axis: target})))
        return lax.ppermute(value, "dp", every)

    def swap(self, value):
        return self.send(value, "c", PAIR)


PAIR = [(0, 1), (1, 0)]
PAIRS = [(0, 1), (1, 0), (2, 3), (3, 2)]
MIDDLE = [(1, 2), (2, 1)]
INWARD = [(0, 1), (3, 2)]
OUTWARD = [(1, 0), (2, 3)]


def line_reduce(plan, axis, blocks):
    if len(blocks) == 1:
        return [blocks[0]]
    if len(blocks) == 2:
        return [blocks[0], plan.send(blocks[1], axis, PAIR)]
    in_three = plan.send(blocks[3], axis, INWARD)
    in_two = plan.send(blocks[2], axis, INWARD)
    across_two = plan.send(blocks[2] + in_three, axis, MIDDLE)
    across_three = plan.send(blocks[3] + in_two, axis, MIDDLE)
    pair = plan.send(blocks[1] + across_two, axis, PAIRS)
    return [blocks[0], pair, across_three]


def line_gather(plan, axis, count, value):
    if count == 1:
        return [value]
    if count == 2:
        return [value, plan.send(value, axis, PAIR)]
    pair = plan.send(value, axis, PAIRS)
    across_three = plan.send(value, axis, MIDDLE)
    across_two = plan.send(pair, axis, MIDDLE)
    out_two = plan.send(across_three, axis, OUTWARD)
    out_three = plan.send(across_two, axis, OUTWARD)
    return [value, pair, across_two + out_two, across_three + out_three]


def place_kernel(plan, place_ref, owner_ref, norm_ref, grads_ref, *refs):
    out_refs, refs = refs[: 2 * plan.nz], refs[2 * plan.nz :]
    position_ref, raw, moved, position, sem_in, sem_position, sem_out = refs
    fetch = pltpu.make_async_copy(grads_ref, raw, sem_in)
    fetch.start()
    lists = plan.lists
    owners = owner_ref[...]
    my_z, my_x, my_c = place_ref[0], place_ref[1], place_ref[2]
    lane_in = lax.broadcasted_iota(jnp.int32, (LANE, LANE), 0)
    lane_out = lax.broadcasted_iota(jnp.int32, (LANE, LANE), 1)
    before = (lane_in < lane_out).astype(jnp.bfloat16)
    every = jnp.ones((LANE, LANE), jnp.bfloat16)
    row_out = lax.broadcasted_iota(jnp.int32, (lists, lists), 0)
    row_in = lax.broadcasted_iota(jnp.int32, (lists, lists), 1)
    above = (row_in < row_out).astype(jnp.bfloat16)
    result = jnp.zeros((lists, LANE), jnp.int32)
    for z in range(plan.nz):
        for x in range(plan.nx):
            for c in range(2):
                mine = owners == plan.index(z, x, c)
                flags = mine.astype(jnp.float32).astype(jnp.bfloat16)
                inner = jnp.dot(flags, before, preferred_element_type=jnp.float32)
                totals = jnp.dot(flags, every, preferred_element_type=jnp.float32)
                outer = jnp.dot(above, totals.astype(jnp.bfloat16), preferred_element_type=jnp.float32)
                rank = (inner + outer).astype(jnp.int32)
                start = plan.start(my_z ^ z, my_x ^ x, my_c ^ c)
                first_norm = plan.index(z, x, c) * plan.norm_each
                tail = [jnp.zeros((plan.tail, LANE), jnp.float32)]
                for row in range(min(first_norm + plan.norm_each, plan.norm_rows) - 1, first_norm - 1, -1):
                    part = norm_ref[row * LANE // D : row * LANE // D + 1, row * LANE % D : row * LANE % D + LANE]
                    tail.insert(0, part.astype(jnp.float32))
                tail = jnp.concatenate(tail, 0)[: plan.tail]
                moved[pl.ds(pl.multiple_of(start + plan.own, 8), plan.tail), :] = tail
                result = jnp.where(mine, rank + start, result)
    position_ref[...] = result
    to_scalar = pltpu.make_async_copy(position_ref, position, sem_position)
    to_scalar.start()
    to_scalar.wait()
    fetch.wait()

    @pl.loop(0, plan.blocks // LANE)
    def _(line):
        for part in range(0, LANE, 16):
            rows = raw[pl.ds(pl.multiple_of(line * LANE + part, 16), 16), :].astype(jnp.float32)
            for u in range(16):
                moved[pl.ds(position[line, part + u], 1), :] = rows[u : u + 1, :]

    copies = []
    for i, out in enumerate(out_refs):
        start = (i // plan.nz) * plan.half + (plan.nz - 1 - i % plan.nz) * plan.group
        copies.append(pltpu.make_async_copy(moved.at[pl.ds(start, plan.group)], out, sem_out.at[i]))
    for copy in copies:
        copy.start()
    for copy in copies:
        copy.wait()


def place(plan, my_place, owners, norm_grads, grads):
    shapes = [(plan.group, LANE)] * (2 * plan.nz)
    outs = pl.pallas_call(
        functools.partial(place_kernel, plan),
        out_shape=[jax.ShapeDtypeStruct(s, jnp.float32) for s in shapes]
        + [jax.ShapeDtypeStruct((plan.lists, LANE), jnp.int32)],
        in_specs=[
            pl.BlockSpec(memory_space=pltpu.SMEM),
            pl.BlockSpec(memory_space=pltpu.VMEM),
            pl.BlockSpec(memory_space=pltpu.VMEM),
            pl.BlockSpec(memory_space=pl.ANY),
        ],
        out_specs=[pl.BlockSpec(memory_space=pl.ANY)] * len(shapes) + [pl.BlockSpec(memory_space=pltpu.VMEM)],
        scratch_shapes=[
            pltpu.VMEM((plan.blocks, LANE), jnp.bfloat16),
            pltpu.VMEM((2 * plan.half, LANE), jnp.float32),
            pltpu.SMEM((plan.lists, LANE), jnp.int32),
            pltpu.SemaphoreType.DMA,
            pltpu.SemaphoreType.DMA,
            pltpu.SemaphoreType.DMA((len(shapes),)),
        ],
        compiler_params=pltpu.CompilerParams(vmem_limit_bytes=58 * MIB),
        name="place_gradients",
    )(my_place, owners, norm_grads, grads)
    return outs[: plan.nz][::-1], outs[plan.nz : 2 * plan.nz][::-1], outs[-1]


def owned_kernel(plan, place_ref, owner_ref, weights_ref, owned_ref, natural_ref, held, listed, order, sem_in, sem_order):
    fetch = pltpu.make_async_copy(weights_ref, held, sem_in)
    fetch.start()
    lists = plan.lists
    me = plan.index(place_ref[0], place_ref[1], place_ref[2])
    flags = (owner_ref[...] == me).astype(jnp.float32).astype(jnp.bfloat16)
    lane_in = lax.broadcasted_iota(jnp.int32, (LANE, LANE), 0)
    lane_out = lax.broadcasted_iota(jnp.int32, (LANE, LANE), 1)
    upto = (lane_in <= lane_out).astype(jnp.float32).astype(jnp.bfloat16)
    inner = jnp.dot(flags, upto, preferred_element_type=jnp.float32).astype(jnp.bfloat16)
    totals = lax.dot_general(
        jnp.ones((8, LANE), jnp.bfloat16), flags, (((1,), (1,)), ((), ())), preferred_element_type=jnp.float32
    )
    row_in = lax.broadcasted_iota(jnp.int32, (lists, lists), 0)
    row_out = lax.broadcasted_iota(jnp.int32, (lists, lists), 1)
    upto = (row_in <= row_out).astype(jnp.float32).astype(jnp.bfloat16)
    ends = jnp.dot(totals.astype(jnp.bfloat16), upto, preferred_element_type=jnp.float32)[0:1, :]
    place_of = lax.broadcasted_iota(jnp.int32, (LANE, lists), 1).astype(jnp.float32)
    rank_of = lax.broadcasted_iota(jnp.int32, (LANE, 1), 0)
    for step in range(listed.shape[0]):
        if step * LANE >= plan.own:
            break
        rank = (rank_of + step * LANE).astype(jnp.float32)
        passed = ends <= rank
        line = jnp.sum(passed.astype(jnp.float32), axis=1, keepdims=True)
        before = jnp.max(jnp.where(passed, ends, 0.0), axis=1, keepdims=True)
        chosen = (place_of == line).astype(jnp.float32).astype(jnp.bfloat16)
        counts = jnp.dot(chosen, inner, preferred_element_type=jnp.float32)
        column = jnp.sum((counts <= rank - before).astype(jnp.float32), axis=1, keepdims=True)
        block = jnp.broadcast_to((line * LANE + column).astype(jnp.int32), (LANE, LANE))
        natural_ref[step * LANE : (step + 1) * LANE, :] = block
        listed[step : step + 1, :] = jnp.sum(jnp.where(lane_in == lane_out, block, 0), axis=0, keepdims=True)
    to_scalar = pltpu.make_async_copy(listed, order, sem_order)
    to_scalar.start()
    to_scalar.wait()
    fetch.wait()

    def pick(line, count):
        for u in range(count):
            owned_ref[pl.ds(line * LANE + u, 1), :] = held[pl.ds(order[line, u], 1), :]

    @pl.loop(0, plan.own // LANE)
    def _(line):
        pick(line, LANE)

    if plan.own % LANE:
        pick(plan.own // LANE, plan.own % LANE)


def owned(plan, my_place, owners, weights):
    high_rows = -(-plan.own // (8 * LANE)) * 8
    ranks = -(-plan.own // LANE) * LANE
    vmem = pl.BlockSpec(memory_space=pltpu.VMEM)
    return pl.pallas_call(
        functools.partial(owned_kernel, plan),
        out_shape=[
            jax.ShapeDtypeStruct((plan.own, LANE), jnp.float32),
            jax.ShapeDtypeStruct((ranks, LANE), jnp.int32),
        ],
        in_specs=[pl.BlockSpec(memory_space=pltpu.SMEM), vmem, pl.BlockSpec(memory_space=pl.ANY)],
        out_specs=[vmem] * 2,
        scratch_shapes=[
            pltpu.VMEM((plan.blocks, LANE), jnp.float32),
            pltpu.VMEM((high_rows, LANE), jnp.int32),
            pltpu.SMEM((high_rows, LANE), jnp.int32),
            pltpu.SemaphoreType.DMA,
            pltpu.SemaphoreType.DMA,
        ],
        compiler_params=pltpu.CompilerParams(vmem_limit_bytes=58 * MIB),
        cost_estimate=pl.CostEstimate(flops=0, bytes_accessed=20 * MIB, transcendentals=0),
        name="owned_weights",
    )(my_place, owners, weights)


def update_kernel(plan, terms, *refs):
    parts, refs = refs[:terms], refs[terms:]
    first_ref, second_ref, weight_ref, natural_ref = refs[:4]
    new_first_ref, new_second_ref, block_ref, stats_ref = refs[4:]
    gradient = parts[0][: plan.block, :]
    for part in parts[1:]:
        gradient = gradient + part[: plan.block, :]
    block_ref[plan.own :, :] = gradient[plan.own :, :]
    gradient = gradient[: plan.own, :]
    moment_one = beta_one * first_ref[...] + (1.0 - beta_one) * gradient
    moment_two = beta_two * second_ref[...] + (1.0 - beta_two) * gradient * gradient
    new_first_ref[...] = moment_one
    new_second_ref[...] = moment_two
    step = moment_one / bias_one / (jnp.sqrt(moment_two / bias_two) + epsilon)
    block_ref[: plan.own, :] = step
    weight = weight_ref[...]
    direction = step + decay_rate * weight
    natural = natural_ref[: plan.own, :]
    limits = (0,) + plan.bounds + (plan.blocks,)
    lane = lax.broadcasted_iota(jnp.int32, (8, LANE), 1)
    rank = lax.broadcasted_iota(jnp.int32, (8, LANE), 0)
    stats = jnp.zeros((8, LANE), jnp.float32)
    for column, squares in enumerate((weight * weight, direction * direction)):
        for k in range(matrices):
            inside = (natural >= limits[k]) & (natural < limits[k + 1])
            kept = jnp.where(inside, squares, 0.0).reshape(plan.own // 8, 8, LANE)
            total = jnp.sum(jnp.sum(kept, axis=0))
            stats = jnp.where((rank == plan.norm_each + k) & (lane == column), total, stats)
    stats_ref[...] = stats


def update(plan, parts, first, second, weight, natural):
    vmem = pl.BlockSpec(memory_space=pltpu.VMEM)
    shapes = [(plan.own, LANE), (plan.own, LANE), (plan.block, LANE), (plan.tail, LANE)]
    return pl.pallas_call(
        functools.partial(update_kernel, plan, len(parts)),
        out_shape=[jax.ShapeDtypeStruct(s, jnp.float32) for s in shapes],
        in_specs=[vmem] * (len(parts) + 4),
        out_specs=[vmem] * len(shapes),
        compiler_params=pltpu.CompilerParams(vmem_limit_bytes=58 * MIB),
        name="moments",
    )(*parts, first, second, weight, natural)


def tails_kernel(plan, slots, place_ref, *refs):
    pieces, refs = refs[: len(slots)], refs[len(slots) :]
    norm_ref, ratio_ref, held, sems = refs
    copies = []
    for i, (piece, (far_z, far_x, far_c)) in enumerate(zip(pieces, slots)):
        d = plan.index(place_ref[0] ^ far_z, place_ref[1] ^ far_x, place_ref[2] ^ far_c)
        copies.append(pltpu.make_async_copy(piece.at[pl.ds(plan.own, plan.tail)], held.at[d], sems.at[i]))
    for copy in copies:
        copy.start()
    for copy in copies:
        copy.wait()
    total = held[0]
    for d in range(1, plan.replicas):
        total = total + held[d]
    for row in range(plan.norm_rows):
        norm_ref[row : row + 1, :] = held[row // plan.norm_each, pl.ds(row % plan.norm_each, 1), :]
    for k in range(matrices):
        row = plan.norm_each + k
        weight_square, direction_square = total[row : row + 1, 0:1], total[row : row + 1, 1:2]
        ratio = jnp.sqrt(weight_square) / (jnp.sqrt(direction_square) + epsilon)
        ratio_ref[k : k + 1, :] = jnp.broadcast_to(ratio, (1, LANE))


def tails(plan, my_place, pieces, slots):
    vmem = pl.BlockSpec(memory_space=pltpu.VMEM)
    return pl.pallas_call(
        functools.partial(tails_kernel, plan, slots),
        out_shape=[
            jax.ShapeDtypeStruct((plan.norm_rows, LANE), jnp.float32),
            jax.ShapeDtypeStruct((matrices, LANE), jnp.float32),
        ],
        in_specs=[pl.BlockSpec(memory_space=pltpu.SMEM)] + [pl.BlockSpec(memory_space=pl.ANY)] * len(pieces),
        out_specs=[vmem, vmem],
        scratch_shapes=[
            pltpu.VMEM((plan.replicas, plan.tail, LANE), jnp.float32),
            pltpu.SemaphoreType.DMA((len(pieces),)),
        ],
        name="tails",
    )(my_place, *pieces)


def finish_kernel(plan, tile, slots, position_ref, rates_ref, weights_ref, *refs):
    pieces, refs = refs[: len(slots)], refs[len(slots) :]
    out_ref, held, sems = refs
    now = pl.program_id(0)

    @pl.when(now == 0)
    def _():
        copies = [
            pltpu.make_async_copy(piece, held.at[pl.ds(plan.start(*slot), plan.block)], sems.at[i])
            for i, (piece, slot) in enumerate(zip(pieces, slots))
        ]
        for copy in copies:
            copy.start()
        for copy in copies:
            copy.wait()

    matrix = jnp.int32(0)
    for bound in plan.bounds:
        matrix = matrix + (now * tile >= bound).astype(jnp.int32)
    rate = rates_ref[matrix]
    lines = tile // LANE

    @pl.loop(0, lines)
    def _(line):
        for group in range(0, LANE, 8):
            rows = [held[pl.ds(position_ref[now * lines + line, group + u], 1), :] for u in range(8)]
            here = pl.ds(pl.multiple_of(line * LANE + group, 8), 8)
            weight = weights_ref[here, :]
            direction = jnp.concatenate(rows, 0) + decay_rate * weight
            out_ref[here, :] = weight - rate * direction


def finish(plan, position, rates, weights, pieces, slots):
    tile = LANE
    while tile < 1024 and all(b % (2 * tile) == 0 for b in plan.bounds + (plan.blocks,)):
        tile *= 2
    smem = pl.BlockSpec(memory_space=pltpu.SMEM)
    return pl.pallas_call(
        functools.partial(finish_kernel, plan, tile, slots),
        grid=(plan.blocks // tile,),
        out_shape=jax.ShapeDtypeStruct((plan.blocks, LANE), jnp.float32),
        in_specs=[smem, smem, pl.BlockSpec((tile, LANE), lambda i: (i, 0))]
        + [pl.BlockSpec(memory_space=pl.ANY)] * len(pieces),
        out_specs=pl.BlockSpec((tile, LANE), lambda i: (i, 0)),
        scratch_shapes=[
            pltpu.VMEM((2 * plan.half, LANE), jnp.float32),
            pltpu.SemaphoreType.DMA((len(pieces),)),
        ],
        compiler_params=pltpu.CompilerParams(vmem_limit_bytes=58 * MIB),
        name="new_weights",
    )(position, rates, weights, *pieces)


def adam_step(gradient, moment_one, moment_two, weight):
    moment_one = beta_one * moment_one + (1.0 - beta_one) * gradient
    moment_two = beta_two * moment_two + (1.0 - beta_two) * gradient * gradient
    step = moment_one / bias_one / (jnp.sqrt(moment_two / bias_two) + epsilon) + decay_rate * weight
    return (moment_one, moment_two, step)


def local(gradients, weights, first_moment, second_moment, owner_list, norm_grads, norm_state):
    plan = Plan(lax.axis_size("dp"), lax.axis_size("mp"), weights.shape[0])
    me = lax.axis_index("dp").astype(jnp.int32)
    my_place = jnp.stack([me // (2 * plan.nx), (me // 2) % plan.nx, me % 2]).astype(jnp.int32)
    owners = jnp.pad(owner_list[0], (0, plan.lists * LANE - plan.blocks), constant_values=-1)
    owners = owners.reshape(plan.lists, LANE)
    siblings, blocks, position = place(plan, my_place, owners, norm_grads[0], gradients[0])
    weight_own, natural = owned(plan, my_place, owners, weights)

    others = [None] * plan.nz
    for z in reversed(range(plan.nz)):
        others[z] = plan.swap(siblings[z])
    near = []
    for z in reversed(range(plan.nz)):
        parts = [
            blocks[z][x * plan.block : (x + 1) * plan.block] + others[z][x * plan.block : (x + 1) * plan.block]
            for x in range(1, plan.nx)
        ]
        terms = line_reduce(plan, "x", [None] + parts)[1:]
        if z:
            mine = blocks[z][: plan.block] + others[z][: plan.block]
            near.insert(0, sum(terms, mine))
        else:
            near.insert(0, None)
            near_terms = [blocks[z], others[z]] + terms
    parts = near_terms + line_reduce(plan, "z", near)[1:]
    new_first, new_second, block, stats = update(
        plan, parts, first_moment[0], second_moment[0], weight_own, natural
    )

    hop = 1
    while hop < plan.narrow:
        stats = stats + lax.ppermute(stats, "mp", [(i, i ^ hop) for i in range(plan.narrow)])
        hop *= 2
    block = lax.dynamic_update_slice(block, block[plan.own :] + stats, (plan.own, 0))
    pieces, slots = [], []
    for far_z, value in enumerate(line_gather(plan, "z", plan.nz, block)):
        for far_x, piece in enumerate(line_gather(plan, "x", plan.nx, value)):
            pieces += [piece, plan.swap(piece)]
            slots += [(far_z, far_x, 0), (far_z, far_x, 1)]
    norm_sum, ratios = tails(plan, my_place, pieces, slots)
    norm_sum, ratios = norm_sum.reshape(norm_grads.shape[1:]), ratios[:, 0]
    new_weights = finish(plan, position, learning * ratios, weights, pieces, slots)

    gain_rows = norm_state[0]
    norm_one, norm_two, norm_update = adam_step(norm_sum, norm_state[1], norm_state[2], gain_rows)
    norm_ratio = jnp.sqrt(jnp.sum(gain_rows * gain_rows, axis=1)) / (
        jnp.sqrt(jnp.sum(norm_update * norm_update, axis=1)) + epsilon
    )
    new_gains = gain_rows - learning * norm_ratio[:, None] * norm_update
    new_state = jnp.stack([new_gains, norm_one, norm_two])
    trust_ratios = jnp.concatenate([ratios, norm_ratio])
    return (new_weights, new_first[None], new_second[None], new_state, trust_ratios)


def solution(mesh):
    in_specs = (
        P("dp", "mp", None),
        P("mp", None),
        P("mp", "dp", None),
        P("mp", "dp", None),
        P("mp", None),
        P("dp", None, None),
        P(),
    )
    out_specs = (P("mp", None), P("mp", "dp", None), P("mp", "dp", None), P(), P())
    return jax.shard_map(local, mesh=mesh, in_specs=in_specs, out_specs=out_specs, check_vma=False)
```

```python
import functools

import jax
import jax.numpy as jnp
from jax import lax
from jax.experimental import pallas as pl
from jax.experimental.pallas import tpu as pltpu
from jax.sharding import PartitionSpec as P

D = 1024
NTAB = 8
NKEYS = 256
KDIM = 128
LANE = 128
VROW_DEV = 512

beta_one = 0.9
beta_two = 0.99
bias_one = 1.0 - 0.9**4
bias_two = 1.0 - 0.99**4
epsilon = 1e-06
learning = 0.02
decay_rate = 0.01
matrices = 5
MIB = 1 << 20


def matrix_bounds(narrow):
    query_blocks = D * D // (LANE * narrow)
    key_blocks = NTAB * NKEYS * KDIM // (LANE * narrow)
    value_blocks = VROW_DEV * D // LANE
    return (
        query_blocks,
        query_blocks + key_blocks,
        query_blocks + key_blocks + value_blocks,
        2 * query_blocks + key_blocks + value_blocks,
    )


class Plan:
    def __init__(self, replicas, narrow, blocks):
        self.replicas, self.narrow, self.blocks = replicas, narrow, blocks
        chips = replicas // 2
        self.nz = 4 if chips % 4 == 0 else chips
        self.nx = chips // self.nz
        assert self.nz in (1, 2, 4) and self.nx in (1, 2, 4)
        self.own = blocks // replicas
        self.tail = 8
        self.norm_rows = 2 * D // LANE
        self.norm_each = -(-self.norm_rows // replicas)
        self.block = self.own + self.tail
        self.group = self.nx * self.block
        self.half = self.nz * self.group
        self.lists = -(-blocks // (8 * LANE)) * 8
        self.bounds = matrix_bounds(narrow)

    def index(self, z, x, c):
        return (z * self.nx + x) * 2 + c

    def start(self, far_z, far_x, far_c):
        return (1 - far_c) * self.half + far_z * self.group + far_x * self.block

    def send(self, value, axis, pairs):
        every = []
        for z in range(self.nz):
            for x in range(self.nx):
                for c in range(2):
                    here = {"z": z, "x": x, "c": c}
                    for source, target in pairs:
                        if here[axis] == source:
                            every.append((self.index(z, x, c), self.index(**{**here, axis: target})))
        return lax.ppermute(value, "dp", every)

    def swap(self, value):
        return self.send(value, "c", PAIR)


PAIR = [(0, 1), (1, 0)]
PAIRS = [(0, 1), (1, 0), (2, 3), (3, 2)]
MIDDLE = [(1, 2), (2, 1)]
INWARD = [(0, 1), (3, 2)]
OUTWARD = [(1, 0), (2, 3)]


def line_reduce(plan, axis, blocks):
    if len(blocks) == 1:
        return [blocks[0]]
    if len(blocks) == 2:
        return [blocks[0], plan.send(blocks[1], axis, PAIR)]
    in_three = plan.send(blocks[3], axis, INWARD)
    in_two = plan.send(blocks[2], axis, INWARD)
    across_two = plan.send(blocks[2] + in_three, axis, MIDDLE)
    across_three = plan.send(blocks[3] + in_two, axis, MIDDLE)
    pair = plan.send(blocks[1] + across_two, axis, PAIRS)
    return [blocks[0], pair, across_three]


def together(*values):
    return lax.optimization_barrier(values)


def gather(plan, block):
    found = {}

    def add(far_z, line):
        for far_x, value in enumerate(line):
            found[far_z, far_x, 0] = value

    def along_x(value):
        return line_gather(plan, "x", plan.nx, value)

    def swapped(*far_zs):
        for far_z in far_zs:
            for far_x in range(plan.nx):
                found[far_z, far_x, 1] = plan.swap(found[far_z, far_x, 0])

    if plan.nz != 4:
        for far_z, value in enumerate(line_gather(plan, "z", plan.nz, block)):
            add(far_z, along_x(value))
            swapped(far_z)
        return list(found.items())
    line = along_x(block)
    pair = plan.send(block, "z", PAIRS)
    three = plan.send(block, "z", MIDDLE)
    pair, three, *line = together(pair, three, *line)
    add(0, line)
    line = along_x(pair)
    two = plan.send(pair, "z", MIDDLE)
    out_two = plan.send(three, "z", OUTWARD)
    swapped(0)
    two, out_two, *line = together(two, out_two, *line)
    add(1, line)
    line = along_x(two + out_two)
    out_three = plan.send(two, "z", OUTWARD)
    swapped(1)
    out_three, *line = together(out_three, *line)
    add(2, line)
    add(3, along_x(three + out_three))
    swapped(2)
    swapped(3)
    return list(found.items())


def line_gather(plan, axis, count, value):
    if count == 1:
        return [value]
    if count == 2:
        return [value, plan.send(value, axis, PAIR)]
    pair = plan.send(value, axis, PAIRS)
    across_three = plan.send(value, axis, MIDDLE)
    across_two = plan.send(pair, axis, MIDDLE)
    out_two = plan.send(across_three, axis, OUTWARD)
    out_three = plan.send(across_two, axis, OUTWARD)
    return [value, pair, across_two + out_two, across_three + out_three]


def place_kernel(plan, place_ref, owner_ref, norm_ref, grads_ref, *refs):
    out_refs, refs = refs[: 2 * plan.nz], refs[2 * plan.nz :]
    position_ref, raw, moved, position, sem_in, sem_position, sem_out = refs
    fetch = pltpu.make_async_copy(grads_ref, raw, sem_in)
    fetch.start()
    lists = plan.lists
    owners = owner_ref[...]
    my_z, my_x, my_c = place_ref[0], place_ref[1], place_ref[2]
    lane_in = lax.broadcasted_iota(jnp.int32, (LANE, LANE), 0)
    lane_out = lax.broadcasted_iota(jnp.int32, (LANE, LANE), 1)
    before = (lane_in < lane_out).astype(jnp.bfloat16)
    every = jnp.ones((LANE, LANE), jnp.bfloat16)
    row_out = lax.broadcasted_iota(jnp.int32, (lists, lists), 0)
    row_in = lax.broadcasted_iota(jnp.int32, (lists, lists), 1)
    above = (row_in < row_out).astype(jnp.bfloat16)
    result = jnp.zeros((lists, LANE), jnp.int32)
    for z in range(plan.nz):
        for x in range(plan.nx):
            for c in range(2):
                mine = owners == plan.index(z, x, c)
                flags = mine.astype(jnp.float32).astype(jnp.bfloat16)
                inner = jnp.dot(flags, before, preferred_element_type=jnp.float32)
                totals = jnp.dot(flags, every, preferred_element_type=jnp.float32)
                outer = jnp.dot(above, totals.astype(jnp.bfloat16), preferred_element_type=jnp.float32)
                rank = (inner + outer).astype(jnp.int32)
                start = plan.start(my_z ^ z, my_x ^ x, my_c ^ c)
                first_norm = plan.index(z, x, c) * plan.norm_each
                tail = [jnp.zeros((plan.tail, LANE), jnp.float32)]
                for row in range(min(first_norm + plan.norm_each, plan.norm_rows) - 1, first_norm - 1, -1):
                    part = norm_ref[row * LANE // D : row * LANE // D + 1, row * LANE % D : row * LANE % D + LANE]
                    tail.insert(0, part.astype(jnp.float32))
                tail = jnp.concatenate(tail, 0)[: plan.tail]
                moved[pl.ds(pl.multiple_of(start + plan.own, 8), plan.tail), :] = tail
                result = jnp.where(mine, rank + start, result)
    position_ref[...] = result
    to_scalar = pltpu.make_async_copy(position_ref, position, sem_position)
    to_scalar.start()
    to_scalar.wait()
    fetch.wait()

    @pl.loop(0, plan.blocks // LANE)
    def _(line):
        for part in range(0, LANE, 16):
            rows = raw[pl.ds(pl.multiple_of(line * LANE + part, 16), 16), :].astype(jnp.float32)
            for u in range(16):
                moved[pl.ds(position[line, part + u], 1), :] = rows[u : u + 1, :]

    copies = []
    for i, out in enumerate(out_refs):
        start = (i // plan.nz) * plan.half + (plan.nz - 1 - i % plan.nz) * plan.group
        copies.append(pltpu.make_async_copy(moved.at[pl.ds(start, plan.group)], out, sem_out.at[i]))
    for copy in copies:
        copy.start()
    for copy in copies:
        copy.wait()


def place(plan, my_place, owners, norm_grads, grads):
    shapes = [(plan.group, LANE)] * (2 * plan.nz)
    outs = pl.pallas_call(
        functools.partial(place_kernel, plan),
        out_shape=[jax.ShapeDtypeStruct(s, jnp.float32) for s in shapes]
        + [jax.ShapeDtypeStruct((plan.lists, LANE), jnp.int32)],
        in_specs=[
            pl.BlockSpec(memory_space=pltpu.SMEM),
            pl.BlockSpec(memory_space=pltpu.VMEM),
            pl.BlockSpec(memory_space=pltpu.VMEM),
            pl.BlockSpec(memory_space=pl.ANY),
        ],
        out_specs=[pl.BlockSpec(memory_space=pl.ANY)] * len(shapes) + [pl.BlockSpec(memory_space=pltpu.VMEM)],
        scratch_shapes=[
            pltpu.VMEM((plan.blocks, LANE), jnp.bfloat16),
            pltpu.VMEM((2 * plan.half, LANE), jnp.float32),
            pltpu.SMEM((plan.lists, LANE), jnp.int32),
            pltpu.SemaphoreType.DMA,
            pltpu.SemaphoreType.DMA,
            pltpu.SemaphoreType.DMA((len(shapes),)),
        ],
        compiler_params=pltpu.CompilerParams(vmem_limit_bytes=58 * MIB),
        name="place_gradients",
    )(my_place, owners, norm_grads, grads)
    return outs[: plan.nz][::-1], outs[plan.nz : 2 * plan.nz][::-1], outs[-1]


def owned_kernel(plan, place_ref, owner_ref, weights_ref, owned_ref, natural_ref, held, listed, order, sem_in, sem_order):
    fetch = pltpu.make_async_copy(weights_ref, held, sem_in)
    fetch.start()
    lists = plan.lists
    me = plan.index(place_ref[0], place_ref[1], place_ref[2])
    flags = (owner_ref[...] == me).astype(jnp.float32).astype(jnp.bfloat16)
    lane_in = lax.broadcasted_iota(jnp.int32, (LANE, LANE), 0)
    lane_out = lax.broadcasted_iota(jnp.int32, (LANE, LANE), 1)
    upto = (lane_in <= lane_out).astype(jnp.float32).astype(jnp.bfloat16)
    inner = jnp.dot(flags, upto, preferred_element_type=jnp.float32).astype(jnp.bfloat16)
    totals = lax.dot_general(
        jnp.ones((8, LANE), jnp.bfloat16), flags, (((1,), (1,)), ((), ())), preferred_element_type=jnp.float32
    )
    row_in = lax.broadcasted_iota(jnp.int32, (lists, lists), 0)
    row_out = lax.broadcasted_iota(jnp.int32, (lists, lists), 1)
    upto = (row_in <= row_out).astype(jnp.float32).astype(jnp.bfloat16)
    ends = jnp.dot(totals.astype(jnp.bfloat16), upto, preferred_element_type=jnp.float32)[0:1, :]
    place_of = lax.broadcasted_iota(jnp.int32, (LANE, lists), 1).astype(jnp.float32)
    rank_of = lax.broadcasted_iota(jnp.int32, (LANE, 1), 0)
    for step in range(listed.shape[0]):
        if step * LANE >= plan.own:
            break
        rank = (rank_of + step * LANE).astype(jnp.float32)
        passed = ends <= rank
        line = jnp.sum(passed.astype(jnp.float32), axis=1, keepdims=True)
        before = jnp.max(jnp.where(passed, ends, 0.0), axis=1, keepdims=True)
        chosen = (place_of == line).astype(jnp.float32).astype(jnp.bfloat16)
        counts = jnp.dot(chosen, inner, preferred_element_type=jnp.float32)
        column = jnp.sum((counts <= rank - before).astype(jnp.float32), axis=1, keepdims=True)
        block = jnp.broadcast_to((line * LANE + column).astype(jnp.int32), (LANE, LANE))
        natural_ref[step * LANE : (step + 1) * LANE, :] = block
        listed[step : step + 1, :] = jnp.sum(jnp.where(lane_in == lane_out, block, 0), axis=0, keepdims=True)
    to_scalar = pltpu.make_async_copy(listed, order, sem_order)
    to_scalar.start()
    to_scalar.wait()
    fetch.wait()

    def pick(line, count):
        for u in range(count):
            owned_ref[pl.ds(line * LANE + u, 1), :] = held[pl.ds(order[line, u], 1), :]

    @pl.loop(0, plan.own // LANE)
    def _(line):
        pick(line, LANE)

    if plan.own % LANE:
        pick(plan.own // LANE, plan.own % LANE)


def owned(plan, my_place, owners, weights):
    high_rows = -(-plan.own // (8 * LANE)) * 8
    ranks = -(-plan.own // LANE) * LANE
    vmem = pl.BlockSpec(memory_space=pltpu.VMEM)
    return pl.pallas_call(
        functools.partial(owned_kernel, plan),
        out_shape=[
            jax.ShapeDtypeStruct((plan.own, LANE), jnp.float32),
            jax.ShapeDtypeStruct((ranks, LANE), jnp.int32),
        ],
        in_specs=[pl.BlockSpec(memory_space=pltpu.SMEM), vmem, pl.BlockSpec(memory_space=pl.ANY)],
        out_specs=[vmem] * 2,
        scratch_shapes=[
            pltpu.VMEM((plan.blocks, LANE), jnp.float32),
            pltpu.VMEM((high_rows, LANE), jnp.int32),
            pltpu.SMEM((high_rows, LANE), jnp.int32),
            pltpu.SemaphoreType.DMA,
            pltpu.SemaphoreType.DMA,
        ],
        compiler_params=pltpu.CompilerParams(vmem_limit_bytes=58 * MIB),
        cost_estimate=pl.CostEstimate(flops=0, bytes_accessed=20 * MIB, transcendentals=0),
        name="owned_weights",
    )(my_place, owners, weights)


def update_kernel(plan, terms, *refs):
    parts, refs = refs[:terms], refs[terms:]
    first_ref, second_ref, weight_ref, natural_ref = refs[:4]
    new_first_ref, new_second_ref, block_ref, stats_ref = refs[4:]
    gradient = parts[0][: plan.block, :]
    for part in parts[1:]:
        gradient = gradient + part[: plan.block, :]
    block_ref[plan.own :, :] = gradient[plan.own :, :]
    gradient = gradient[: plan.own, :]
    moment_one = beta_one * first_ref[...] + (1.0 - beta_one) * gradient
    moment_two = beta_two * second_ref[...] + (1.0 - beta_two) * gradient * gradient
    new_first_ref[...] = moment_one
    new_second_ref[...] = moment_two
    step = moment_one / bias_one / (jnp.sqrt(moment_two / bias_two) + epsilon)
    block_ref[: plan.own, :] = step
    weight = weight_ref[...]
    direction = step + decay_rate * weight
    natural = natural_ref[: plan.own, :]
    limits = (0,) + plan.bounds + (plan.blocks,)
    lane = lax.broadcasted_iota(jnp.int32, (8, LANE), 1)
    rank = lax.broadcasted_iota(jnp.int32, (8, LANE), 0)
    stats = jnp.zeros((8, LANE), jnp.float32)
    for column, squares in enumerate((weight * weight, direction * direction)):
        for k in range(matrices):
            inside = (natural >= limits[k]) & (natural < limits[k + 1])
            kept = jnp.where(inside, squares, 0.0).reshape(plan.own // 8, 8, LANE)
            total = jnp.sum(jnp.sum(kept, axis=0))
            stats = jnp.where((rank == plan.norm_each + k) & (lane == column), total, stats)
    stats_ref[...] = stats


def update(plan, parts, first, second, weight, natural):
    vmem = pl.BlockSpec(memory_space=pltpu.VMEM)
    shapes = [(plan.own, LANE), (plan.own, LANE), (plan.block, LANE), (plan.tail, LANE)]
    return pl.pallas_call(
        functools.partial(update_kernel, plan, len(parts)),
        out_shape=[jax.ShapeDtypeStruct(s, jnp.float32) for s in shapes],
        in_specs=[vmem] * (len(parts) + 4),
        out_specs=[vmem] * len(shapes),
        compiler_params=pltpu.CompilerParams(vmem_limit_bytes=20 * MIB),
        name="moments",
    )(*parts, first, second, weight, natural)


def adam_rows(gradient, moment_one, moment_two, weight):
    moment_one = beta_one * moment_one + (1.0 - beta_one) * gradient
    moment_two = beta_two * moment_two + (1.0 - beta_two) * gradient * gradient
    step = moment_one / bias_one / (jnp.sqrt(moment_two / bias_two) + epsilon) + decay_rate * weight
    return (moment_one, moment_two, step)


def finish_kernel(plan, tile, slots, place_ref, position_ref, norm_ref, weights_ref, *refs):
    pieces, refs = refs[: len(slots)], refs[len(slots) :]
    out_ref, new_norm_ref, trust_ref, held, norms, rates, sems = refs
    now = pl.program_id(0)

    @pl.when(now == 0)
    def _():
        copies = [
            pltpu.make_async_copy(piece, held.at[pl.ds(plan.start(*slot), plan.block)], sems.at[i])
            for i, (piece, slot) in enumerate(zip(pieces, slots))
        ]
        for copy in copies:
            copy.start()
        for copy in copies:
            copy.wait()
        total = jnp.zeros((plan.tail, LANE), jnp.float32)
        for z in range(plan.nz):
            for x in range(plan.nx):
                for c in range(2):
                    start = plan.start(place_ref[0] ^ z, place_ref[1] ^ x, place_ref[2] ^ c) + plan.own
                    tail = held[pl.ds(pl.multiple_of(start, 8), plan.tail), :]
                    total = total + tail
                    first = plan.index(z, x, c) * plan.norm_each
                    for row in range(first, min(first + plan.norm_each, plan.norm_rows)):
                        norms[row : row + 1, :] = tail[row - first : row - first + 1, :]
        for k in range(matrices):
            row = plan.norm_each + k
            weight_square, direction_square = total[row : row + 1, 0:1], total[row : row + 1, 1:2]
            ratio = jnp.sqrt(weight_square) / (jnp.sqrt(direction_square) + epsilon)
            rates[k : k + 1, :] = jnp.broadcast_to(learning * ratio, (1, LANE))
            trust_ref[k] = jnp.sum(ratio)
        each = plan.norm_rows // 2
        for i in range(2):
            rows = pl.ds(i * each, each)
            gains = norm_ref[0, rows, :]
            one, two, step = adam_rows(norms[rows, :], norm_ref[1, rows, :], norm_ref[2, rows, :], gains)
            gain_square = jnp.sum(jnp.sum(gains * gains, axis=1, keepdims=True), axis=0, keepdims=True)
            step_square = jnp.sum(jnp.sum(step * step, axis=1, keepdims=True), axis=0, keepdims=True)
            ratio = jnp.sqrt(gain_square) / (jnp.sqrt(step_square) + epsilon)
            trust_ref[matrices + i] = jnp.sum(ratio)
            for j, value in enumerate((gains - learning * ratio * step, one, two)):
                for row in range(each):
                    new_norm_ref[j, i : i + 1, row * LANE : (row + 1) * LANE] = value[row : row + 1, :]

    matrix = jnp.int32(0)
    for bound in plan.bounds:
        matrix = matrix + (now * tile >= bound).astype(jnp.int32)
    rate = jnp.broadcast_to(rates[pl.ds(matrix, 1), :], (8, LANE))
    lines = tile // LANE

    @pl.loop(0, lines)
    def _(line):
        for group in range(0, LANE, 8):
            rows = [held[pl.ds(position_ref[now * lines + line, group + u], 1), :] for u in range(8)]
            here = pl.ds(pl.multiple_of(line * LANE + group, 8), 8)
            weight = weights_ref[here, :]
            direction = jnp.concatenate(rows, 0) + decay_rate * weight
            out_ref[here, :] = weight - rate * direction


def finish(plan, my_place, position, norm_state, weights, pieces, slots):
    tile = LANE
    while tile < 1024 and all(b % (2 * tile) == 0 for b in plan.bounds + (plan.blocks,)):
        tile *= 2
    smem = pl.BlockSpec(memory_space=pltpu.SMEM)
    vmem = pl.BlockSpec(memory_space=pltpu.VMEM)
    return pl.pallas_call(
        functools.partial(finish_kernel, plan, tile, slots),
        grid=(plan.blocks // tile,),
        out_shape=[
            jax.ShapeDtypeStruct((plan.blocks, LANE), jnp.float32),
            jax.ShapeDtypeStruct(norm_state.shape, jnp.float32),
            jax.ShapeDtypeStruct((matrices + 2,), jnp.float32),
        ],
        in_specs=[smem, smem, vmem, pl.BlockSpec((tile, LANE), lambda i: (i, 0))]
        + [pl.BlockSpec(memory_space=pl.ANY)] * len(pieces),
        out_specs=[pl.BlockSpec((tile, LANE), lambda i: (i, 0)), vmem, smem],
        scratch_shapes=[
            pltpu.VMEM((2 * plan.half, LANE), jnp.float32),
            pltpu.VMEM((plan.norm_rows, LANE), jnp.float32),
            pltpu.VMEM((8, LANE), jnp.float32),
            pltpu.SemaphoreType.DMA((len(pieces),)),
        ],
        compiler_params=pltpu.CompilerParams(vmem_limit_bytes=58 * MIB),
        name="new_weights",
    )(my_place, position, norm_state.reshape(3, plan.norm_rows, LANE), weights, *pieces)


def local(gradients, weights, first_moment, second_moment, owner_list, norm_grads, norm_state):
    plan = Plan(lax.axis_size("dp"), lax.axis_size("mp"), weights.shape[0])
    me = lax.axis_index("dp").astype(jnp.int32)
    my_place = jnp.stack([me // (2 * plan.nx), (me // 2) % plan.nx, me % 2]).astype(jnp.int32)
    owners = jnp.pad(owner_list[0], (0, plan.lists * LANE - plan.blocks), constant_values=-1)
    owners = owners.reshape(plan.lists, LANE)
    siblings, blocks, position = place(plan, my_place, owners, norm_grads[0], gradients[0])
    weight_own, natural = owned(plan, my_place, owners, weights)

    mine, theirs = [None] * plan.nz, [None] * plan.nz
    for z in reversed(range(plan.nz)):
        other = plan.swap(siblings[z])
        both = [
            blocks[z][x * plan.block : (x + 1) * plan.block] + other[x * plan.block : (x + 1) * plan.block]
            for x in range(plan.nx)
        ]
        mine[z], theirs[z] = both[0], both[1:]
    if plan.nz == 4:
        theirs[:3] = together(*theirs[:3])
        mine[2], weight_own, natural = together(mine[2], weight_own, natural)
    near = []
    for z in reversed(range(plan.nz)):
        terms = line_reduce(plan, "x", [mine[z]] + theirs[z])
        near.insert(0, sum(terms[1:], terms[0]) if z else None)
    parts = terms + line_reduce(plan, "z", near)[1:]
    new_first, new_second, block, stats = update(
        plan, parts, first_moment[0], second_moment[0], weight_own, natural
    )

    hop = 1
    while hop < plan.narrow:
        stats = stats + lax.ppermute(stats, "mp", [(i, i ^ hop) for i in range(plan.narrow)])
        hop *= 2
    block = lax.dynamic_update_slice(block, block[plan.own :] + stats, (plan.own, 0))
    found = gather(plan, block)
    slots, pieces = [slot for slot, _ in found], [piece for _, piece in found]
    new_weights, new_state, trust_ratios = finish(plan, my_place, position, norm_state, weights, pieces, slots)
    return (new_weights, new_first[None], new_second[None], new_state, trust_ratios)


def solution(mesh):
    in_specs = (
        P("dp", "mp", None),
        P("mp", None),
        P("mp", "dp", None),
        P("mp", "dp", None),
        P("mp", None),
        P("dp", None, None),
        P(),
    )
    out_specs = (P("mp", None), P("mp", "dp", None), P("mp", "dp", None), P(), P())
    return jax.shard_map(local, mesh=mesh, in_specs=in_specs, out_specs=out_specs, check_vma=False)
```

```python
import functools

import jax
import jax.numpy as jnp
from jax import lax
from jax.experimental import pallas as pl
from jax.experimental.pallas import tpu as pltpu
from jax.sharding import PartitionSpec as P

D = 1024
NTAB = 8
NKEYS = 256
KDIM = 128
LANE = 128
VROW_DEV = 512

beta_one = 0.9
beta_two = 0.99
bias_one = 1.0 - 0.9**4
bias_two = 1.0 - 0.99**4
epsilon = 1e-06
learning = 0.02
decay_rate = 0.01
matrices = 5
MIB = 1 << 20


def matrix_bounds(narrow):
    query_blocks = D * D // (LANE * narrow)
    key_blocks = NTAB * NKEYS * KDIM // (LANE * narrow)
    value_blocks = VROW_DEV * D // LANE
    return (
        query_blocks,
        query_blocks + key_blocks,
        query_blocks + key_blocks + value_blocks,
        2 * query_blocks + key_blocks + value_blocks,
    )


class Plan:
    def __init__(self, replicas, narrow, blocks):
        self.replicas, self.narrow, self.blocks = replicas, narrow, blocks
        chips = replicas // 2
        self.nz = 4 if chips % 4 == 0 else chips
        self.nx = chips // self.nz
        assert self.nz in (1, 2, 4) and self.nx in (1, 2, 4)
        self.own = blocks // replicas
        self.tail = 8
        self.norm_rows = 2 * D // LANE
        self.norm_each = -(-self.norm_rows // replicas)
        self.block = self.own + self.tail
        self.group = self.nx * self.block
        self.half = self.nz * self.group
        self.lists = -(-blocks // (8 * LANE)) * 8
        self.bounds = matrix_bounds(narrow)

    def index(self, z, x, c):
        return (z * self.nx + x) * 2 + c

    def start(self, far_z, far_x, far_c):
        return (1 - far_c) * self.half + far_z * self.group + far_x * self.block

    def send(self, value, axis, pairs):
        every = []
        for z in range(self.nz):
            for x in range(self.nx):
                for c in range(2):
                    here = {"z": z, "x": x, "c": c}
                    for source, target in pairs:
                        if here[axis] == source:
                            every.append((self.index(z, x, c), self.index(**{**here, axis: target})))
        return lax.ppermute(value, "dp", every)

    def swap(self, value):
        return self.send(value, "c", PAIR)


PAIR = [(0, 1), (1, 0)]
PAIRS = [(0, 1), (1, 0), (2, 3), (3, 2)]
MIDDLE = [(1, 2), (2, 1)]
INWARD = [(0, 1), (3, 2)]
OUTWARD = [(1, 0), (2, 3)]


def line_reduce(plan, axis, blocks):
    if len(blocks) == 1:
        return [blocks[0]]
    if len(blocks) == 2:
        return [blocks[0], plan.send(blocks[1], axis, PAIR)]
    in_three = plan.send(blocks[3], axis, INWARD)
    in_two = plan.send(blocks[2], axis, INWARD)
    across_two = plan.send(blocks[2] + in_three, axis, MIDDLE)
    across_three = plan.send(blocks[3] + in_two, axis, MIDDLE)
    pair = plan.send(blocks[1] + across_two, axis, PAIRS)
    return [blocks[0], pair, across_three]


def together(*values):
    return lax.optimization_barrier(values)


def reduce(plan, mine, theirs, beside):
    def along_x(z, own):
        terms = line_reduce(plan, "x", [own] + theirs[z])
        return terms

    three = along_x(3, mine[3])
    two = along_x(2, mine[2])
    near_three = sum(three[1:], three[0])
    in_three = plan.send(near_three, "z", INWARD)
    in_three, *two = together(in_three, *two, *beside)
    two, beside = two[: -len(beside)], two[-len(beside) :]
    near_two = sum(two[1:], two[0])
    one = along_x(1, mine[1])
    across_two = plan.send(near_two + in_three, "z", MIDDLE)
    in_two = plan.send(near_two, "z", INWARD)
    across_two, in_two, *one = together(across_two, in_two, *one)
    zero = along_x(0, mine[0])
    pair = plan.send(sum(one[1:], one[0]) + across_two, "z", PAIRS)
    across_three = plan.send(near_three + in_two, "z", MIDDLE)
    return zero + [pair, across_three] + beside


def gather(plan, block):
    found = {}

    def add(far_z, line):
        for far_x, value in enumerate(line):
            found[far_z, far_x, 0] = value

    def along_x(value):
        return line_gather(plan, "x", plan.nx, value)

    def swapped(*far_zs):
        for far_z in far_zs:
            for far_x in range(plan.nx):
                found[far_z, far_x, 1] = plan.swap(found[far_z, far_x, 0])

    if plan.nz != 4:
        for far_z, value in enumerate(line_gather(plan, "z", plan.nz, block)):
            add(far_z, along_x(value))
            swapped(far_z)
        return list(found.items())
    line = along_x(block)
    pair = plan.send(block, "z", PAIRS)
    three = plan.send(block, "z", MIDDLE)
    pair, three, *line = together(pair, three, *line)
    add(0, line)
    line = along_x(pair)
    two = plan.send(pair, "z", MIDDLE)
    out_two = plan.send(three, "z", OUTWARD)
    swapped(0)
    two, out_two, *line = together(two, out_two, *line)
    add(1, line)
    line = along_x(two + out_two)
    out_three = plan.send(two, "z", OUTWARD)
    swapped(1)
    out_three, *line = together(out_three, *line)
    add(2, line)
    add(3, along_x(three + out_three))
    swapped(2)
    swapped(3)
    return list(found.items())


def line_gather(plan, axis, count, value):
    if count == 1:
        return [value]
    if count == 2:
        return [value, plan.send(value, axis, PAIR)]
    pair = plan.send(value, axis, PAIRS)
    across_three = plan.send(value, axis, MIDDLE)
    across_two = plan.send(pair, axis, MIDDLE)
    out_two = plan.send(across_three, axis, OUTWARD)
    out_three = plan.send(across_two, axis, OUTWARD)
    return [value, pair, across_two + out_two, across_three + out_three]


def place_kernel(plan, place_ref, owner_ref, norm_ref, grads_ref, *refs):
    out_refs, refs = refs[: 2 * plan.nz], refs[2 * plan.nz :]
    position_ref, raw, moved, position, sem_in, sem_position, sem_out = refs
    fetch = pltpu.make_async_copy(grads_ref, raw, sem_in)
    fetch.start()
    lists = plan.lists
    owners = owner_ref[...]
    my_z, my_x, my_c = place_ref[0], place_ref[1], place_ref[2]
    lane_in = lax.broadcasted_iota(jnp.int32, (LANE, LANE), 0)
    lane_out = lax.broadcasted_iota(jnp.int32, (LANE, LANE), 1)
    before = (lane_in < lane_out).astype(jnp.bfloat16)
    every = jnp.ones((LANE, LANE), jnp.bfloat16)
    row_out = lax.broadcasted_iota(jnp.int32, (lists, lists), 0)
    row_in = lax.broadcasted_iota(jnp.int32, (lists, lists), 1)
    above = (row_in < row_out).astype(jnp.bfloat16)
    result = jnp.zeros((lists, LANE), jnp.int32)
    for z in range(plan.nz):
        for x in range(plan.nx):
            for c in range(2):
                mine = owners == plan.index(z, x, c)
                flags = mine.astype(jnp.float32).astype(jnp.bfloat16)
                inner = jnp.dot(flags, before, preferred_element_type=jnp.float32)
                totals = jnp.dot(flags, every, preferred_element_type=jnp.float32)
                outer = jnp.dot(above, totals.astype(jnp.bfloat16), preferred_element_type=jnp.float32)
                rank = (inner + outer).astype(jnp.int32)
                start = plan.start(my_z ^ z, my_x ^ x, my_c ^ c)
                first_norm = plan.index(z, x, c) * plan.norm_each
                tail = [jnp.zeros((plan.tail, LANE), jnp.float32)]
                for row in range(min(first_norm + plan.norm_each, plan.norm_rows) - 1, first_norm - 1, -1):
                    part = norm_ref[row * LANE // D : row * LANE // D + 1, row * LANE % D : row * LANE % D + LANE]
                    tail.insert(0, part.astype(jnp.float32))
                tail = jnp.concatenate(tail, 0)[: plan.tail]
                moved[pl.ds(pl.multiple_of(start + plan.own, 8), plan.tail), :] = tail
                result = jnp.where(mine, rank + start, result)
    position_ref[...] = result
    to_scalar = pltpu.make_async_copy(position_ref, position, sem_position)
    to_scalar.start()
    to_scalar.wait()
    fetch.wait()

    @pl.loop(0, plan.blocks // LANE)
    def _(line):
        for part in range(0, LANE, 16):
            rows = raw[pl.ds(pl.multiple_of(line * LANE + part, 16), 16), :].astype(jnp.float32)
            for u in range(16):
                moved[pl.ds(position[line, part + u], 1), :] = rows[u : u + 1, :]

    copies = []
    for i, out in enumerate(out_refs):
        start = (i // plan.nz) * plan.half + (plan.nz - 1 - i % plan.nz) * plan.group
        copies.append(pltpu.make_async_copy(moved.at[pl.ds(start, plan.group)], out, sem_out.at[i]))
    for copy in copies:
        copy.start()
    for copy in copies:
        copy.wait()


def place(plan, my_place, owners, norm_grads, grads):
    shapes = [(plan.group, LANE)] * (2 * plan.nz)
    outs = pl.pallas_call(
        functools.partial(place_kernel, plan),
        out_shape=[jax.ShapeDtypeStruct(s, jnp.float32) for s in shapes]
        + [jax.ShapeDtypeStruct((plan.lists, LANE), jnp.int32)],
        in_specs=[
            pl.BlockSpec(memory_space=pltpu.SMEM),
            pl.BlockSpec(memory_space=pltpu.VMEM),
            pl.BlockSpec(memory_space=pltpu.VMEM),
            pl.BlockSpec(memory_space=pl.ANY),
        ],
        out_specs=[pl.BlockSpec(memory_space=pl.ANY)] * len(shapes) + [pl.BlockSpec(memory_space=pltpu.VMEM)],
        scratch_shapes=[
            pltpu.VMEM((plan.blocks, LANE), jnp.bfloat16),
            pltpu.VMEM((2 * plan.half, LANE), jnp.float32),
            pltpu.SMEM((plan.lists, LANE), jnp.int32),
            pltpu.SemaphoreType.DMA,
            pltpu.SemaphoreType.DMA,
            pltpu.SemaphoreType.DMA((len(shapes),)),
        ],
        compiler_params=pltpu.CompilerParams(vmem_limit_bytes=58 * MIB),
        name="place_gradients",
    )(my_place, owners, norm_grads, grads)
    return list(outs[: plan.nz][::-1]), outs[plan.nz : 2 * plan.nz][::-1], outs[-1]


def owned_kernel(plan, place_ref, owner_ref, weights_ref, owned_ref, natural_ref, held, listed, order, sem_in, sem_order):
    fetch = pltpu.make_async_copy(weights_ref, held, sem_in)
    fetch.start()
    lists = plan.lists
    me = plan.index(place_ref[0], place_ref[1], place_ref[2])
    flags = (owner_ref[...] == me).astype(jnp.float32).astype(jnp.bfloat16)
    lane_in = lax.broadcasted_iota(jnp.int32, (LANE, LANE), 0)
    lane_out = lax.broadcasted_iota(jnp.int32, (LANE, LANE), 1)
    upto = (lane_in <= lane_out).astype(jnp.float32).astype(jnp.bfloat16)
    inner = jnp.dot(flags, upto, preferred_element_type=jnp.float32).astype(jnp.bfloat16)
    totals = lax.dot_general(
        jnp.ones((8, LANE), jnp.bfloat16), flags, (((1,), (1,)), ((), ())), preferred_element_type=jnp.float32
    )
    row_in = lax.broadcasted_iota(jnp.int32, (lists, lists), 0)
    row_out = lax.broadcasted_iota(jnp.int32, (lists, lists), 1)
    upto = (row_in <= row_out).astype(jnp.float32).astype(jnp.bfloat16)
    ends = jnp.dot(totals.astype(jnp.bfloat16), upto, preferred_element_type=jnp.float32)[0:1, :]
    place_of = lax.broadcasted_iota(jnp.int32, (LANE, lists), 1).astype(jnp.float32)
    rank_of = lax.broadcasted_iota(jnp.int32, (LANE, 1), 0)
    for step in range(listed.shape[0]):
        if step * LANE >= plan.own:
            break
        rank = (rank_of + step * LANE).astype(jnp.float32)
        passed = ends <= rank
        line = jnp.sum(passed.astype(jnp.float32), axis=1, keepdims=True)
        before = jnp.max(jnp.where(passed, ends, 0.0), axis=1, keepdims=True)
        chosen = (place_of == line).astype(jnp.float32).astype(jnp.bfloat16)
        counts = jnp.dot(chosen, inner, preferred_element_type=jnp.float32)
        column = jnp.sum((counts <= rank - before).astype(jnp.float32), axis=1, keepdims=True)
        block = jnp.broadcast_to((line * LANE + column).astype(jnp.int32), (LANE, LANE))
        natural_ref[step * LANE : (step + 1) * LANE, :] = block
        listed[step : step + 1, :] = jnp.sum(jnp.where(lane_in == lane_out, block, 0), axis=0, keepdims=True)
    to_scalar = pltpu.make_async_copy(listed, order, sem_order)
    to_scalar.start()
    to_scalar.wait()
    fetch.wait()

    def pick(line, count):
        for u in range(count):
            owned_ref[pl.ds(line * LANE + u, 1), :] = held[pl.ds(order[line, u], 1), :]

    @pl.loop(0, plan.own // LANE)
    def _(line):
        pick(line, LANE)

    if plan.own % LANE:
        pick(plan.own // LANE, plan.own % LANE)


def owned(plan, my_place, owners, weights):
    high_rows = -(-plan.own // (8 * LANE)) * 8
    ranks = -(-plan.own // LANE) * LANE
    vmem = pl.BlockSpec(memory_space=pltpu.VMEM)
    return pl.pallas_call(
        functools.partial(owned_kernel, plan),
        out_shape=[
            jax.ShapeDtypeStruct((plan.own, LANE), jnp.float32),
            jax.ShapeDtypeStruct((ranks, LANE), jnp.int32),
        ],
        in_specs=[pl.BlockSpec(memory_space=pltpu.SMEM), vmem, pl.BlockSpec(memory_space=pl.ANY)],
        out_specs=[vmem] * 2,
        scratch_shapes=[
            pltpu.VMEM((plan.blocks, LANE), jnp.float32),
            pltpu.VMEM((high_rows, LANE), jnp.int32),
            pltpu.SMEM((high_rows, LANE), jnp.int32),
            pltpu.SemaphoreType.DMA,
            pltpu.SemaphoreType.DMA,
        ],
        compiler_params=pltpu.CompilerParams(vmem_limit_bytes=58 * MIB),
        cost_estimate=pl.CostEstimate(flops=0, bytes_accessed=20 * MIB, transcendentals=0),
        name="owned_weights",
    )(my_place, owners, weights)


def update_kernel(plan, terms, *refs):
    parts, refs = refs[:terms], refs[terms:]
    first_ref, second_ref, weight_ref, natural_ref = refs[:4]
    new_first_ref, new_second_ref, block_ref, stats_ref = refs[4:]
    gradient = parts[0][: plan.block, :]
    for part in parts[1:]:
        gradient = gradient + part[: plan.block, :]
    block_ref[plan.own :, :] = gradient[plan.own :, :]
    gradient = gradient[: plan.own, :]
    moment_one = beta_one * first_ref[...] + (1.0 - beta_one) * gradient
    moment_two = beta_two * second_ref[...] + (1.0 - beta_two) * gradient * gradient
    new_first_ref[...] = moment_one
    new_second_ref[...] = moment_two
    step = moment_one / bias_one / (jnp.sqrt(moment_two / bias_two) + epsilon)
    block_ref[: plan.own, :] = step
    weight = weight_ref[...]
    direction = step + decay_rate * weight
    natural = natural_ref[: plan.own, :]
    limits = (0,) + plan.bounds + (plan.blocks,)
    lane = lax.broadcasted_iota(jnp.int32, (8, LANE), 1)
    rank = lax.broadcasted_iota(jnp.int32, (8, LANE), 0)
    stats = jnp.zeros((8, LANE), jnp.float32)
    for column, squares in enumerate((weight * weight, direction * direction)):
        for k in range(matrices):
            inside = (natural >= limits[k]) & (natural < limits[k + 1])
            kept = jnp.where(inside, squares, 0.0).reshape(plan.own // 8, 8, LANE)
            total = jnp.sum(jnp.sum(kept, axis=0))
            stats = jnp.where((rank == plan.norm_each + k) & (lane == column), total, stats)
    stats_ref[...] = stats


def update(plan, parts, first, second, weight, natural):
    vmem = pl.BlockSpec(memory_space=pltpu.VMEM)
    shapes = [(plan.own, LANE), (plan.own, LANE), (plan.block, LANE), (plan.tail, LANE)]
    return pl.pallas_call(
        functools.partial(update_kernel, plan, len(parts)),
        out_shape=[jax.ShapeDtypeStruct(s, jnp.float32) for s in shapes],
        in_specs=[vmem] * (len(parts) + 4),
        out_specs=[vmem] * len(shapes),
        compiler_params=pltpu.CompilerParams(vmem_limit_bytes=20 * MIB),
        name="moments",
    )(*parts, first, second, weight, natural)


def adam_rows(gradient, moment_one, moment_two, weight):
    moment_one = beta_one * moment_one + (1.0 - beta_one) * gradient
    moment_two = beta_two * moment_two + (1.0 - beta_two) * gradient * gradient
    step = moment_one / bias_one / (jnp.sqrt(moment_two / bias_two) + epsilon) + decay_rate * weight
    return (moment_one, moment_two, step)


def finish_kernel(plan, tile, slots, place_ref, position_ref, norm_ref, weights_ref, *refs):
    pieces, refs = refs[: len(slots)], refs[len(slots) :]
    out_ref, new_norm_ref, trust_ref, held, norms, rates, sems = refs
    now = pl.program_id(0)

    @pl.when(now == 0)
    def _():
        copies = [
            pltpu.make_async_copy(piece, held.at[pl.ds(plan.start(*slot), plan.block)], sems.at[i])
            for i, (piece, slot) in enumerate(zip(pieces, slots))
        ]
        for copy in copies:
            copy.start()
        for copy in copies:
            copy.wait()
        total = jnp.zeros((plan.tail, LANE), jnp.float32)
        for z in range(plan.nz):
            for x in range(plan.nx):
                for c in range(2):
                    start = plan.start(place_ref[0] ^ z, place_ref[1] ^ x, place_ref[2] ^ c) + plan.own
                    tail = held[pl.ds(pl.multiple_of(start, 8), plan.tail), :]
                    total = total + tail
                    first = plan.index(z, x, c) * plan.norm_each
                    for row in range(first, min(first + plan.norm_each, plan.norm_rows)):
                        norms[row : row + 1, :] = tail[row - first : row - first + 1, :]
        for k in range(matrices):
            row = plan.norm_each + k
            weight_square, direction_square = total[row : row + 1, 0:1], total[row : row + 1, 1:2]
            ratio = jnp.sqrt(weight_square) / (jnp.sqrt(direction_square) + epsilon)
            rates[k : k + 1, :] = jnp.broadcast_to(learning * ratio, (1, LANE))
            trust_ref[k] = jnp.sum(ratio)
        each = plan.norm_rows // 2
        for i in range(2):
            gains, first, second = (
                jnp.concatenate([norm_ref[j, i : i + 1, row * LANE : (row + 1) * LANE] for row in range(each)], 0)
                for j in range(3)
            )
            one, two, step = adam_rows(norms[i * each : (i + 1) * each, :], first, second, gains)
            gain_square = jnp.sum(jnp.sum(gains * gains, axis=1, keepdims=True), axis=0, keepdims=True)
            step_square = jnp.sum(jnp.sum(step * step, axis=1, keepdims=True), axis=0, keepdims=True)
            ratio = jnp.sqrt(gain_square) / (jnp.sqrt(step_square) + epsilon)
            trust_ref[matrices + i] = jnp.sum(ratio)
            for j, value in enumerate((gains - learning * ratio * step, one, two)):
                for row in range(each):
                    new_norm_ref[j, i : i + 1, row * LANE : (row + 1) * LANE] = value[row : row + 1, :]

    matrix = jnp.int32(0)
    for bound in plan.bounds:
        matrix = matrix + (now * tile >= bound).astype(jnp.int32)
    rate = jnp.broadcast_to(rates[pl.ds(matrix, 1), :], (8, LANE))
    lines = tile // LANE

    @pl.loop(0, lines)
    def _(line):
        for group in range(0, LANE, 8):
            rows = [held[pl.ds(position_ref[now * lines + line, group + u], 1), :] for u in range(8)]
            here = pl.ds(pl.multiple_of(line * LANE + group, 8), 8)
            weight = weights_ref[here, :]
            direction = jnp.concatenate(rows, 0) + decay_rate * weight
            out_ref[here, :] = weight - rate * direction


def finish(plan, my_place, position, norm_state, weights, pieces, slots):
    tile = LANE
    while tile < 1024 and all(b % (2 * tile) == 0 for b in plan.bounds + (plan.blocks,)):
        tile *= 2
    smem = pl.BlockSpec(memory_space=pltpu.SMEM)
    vmem = pl.BlockSpec(memory_space=pltpu.VMEM)
    return pl.pallas_call(
        functools.partial(finish_kernel, plan, tile, slots),
        grid=(plan.blocks // tile,),
        out_shape=[
            jax.ShapeDtypeStruct((plan.blocks, LANE), jnp.float32),
            jax.ShapeDtypeStruct(norm_state.shape, jnp.float32),
            jax.ShapeDtypeStruct((matrices + 2,), jnp.float32),
        ],
        in_specs=[smem, smem, vmem, pl.BlockSpec((tile, LANE), lambda i: (i, 0))]
        + [pl.BlockSpec(memory_space=pl.ANY)] * len(pieces),
        out_specs=[pl.BlockSpec((tile, LANE), lambda i: (i, 0)), vmem, smem],
        scratch_shapes=[
            pltpu.VMEM((2 * plan.half, LANE), jnp.float32),
            pltpu.VMEM((plan.norm_rows, LANE), jnp.float32),
            pltpu.VMEM((8, LANE), jnp.float32),
            pltpu.SemaphoreType.DMA((len(pieces),)),
        ],
        compiler_params=pltpu.CompilerParams(vmem_limit_bytes=58 * MIB),
        name="new_weights",
    )(my_place, position, norm_state, weights, *pieces)


def local(gradients, weights, first_moment, second_moment, owner_list, norm_grads, norm_state):
    plan = Plan(lax.axis_size("dp"), lax.axis_size("mp"), weights.shape[0])
    me = lax.axis_index("dp").astype(jnp.int32)
    my_place = jnp.stack([me // (2 * plan.nx), (me // 2) % plan.nx, me % 2]).astype(jnp.int32)
    owners = jnp.pad(owner_list[0], (0, plan.lists * LANE - plan.blocks), constant_values=-1)
    owners = owners.reshape(plan.lists, LANE)
    siblings, blocks, position = place(plan, my_place, owners, norm_grads[0], gradients[0])
    weight_own, natural = owned(plan, my_place, owners, weights)

    mine, theirs = [None] * plan.nz, [None] * plan.nz
    for z in reversed(range(plan.nz)):
        other = plan.swap(siblings[z])
        both = [
            blocks[z][x * plan.block : (x + 1) * plan.block] + other[x * plan.block : (x + 1) * plan.block]
            for x in range(plan.nx)
        ]
        mine[z], theirs[z] = both[0], both[1:]
        if z == 3:
            theirs[3], siblings[2], siblings[1], siblings[0] = together(theirs[3], *siblings[2::-1])
    if plan.nz == 4:
        parts = reduce(plan, mine, theirs, (weight_own, natural))
        parts, (weight_own, natural) = parts[:-2], parts[-2:]
    else:
        near = []
        for z in reversed(range(plan.nz)):
            terms = line_reduce(plan, "x", [mine[z]] + theirs[z])
            near.insert(0, sum(terms[1:], terms[0]) if z else None)
        parts = terms + line_reduce(plan, "z", near)[1:]
    new_first, new_second, block, stats = update(
        plan, parts, first_moment[0], second_moment[0], weight_own, natural
    )

    hop = 1
    while hop < plan.narrow:
        stats = stats + lax.ppermute(stats, "mp", [(i, i ^ hop) for i in range(plan.narrow)])
        hop *= 2
    block = lax.dynamic_update_slice(block, block[plan.own :] + stats, (plan.own, 0))
    found = gather(plan, block)
    slots, pieces = [slot for slot, _ in found], [piece for _, piece in found]
    new_weights, new_state, trust_ratios = finish(plan, my_place, position, norm_state, weights, pieces, slots)
    return (new_weights, new_first[None], new_second[None], new_state, trust_ratios)


def solution(mesh):
    in_specs = (
        P("dp", "mp", None),
        P("mp", None),
        P("mp", "dp", None),
        P("mp", "dp", None),
        P("mp", None),
        P("dp", None, None),
        P(),
    )
    out_specs = (P("mp", None), P("mp", "dp", None), P("mp", "dp", None), P(), P())
    return jax.shard_map(local, mesh=mesh, in_specs=in_specs, out_specs=out_specs, check_vma=False)
```

```python
import functools

import jax
import jax.numpy as jnp
from jax import lax
from jax.experimental import pallas as pl
from jax.experimental.pallas import tpu as pltpu
from jax.sharding import PartitionSpec as P

D = 1024
NTAB = 8
NKEYS = 256
KDIM = 128
LANE = 128
VROW_DEV = 512

beta_one = 0.9
beta_two = 0.99
bias_one = 1.0 - 0.9**4
bias_two = 1.0 - 0.99**4
epsilon = 1e-06
learning = 0.02
decay_rate = 0.01
matrices = 5
MIB = 1 << 20
SPLIT = 0.5


def matrix_bounds(narrow):
    query_blocks = D * D // (LANE * narrow)
    key_blocks = NTAB * NKEYS * KDIM // (LANE * narrow)
    value_blocks = VROW_DEV * D // LANE
    return (
        query_blocks,
        query_blocks + key_blocks,
        query_blocks + key_blocks + value_blocks,
        2 * query_blocks + key_blocks + value_blocks,
    )


class Plan:
    def __init__(self, replicas, narrow, blocks):
        self.replicas, self.narrow, self.blocks = replicas, narrow, blocks
        chips = replicas // 2
        self.nz = 4 if chips % 4 == 0 else chips
        self.nx = chips // self.nz
        assert self.nz in (1, 2, 4) and self.nx in (1, 2, 4)
        self.own = blocks // replicas
        self.tail = 8
        self.norm_rows = 2 * D // LANE
        self.norm_each = -(-self.norm_rows // replicas)
        first = int(self.own * SPLIT / 8 + 0.5) * 8
        self.rows = (first, self.own - first)
        self.blocks_of = (first + self.tail, self.own - first)
        self.groups = tuple(self.nx * block for block in self.blocks_of)
        self.offsets = (0, self.nz * self.groups[0])
        self.half = self.nz * sum(self.groups)
        self.lists = -(-blocks // (8 * LANE)) * 8
        self.bounds = matrix_bounds(narrow)

    def order(self):
        return [(z, stream, far_c) for far_c in (1, 0) for z in reversed(range(self.nz)) for stream in range(2)]

    def index(self, z, x, c):
        return (z * self.nx + x) * 2 + c

    def start(self, stream, far_z, far_x, far_c):
        there = far_z * self.groups[stream] + far_x * self.blocks_of[stream]
        return (1 - far_c) * self.half + self.offsets[stream] + there

    def send(self, value, axis, pairs):
        every = []
        for z in range(self.nz):
            for x in range(self.nx):
                for c in range(2):
                    here = {"z": z, "x": x, "c": c}
                    for source, target in pairs:
                        if here[axis] == source:
                            every.append((self.index(z, x, c), self.index(**{**here, axis: target})))
        return lax.ppermute(value, "dp", every)

    def swap(self, value):
        return self.send(value, "c", PAIR)


PAIR = [(0, 1), (1, 0)]
PAIRS = [(0, 1), (1, 0), (2, 3), (3, 2)]
MIDDLE = [(1, 2), (2, 1)]
INWARD = [(0, 1), (3, 2)]
OUTWARD = [(1, 0), (2, 3)]


def line_reduce(plan, axis, blocks):
    if len(blocks) == 1:
        return [blocks[0]]
    if len(blocks) == 2:
        return [blocks[0], plan.send(blocks[1], axis, PAIR)]
    in_three = plan.send(blocks[3], axis, INWARD)
    in_two = plan.send(blocks[2], axis, INWARD)
    across_two = plan.send(blocks[2] + in_three, axis, MIDDLE)
    across_three = plan.send(blocks[3] + in_two, axis, MIDDLE)
    pair = plan.send(blocks[1] + across_two, axis, PAIRS)
    return [blocks[0], pair, across_three]


def together(*values):
    return lax.optimization_barrier(values)


def reduce(plan, mine, theirs, beside):
    def along_x(z, own):
        terms = line_reduce(plan, "x", [own] + theirs[z])
        return terms

    three = along_x(3, mine[3])
    two = along_x(2, mine[2])
    near_three = sum(three[1:], three[0])
    in_three = plan.send(near_three, "z", INWARD)
    count = len(two)
    in_three, *two = together(in_three, *two, *beside)
    two, beside = two[:count], two[count:]
    near_two = sum(two[1:], two[0])
    one = along_x(1, mine[1])
    across_two = plan.send(near_two + in_three, "z", MIDDLE)
    in_two = plan.send(near_two, "z", INWARD)
    across_two, in_two, *one = together(across_two, in_two, *one)
    zero = along_x(0, mine[0])
    pair = plan.send(sum(one[1:], one[0]) + across_two, "z", PAIRS)
    across_three = plan.send(near_three + in_two, "z", MIDDLE)
    return zero + [pair, across_three] + beside


def gather(plan, block):
    found = {}

    def add(far_z, line):
        for far_x, value in enumerate(line):
            found[far_z, far_x, 0] = value

    def along_x(value):
        return line_gather(plan, "x", plan.nx, value)

    def swapped(*far_zs):
        for far_z in far_zs:
            for far_x in range(plan.nx):
                found[far_z, far_x, 1] = plan.swap(found[far_z, far_x, 0])

    if plan.nz != 4:
        for far_z, value in enumerate(line_gather(plan, "z", plan.nz, block)):
            add(far_z, along_x(value))
            swapped(far_z)
        return list(found.items())
    line = along_x(block)
    pair = plan.send(block, "z", PAIRS)
    three = plan.send(block, "z", MIDDLE)
    pair, three, *line = together(pair, three, *line)
    add(0, line)
    line = along_x(pair)
    two = plan.send(pair, "z", MIDDLE)
    out_two = plan.send(three, "z", OUTWARD)
    swapped(0)
    two, out_two, *line = together(two, out_two, *line)
    add(1, line)
    line = along_x(two + out_two)
    out_three = plan.send(two, "z", OUTWARD)
    swapped(1)
    out_three, *line = together(out_three, *line)
    add(2, line)
    add(3, along_x(three + out_three))
    swapped(2)
    swapped(3)
    return list(found.items())


def line_gather(plan, axis, count, value):
    if count == 1:
        return [value]
    if count == 2:
        return [value, plan.send(value, axis, PAIR)]
    pair = plan.send(value, axis, PAIRS)
    across_three = plan.send(value, axis, MIDDLE)
    across_two = plan.send(pair, axis, MIDDLE)
    out_two = plan.send(across_three, axis, OUTWARD)
    out_three = plan.send(across_two, axis, OUTWARD)
    return [value, pair, across_two + out_two, across_three + out_three]


def place_kernel(plan, place_ref, owner_ref, norm_ref, grads_ref, *refs):
    out_refs, refs = refs[: 4 * plan.nz], refs[4 * plan.nz :]
    position_ref, limit_ref, raw, moved, position, sem_in, sem_position, sem_out = refs
    fetch = pltpu.make_async_copy(grads_ref, raw, sem_in)
    fetch.start()
    lists = plan.lists
    owners = owner_ref[...]
    my_z, my_x, my_c = place_ref[0], place_ref[1], place_ref[2]
    lane_in = lax.broadcasted_iota(jnp.int32, (LANE, LANE), 0)
    lane_out = lax.broadcasted_iota(jnp.int32, (LANE, LANE), 1)
    before = (lane_in < lane_out).astype(jnp.bfloat16)
    every = jnp.ones((LANE, LANE), jnp.bfloat16)
    row_out = lax.broadcasted_iota(jnp.int32, (lists, lists), 0)
    row_in = lax.broadcasted_iota(jnp.int32, (lists, lists), 1)
    above = (row_in < row_out).astype(jnp.bfloat16)
    result = jnp.zeros((lists, LANE), jnp.int32)
    second = jnp.zeros((lists, LANE), jnp.bool_)
    for z in range(plan.nz):
        for x in range(plan.nx):
            for c in range(2):
                mine = owners == plan.index(z, x, c)
                flags = mine.astype(jnp.float32).astype(jnp.bfloat16)
                inner = jnp.dot(flags, before, preferred_element_type=jnp.float32)
                totals = jnp.dot(flags, every, preferred_element_type=jnp.float32)
                outer = jnp.dot(above, totals.astype(jnp.bfloat16), preferred_element_type=jnp.float32)
                rank = (inner + outer).astype(jnp.int32)
                slot = (my_z ^ z, my_x ^ x, my_c ^ c)
                start, start_second = plan.start(0, *slot), plan.start(1, *slot) - plan.rows[0]
                first_norm = plan.index(z, x, c) * plan.norm_each
                tail = [jnp.zeros((plan.tail, LANE), jnp.float32)]
                for row in range(min(first_norm + plan.norm_each, plan.norm_rows) - 1, first_norm - 1, -1):
                    part = norm_ref[row * LANE // D : row * LANE // D + 1, row * LANE % D : row * LANE % D + LANE]
                    tail.insert(0, part.astype(jnp.float32))
                tail = jnp.concatenate(tail, 0)[: plan.tail]
                moved[pl.ds(pl.multiple_of(start + plan.rows[0], 8), plan.tail), :] = tail
                late = mine & (rank >= plan.rows[0])
                second = second | late
                result = jnp.where(mine, rank + jnp.where(late, start_second, start), result)
    position_ref[...] = result
    natural = lax.broadcasted_iota(jnp.int32, (lists, LANE), 0) * LANE + lax.broadcasted_iota(jnp.int32, (lists, LANE), 1)
    limit_ref[0] = jnp.min(jnp.where(second, natural, plan.blocks))
    to_scalar = pltpu.make_async_copy(position_ref, position, sem_position)
    to_scalar.start()
    to_scalar.wait()
    fetch.wait()

    @pl.loop(0, plan.blocks // LANE)
    def _(line):
        for part in range(0, LANE, 16):
            rows = raw[pl.ds(pl.multiple_of(line * LANE + part, 16), 16), :].astype(jnp.float32)
            for u in range(16):
                moved[pl.ds(position[line, part + u], 1), :] = rows[u : u + 1, :]

    copies = []
    for i, (out, (z, stream, far_c)) in enumerate(zip(out_refs, plan.order())):
        start = plan.start(stream, z, 0, far_c)
        copies.append(pltpu.make_async_copy(moved.at[pl.ds(start, plan.groups[stream])], out, sem_out.at[i]))
    for copy in copies:
        copy.start()
    for copy in copies:
        copy.wait()


def place(plan, my_place, owners, norm_grads, grads):
    shapes = [(plan.groups[stream], LANE) for _, stream, _ in plan.order()]
    outs = pl.pallas_call(
        functools.partial(place_kernel, plan),
        out_shape=[jax.ShapeDtypeStruct(s, jnp.float32) for s in shapes]
        + [jax.ShapeDtypeStruct((plan.lists, LANE), jnp.int32), jax.ShapeDtypeStruct((1,), jnp.int32)],
        in_specs=[
            pl.BlockSpec(memory_space=pltpu.SMEM),
            pl.BlockSpec(memory_space=pltpu.VMEM),
            pl.BlockSpec(memory_space=pltpu.VMEM),
            pl.BlockSpec(memory_space=pl.ANY),
        ],
        out_specs=[pl.BlockSpec(memory_space=pl.ANY)] * len(shapes)
        + [pl.BlockSpec(memory_space=pltpu.VMEM), pl.BlockSpec(memory_space=pltpu.SMEM)],
        scratch_shapes=[
            pltpu.VMEM((plan.blocks, LANE), jnp.bfloat16),
            pltpu.VMEM((2 * plan.half, LANE), jnp.float32),
            pltpu.SMEM((plan.lists, LANE), jnp.int32),
            pltpu.SemaphoreType.DMA,
            pltpu.SemaphoreType.DMA,
            pltpu.SemaphoreType.DMA((len(shapes),)),
        ],
        compiler_params=pltpu.CompilerParams(vmem_limit_bytes=58 * MIB),
        name="place_gradients",
    )(my_place, owners, norm_grads, grads)
    return dict(zip(plan.order(), outs)), outs[-2], outs[-1]


def owned_kernel(plan, place_ref, owner_ref, weights_ref, owned_ref, natural_ref, held, listed, order, sem_in, sem_order):
    fetch = pltpu.make_async_copy(weights_ref, held, sem_in)
    fetch.start()
    lists = plan.lists
    me = plan.index(place_ref[0], place_ref[1], place_ref[2])
    flags = (owner_ref[...] == me).astype(jnp.float32).astype(jnp.bfloat16)
    lane_in = lax.broadcasted_iota(jnp.int32, (LANE, LANE), 0)
    lane_out = lax.broadcasted_iota(jnp.int32, (LANE, LANE), 1)
    upto = (lane_in <= lane_out).astype(jnp.float32).astype(jnp.bfloat16)
    inner = jnp.dot(flags, upto, preferred_element_type=jnp.float32).astype(jnp.bfloat16)
    totals = lax.dot_general(
        jnp.ones((8, LANE), jnp.bfloat16), flags, (((1,), (1,)), ((), ())), preferred_element_type=jnp.float32
    )
    row_in = lax.broadcasted_iota(jnp.int32, (lists, lists), 0)
    row_out = lax.broadcasted_iota(jnp.int32, (lists, lists), 1)
    upto = (row_in <= row_out).astype(jnp.float32).astype(jnp.bfloat16)
    ends = jnp.dot(totals.astype(jnp.bfloat16), upto, preferred_element_type=jnp.float32)[0:1, :]
    place_of = lax.broadcasted_iota(jnp.int32, (LANE, lists), 1).astype(jnp.float32)
    rank_of = lax.broadcasted_iota(jnp.int32, (LANE, 1), 0)
    for step in range(listed.shape[0]):
        if step * LANE >= plan.own:
            break
        rank = (rank_of + step * LANE).astype(jnp.float32)
        passed = ends <= rank
        line = jnp.sum(passed.astype(jnp.float32), axis=1, keepdims=True)
        before = jnp.max(jnp.where(passed, ends, 0.0), axis=1, keepdims=True)
        chosen = (place_of == line).astype(jnp.float32).astype(jnp.bfloat16)
        counts = jnp.dot(chosen, inner, preferred_element_type=jnp.float32)
        column = jnp.sum((counts <= rank - before).astype(jnp.float32), axis=1, keepdims=True)
        block = jnp.broadcast_to((line * LANE + column).astype(jnp.int32), (LANE, LANE))
        natural_ref[step * LANE : (step + 1) * LANE, :] = block
        listed[step : step + 1, :] = jnp.sum(jnp.where(lane_in == lane_out, block, 0), axis=0, keepdims=True)
    to_scalar = pltpu.make_async_copy(listed, order, sem_order)
    to_scalar.start()
    to_scalar.wait()
    fetch.wait()

    def pick(line, count):
        for u in range(count):
            owned_ref[pl.ds(line * LANE + u, 1), :] = held[pl.ds(order[line, u], 1), :]

    @pl.loop(0, plan.own // LANE)
    def _(line):
        pick(line, LANE)

    if plan.own % LANE:
        pick(plan.own // LANE, plan.own % LANE)


def owned(plan, my_place, owners, weights):
    high_rows = -(-plan.own // (8 * LANE)) * 8
    ranks = -(-plan.own // LANE) * LANE
    vmem = pl.BlockSpec(memory_space=pltpu.VMEM)
    return pl.pallas_call(
        functools.partial(owned_kernel, plan),
        out_shape=[
            jax.ShapeDtypeStruct((plan.own, LANE), jnp.float32),
            jax.ShapeDtypeStruct((ranks, LANE), jnp.int32),
        ],
        in_specs=[pl.BlockSpec(memory_space=pltpu.SMEM), vmem, pl.BlockSpec(memory_space=pl.ANY)],
        out_specs=[vmem] * 2,
        scratch_shapes=[
            pltpu.VMEM((plan.blocks, LANE), jnp.float32),
            pltpu.VMEM((high_rows, LANE), jnp.int32),
            pltpu.SMEM((high_rows, LANE), jnp.int32),
            pltpu.SemaphoreType.DMA,
            pltpu.SemaphoreType.DMA,
        ],
        compiler_params=pltpu.CompilerParams(vmem_limit_bytes=58 * MIB),
        cost_estimate=pl.CostEstimate(flops=0, bytes_accessed=20 * MIB, transcendentals=0),
        name="owned_weights",
    )(my_place, owners, weights)


def update_kernel(plan, counts, *refs):
    parts, refs = refs[: sum(counts)], refs[sum(counts) :]
    first_ref, second_ref, weight_ref, natural_ref = refs[:4]
    new_first_ref, new_second_ref, block_ref, block_second_ref, stats_ref = refs[4:]
    gradients = []
    for stream, terms in enumerate((parts[: counts[0]], parts[counts[0] :])):
        gradient = terms[0][...]
        for term in terms[1:]:
            gradient = gradient + term[...]
        gradients.append(gradient)
    block_ref[plan.rows[0] :, :] = gradients[0][plan.rows[0] :, :]
    gradient = jnp.concatenate([gradients[0][: plan.rows[0], :], gradients[1]], 0)
    moment_one = beta_one * first_ref[...] + (1.0 - beta_one) * gradient
    moment_two = beta_two * second_ref[...] + (1.0 - beta_two) * gradient * gradient
    new_first_ref[...] = moment_one
    new_second_ref[...] = moment_two
    step = moment_one / bias_one / (jnp.sqrt(moment_two / bias_two) + epsilon)
    block_ref[: plan.rows[0], :] = step[: plan.rows[0], :]
    block_second_ref[...] = step[plan.rows[0] :, :]
    weight = weight_ref[...]
    direction = step + decay_rate * weight
    natural = natural_ref[: plan.own, :]
    limits = (0,) + plan.bounds + (plan.blocks,)
    lane = lax.broadcasted_iota(jnp.int32, (8, LANE), 1)
    rank = lax.broadcasted_iota(jnp.int32, (8, LANE), 0)
    stats = jnp.zeros((8, LANE), jnp.float32)
    for column, squares in enumerate((weight * weight, direction * direction)):
        for k in range(matrices):
            inside = (natural >= limits[k]) & (natural < limits[k + 1])
            kept = jnp.where(inside, squares, 0.0).reshape(plan.own // 8, 8, LANE)
            total = jnp.sum(jnp.sum(kept, axis=0))
            stats = jnp.where((rank == plan.norm_each + k) & (lane == column), total, stats)
    stats_ref[...] = stats


def update(plan, parts, first, second, weight, natural):
    vmem = pl.BlockSpec(memory_space=pltpu.VMEM)
    counts = tuple(len(terms) for terms in parts)
    shapes = [(plan.own, LANE), (plan.own, LANE)] + [(block, LANE) for block in plan.blocks_of] + [(plan.tail, LANE)]
    return pl.pallas_call(
        functools.partial(update_kernel, plan, counts),
        out_shape=[jax.ShapeDtypeStruct(s, jnp.float32) for s in shapes],
        in_specs=[vmem] * (sum(counts) + 4),
        out_specs=[vmem] * len(shapes),
        compiler_params=pltpu.CompilerParams(vmem_limit_bytes=20 * MIB),
        name="moments",
    )(*parts[0], *parts[1], first, second, weight, natural)


def adam_rows(gradient, moment_one, moment_two, weight):
    moment_one = beta_one * moment_one + (1.0 - beta_one) * gradient
    moment_two = beta_two * moment_two + (1.0 - beta_two) * gradient * gradient
    step = moment_one / bias_one / (jnp.sqrt(moment_two / bias_two) + epsilon) + decay_rate * weight
    return (moment_one, moment_two, step)


def fetch(plan, pieces, slots, held, sems):
    copies = [
        pltpu.make_async_copy(piece, held.at[pl.ds(plan.start(*slot), piece.shape[0])], sems.at[i])
        for i, (piece, slot) in enumerate(zip(pieces, slots))
    ]
    for copy in copies:
        copy.start()
    for copy in copies:
        copy.wait()


def tile_of(plan):
    tile = LANE
    while tile < 512 and all(b % (2 * tile) == 0 for b in plan.bounds + (plan.blocks,)):
        tile *= 2
    return tile


def new_tile(plan, tile, now, position_ref, rates, weights_ref, held, out_ref):
    matrix = jnp.int32(0)
    for bound in plan.bounds:
        matrix = matrix + (now * tile >= bound).astype(jnp.int32)
    rate = jnp.broadcast_to(rates[pl.ds(matrix, 1), :], (8, LANE))
    lines = tile // LANE

    @pl.loop(0, lines)
    def _(line):
        for group in range(0, LANE, 8):
            rows = [held[pl.ds(position_ref[now * lines + line, group + u], 1), :] for u in range(8)]
            here = pl.ds(pl.multiple_of(line * LANE + group, 8), 8)
            weight = weights_ref[here, :]
            direction = jnp.concatenate(rows, 0) + decay_rate * weight
            out_ref[here, :] = weight - rate * direction


def early_kernel(plan, slots, limit_ref, place_ref, position_ref, norm_ref, weights_ref, *refs):
    pieces, refs = refs[: len(slots)], refs[len(slots) :]
    out_ref, rates, new_norm_ref, trust_ref, held, norms, sems = refs
    now = pl.program_id(0)
    tile = tile_of(plan)

    @pl.when(now == 0)
    def _():
        fetch(plan, pieces, slots, held, sems)
        total = jnp.zeros((plan.tail, LANE), jnp.float32)
        for z in range(plan.nz):
            for x in range(plan.nx):
                for c in range(2):
                    start = plan.start(0, place_ref[0] ^ z, place_ref[1] ^ x, place_ref[2] ^ c) + plan.rows[0]
                    tail = held[pl.ds(pl.multiple_of(start, 8), plan.tail), :]
                    total = total + tail
                    first = plan.index(z, x, c) * plan.norm_each
                    for row in range(first, min(first + plan.norm_each, plan.norm_rows)):
                        norms[row : row + 1, :] = tail[row - first : row - first + 1, :]
        rates[...] = jnp.zeros_like(rates)
        for k in range(matrices):
            row = plan.norm_each + k
            weight_square, direction_square = total[row : row + 1, 0:1], total[row : row + 1, 1:2]
            ratio = jnp.sqrt(weight_square) / (jnp.sqrt(direction_square) + epsilon)
            rates[k : k + 1, :] = jnp.broadcast_to(learning * ratio, (1, LANE))
            trust_ref[k] = jnp.sum(ratio)
        each = plan.norm_rows // 2
        for i in range(2):
            gains, first, second = (
                jnp.concatenate([norm_ref[j, i : i + 1, row * LANE : (row + 1) * LANE] for row in range(each)], 0)
                for j in range(3)
            )
            one, two, step = adam_rows(norms[i * each : (i + 1) * each, :], first, second, gains)
            gain_square = jnp.sum(jnp.sum(gains * gains, axis=1, keepdims=True), axis=0, keepdims=True)
            step_square = jnp.sum(jnp.sum(step * step, axis=1, keepdims=True), axis=0, keepdims=True)
            ratio = jnp.sqrt(gain_square) / (jnp.sqrt(step_square) + epsilon)
            trust_ref[matrices + i] = jnp.sum(ratio)
            for j, value in enumerate((gains - learning * ratio * step, one, two)):
                for row in range(each):
                    new_norm_ref[j, i : i + 1, row * LANE : (row + 1) * LANE] = value[row : row + 1, :]

    @pl.when((now + 1) * tile <= limit_ref[0])
    def _():
        new_tile(plan, tile, now, position_ref, rates, weights_ref, held, out_ref)


def late_kernel(plan, slots, limit_ref, position_ref, rates_ref, weights_ref, early_ref, *refs):
    pieces, refs = refs[: len(slots)], refs[len(slots) :]
    out_ref, held, sems = refs
    now = pl.program_id(0)
    tile = tile_of(plan)

    @pl.when(now == 0)
    def _():
        fetch(plan, pieces, slots, held, sems)

    @pl.when((now + 1) * tile > limit_ref[0])
    def _():
        new_tile(plan, tile, now, position_ref, rates_ref, weights_ref, held, out_ref)


def finish(plan, my_place, limit, position, norm_state, weights, founds):
    tile = tile_of(plan)
    count = plan.blocks // tile
    smem = pl.BlockSpec(memory_space=pltpu.SMEM)
    vmem = pl.BlockSpec(memory_space=pltpu.VMEM)
    anywhere = pl.BlockSpec(memory_space=pl.ANY)
    params = pltpu.CompilerParams(vmem_limit_bytes=24 * MIB)
    slots = [[(stream,) + slot for slot, _ in found] for stream, found in enumerate(founds)]
    pieces = [[piece for _, piece in found] for found in founds]

    def early_tile(i, limit_ref):
        return (jnp.maximum(jnp.minimum(i, limit_ref[0] // tile - 1), 0), 0)

    def late_tile(i, limit_ref):
        return (jnp.minimum(jnp.maximum(i, limit_ref[0] // tile), count - 1), 0)

    shape = jax.ShapeDtypeStruct((plan.blocks, LANE), jnp.float32)
    early, rates, new_norm, trust = pl.pallas_call(
        functools.partial(early_kernel, plan, slots[0]),
        grid_spec=pltpu.PrefetchScalarGridSpec(
            num_scalar_prefetch=1,
            grid=(count,),
            in_specs=[smem, smem, vmem, pl.BlockSpec((tile, LANE), early_tile)] + [anywhere] * len(pieces[0]),
            out_specs=[pl.BlockSpec((tile, LANE), early_tile), vmem, vmem, smem],
            scratch_shapes=[
                pltpu.VMEM((2 * plan.half, LANE), jnp.float32),
                pltpu.VMEM((plan.norm_rows, LANE), jnp.float32),
                pltpu.SemaphoreType.DMA((len(pieces[0]),)),
            ],
        ),
        out_shape=[
            shape,
            jax.ShapeDtypeStruct((8, LANE), jnp.float32),
            jax.ShapeDtypeStruct(norm_state.shape, jnp.float32),
            jax.ShapeDtypeStruct((matrices + 2,), jnp.float32),
        ],
        compiler_params=params,
        cost_estimate=pl.CostEstimate(flops=0, bytes_accessed=36 * MIB, transcendentals=0),
        name="new_weights_early",
    )(limit, my_place, position, norm_state, weights, *pieces[0])
    new_weights = pl.pallas_call(
        functools.partial(late_kernel, plan, slots[0] + slots[1]),
        grid_spec=pltpu.PrefetchScalarGridSpec(
            num_scalar_prefetch=1,
            grid=(count,),
            in_specs=[smem, vmem, pl.BlockSpec((tile, LANE), late_tile), anywhere]
            + [anywhere] * len(pieces[0] + pieces[1]),
            out_specs=pl.BlockSpec((tile, LANE), late_tile),
            scratch_shapes=[
                pltpu.VMEM((2 * plan.half, LANE), jnp.float32),
                pltpu.SemaphoreType.DMA((len(pieces[0] + pieces[1]),)),
            ],
        ),
        out_shape=shape,
        input_output_aliases={4: 0},
        compiler_params=params,
        name="new_weights_late",
    )(limit, position, rates, weights, early, *pieces[0], *pieces[1])
    return new_weights, new_norm, trust


def local(gradients, weights, first_moment, second_moment, owner_list, norm_grads, norm_state):
    plan = Plan(lax.axis_size("dp"), lax.axis_size("mp"), weights.shape[0])
    me = lax.axis_index("dp").astype(jnp.int32)
    my_place = jnp.stack([me // (2 * plan.nx), (me // 2) % plan.nx, me % 2]).astype(jnp.int32)
    owners = jnp.pad(owner_list[0], (0, plan.lists * LANE - plan.blocks), constant_values=-1)
    owners = owners.reshape(plan.lists, LANE)
    placed, position, limit = place(plan, my_place, owners, norm_grads[0], gradients[0])
    weight_own, natural = owned(plan, my_place, owners, weights)

    mine, theirs = ([None] * plan.nz, [None] * plan.nz), ([None] * plan.nz, [None] * plan.nz)
    for z in reversed(range(plan.nz)):
        for stream in range(2):
            other, here, block = plan.swap(placed[z, stream, 1]), placed[z, stream, 0], plan.blocks_of[stream]
            both = [
                here[x * block : (x + 1) * block] + other[x * block : (x + 1) * block] for x in range(plan.nx)
            ]
            mine[stream][z], theirs[stream][z] = both[0], both[1:]
            if z == 3 and stream == 0:
                later = [slot for slot in plan.order() if slot[2] == 1 and slot != (3, 0, 1)]
                theirs[0][3], *values = together(theirs[0][3], *(placed[slot] for slot in later))
                placed.update(zip(later, values))
    parts = []
    for stream in range(2):
        if plan.nz == 4:
            beside = (weight_own, natural) if stream == 0 else ()
            terms = reduce(plan, mine[stream], theirs[stream], beside)
            if stream == 0:
                terms, (weight_own, natural) = terms[:-2], terms[-2:]
                terms = [sum(terms[1:], terms[0])]
            parts.append(terms)
        else:
            near = []
            for z in reversed(range(plan.nz)):
                terms = line_reduce(plan, "x", [mine[stream][z]] + theirs[stream][z])
                near.insert(0, sum(terms[1:], terms[0]) if z else None)
            parts.append(terms + line_reduce(plan, "z", near)[1:])
    new_first, new_second, block, block_second, stats = update(
        plan, parts, first_moment[0], second_moment[0], weight_own, natural
    )

    hop = 1
    while hop < plan.narrow:
        stats = stats + lax.ppermute(stats, "mp", [(i, i ^ hop) for i in range(plan.narrow)])
        hop *= 2
    block = lax.dynamic_update_slice(block, block[plan.rows[0] :] + stats, (plan.rows[0], 0))
    founds = [gather(plan, block), gather(plan, block_second)]
    new_weights, new_state, trust_ratios = finish(plan, my_place, limit, position, norm_state, weights, founds)
    return (new_weights, new_first[None], new_second[None], new_state, trust_ratios)


def solution(mesh):
    in_specs = (
        P("dp", "mp", None),
        P("mp", None),
        P("mp", "dp", None),
        P("mp", "dp", None),
        P("mp", None),
        P("dp", None, None),
        P(),
    )
    out_specs = (P("mp", None), P("mp", "dp", None), P("mp", "dp", None), P(), P())
    return jax.shard_map(local, mesh=mesh, in_specs=in_specs, out_specs=out_specs, check_vma=False)
```

```python
import functools

import jax
import jax.numpy as jnp
from jax import lax
from jax.experimental import pallas as pl
from jax.experimental.pallas import tpu as pltpu
from jax.sharding import PartitionSpec as P

D = 1024
NTAB = 8
NKEYS = 256
KDIM = 128
LANE = 128
VROW_DEV = 512

beta_one = 0.9
beta_two = 0.99
bias_one = 1.0 - 0.9**4
bias_two = 1.0 - 0.99**4
epsilon = 1e-06
learning = 0.02
decay_rate = 0.01
matrices = 5
MIB = 1 << 20
TILES = 4
PHASES = 4


def matrix_bounds(narrow):
    query_blocks = D * D // (LANE * narrow)
    key_blocks = NTAB * NKEYS * KDIM // (LANE * narrow)
    value_blocks = VROW_DEV * D // LANE
    return (
        query_blocks,
        query_blocks + key_blocks,
        query_blocks + key_blocks + value_blocks,
        2 * query_blocks + key_blocks + value_blocks,
    )


class Plan:
    def __init__(self, replicas, narrow, blocks):
        self.replicas, self.narrow, self.blocks = replicas, narrow, blocks
        chips = replicas // 2
        self.nz = 4 if chips % 4 == 0 else chips
        self.nx = chips // self.nz
        assert self.nz in (1, 2, 4) and self.nx in (1, 2, 4)
        self.own = blocks // replicas
        self.tail = 8
        self.norm_rows = 2 * D // LANE
        self.norm_each = -(-self.norm_rows // replicas)
        self.block = self.own + self.tail
        self.group = self.nx * self.block
        self.half = self.nz * self.group
        self.lists = -(-blocks // (8 * LANE)) * 8
        self.bounds = matrix_bounds(narrow)

    def index(self, z, x, c):
        return (z * self.nx + x) * 2 + c

    def start(self, far_z, far_x, far_c):
        return (1 - far_c) * self.half + far_z * self.group + far_x * self.block

    def send(self, value, axis, pairs):
        every = []
        for z in range(self.nz):
            for x in range(self.nx):
                for c in range(2):
                    here = {"z": z, "x": x, "c": c}
                    for source, target in pairs:
                        if here[axis] == source:
                            every.append((self.index(z, x, c), self.index(**{**here, axis: target})))
        return lax.ppermute(value, "dp", every)

    def swap(self, value):
        return self.send(value, "c", PAIR)


PAIR = [(0, 1), (1, 0)]
PAIRS = [(0, 1), (1, 0), (2, 3), (3, 2)]
MIDDLE = [(1, 2), (2, 1)]
INWARD = [(0, 1), (3, 2)]
OUTWARD = [(1, 0), (2, 3)]


def line_reduce(plan, axis, blocks):
    if len(blocks) == 1:
        return [blocks[0]]
    if len(blocks) == 2:
        return [blocks[0], plan.send(blocks[1], axis, PAIR)]
    in_three = plan.send(blocks[3], axis, INWARD)
    in_two = plan.send(blocks[2], axis, INWARD)
    across_two = plan.send(blocks[2] + in_three, axis, MIDDLE)
    across_three = plan.send(blocks[3] + in_two, axis, MIDDLE)
    pair = plan.send(blocks[1] + across_two, axis, PAIRS)
    return [blocks[0], pair, across_three]


def together(*values):
    return lax.optimization_barrier(values)


def reduce(plan, mine, theirs, beside):
    def along_x(z, own):
        terms = line_reduce(plan, "x", [own] + theirs[z])
        return terms

    three = along_x(3, mine[3])
    two = along_x(2, mine[2])
    near_three = sum(three[1:], three[0])
    in_three = plan.send(near_three, "z", INWARD)
    in_three, *two = together(in_three, *two, *beside)
    two, beside = two[: -len(beside)], two[-len(beside) :]
    near_two = sum(two[1:], two[0])
    one = along_x(1, mine[1])
    across_two = plan.send(near_two + in_three, "z", MIDDLE)
    in_two = plan.send(near_two, "z", INWARD)
    across_two, in_two, *one = together(across_two, in_two, *one)
    zero = along_x(0, mine[0])
    pair = plan.send(sum(one[1:], one[0]) + across_two, "z", PAIRS)
    across_three = plan.send(near_three + in_two, "z", MIDDLE)
    return zero + [pair, across_three] + beside


def gather(plan, block):
    found = {}

    def add(far_z, line):
        for far_x, value in enumerate(line):
            found[far_z, far_x, 0] = value

    def along_x(value):
        return line_gather(plan, "x", plan.nx, value)

    def swapped(*far_zs):
        for far_z in far_zs:
            for far_x in range(plan.nx):
                if (far_z, far_x, 1) not in found:
                    found[far_z, far_x, 1] = plan.swap(found[far_z, far_x, 0])

    if plan.nz != 4:
        for far_z, value in enumerate(line_gather(plan, "z", plan.nz, block)):
            add(far_z, along_x(value))
            swapped(far_z)
        return list(found.items())
    line = along_x(block)
    pair = plan.send(block, "z", PAIRS)
    found[0, 0, 1], same = together(plan.swap(block), block)
    three = plan.send(same, "z", MIDDLE)
    pair, three, *line = together(pair, three, *line)
    add(0, line)
    line = along_x(pair)
    two = plan.send(pair, "z", MIDDLE)
    out_two = plan.send(three, "z", OUTWARD)
    swapped(0)
    two, out_two, *line = together(two, out_two, *line)
    add(1, line)
    line = along_x(two + out_two)
    out_three = plan.send(two, "z", OUTWARD)
    swapped(1)
    out_three, *line = together(out_three, *line)
    add(2, line)
    add(3, along_x(three + out_three))
    swapped(2)
    swapped(3)
    return list(found.items())


def line_gather(plan, axis, count, value):
    if count == 1:
        return [value]
    if count == 2:
        return [value, plan.send(value, axis, PAIR)]
    pair = plan.send(value, axis, PAIRS)
    across_three = plan.send(value, axis, MIDDLE)
    across_two = plan.send(pair, axis, MIDDLE)
    out_two = plan.send(across_three, axis, OUTWARD)
    out_three = plan.send(across_two, axis, OUTWARD)
    return [value, pair, across_two + out_two, across_three + out_three]


def place_kernel(plan, place_ref, owner_ref, norm_ref, grads_ref, *refs):
    out_refs, refs = refs[: 2 * plan.nz], refs[2 * plan.nz :]
    position_ref, raw, moved, position, sem_in, sem_position, sem_out = refs
    fetch = pltpu.make_async_copy(grads_ref, raw, sem_in)
    fetch.start()
    lists = plan.lists
    owners = owner_ref[...]
    my_z, my_x, my_c = place_ref[0], place_ref[1], place_ref[2]
    lane_in = lax.broadcasted_iota(jnp.int32, (LANE, LANE), 0)
    lane_out = lax.broadcasted_iota(jnp.int32, (LANE, LANE), 1)
    before = (lane_in < lane_out).astype(jnp.bfloat16)
    every = jnp.ones((LANE, LANE), jnp.bfloat16)
    row_out = lax.broadcasted_iota(jnp.int32, (lists, lists), 0)
    row_in = lax.broadcasted_iota(jnp.int32, (lists, lists), 1)
    above = (row_in < row_out).astype(jnp.bfloat16)
    result = jnp.zeros((lists, LANE), jnp.int32)
    ranks = jnp.full((lists, LANE), plan.own, jnp.int32)
    for z in range(plan.nz):
        for x in range(plan.nx):
            for c in range(2):
                mine = owners == plan.index(z, x, c)
                flags = mine.astype(jnp.float32).astype(jnp.bfloat16)
                inner = jnp.dot(flags, before, preferred_element_type=jnp.float32)
                totals = jnp.dot(flags, every, preferred_element_type=jnp.float32)
                outer = jnp.dot(above, totals.astype(jnp.bfloat16), preferred_element_type=jnp.float32)
                rank = (inner + outer).astype(jnp.int32)
                start = plan.start(my_z ^ z, my_x ^ x, my_c ^ c)
                first_norm = plan.index(z, x, c) * plan.norm_each
                tail = [jnp.zeros((plan.tail, LANE), jnp.float32)]
                for row in range(min(first_norm + plan.norm_each, plan.norm_rows) - 1, first_norm - 1, -1):
                    part = norm_ref[row * LANE // D : row * LANE // D + 1, row * LANE % D : row * LANE % D + LANE]
                    tail.insert(0, part.astype(jnp.float32))
                tail = jnp.concatenate(tail, 0)[: plan.tail]
                moved[pl.ds(pl.multiple_of(start + plan.own, 8), plan.tail), :] = tail
                result = jnp.where(mine, rank + start, result)
                ranks = jnp.where(mine, rank, ranks)
    position_ref[...] = result
    to_scalar = pltpu.make_async_copy(position_ref, position, sem_position)
    to_scalar.start()
    to_scalar.wait()
    fetch.wait()

    line_of = lax.broadcasted_iota(jnp.int32, (lists, LANE), 0)
    cuts = [plan.own * (i + 1) // (8 * PHASES) * 8 for i in range(PHASES - 1)] + [plan.own]
    begin = jnp.int32(0)
    copies = []
    for phase, cut in enumerate(cuts):
        end = plan.blocks // LANE
        if phase < PHASES - 1:
            end = jnp.max(jnp.where(ranks < cut, line_of + 1, 0))

        @pl.loop(begin, end)
        def _(line):
            for part in range(0, LANE, 16):
                rows = raw[pl.ds(pl.multiple_of(line * LANE + part, 16), 16), :].astype(jnp.float32)
                for u in range(16):
                    moved[pl.ds(position[line, part + u], 1), :] = rows[u : u + 1, :]

        begin = end
        low = cuts[phase - 1] if phase else 0
        high = cut if phase < PHASES - 1 else plan.block
        for i, out in enumerate(out_refs):
            start = (i // plan.nz) * plan.half + (plan.nz - 1 - i % plan.nz) * plan.group
            for x in range(plan.nx):
                rows = pl.ds(x * plan.block + low, high - low)
                source = moved.at[pl.ds(start + x * plan.block + low, high - low)]
                copies.append(pltpu.make_async_copy(source, out.at[rows], sem_out.at[len(copies)]))
                copies[-1].start()
    for copy in copies:
        copy.wait()


def place(plan, my_place, owners, norm_grads, grads):
    shapes = [(plan.group, LANE)] * (2 * plan.nz)
    outs = pl.pallas_call(
        functools.partial(place_kernel, plan),
        out_shape=[jax.ShapeDtypeStruct(s, jnp.float32) for s in shapes]
        + [jax.ShapeDtypeStruct((plan.lists, LANE), jnp.int32)],
        in_specs=[
            pl.BlockSpec(memory_space=pltpu.SMEM),
            pl.BlockSpec(memory_space=pltpu.VMEM),
            pl.BlockSpec(memory_space=pltpu.VMEM),
            pl.BlockSpec(memory_space=pl.ANY),
        ],
        out_specs=[pl.BlockSpec(memory_space=pl.ANY)] * len(shapes) + [pl.BlockSpec(memory_space=pltpu.VMEM)],
        scratch_shapes=[
            pltpu.VMEM((plan.blocks, LANE), jnp.bfloat16),
            pltpu.VMEM((2 * plan.half, LANE), jnp.float32),
            pltpu.SMEM((plan.lists, LANE), jnp.int32),
            pltpu.SemaphoreType.DMA,
            pltpu.SemaphoreType.DMA,
            pltpu.SemaphoreType.DMA((len(shapes) * plan.nx * PHASES,)),
        ],
        compiler_params=pltpu.CompilerParams(vmem_limit_bytes=58 * MIB),
        name="place_gradients",
    )(my_place, owners, norm_grads, grads)
    return list(outs[: plan.nz][::-1]), outs[plan.nz : 2 * plan.nz][::-1], outs[-1]


def owned_kernel(plan, place_ref, owner_ref, weights_ref, owned_ref, natural_ref, held, listed, order, sem_in, sem_order):
    fetch = pltpu.make_async_copy(weights_ref, held, sem_in)
    fetch.start()
    lists = plan.lists
    me = plan.index(place_ref[0], place_ref[1], place_ref[2])
    flags = (owner_ref[...] == me).astype(jnp.float32).astype(jnp.bfloat16)
    lane_in = lax.broadcasted_iota(jnp.int32, (LANE, LANE), 0)
    lane_out = lax.broadcasted_iota(jnp.int32, (LANE, LANE), 1)
    upto = (lane_in <= lane_out).astype(jnp.float32).astype(jnp.bfloat16)
    inner = jnp.dot(flags, upto, preferred_element_type=jnp.float32).astype(jnp.bfloat16)
    totals = lax.dot_general(
        jnp.ones((8, LANE), jnp.bfloat16), flags, (((1,), (1,)), ((), ())), preferred_element_type=jnp.float32
    )
    row_in = lax.broadcasted_iota(jnp.int32, (lists, lists), 0)
    row_out = lax.broadcasted_iota(jnp.int32, (lists, lists), 1)
    upto = (row_in <= row_out).astype(jnp.float32).astype(jnp.bfloat16)
    ends = jnp.dot(totals.astype(jnp.bfloat16), upto, preferred_element_type=jnp.float32)[0:1, :]
    place_of = lax.broadcasted_iota(jnp.int32, (LANE, lists), 1).astype(jnp.float32)
    rank_of = lax.broadcasted_iota(jnp.int32, (LANE, 1), 0)
    for step in range(listed.shape[0]):
        if step * LANE >= plan.own:
            break
        rank = (rank_of + step * LANE).astype(jnp.float32)
        passed = ends <= rank
        line = jnp.sum(passed.astype(jnp.float32), axis=1, keepdims=True)
        before = jnp.max(jnp.where(passed, ends, 0.0), axis=1, keepdims=True)
        chosen = (place_of == line).astype(jnp.float32).astype(jnp.bfloat16)
        counts = jnp.dot(chosen, inner, preferred_element_type=jnp.float32)
        column = jnp.sum((counts <= rank - before).astype(jnp.float32), axis=1, keepdims=True)
        block = jnp.broadcast_to((line * LANE + column).astype(jnp.int32), (LANE, LANE))
        natural_ref[step * LANE : (step + 1) * LANE, :] = block
        listed[step : step + 1, :] = jnp.sum(jnp.where(lane_in == lane_out, block, 0), axis=0, keepdims=True)
    to_scalar = pltpu.make_async_copy(listed, order, sem_order)
    to_scalar.start()
    to_scalar.wait()
    fetch.wait()

    def pick(line, count):
        for u in range(count):
            owned_ref[pl.ds(line * LANE + u, 1), :] = held[pl.ds(order[line, u], 1), :]

    @pl.loop(0, plan.own // LANE)
    def _(line):
        pick(line, LANE)

    if plan.own % LANE:
        pick(plan.own // LANE, plan.own % LANE)


def owned(plan, my_place, owners, weights):
    high_rows = -(-plan.own // (8 * LANE)) * 8
    ranks = -(-plan.own // LANE) * LANE
    vmem = pl.BlockSpec(memory_space=pltpu.VMEM)
    return pl.pallas_call(
        functools.partial(owned_kernel, plan),
        out_shape=[
            jax.ShapeDtypeStruct((plan.own, LANE), jnp.float32),
            jax.ShapeDtypeStruct((ranks, LANE), jnp.int32),
        ],
        in_specs=[pl.BlockSpec(memory_space=pltpu.SMEM), vmem, pl.BlockSpec(memory_space=pl.ANY)],
        out_specs=[vmem] * 2,
        scratch_shapes=[
            pltpu.VMEM((plan.blocks, LANE), jnp.float32),
            pltpu.VMEM((high_rows, LANE), jnp.int32),
            pltpu.SMEM((high_rows, LANE), jnp.int32),
            pltpu.SemaphoreType.DMA,
            pltpu.SemaphoreType.DMA,
        ],
        compiler_params=pltpu.CompilerParams(vmem_limit_bytes=58 * MIB),
        cost_estimate=pl.CostEstimate(flops=0, bytes_accessed=20 * MIB, transcendentals=0),
        name="owned_weights",
    )(my_place, owners, weights)


def update_kernel(plan, terms, *refs):
    parts, refs = refs[:terms], refs[terms:]
    first_ref, second_ref, weight_ref, natural_ref = refs[:4]
    new_first_ref, new_second_ref, block_ref, stats_ref = refs[4:]
    gradient = parts[0][: plan.block, :]
    for part in parts[1:]:
        gradient = gradient + part[: plan.block, :]
    block_ref[plan.own :, :] = gradient[plan.own :, :]
    gradient = gradient[: plan.own, :]
    moment_one = beta_one * first_ref[...] + (1.0 - beta_one) * gradient
    moment_two = beta_two * second_ref[...] + (1.0 - beta_two) * gradient * gradient
    new_first_ref[...] = moment_one
    new_second_ref[...] = moment_two
    step = moment_one / bias_one / (jnp.sqrt(moment_two / bias_two) + epsilon)
    block_ref[: plan.own, :] = step
    weight = weight_ref[...]
    direction = step + decay_rate * weight
    natural = natural_ref[: plan.own, :]
    limits = (0,) + plan.bounds + (plan.blocks,)
    lane = lax.broadcasted_iota(jnp.int32, (8, LANE), 1)
    rank = lax.broadcasted_iota(jnp.int32, (8, LANE), 0)
    stats = jnp.zeros((8, LANE), jnp.float32)
    for column, squares in enumerate((weight * weight, direction * direction)):
        for k in range(matrices):
            inside = (natural >= limits[k]) & (natural < limits[k + 1])
            kept = jnp.where(inside, squares, 0.0).reshape(plan.own // 8, 8, LANE)
            total = jnp.sum(jnp.sum(kept, axis=0))
            stats = jnp.where((rank == plan.norm_each + k) & (lane == column), total, stats)
    stats_ref[...] = stats


def update(plan, parts, first, second, weight, natural):
    vmem = pl.BlockSpec(memory_space=pltpu.VMEM)
    shapes = [(plan.own, LANE), (plan.own, LANE), (plan.block, LANE), (plan.tail, LANE)]
    return pl.pallas_call(
        functools.partial(update_kernel, plan, len(parts)),
        out_shape=[jax.ShapeDtypeStruct(s, jnp.float32) for s in shapes],
        in_specs=[vmem] * (len(parts) + 4),
        out_specs=[vmem] * len(shapes),
        compiler_params=pltpu.CompilerParams(vmem_limit_bytes=20 * MIB),
        name="moments",
    )(*parts, first, second, weight, natural)


def adam_rows(gradient, moment_one, moment_two, weight):
    moment_one = beta_one * moment_one + (1.0 - beta_one) * gradient
    moment_two = beta_two * moment_two + (1.0 - beta_two) * gradient * gradient
    step = moment_one / bias_one / (jnp.sqrt(moment_two / bias_two) + epsilon) + decay_rate * weight
    return (moment_one, moment_two, step)


def finish_kernel(plan, tile, slots, place_ref, position_ref, norm_ref, weights_ref, *refs):
    pieces, refs = refs[: len(slots)], refs[len(slots) :]
    out_ref, new_norm_ref, trust_ref, held, norms, rates, sems = refs
    now = pl.program_id(0)

    @pl.when(now == 0)
    def _():
        copies = [
            pltpu.make_async_copy(piece, held.at[pl.ds(plan.start(*slot), plan.block)], sems.at[i])
            for i, (piece, slot) in enumerate(zip(pieces, slots))
        ]
        for copy in copies:
            copy.start()
        for copy in copies:
            copy.wait()
        total = jnp.zeros((plan.tail, LANE), jnp.float32)
        for z in range(plan.nz):
            for x in range(plan.nx):
                for c in range(2):
                    start = plan.start(place_ref[0] ^ z, place_ref[1] ^ x, place_ref[2] ^ c) + plan.own
                    tail = held[pl.ds(pl.multiple_of(start, 8), plan.tail), :]
                    total = total + tail
                    first = plan.index(z, x, c) * plan.norm_each
                    for row in range(first, min(first + plan.norm_each, plan.norm_rows)):
                        norms[row : row + 1, :] = tail[row - first : row - first + 1, :]
        for k in range(matrices):
            row = plan.norm_each + k
            weight_square, direction_square = total[row : row + 1, 0:1], total[row : row + 1, 1:2]
            ratio = jnp.sqrt(weight_square) / (jnp.sqrt(direction_square) + epsilon)
            rates[k : k + 1, :] = jnp.broadcast_to(learning * ratio, (1, LANE))
            trust_ref[k] = jnp.sum(ratio)
        each = plan.norm_rows // 2
        for i in range(2):
            gains, first, second = (
                jnp.concatenate([norm_ref[j, i : i + 1, row * LANE : (row + 1) * LANE] for row in range(each)], 0)
                for j in range(3)
            )
            one, two, step = adam_rows(norms[i * each : (i + 1) * each, :], first, second, gains)
            gain_square = jnp.sum(jnp.sum(gains * gains, axis=1, keepdims=True), axis=0, keepdims=True)
            step_square = jnp.sum(jnp.sum(step * step, axis=1, keepdims=True), axis=0, keepdims=True)
            ratio = jnp.sqrt(gain_square) / (jnp.sqrt(step_square) + epsilon)
            trust_ref[matrices + i] = jnp.sum(ratio)
            for j, value in enumerate((gains - learning * ratio * step, one, two)):
                for row in range(each):
                    new_norm_ref[j, i : i + 1, row * LANE : (row + 1) * LANE] = value[row : row + 1, :]

    lines = tile // LANE

    @pl.loop(0, lines)
    def _(line):
        matrix = jnp.int32(0)
        for bound in plan.bounds:
            matrix = matrix + (now * lines + line >= bound // LANE).astype(jnp.int32)
        rate = jnp.broadcast_to(rates[pl.ds(matrix, 1), :], (8, LANE))
        for group in range(0, LANE, 8):
            rows = [held[pl.ds(position_ref[now * lines + line, group + u], 1), :] for u in range(8)]
            here = pl.ds(pl.multiple_of(line * LANE + group, 8), 8)
            weight = weights_ref[here, :]
            direction = jnp.concatenate(rows, 0) + decay_rate * weight
            out_ref[here, :] = weight - rate * direction


def finish(plan, my_place, position, norm_state, weights, pieces, slots):
    assert all(bound % LANE == 0 for bound in plan.bounds + (plan.blocks,))
    tile = plan.blocks // next(n for n in (TILES, 4, 2, 1) if plan.blocks // LANE % n == 0)
    smem = pl.BlockSpec(memory_space=pltpu.SMEM)
    vmem = pl.BlockSpec(memory_space=pltpu.VMEM)
    return pl.pallas_call(
        functools.partial(finish_kernel, plan, tile, slots),
        grid=(plan.blocks // tile,),
        out_shape=[
            jax.ShapeDtypeStruct((plan.blocks, LANE), jnp.float32),
            jax.ShapeDtypeStruct(norm_state.shape, jnp.float32),
            jax.ShapeDtypeStruct((matrices + 2,), jnp.float32),
        ],
        in_specs=[smem, smem, vmem, pl.BlockSpec((tile, LANE), lambda i: (i, 0))]
        + [pl.BlockSpec(memory_space=pl.ANY)] * len(pieces),
        out_specs=[pl.BlockSpec((tile, LANE), lambda i: (i, 0)), vmem, smem],
        scratch_shapes=[
            pltpu.VMEM((2 * plan.half, LANE), jnp.float32),
            pltpu.VMEM((plan.norm_rows, LANE), jnp.float32),
            pltpu.VMEM((8, LANE), jnp.float32),
            pltpu.SemaphoreType.DMA((len(pieces),)),
        ],
        compiler_params=pltpu.CompilerParams(vmem_limit_bytes=58 * MIB),
        name="new_weights",
    )(my_place, position, norm_state, weights, *pieces)


def local(gradients, weights, first_moment, second_moment, owner_list, norm_grads, norm_state):
    plan = Plan(lax.axis_size("dp"), lax.axis_size("mp"), weights.shape[0])
    me = lax.axis_index("dp").astype(jnp.int32)
    my_place = jnp.stack([me // (2 * plan.nx), (me // 2) % plan.nx, me % 2]).astype(jnp.int32)
    owners = jnp.pad(owner_list[0], (0, plan.lists * LANE - plan.blocks), constant_values=-1)
    owners = owners.reshape(plan.lists, LANE)
    siblings, blocks, position = place(plan, my_place, owners, norm_grads[0], gradients[0])
    weight_own, natural = owned(plan, my_place, owners, weights)

    mine, theirs = [None] * plan.nz, [None] * plan.nz
    for z in reversed(range(plan.nz)):
        other = plan.swap(siblings[z])
        both = [
            blocks[z][x * plan.block : (x + 1) * plan.block] + other[x * plan.block : (x + 1) * plan.block]
            for x in range(plan.nx)
        ]
        mine[z], theirs[z] = both[0], both[1:]
        if z == 3:
            theirs[3], siblings[2], siblings[1], siblings[0] = together(theirs[3], *siblings[2::-1])
    if plan.nz == 4:
        parts = reduce(plan, mine, theirs, (weight_own, natural))
        parts, (weight_own, natural) = parts[:-2], parts[-2:]
    else:
        near = []
        for z in reversed(range(plan.nz)):
            terms = line_reduce(plan, "x", [mine[z]] + theirs[z])
            near.insert(0, sum(terms[1:], terms[0]) if z else None)
        parts = terms + line_reduce(plan, "z", near)[1:]
    new_first, new_second, block, stats = update(
        plan, parts, first_moment[0], second_moment[0], weight_own, natural
    )

    hop = 1
    while hop < plan.narrow:
        stats = stats + lax.ppermute(stats, "mp", [(i, i ^ hop) for i in range(plan.narrow)])
        hop *= 2
    block = lax.dynamic_update_slice(block, block[plan.own :] + stats, (plan.own, 0))
    found = gather(plan, block)
    slots, pieces = [slot for slot, _ in found], [piece for _, piece in found]
    new_weights, new_state, trust_ratios = finish(plan, my_place, position, norm_state, weights, pieces, slots)
    return (new_weights, new_first[None], new_second[None], new_state, trust_ratios)


def solution(mesh):
    in_specs = (
        P("dp", "mp", None),
        P("mp", None),
        P("mp", "dp", None),
        P("mp", "dp", None),
        P("mp", None),
        P("dp", None, None),
        P(),
    )
    out_specs = (P("mp", None), P("mp", "dp", None), P("mp", "dp", None), P(), P())
    return jax.shard_map(local, mesh=mesh, in_specs=in_specs, out_specs=out_specs, check_vma=False)
```

```python
import functools

import jax
import jax.numpy as jnp
from jax import lax
from jax.experimental import pallas as pl
from jax.experimental.pallas import tpu as pltpu
from jax.sharding import PartitionSpec as P

D = 1024
NTAB = 8
NKEYS = 256
KDIM = 128
LANE = 128
VROW_DEV = 512

beta_one = 0.9
beta_two = 0.99
bias_one = 1.0 - 0.9**4
bias_two = 1.0 - 0.99**4
epsilon = 1e-06
learning = 0.02
decay_rate = 0.01
matrices = 5
MIB = 1 << 20
TILES = 8
PHASES = 2


def matrix_bounds(narrow):
    query_blocks = D * D // (LANE * narrow)
    key_blocks = NTAB * NKEYS * KDIM // (LANE * narrow)
    value_blocks = VROW_DEV * D // LANE
    return (
        query_blocks,
        query_blocks + key_blocks,
        query_blocks + key_blocks + value_blocks,
        2 * query_blocks + key_blocks + value_blocks,
    )


class Plan:
    def __init__(self, replicas, narrow, blocks):
        self.replicas, self.narrow, self.blocks = replicas, narrow, blocks
        chips = replicas // 2
        self.nz = 4 if chips % 4 == 0 else chips
        self.nx = chips // self.nz
        assert self.nz in (1, 2, 4) and self.nx in (1, 2, 4)
        self.own = blocks // replicas
        self.tail = 8
        self.norm_rows = 2 * D // LANE
        self.norm_each = -(-self.norm_rows // replicas)
        self.block = self.own + self.tail
        self.group = self.nx * self.block
        self.half = self.nz * self.group
        self.lists = -(-blocks // (8 * LANE)) * 8
        self.bounds = matrix_bounds(narrow)

    def index(self, z, x, c):
        return (z * self.nx + x) * 2 + c

    def start(self, far_z, far_x, far_c):
        return (1 - far_c) * self.half + far_z * self.group + far_x * self.block

    def send(self, value, axis, pairs):
        every = []
        for z in range(self.nz):
            for x in range(self.nx):
                for c in range(2):
                    here = {"z": z, "x": x, "c": c}
                    for source, target in pairs:
                        if here[axis] == source:
                            every.append((self.index(z, x, c), self.index(**{**here, axis: target})))
        return lax.ppermute(value, "dp", every)

    def swap(self, value):
        return self.send(value, "c", PAIR)


PAIR = [(0, 1), (1, 0)]
PAIRS = [(0, 1), (1, 0), (2, 3), (3, 2)]
MIDDLE = [(1, 2), (2, 1)]
INWARD = [(0, 1), (3, 2)]
OUTWARD = [(1, 0), (2, 3)]


def line_reduce(plan, axis, blocks):
    if len(blocks) == 1:
        return [blocks[0]]
    if len(blocks) == 2:
        return [blocks[0], plan.send(blocks[1], axis, PAIR)]
    in_three = plan.send(blocks[3], axis, INWARD)
    in_two = plan.send(blocks[2], axis, INWARD)
    across_two = plan.send(blocks[2] + in_three, axis, MIDDLE)
    across_three = plan.send(blocks[3] + in_two, axis, MIDDLE)
    pair = plan.send(blocks[1] + across_two, axis, PAIRS)
    return [blocks[0], pair, across_three]


def together(*values):
    return lax.optimization_barrier(values)


def reduce(plan, mine, theirs, beside):
    def along_x(z, own):
        terms = line_reduce(plan, "x", [own] + theirs[z])
        return terms

    three = along_x(3, mine[3])
    two = along_x(2, mine[2])
    near_three = sum(three[1:], three[0])
    in_three = plan.send(near_three, "z", INWARD)
    in_three, near_two, *beside = together(in_three, sum(two[1:], two[0]), *beside)
    one = along_x(1, mine[1])
    across_two = plan.send(near_two + in_three, "z", MIDDLE)
    in_two = plan.send(near_two, "z", INWARD)
    across_two, in_two, near_one = together(across_two, in_two, sum(one[1:], one[0]))
    zero = along_x(0, mine[0])
    pair = plan.send(near_one + across_two, "z", PAIRS)
    across_three = plan.send(near_three + in_two, "z", MIDDLE)
    return zero + [pair, across_three] + beside


def gather(plan, block):
    found = {}

    def add(far_z, line):
        for far_x, value in enumerate(line):
            found[far_z, far_x, 0] = value

    def along_x(value):
        return line_gather(plan, "x", plan.nx, value)

    def swapped(*far_zs):
        for far_z in far_zs:
            for far_x in range(plan.nx):
                if (far_z, far_x, 1) not in found:
                    found[far_z, far_x, 1] = plan.swap(found[far_z, far_x, 0])

    if plan.nz != 4:
        for far_z, value in enumerate(line_gather(plan, "z", plan.nz, block)):
            add(far_z, along_x(value))
            swapped(far_z)
        return list(found.items())
    line = along_x(block)
    pair = plan.send(block, "z", PAIRS)
    three = plan.send(block, "z", MIDDLE)
    pair, three, *line = together(pair, three, *line)
    add(0, line)
    line = along_x(pair)
    two = plan.send(pair, "z", MIDDLE)
    out_two = plan.send(three, "z", OUTWARD)
    swapped(0)
    two, out_two, *line = together(two, out_two, *line)
    add(1, line)
    line = along_x(two + out_two)
    out_three = plan.send(two, "z", OUTWARD)
    swapped(1)
    out_three, *line = together(out_three, *line)
    add(2, line)
    add(3, along_x(three + out_three))
    swapped(2)
    swapped(3)
    return list(found.items())


def line_gather(plan, axis, count, value):
    if count == 1:
        return [value]
    if count == 2:
        return [value, plan.send(value, axis, PAIR)]
    pair = plan.send(value, axis, PAIRS)
    across_three = plan.send(value, axis, MIDDLE)
    across_two = plan.send(pair, axis, MIDDLE)
    out_two = plan.send(across_three, axis, OUTWARD)
    out_three = plan.send(across_two, axis, OUTWARD)
    return [value, pair, across_two + out_two, across_three + out_three]


def place_kernel(plan, place_ref, owner_ref, norm_ref, grads_ref, *refs):
    out_refs, refs = refs[: 2 * plan.nz], refs[2 * plan.nz :]
    position_ref, raw, moved, position, sem_in, sem_position, sem_out = refs
    fetch = pltpu.make_async_copy(grads_ref, raw, sem_in)
    fetch.start()
    lists = plan.lists
    owners = owner_ref[...]
    my_z, my_x, my_c = place_ref[0], place_ref[1], place_ref[2]
    count = plan.replicas
    lane_in = lax.broadcasted_iota(jnp.int32, (LANE, LANE), 0)
    lane_out = lax.broadcasted_iota(jnp.int32, (LANE, LANE), 1)
    before = (lane_in < lane_out).astype(jnp.float32).astype(jnp.bfloat16)
    row_out = lax.broadcasted_iota(jnp.int32, (lists, lists), 0)
    row_in = lax.broadcasted_iota(jnp.int32, (lists, lists), 1)
    above = (row_in < row_out).astype(jnp.float32).astype(jnp.bfloat16)
    flags = [(owners == d).astype(jnp.float32).astype(jnp.bfloat16) for d in range(count)]
    inner = jnp.dot(jnp.concatenate(flags, 0), before, preferred_element_type=jnp.float32)
    owner_in = lax.broadcasted_iota(jnp.int32, (count * LANE, LANE), 0)
    owner_out = lax.broadcasted_iota(jnp.int32, (count * LANE, LANE), 1)
    pick = (owner_in // LANE == owner_out).astype(jnp.float32).astype(jnp.bfloat16)
    totals = jnp.dot(jnp.concatenate(flags, 1), pick, preferred_element_type=jnp.float32)
    outer = jnp.dot(above, totals.astype(jnp.bfloat16), preferred_element_type=jnp.float32)
    ranks = jnp.full((lists, LANE), plan.own, jnp.int32)
    result = jnp.zeros((lists, LANE), jnp.int32)
    for z in range(plan.nz):
        for x in range(plan.nx):
            for c in range(2):
                d = plan.index(z, x, c)
                mine = owners == d
                rank = (inner[d * lists : (d + 1) * lists, :] + outer[:, d : d + 1]).astype(jnp.int32)
                start = plan.start(my_z ^ z, my_x ^ x, my_c ^ c)
                first_norm = d * plan.norm_each
                tail = [jnp.zeros((plan.tail, LANE), jnp.float32)]
                for row in range(min(first_norm + plan.norm_each, plan.norm_rows) - 1, first_norm - 1, -1):
                    part = norm_ref[row * LANE // D : row * LANE // D + 1, row * LANE % D : row * LANE % D + LANE]
                    tail.insert(0, part.astype(jnp.float32))
                tail = jnp.concatenate(tail, 0)[: plan.tail]
                moved[pl.ds(pl.multiple_of(start + plan.own, 8), plan.tail), :] = tail
                result = jnp.where(mine, rank + start, result)
                ranks = jnp.where(mine, rank, ranks)
    position_ref[...] = result
    to_scalar = pltpu.make_async_copy(position_ref, position, sem_position)
    to_scalar.start()
    to_scalar.wait()
    fetch.wait()

    line_of = lax.broadcasted_iota(jnp.int32, (lists, LANE), 0)
    cuts = [plan.own * (i + 1) // (8 * PHASES) * 8 for i in range(PHASES - 1)] + [plan.own]
    begin = jnp.int32(0)
    copies = []
    for phase, cut in enumerate(cuts):
        end = plan.blocks // LANE
        if phase < PHASES - 1:
            end = jnp.max(jnp.where(ranks < cut, line_of + 1, 0))

        @pl.loop(begin, end)
        def _(line):
            for part in range(0, LANE, 16):
                rows = raw[pl.ds(pl.multiple_of(line * LANE + part, 16), 16), :].astype(jnp.float32)
                for u in range(16):
                    moved[pl.ds(position[line, part + u], 1), :] = rows[u : u + 1, :]

        begin = end
        low = cuts[phase - 1] if phase else 0
        high = cut if phase < PHASES - 1 else plan.block
        for i, out in enumerate(out_refs):
            start = (i // plan.nz) * plan.half + (plan.nz - 1 - i % plan.nz) * plan.group
            for x in range(plan.nx):
                rows = pl.ds(x * plan.block + low, high - low)
                source = moved.at[pl.ds(start + x * plan.block + low, high - low)]
                copies.append(pltpu.make_async_copy(source, out.at[rows], sem_out.at[len(copies)]))
                copies[-1].start()
    for copy in copies:
        copy.wait()


def place(plan, my_place, owners, norm_grads, grads):
    shapes = [(plan.group, LANE)] * (2 * plan.nz)
    outs = pl.pallas_call(
        functools.partial(place_kernel, plan),
        out_shape=[jax.ShapeDtypeStruct(s, jnp.float32) for s in shapes]
        + [jax.ShapeDtypeStruct((plan.lists, LANE), jnp.int32)],
        in_specs=[
            pl.BlockSpec(memory_space=pltpu.SMEM),
            pl.BlockSpec(memory_space=pltpu.VMEM),
            pl.BlockSpec(memory_space=pltpu.VMEM),
            pl.BlockSpec(memory_space=pl.ANY),
        ],
        out_specs=[pl.BlockSpec(memory_space=pl.ANY)] * len(shapes) + [pl.BlockSpec(memory_space=pltpu.VMEM)],
        scratch_shapes=[
            pltpu.VMEM((plan.blocks, LANE), jnp.bfloat16),
            pltpu.VMEM((2 * plan.half, LANE), jnp.float32),
            pltpu.SMEM((plan.lists, LANE), jnp.int32),
            pltpu.SemaphoreType.DMA,
            pltpu.SemaphoreType.DMA,
            pltpu.SemaphoreType.DMA((len(shapes) * plan.nx * PHASES,)),
        ],
        compiler_params=pltpu.CompilerParams(vmem_limit_bytes=58 * MIB),
        name="place_gradients",
    )(my_place, owners, norm_grads, grads)
    return list(outs[: plan.nz][::-1]), outs[plan.nz : 2 * plan.nz][::-1], outs[-1]


def owned_kernel(plan, place_ref, owner_ref, weights_ref, owned_ref, natural_ref, held, listed, order, sem_in, sem_order):
    fetch = pltpu.make_async_copy(weights_ref, held, sem_in)
    fetch.start()
    lists = plan.lists
    me = plan.index(place_ref[0], place_ref[1], place_ref[2])
    flags = (owner_ref[...] == me).astype(jnp.float32).astype(jnp.bfloat16)
    lane_in = lax.broadcasted_iota(jnp.int32, (LANE, LANE), 0)
    lane_out = lax.broadcasted_iota(jnp.int32, (LANE, LANE), 1)
    upto = (lane_in <= lane_out).astype(jnp.float32).astype(jnp.bfloat16)
    inner = jnp.dot(flags, upto, preferred_element_type=jnp.float32).astype(jnp.bfloat16)
    totals = lax.dot_general(
        jnp.ones((8, LANE), jnp.bfloat16), flags, (((1,), (1,)), ((), ())), preferred_element_type=jnp.float32
    )
    row_in = lax.broadcasted_iota(jnp.int32, (lists, lists), 0)
    row_out = lax.broadcasted_iota(jnp.int32, (lists, lists), 1)
    upto = (row_in <= row_out).astype(jnp.float32).astype(jnp.bfloat16)
    ends = jnp.dot(totals.astype(jnp.bfloat16), upto, preferred_element_type=jnp.float32)[0:1, :]
    place_of = lax.broadcasted_iota(jnp.int32, (LANE, lists), 1).astype(jnp.float32)
    rank_of = lax.broadcasted_iota(jnp.int32, (LANE, 1), 0)
    for step in range(listed.shape[0]):
        if step * LANE >= plan.own:
            break
        rank = (rank_of + step * LANE).astype(jnp.float32)
        passed = ends <= rank
        line = jnp.sum(passed.astype(jnp.float32), axis=1, keepdims=True)
        before = jnp.max(jnp.where(passed, ends, 0.0), axis=1, keepdims=True)
        chosen = (place_of == line).astype(jnp.float32).astype(jnp.bfloat16)
        counts = jnp.dot(chosen, inner, preferred_element_type=jnp.float32)
        column = jnp.sum((counts <= rank - before).astype(jnp.float32), axis=1, keepdims=True)
        block = jnp.broadcast_to((line * LANE + column).astype(jnp.int32), (LANE, LANE))
        natural_ref[step * LANE : (step + 1) * LANE, :] = block
        listed[step : step + 1, :] = jnp.sum(jnp.where(lane_in == lane_out, block, 0), axis=0, keepdims=True)
    to_scalar = pltpu.make_async_copy(listed, order, sem_order)
    to_scalar.start()
    to_scalar.wait()
    fetch.wait()

    def pick(line, count):
        for u in range(count):
            owned_ref[pl.ds(line * LANE + u, 1), :] = held[pl.ds(order[line, u], 1), :]

    @pl.loop(0, plan.own // LANE)
    def _(line):
        pick(line, LANE)

    if plan.own % LANE:
        pick(plan.own // LANE, plan.own % LANE)


def owned(plan, my_place, owners, weights):
    high_rows = -(-plan.own // (8 * LANE)) * 8
    ranks = -(-plan.own // LANE) * LANE
    vmem = pl.BlockSpec(memory_space=pltpu.VMEM)
    return pl.pallas_call(
        functools.partial(owned_kernel, plan),
        out_shape=[
            jax.ShapeDtypeStruct((plan.own, LANE), jnp.float32),
            jax.ShapeDtypeStruct((ranks, LANE), jnp.int32),
        ],
        in_specs=[pl.BlockSpec(memory_space=pltpu.SMEM), vmem, pl.BlockSpec(memory_space=pl.ANY)],
        out_specs=[vmem] * 2,
        scratch_shapes=[
            pltpu.VMEM((plan.blocks, LANE), jnp.float32),
            pltpu.VMEM((high_rows, LANE), jnp.int32),
            pltpu.SMEM((high_rows, LANE), jnp.int32),
            pltpu.SemaphoreType.DMA,
            pltpu.SemaphoreType.DMA,
        ],
        compiler_params=pltpu.CompilerParams(vmem_limit_bytes=58 * MIB),
        cost_estimate=pl.CostEstimate(flops=0, bytes_accessed=20 * MIB, transcendentals=0),
        name="owned_weights",
    )(my_place, owners, weights)


def update_kernel(plan, terms, *refs):
    parts, refs = refs[:terms], refs[terms:]
    first_ref, second_ref, weight_ref, natural_ref = refs[:4]
    new_first_ref, new_second_ref, block_ref, stats_ref = refs[4:]
    gradient = parts[0][: plan.block, :]
    for part in parts[1:]:
        gradient = gradient + part[: plan.block, :]
    block_ref[plan.own :, :] = gradient[plan.own :, :]
    gradient = gradient[: plan.own, :]
    moment_one = beta_one * first_ref[...] + (1.0 - beta_one) * gradient
    moment_two = beta_two * second_ref[...] + (1.0 - beta_two) * gradient * gradient
    new_first_ref[...] = moment_one
    new_second_ref[...] = moment_two
    step = moment_one / bias_one / (jnp.sqrt(moment_two / bias_two) + epsilon)
    block_ref[: plan.own, :] = step
    weight = weight_ref[...]
    direction = step + decay_rate * weight
    natural = natural_ref[: plan.own, :]
    limits = (0,) + plan.bounds + (plan.blocks,)
    lane = lax.broadcasted_iota(jnp.int32, (8, LANE), 1)
    rank = lax.broadcasted_iota(jnp.int32, (8, LANE), 0)
    stats = jnp.zeros((8, LANE), jnp.float32)
    for column, squares in enumerate((weight * weight, direction * direction)):
        for k in range(matrices):
            inside = (natural >= limits[k]) & (natural < limits[k + 1])
            kept = jnp.where(inside, squares, 0.0).reshape(plan.own // 8, 8, LANE)
            total = jnp.sum(jnp.sum(kept, axis=0))
            stats = jnp.where((rank == plan.norm_each + k) & (lane == column), total, stats)
    stats_ref[...] = stats


def update(plan, parts, first, second, weight, natural):
    vmem = pl.BlockSpec(memory_space=pltpu.VMEM)
    shapes = [(plan.own, LANE), (plan.own, LANE), (plan.block, LANE), (plan.tail, LANE)]
    return pl.pallas_call(
        functools.partial(update_kernel, plan, len(parts)),
        out_shape=[jax.ShapeDtypeStruct(s, jnp.float32) for s in shapes],
        in_specs=[vmem] * (len(parts) + 4),
        out_specs=[vmem] * len(shapes),
        compiler_params=pltpu.CompilerParams(vmem_limit_bytes=20 * MIB),
        name="moments",
    )(*parts, first, second, weight, natural)


def adam_rows(gradient, moment_one, moment_two, weight):
    moment_one = beta_one * moment_one + (1.0 - beta_one) * gradient
    moment_two = beta_two * moment_two + (1.0 - beta_two) * gradient * gradient
    step = moment_one / bias_one / (jnp.sqrt(moment_two / bias_two) + epsilon) + decay_rate * weight
    return (moment_one, moment_two, step)


def finish_kernel(plan, tile, slots, place_ref, position_ref, norm_ref, weights_ref, *refs):
    pieces, refs = refs[: len(slots)], refs[len(slots) :]
    out_ref, new_norm_ref, trust_ref, held, norms, rates = refs
    now = pl.program_id(0)

    @pl.when(now == 0)
    def _():
        for piece, slot in zip(pieces, slots):
            held[pl.ds(plan.start(*slot), plan.block), :] = piece[...]
        total = jnp.zeros((plan.tail, LANE), jnp.float32)
        for z in range(plan.nz):
            for x in range(plan.nx):
                for c in range(2):
                    start = plan.start(place_ref[0] ^ z, place_ref[1] ^ x, place_ref[2] ^ c) + plan.own
                    tail = held[pl.ds(pl.multiple_of(start, 8), plan.tail), :]
                    total = total + tail
                    first = plan.index(z, x, c) * plan.norm_each
                    for row in range(first, min(first + plan.norm_each, plan.norm_rows)):
                        norms[row : row + 1, :] = tail[row - first : row - first + 1, :]
        for k in range(matrices):
            row = plan.norm_each + k
            weight_square, direction_square = total[row : row + 1, 0:1], total[row : row + 1, 1:2]
            ratio = jnp.sqrt(weight_square) / (jnp.sqrt(direction_square) + epsilon)
            rates[k : k + 1, :] = jnp.broadcast_to(learning * ratio, (1, LANE))
            trust_ref[k] = jnp.sum(ratio)
        each = plan.norm_rows // 2
        for i in range(2):
            gains, first, second = (
                jnp.concatenate([norm_ref[j, i : i + 1, row * LANE : (row + 1) * LANE] for row in range(each)], 0)
                for j in range(3)
            )
            one, two, step = adam_rows(norms[i * each : (i + 1) * each, :], first, second, gains)
            gain_square = jnp.sum(jnp.sum(gains * gains, axis=1, keepdims=True), axis=0, keepdims=True)
            step_square = jnp.sum(jnp.sum(step * step, axis=1, keepdims=True), axis=0, keepdims=True)
            ratio = jnp.sqrt(gain_square) / (jnp.sqrt(step_square) + epsilon)
            trust_ref[matrices + i] = jnp.sum(ratio)
            for j, value in enumerate((gains - learning * ratio * step, one, two)):
                for row in range(each):
                    new_norm_ref[j, i : i + 1, row * LANE : (row + 1) * LANE] = value[row : row + 1, :]

    lines = tile // LANE

    @pl.loop(0, lines)
    def _(line):
        matrix = jnp.int32(0)
        for bound in plan.bounds:
            matrix = matrix + (now * lines + line >= bound // LANE).astype(jnp.int32)
        rate = jnp.broadcast_to(rates[pl.ds(matrix, 1), :], (8, LANE))
        for group in range(0, LANE, 8):
            rows = [held[pl.ds(position_ref[now * lines + line, group + u], 1), :] for u in range(8)]
            here = pl.ds(pl.multiple_of(line * LANE + group, 8), 8)
            weight = weights_ref[here, :]
            direction = jnp.concatenate(rows, 0) + decay_rate * weight
            out_ref[here, :] = weight - rate * direction


def finish(plan, my_place, position, norm_state, weights, pieces, slots):
    assert all(bound % LANE == 0 for bound in plan.bounds + (plan.blocks,))
    tile = plan.blocks // next(n for n in (TILES, 4, 2, 1) if plan.blocks // LANE % n == 0)
    smem = pl.BlockSpec(memory_space=pltpu.SMEM)
    vmem = pl.BlockSpec(memory_space=pltpu.VMEM)
    return pl.pallas_call(
        functools.partial(finish_kernel, plan, tile, slots),
        grid=(plan.blocks // tile,),
        out_shape=[
            jax.ShapeDtypeStruct((plan.blocks, LANE), jnp.float32),
            jax.ShapeDtypeStruct(norm_state.shape, jnp.float32),
            jax.ShapeDtypeStruct((matrices + 2,), jnp.float32),
        ],
        in_specs=[smem, smem, vmem, pl.BlockSpec((tile, LANE), lambda i: (i, 0))]
        + [vmem] * len(pieces),
        out_specs=[pl.BlockSpec((tile, LANE), lambda i: (i, 0)), vmem, smem],
        scratch_shapes=[
            pltpu.VMEM((2 * plan.half, LANE), jnp.float32),
            pltpu.VMEM((plan.norm_rows, LANE), jnp.float32),
            pltpu.VMEM((8, LANE), jnp.float32),
        ],
        compiler_params=pltpu.CompilerParams(vmem_limit_bytes=20 * MIB),
        name="new_weights",
    )(my_place, position, norm_state, weights, *pieces)


def local(gradients, weights, first_moment, second_moment, owner_list, norm_grads, norm_state):
    plan = Plan(lax.axis_size("dp"), lax.axis_size("mp"), weights.shape[0])
    me = lax.axis_index("dp").astype(jnp.int32)
    my_place = jnp.stack([me // (2 * plan.nx), (me // 2) % plan.nx, me % 2]).astype(jnp.int32)
    owners = jnp.pad(owner_list[0], (0, plan.lists * LANE - plan.blocks), constant_values=-1)
    owners = owners.reshape(plan.lists, LANE)
    siblings, blocks, position = place(plan, my_place, owners, norm_grads[0], gradients[0])
    weight_own, natural = owned(plan, my_place, owners, weights)

    mine, theirs = [None] * plan.nz, [None] * plan.nz
    for z in reversed(range(plan.nz)):
        other = plan.swap(siblings[z])
        both = [
            blocks[z][x * plan.block : (x + 1) * plan.block] + other[x * plan.block : (x + 1) * plan.block]
            for x in range(plan.nx)
        ]
        mine[z], theirs[z] = both[0], both[1:]
        if z == 3:
            theirs[3], siblings[2], siblings[1], siblings[0] = together(theirs[3], *siblings[2::-1])
    if plan.nz == 4:
        parts = reduce(plan, mine, theirs, (weight_own, natural))
        parts, (weight_own, natural) = parts[:-2], parts[-2:]
    else:
        near = []
        for z in reversed(range(plan.nz)):
            terms = line_reduce(plan, "x", [mine[z]] + theirs[z])
            near.insert(0, sum(terms[1:], terms[0]) if z else None)
        parts = terms + line_reduce(plan, "z", near)[1:]
    new_first, new_second, block, stats = update(
        plan, parts, first_moment[0], second_moment[0], weight_own, natural
    )

    hop = 1
    while hop < plan.narrow:
        stats = stats + lax.ppermute(stats, "mp", [(i, i ^ hop) for i in range(plan.narrow)])
        hop *= 2
    block = lax.dynamic_update_slice(block, block[plan.own :] + stats, (plan.own, 0))
    found = gather(plan, block)
    slots, pieces = [slot for slot, _ in found], [piece for _, piece in found]
    new_weights, new_state, trust_ratios = finish(plan, my_place, position, norm_state, weights, pieces, slots)
    return (new_weights, new_first[None], new_second[None], new_state, trust_ratios)


def solution(mesh):
    in_specs = (
        P("dp", "mp", None),
        P("mp", None),
        P("mp", "dp", None),
        P("mp", "dp", None),
        P("mp", None),
        P("dp", None, None),
        P(),
    )
    out_specs = (P("mp", None), P("mp", "dp", None), P("mp", "dp", None), P(), P())
    return jax.shard_map(local, mesh=mesh, in_specs=in_specs, out_specs=out_specs, check_vma=False)
```

```python
import functools

import jax
import jax.numpy as jnp
from jax import lax
from jax.experimental import pallas as pl
from jax.experimental.pallas import tpu as pltpu
from jax.sharding import PartitionSpec as P

D = 1024
NTAB = 8
NKEYS = 256
KDIM = 128
LANE = 128
VROW_DEV = 512

beta_one = 0.9
beta_two = 0.99
bias_one = 1.0 - 0.9**4
bias_two = 1.0 - 0.99**4
epsilon = 1e-06
learning = 0.02
decay_rate = 0.01
matrices = 5
MIB = 1 << 20
TILES = 8
PHASES = 2


def matrix_bounds(narrow):
    query_blocks = D * D // (LANE * narrow)
    key_blocks = NTAB * NKEYS * KDIM // (LANE * narrow)
    value_blocks = VROW_DEV * D // LANE
    return (
        query_blocks,
        query_blocks + key_blocks,
        query_blocks + key_blocks + value_blocks,
        2 * query_blocks + key_blocks + value_blocks,
    )


class Plan:
    def __init__(self, replicas, narrow, blocks):
        self.replicas, self.narrow, self.blocks = replicas, narrow, blocks
        chips = replicas // 2
        self.nz = 4 if chips % 4 == 0 else chips
        self.nx = chips // self.nz
        assert self.nz in (1, 2, 4) and self.nx in (1, 2, 4)
        self.own = blocks // replicas
        self.tail = 8
        self.norm_rows = 2 * D // LANE
        self.norm_each = -(-self.norm_rows // replicas)
        self.block = self.own + self.tail
        self.group = self.nx * self.block
        self.half = self.nz * self.group
        self.lists = -(-blocks // (8 * LANE)) * 8
        self.bounds = matrix_bounds(narrow)

    def index(self, z, x, c):
        return (z * self.nx + x) * 2 + c

    def start(self, far_z, far_x, far_c):
        return (1 - far_c) * self.half + far_z * self.group + far_x * self.block

    def send(self, value, axis, pairs):
        every = []
        for z in range(self.nz):
            for x in range(self.nx):
                for c in range(2):
                    here = {"z": z, "x": x, "c": c}
                    for source, target in pairs:
                        if here[axis] == source:
                            every.append((self.index(z, x, c), self.index(**{**here, axis: target})))
        return lax.ppermute(value, "dp", every)

    def swap(self, value):
        return self.send(value, "c", PAIR)


PAIR = [(0, 1), (1, 0)]
PAIRS = [(0, 1), (1, 0), (2, 3), (3, 2)]
MIDDLE = [(1, 2), (2, 1)]
INWARD = [(0, 1), (3, 2)]
OUTWARD = [(1, 0), (2, 3)]


def line_reduce(plan, axis, blocks):
    if len(blocks) == 1:
        return [blocks[0]]
    if len(blocks) == 2:
        return [blocks[0], plan.send(blocks[1], axis, PAIR)]
    in_three = plan.send(blocks[3], axis, INWARD)
    in_two = plan.send(blocks[2], axis, INWARD)
    across_two = plan.send(blocks[2] + in_three, axis, MIDDLE)
    across_three = plan.send(blocks[3] + in_two, axis, MIDDLE)
    pair = plan.send(blocks[1] + across_two, axis, PAIRS)
    return [blocks[0], pair, across_three]


def together(*values):
    return lax.optimization_barrier(values)


def reduce(plan, mine, theirs, beside):
    def along_x(z, own):
        terms = line_reduce(plan, "x", [own] + theirs[z])
        return terms

    three = along_x(3, mine[3])
    two = along_x(2, mine[2])
    near_three = sum(three[1:], three[0])
    in_three = plan.send(near_three, "z", INWARD)
    in_three, near_two, *beside = together(in_three, sum(two[1:], two[0]), *beside)
    one = along_x(1, mine[1])
    across_two = plan.send(near_two + in_three, "z", MIDDLE)
    in_two = plan.send(near_two, "z", INWARD)
    across_two, in_two, near_one = together(across_two, in_two, sum(one[1:], one[0]))
    zero = along_x(0, mine[0])
    pair = plan.send(near_one + across_two, "z", PAIRS)
    across_three = plan.send(near_three + in_two, "z", MIDDLE)
    return zero + [pair, across_three] + beside


def gather(plan, block):
    found = {}

    def add(far_z, line):
        for far_x, value in enumerate(line):
            found[far_z, far_x, 0] = value

    def along_x(value):
        return line_gather(plan, "x", plan.nx, value)

    def swapped(*far_zs):
        for far_z in far_zs:
            for far_x in range(plan.nx):
                if (far_z, far_x, 1) not in found:
                    found[far_z, far_x, 1] = plan.swap(found[far_z, far_x, 0])

    if plan.nz != 4:
        for far_z, value in enumerate(line_gather(plan, "z", plan.nz, block)):
            add(far_z, along_x(value))
            swapped(far_z)
        return list(found.items())
    pair = plan.send(block, "z", PAIRS)
    three = plan.send(block, "z", MIDDLE)
    line = along_x(block)
    three, found[1, 0, 1], *line = together(three, plan.swap(pair), *line)
    add(0, line)
    line = along_x(pair)
    two = plan.send(pair, "z", MIDDLE)
    out_two = plan.send(three, "z", OUTWARD)
    swapped(0)
    near_two, two, *line = together(two + out_two, two, *line)
    add(1, line)
    line = along_x(near_two)
    out_three = plan.send(two, "z", OUTWARD)
    swapped(1)
    near_three, *line = together(three + out_three, *line)
    add(2, line)
    add(3, along_x(near_three))
    swapped(2)
    swapped(3)
    return list(found.items())


def line_gather(plan, axis, count, value):
    if count == 1:
        return [value]
    if count == 2:
        return [value, plan.send(value, axis, PAIR)]
    pair = plan.send(value, axis, PAIRS)
    across_three = plan.send(value, axis, MIDDLE)
    across_two = plan.send(pair, axis, MIDDLE)
    out_two = plan.send(across_three, axis, OUTWARD)
    out_three = plan.send(across_two, axis, OUTWARD)
    return [value, pair, across_two + out_two, across_three + out_three]


def place_kernel(plan, place_ref, owner_ref, norm_ref, grads_ref, *refs):
    out_refs, refs = refs[: 2 * plan.nz], refs[2 * plan.nz :]
    position_ref, raw, moved, position, sem_in, sem_position, sem_out = refs
    fetch = pltpu.make_async_copy(grads_ref, raw, sem_in)
    fetch.start()
    lists = plan.lists
    owners = owner_ref[...]
    my_z, my_x, my_c = place_ref[0], place_ref[1], place_ref[2]
    count = plan.replicas
    lane_in = lax.broadcasted_iota(jnp.int32, (LANE, LANE), 0)
    lane_out = lax.broadcasted_iota(jnp.int32, (LANE, LANE), 1)
    before = (lane_in < lane_out).astype(jnp.float32).astype(jnp.bfloat16)
    row_out = lax.broadcasted_iota(jnp.int32, (lists, lists), 0)
    row_in = lax.broadcasted_iota(jnp.int32, (lists, lists), 1)
    above = (row_in < row_out).astype(jnp.float32).astype(jnp.bfloat16)
    flags = [(owners == d).astype(jnp.float32).astype(jnp.bfloat16) for d in range(count)]
    inner = jnp.dot(jnp.concatenate(flags, 0), before, preferred_element_type=jnp.float32)
    owner_in = lax.broadcasted_iota(jnp.int32, (count * LANE, LANE), 0)
    owner_out = lax.broadcasted_iota(jnp.int32, (count * LANE, LANE), 1)
    pick = (owner_in // LANE == owner_out).astype(jnp.float32).astype(jnp.bfloat16)
    totals = jnp.dot(jnp.concatenate(flags, 1), pick, preferred_element_type=jnp.float32)
    outer = jnp.dot(above, totals.astype(jnp.bfloat16), preferred_element_type=jnp.float32)
    ranks = jnp.full((lists, LANE), plan.own, jnp.int32)
    result = jnp.zeros((lists, LANE), jnp.int32)
    for z in range(plan.nz):
        for x in range(plan.nx):
            for c in range(2):
                d = plan.index(z, x, c)
                mine = owners == d
                rank = (inner[d * lists : (d + 1) * lists, :] + outer[:, d : d + 1]).astype(jnp.int32)
                start = plan.start(my_z ^ z, my_x ^ x, my_c ^ c)
                first_norm = d * plan.norm_each
                tail = [jnp.zeros((plan.tail, LANE), jnp.float32)]
                for row in range(min(first_norm + plan.norm_each, plan.norm_rows) - 1, first_norm - 1, -1):
                    part = norm_ref[row * LANE // D : row * LANE // D + 1, row * LANE % D : row * LANE % D + LANE]
                    tail.insert(0, part.astype(jnp.float32))
                tail = jnp.concatenate(tail, 0)[: plan.tail]
                moved[pl.ds(pl.multiple_of(start + plan.own, 8), plan.tail), :] = tail
                result = jnp.where(mine, rank + start, result)
                ranks = jnp.where(mine, rank, ranks)
    position_ref[...] = result
    to_scalar = pltpu.make_async_copy(position_ref, position, sem_position)
    to_scalar.start()
    to_scalar.wait()
    fetch.wait()

    line_of = lax.broadcasted_iota(jnp.int32, (lists, LANE), 0)
    cuts = [plan.own * (i + 1) // (8 * PHASES) * 8 for i in range(PHASES - 1)] + [plan.own]
    begin = jnp.int32(0)
    copies = []
    for phase, cut in enumerate(cuts):
        end = plan.blocks // LANE
        if phase < PHASES - 1:
            end = jnp.max(jnp.where(ranks < cut, line_of + 1, 0))

        @pl.loop(begin, end)
        def _(line):
            for part in range(0, LANE, 16):
                rows = raw[pl.ds(pl.multiple_of(line * LANE + part, 16), 16), :].astype(jnp.float32)
                for u in range(16):
                    moved[pl.ds(position[line, part + u], 1), :] = rows[u : u + 1, :]

        begin = end
        low = cuts[phase - 1] if phase else 0
        high = cut if phase < PHASES - 1 else plan.block
        for i, out in enumerate(out_refs):
            start = (i // plan.nz) * plan.half + (plan.nz - 1 - i % plan.nz) * plan.group
            for x in range(plan.nx):
                rows = pl.ds(x * plan.block + low, high - low)
                source = moved.at[pl.ds(start + x * plan.block + low, high - low)]
                copies.append(pltpu.make_async_copy(source, out.at[rows], sem_out.at[len(copies)]))
                copies[-1].start()
    for copy in copies:
        copy.wait()


def place(plan, my_place, owners, norm_grads, grads):
    shapes = [(plan.group, LANE)] * (2 * plan.nz)
    outs = pl.pallas_call(
        functools.partial(place_kernel, plan),
        out_shape=[jax.ShapeDtypeStruct(s, jnp.float32) for s in shapes]
        + [jax.ShapeDtypeStruct((plan.lists, LANE), jnp.int32)],
        in_specs=[
            pl.BlockSpec(memory_space=pltpu.SMEM),
            pl.BlockSpec(memory_space=pltpu.VMEM),
            pl.BlockSpec(memory_space=pltpu.VMEM),
            pl.BlockSpec(memory_space=pl.ANY),
        ],
        out_specs=[pl.BlockSpec(memory_space=pl.ANY)] * len(shapes) + [pl.BlockSpec(memory_space=pltpu.VMEM)],
        scratch_shapes=[
            pltpu.VMEM((plan.blocks, LANE), jnp.bfloat16),
            pltpu.VMEM((2 * plan.half, LANE), jnp.float32),
            pltpu.SMEM((plan.lists, LANE), jnp.int32),
            pltpu.SemaphoreType.DMA,
            pltpu.SemaphoreType.DMA,
            pltpu.SemaphoreType.DMA((len(shapes) * plan.nx * PHASES,)),
        ],
        compiler_params=pltpu.CompilerParams(vmem_limit_bytes=58 * MIB),
        name="place_gradients",
    )(my_place, owners, norm_grads, grads)
    return list(outs[: plan.nz][::-1]), outs[plan.nz : 2 * plan.nz][::-1], outs[-1]


def owned_kernel(plan, place_ref, owner_ref, weights_ref, owned_ref, natural_ref, held, listed, order, sem_in, sem_order):
    fetch = pltpu.make_async_copy(weights_ref, held, sem_in)
    fetch.start()
    lists = plan.lists
    me = plan.index(place_ref[0], place_ref[1], place_ref[2])
    flags = (owner_ref[...] == me).astype(jnp.float32).astype(jnp.bfloat16)
    lane_in = lax.broadcasted_iota(jnp.int32, (LANE, LANE), 0)
    lane_out = lax.broadcasted_iota(jnp.int32, (LANE, LANE), 1)
    upto = (lane_in <= lane_out).astype(jnp.float32).astype(jnp.bfloat16)
    inner = jnp.dot(flags, upto, preferred_element_type=jnp.float32).astype(jnp.bfloat16)
    totals = lax.dot_general(
        jnp.ones((8, LANE), jnp.bfloat16), flags, (((1,), (1,)), ((), ())), preferred_element_type=jnp.float32
    )
    row_in = lax.broadcasted_iota(jnp.int32, (lists, lists), 0)
    row_out = lax.broadcasted_iota(jnp.int32, (lists, lists), 1)
    upto = (row_in <= row_out).astype(jnp.float32).astype(jnp.bfloat16)
    ends = jnp.dot(totals.astype(jnp.bfloat16), upto, preferred_element_type=jnp.float32)[0:1, :]
    place_of = lax.broadcasted_iota(jnp.int32, (LANE, lists), 1).astype(jnp.float32)
    rank_of = lax.broadcasted_iota(jnp.int32, (LANE, 1), 0)
    for step in range(listed.shape[0]):
        if step * LANE >= plan.own:
            break
        rank = (rank_of + step * LANE).astype(jnp.float32)
        passed = ends <= rank
        line = jnp.sum(passed.astype(jnp.float32), axis=1, keepdims=True)
        before = jnp.max(jnp.where(passed, ends, 0.0), axis=1, keepdims=True)
        chosen = (place_of == line).astype(jnp.float32).astype(jnp.bfloat16)
        counts = jnp.dot(chosen, inner, preferred_element_type=jnp.float32)
        column = jnp.sum((counts <= rank - before).astype(jnp.float32), axis=1, keepdims=True)
        block = jnp.broadcast_to((line * LANE + column).astype(jnp.int32), (LANE, LANE))
        natural_ref[step * LANE : (step + 1) * LANE, :] = block
        listed[step : step + 1, :] = jnp.sum(jnp.where(lane_in == lane_out, block, 0), axis=0, keepdims=True)
    to_scalar = pltpu.make_async_copy(listed, order, sem_order)
    to_scalar.start()
    to_scalar.wait()
    fetch.wait()

    def pick(line, count):
        for u in range(count):
            owned_ref[pl.ds(line * LANE + u, 1), :] = held[pl.ds(order[line, u], 1), :]

    @pl.loop(0, plan.own // LANE)
    def _(line):
        pick(line, LANE)

    if plan.own % LANE:
        pick(plan.own // LANE, plan.own % LANE)


def owned(plan, my_place, owners, weights):
    high_rows = -(-plan.own // (8 * LANE)) * 8
    ranks = -(-plan.own // LANE) * LANE
    vmem = pl.BlockSpec(memory_space=pltpu.VMEM)
    return pl.pallas_call(
        functools.partial(owned_kernel, plan),
        out_shape=[
            jax.ShapeDtypeStruct((plan.own, LANE), jnp.float32),
            jax.ShapeDtypeStruct((ranks, LANE), jnp.int32),
        ],
        in_specs=[pl.BlockSpec(memory_space=pltpu.SMEM), vmem, pl.BlockSpec(memory_space=pl.ANY)],
        out_specs=[vmem] * 2,
        scratch_shapes=[
            pltpu.VMEM((plan.blocks, LANE), jnp.float32),
            pltpu.VMEM((high_rows, LANE), jnp.int32),
            pltpu.SMEM((high_rows, LANE), jnp.int32),
            pltpu.SemaphoreType.DMA,
            pltpu.SemaphoreType.DMA,
        ],
        compiler_params=pltpu.CompilerParams(vmem_limit_bytes=58 * MIB),
        cost_estimate=pl.CostEstimate(flops=0, bytes_accessed=20 * MIB, transcendentals=0),
        name="owned_weights",
    )(my_place, owners, weights)


def update_kernel(plan, terms, *refs):
    parts, refs = refs[:terms], refs[terms:]
    first_ref, second_ref, weight_ref, natural_ref = refs[:4]
    new_first_ref, new_second_ref, block_ref, stats_ref = refs[4:]
    gradient = parts[0][: plan.block, :]
    for part in parts[1:]:
        gradient = gradient + part[: plan.block, :]
    block_ref[plan.own :, :] = gradient[plan.own :, :]
    gradient = gradient[: plan.own, :]
    moment_one = beta_one * first_ref[...] + (1.0 - beta_one) * gradient
    moment_two = beta_two * second_ref[...] + (1.0 - beta_two) * gradient * gradient
    new_first_ref[...] = moment_one
    new_second_ref[...] = moment_two
    step = moment_one / bias_one / (jnp.sqrt(moment_two / bias_two) + epsilon)
    block_ref[: plan.own, :] = step
    weight = weight_ref[...]
    direction = step + decay_rate * weight
    natural = natural_ref[: plan.own, :]
    limits = (0,) + plan.bounds + (plan.blocks,)
    lane = lax.broadcasted_iota(jnp.int32, (8, LANE), 1)
    rank = lax.broadcasted_iota(jnp.int32, (8, LANE), 0)
    stats = jnp.zeros((8, LANE), jnp.float32)
    for column, squares in enumerate((weight * weight, direction * direction)):
        for k in range(matrices):
            inside = (natural >= limits[k]) & (natural < limits[k + 1])
            kept = jnp.where(inside, squares, 0.0).reshape(plan.own // 8, 8, LANE)
            total = jnp.sum(jnp.sum(kept, axis=0))
            stats = jnp.where((rank == plan.norm_each + k) & (lane == column), total, stats)
    stats_ref[...] = stats


def update(plan, parts, first, second, weight, natural):
    vmem = pl.BlockSpec(memory_space=pltpu.VMEM)
    shapes = [(plan.own, LANE), (plan.own, LANE), (plan.block, LANE), (plan.tail, LANE)]
    return pl.pallas_call(
        functools.partial(update_kernel, plan, len(parts)),
        out_shape=[jax.ShapeDtypeStruct(s, jnp.float32) for s in shapes],
        in_specs=[vmem] * (len(parts) + 4),
        out_specs=[vmem] * len(shapes),
        compiler_params=pltpu.CompilerParams(vmem_limit_bytes=20 * MIB),
        name="moments",
    )(*parts, first, second, weight, natural)


def adam_rows(gradient, moment_one, moment_two, weight):
    moment_one = beta_one * moment_one + (1.0 - beta_one) * gradient
    moment_two = beta_two * moment_two + (1.0 - beta_two) * gradient * gradient
    step = moment_one / bias_one / (jnp.sqrt(moment_two / bias_two) + epsilon) + decay_rate * weight
    return (moment_one, moment_two, step)


def finish_kernel(plan, tile, slots, place_ref, position_ref, norm_ref, weights_ref, *refs):
    pieces, refs = refs[: len(slots)], refs[len(slots) :]
    out_ref, new_norm_ref, trust_ref, held, norms, rates = refs
    now = pl.program_id(0)

    @pl.when(now == 0)
    def _():
        for piece, slot in zip(pieces, slots):
            held[pl.ds(plan.start(*slot), plan.block), :] = piece[...]
        total = jnp.zeros((plan.tail, LANE), jnp.float32)
        for z in range(plan.nz):
            for x in range(plan.nx):
                for c in range(2):
                    start = plan.start(place_ref[0] ^ z, place_ref[1] ^ x, place_ref[2] ^ c) + plan.own
                    tail = held[pl.ds(pl.multiple_of(start, 8), plan.tail), :]
                    total = total + tail
                    first = plan.index(z, x, c) * plan.norm_each
                    for row in range(first, min(first + plan.norm_each, plan.norm_rows)):
                        norms[row : row + 1, :] = tail[row - first : row - first + 1, :]
        for k in range(matrices):
            row = plan.norm_each + k
            weight_square, direction_square = total[row : row + 1, 0:1], total[row : row + 1, 1:2]
            ratio = jnp.sqrt(weight_square) / (jnp.sqrt(direction_square) + epsilon)
            rates[k : k + 1, :] = jnp.broadcast_to(learning * ratio, (1, LANE))
            trust_ref[k] = jnp.sum(ratio)
        each = plan.norm_rows // 2
        for i in range(2):
            gains, first, second = (
                jnp.concatenate([norm_ref[j, i : i + 1, row * LANE : (row + 1) * LANE] for row in range(each)], 0)
                for j in range(3)
            )
            one, two, step = adam_rows(norms[i * each : (i + 1) * each, :], first, second, gains)
            gain_square = jnp.sum(jnp.sum(gains * gains, axis=1, keepdims=True), axis=0, keepdims=True)
            step_square = jnp.sum(jnp.sum(step * step, axis=1, keepdims=True), axis=0, keepdims=True)
            ratio = jnp.sqrt(gain_square) / (jnp.sqrt(step_square) + epsilon)
            trust_ref[matrices + i] = jnp.sum(ratio)
            for j, value in enumerate((gains - learning * ratio * step, one, two)):
                for row in range(each):
                    new_norm_ref[j, i : i + 1, row * LANE : (row + 1) * LANE] = value[row : row + 1, :]

    lines = tile // LANE

    @pl.loop(0, lines)
    def _(line):
        matrix = jnp.int32(0)
        for bound in plan.bounds:
            matrix = matrix + (now * lines + line >= bound // LANE).astype(jnp.int32)
        rate = jnp.broadcast_to(rates[pl.ds(matrix, 1), :], (8, LANE))
        for group in range(0, LANE, 8):
            rows = [held[pl.ds(position_ref[now * lines + line, group + u], 1), :] for u in range(8)]
            here = pl.ds(pl.multiple_of(line * LANE + group, 8), 8)
            weight = weights_ref[here, :]
            direction = jnp.concatenate(rows, 0) + decay_rate * weight
            out_ref[here, :] = weight - rate * direction


def finish(plan, my_place, position, norm_state, weights, pieces, slots):
    assert all(bound % LANE == 0 for bound in plan.bounds + (plan.blocks,))
    tile = plan.blocks // next(n for n in (TILES, 4, 2, 1) if plan.blocks // LANE % n == 0)
    smem = pl.BlockSpec(memory_space=pltpu.SMEM)
    vmem = pl.BlockSpec(memory_space=pltpu.VMEM)
    return pl.pallas_call(
        functools.partial(finish_kernel, plan, tile, slots),
        grid=(plan.blocks // tile,),
        out_shape=[
            jax.ShapeDtypeStruct((plan.blocks, LANE), jnp.float32),
            jax.ShapeDtypeStruct(norm_state.shape, jnp.float32),
            jax.ShapeDtypeStruct((matrices + 2,), jnp.float32),
        ],
        in_specs=[smem, smem, vmem, pl.BlockSpec((tile, LANE), lambda i: (i, 0))]
        + [vmem] * len(pieces),
        out_specs=[pl.BlockSpec((tile, LANE), lambda i: (i, 0)), vmem, smem],
        scratch_shapes=[
            pltpu.VMEM((2 * plan.half, LANE), jnp.float32),
            pltpu.VMEM((plan.norm_rows, LANE), jnp.float32),
            pltpu.VMEM((8, LANE), jnp.float32),
        ],
        compiler_params=pltpu.CompilerParams(vmem_limit_bytes=20 * MIB),
        name="new_weights",
    )(my_place, position, norm_state, weights, *pieces)


def local(gradients, weights, first_moment, second_moment, owner_list, norm_grads, norm_state):
    plan = Plan(lax.axis_size("dp"), lax.axis_size("mp"), weights.shape[0])
    me = lax.axis_index("dp").astype(jnp.int32)
    my_place = jnp.stack([me // (2 * plan.nx), (me // 2) % plan.nx, me % 2]).astype(jnp.int32)
    owners = jnp.pad(owner_list[0], (0, plan.lists * LANE - plan.blocks), constant_values=-1)
    owners = owners.reshape(plan.lists, LANE)
    siblings, blocks, position = place(plan, my_place, owners, norm_grads[0], gradients[0])
    weight_own, natural = owned(plan, my_place, owners, weights)

    mine, theirs = [None] * plan.nz, [None] * plan.nz
    for z in reversed(range(plan.nz)):
        other = plan.swap(siblings[z])
        both = [
            blocks[z][x * plan.block : (x + 1) * plan.block] + other[x * plan.block : (x + 1) * plan.block]
            for x in range(plan.nx)
        ]
        mine[z], theirs[z] = both[0], both[1:]
        if z == 3:
            theirs[3], siblings[2], siblings[1], siblings[0] = together(theirs[3], *siblings[2::-1])
    if plan.nz == 4:
        parts = reduce(plan, mine, theirs, (weight_own, natural))
        parts, (weight_own, natural) = parts[:-2], parts[-2:]
    else:
        near = []
        for z in reversed(range(plan.nz)):
            terms = line_reduce(plan, "x", [mine[z]] + theirs[z])
            near.insert(0, sum(terms[1:], terms[0]) if z else None)
        parts = terms + line_reduce(plan, "z", near)[1:]
    new_first, new_second, block, stats = update(
        plan, parts, first_moment[0], second_moment[0], weight_own, natural
    )

    hop = 1
    while hop < plan.narrow:
        stats = stats + lax.ppermute(stats, "mp", [(i, i ^ hop) for i in range(plan.narrow)])
        hop *= 2
    block = lax.dynamic_update_slice(block, block[plan.own :] + stats, (plan.own, 0))
    found = gather(plan, block)
    slots, pieces = [slot for slot, _ in found], [piece for _, piece in found]
    new_weights, new_state, trust_ratios = finish(plan, my_place, position, norm_state, weights, pieces, slots)
    return (new_weights, new_first[None], new_second[None], new_state, trust_ratios)


def solution(mesh):
    in_specs = (
        P("dp", "mp", None),
        P("mp", None),
        P("mp", "dp", None),
        P("mp", "dp", None),
        P("mp", None),
        P("dp", None, None),
        P(),
    )
    out_specs = (P("mp", None), P("mp", "dp", None), P("mp", "dp", None), P(), P())
    return jax.shard_map(local, mesh=mesh, in_specs=in_specs, out_specs=out_specs, check_vma=False)
```

```python
import functools

import jax
import jax.numpy as jnp
from jax import lax
from jax.experimental import pallas as pl
from jax.experimental.pallas import tpu as pltpu
from jax.sharding import PartitionSpec as P

D = 1024
NTAB = 8
NKEYS = 256
KDIM = 128
LANE = 128
VROW_DEV = 512

beta_one = 0.9
beta_two = 0.99
bias_one = 1.0 - 0.9**4
bias_two = 1.0 - 0.99**4
epsilon = 1e-06
learning = 0.02
decay_rate = 0.01
matrices = 5
MIB = 1 << 20
TILES = 8
PHASES = 2


def matrix_bounds(narrow):
    query_blocks = D * D // (LANE * narrow)
    key_blocks = NTAB * NKEYS * KDIM // (LANE * narrow)
    value_blocks = VROW_DEV * D // LANE
    return (
        query_blocks,
        query_blocks + key_blocks,
        query_blocks + key_blocks + value_blocks,
        2 * query_blocks + key_blocks + value_blocks,
    )


class Plan:
    def __init__(self, replicas, narrow, blocks):
        self.replicas, self.narrow, self.blocks = replicas, narrow, blocks
        chips = replicas // 2
        self.nz = 4 if chips % 4 == 0 else chips
        self.nx = chips // self.nz
        assert self.nz in (1, 2, 4) and self.nx in (1, 2, 4)
        self.own = blocks // replicas
        self.tail = 8
        self.norm_rows = 2 * D // LANE
        self.norm_each = -(-self.norm_rows // replicas)
        self.block = self.own + self.tail
        self.group = self.nx * self.block
        self.half = self.nz * self.group
        self.lists = -(-blocks // (8 * LANE)) * 8
        self.bounds = matrix_bounds(narrow)

    def index(self, z, x, c):
        return (z * self.nx + x) * 2 + c

    def start(self, far_z, far_x, far_c):
        return (1 - far_c) * self.half + far_z * self.group + far_x * self.block

    def send(self, value, axis, pairs):
        every = []
        for z in range(self.nz):
            for x in range(self.nx):
                for c in range(2):
                    here = {"z": z, "x": x, "c": c}
                    for source, target in pairs:
                        if here[axis] == source:
                            every.append((self.index(z, x, c), self.index(**{**here, axis: target})))
        return lax.ppermute(value, "dp", every)

    def swap(self, value):
        return self.send(value, "c", PAIR)


PAIR = [(0, 1), (1, 0)]
PAIRS = [(0, 1), (1, 0), (2, 3), (3, 2)]
MIDDLE = [(1, 2), (2, 1)]
INWARD = [(0, 1), (3, 2)]
OUTWARD = [(1, 0), (2, 3)]


def line_reduce(plan, axis, blocks):
    if len(blocks) == 1:
        return [blocks[0]]
    if len(blocks) == 2:
        return [blocks[0], plan.send(blocks[1], axis, PAIR)]
    in_three = plan.send(blocks[3], axis, INWARD)
    in_two = plan.send(blocks[2], axis, INWARD)
    across_two = plan.send(blocks[2] + in_three, axis, MIDDLE)
    across_three = plan.send(blocks[3] + in_two, axis, MIDDLE)
    pair = plan.send(blocks[1] + across_two, axis, PAIRS)
    return [blocks[0], pair, across_three]


def together(*values):
    return lax.optimization_barrier(values)


def reduce(plan, mine, theirs, beside):
    def along_x(z, own):
        terms = line_reduce(plan, "x", [own] + theirs[z])
        return terms

    three = along_x(3, mine[3])
    two = along_x(2, mine[2])
    near_three = sum(three[1:], three[0])
    in_three = plan.send(near_three, "z", INWARD)
    in_three, near_two, *beside = together(in_three, sum(two[1:], two[0]), *beside)
    one = along_x(1, mine[1])
    across_two = plan.send(near_two + in_three, "z", MIDDLE)
    in_two = plan.send(near_two, "z", INWARD)
    across_two, in_two, near_one = together(across_two, in_two, sum(one[1:], one[0]))
    zero = along_x(0, mine[0])
    pair = plan.send(near_one + across_two, "z", PAIRS)
    across_three = plan.send(near_three + in_two, "z", MIDDLE)
    return zero + [pair, across_three] + beside


def gather(plan, block):
    found = []

    def along_x(value):
        return line_gather(plan, "x", plan.nx, value)

    def add(far_z, line, skip=0):
        for far_x, value in enumerate(line):
            found.append((value, [(far_z, far_x, 0)]))
        for far_x, value in enumerate(line):
            if far_x >= skip:
                found.append((plan.swap(value), [(far_z, far_x, 1)]))

    if plan.nz != 4:
        for far_z, value in enumerate(line_gather(plan, "z", plan.nz, block)):
            add(far_z, along_x(value))
        return found
    line = along_x(block)
    pair = plan.send(block, "z", PAIRS)
    three = plan.send(block, "z", MIDDLE)
    both, three, *line = together(jnp.concatenate([block, pair]), three, *line)
    line_pair = along_x(pair)
    two = plan.send(pair, "z", MIDDLE)
    out_two = plan.send(three, "z", OUTWARD)
    two, out_two, *line_pair = together(two, out_two, *line_pair)
    found.append((both, [(0, 0, 0), (1, 0, 0)]))
    found.append((plan.swap(both), [(0, 0, 1), (1, 0, 1)]))
    line_two = along_x(two + out_two)
    out_three = plan.send(two, "z", OUTWARD)
    out_three, *line_two = together(out_three, *line_two)
    add(0, line, 1)
    add(1, line_pair, 1)
    add(2, line_two)
    add(3, along_x(three + out_three))
    return [(value, slots) for value, slots in found if slots[0][1:] != (0, 0) or slots[0][0] > 1 or len(slots) > 1]


def line_gather(plan, axis, count, value):
    if count == 1:
        return [value]
    if count == 2:
        return [value, plan.send(value, axis, PAIR)]
    pair = plan.send(value, axis, PAIRS)
    across_three = plan.send(value, axis, MIDDLE)
    across_two = plan.send(pair, axis, MIDDLE)
    out_two = plan.send(across_three, axis, OUTWARD)
    out_three = plan.send(across_two, axis, OUTWARD)
    return [value, pair, across_two + out_two, across_three + out_three]


def place_kernel(plan, place_ref, owner_ref, norm_ref, grads_ref, *refs):
    out_refs, refs = refs[: 2 * plan.nz], refs[2 * plan.nz :]
    position_ref, raw, moved, position, sem_in, sem_position, sem_out = refs
    fetch = pltpu.make_async_copy(grads_ref, raw, sem_in)
    fetch.start()
    lists = plan.lists
    owners = owner_ref[...]
    my_z, my_x, my_c = place_ref[0], place_ref[1], place_ref[2]
    count = plan.replicas
    lane_in = lax.broadcasted_iota(jnp.int32, (LANE, LANE), 0)
    lane_out = lax.broadcasted_iota(jnp.int32, (LANE, LANE), 1)
    before = (lane_in < lane_out).astype(jnp.float32).astype(jnp.bfloat16)
    row_out = lax.broadcasted_iota(jnp.int32, (lists, lists), 0)
    row_in = lax.broadcasted_iota(jnp.int32, (lists, lists), 1)
    above = (row_in < row_out).astype(jnp.float32).astype(jnp.bfloat16)
    flags = [(owners == d).astype(jnp.float32).astype(jnp.bfloat16) for d in range(count)]
    inner = jnp.dot(jnp.concatenate(flags, 0), before, preferred_element_type=jnp.float32)
    owner_in = lax.broadcasted_iota(jnp.int32, (count * LANE, LANE), 0)
    owner_out = lax.broadcasted_iota(jnp.int32, (count * LANE, LANE), 1)
    pick = (owner_in // LANE == owner_out).astype(jnp.float32).astype(jnp.bfloat16)
    totals = jnp.dot(jnp.concatenate(flags, 1), pick, preferred_element_type=jnp.float32)
    outer = jnp.dot(above, totals.astype(jnp.bfloat16), preferred_element_type=jnp.float32)
    ranks = jnp.full((lists, LANE), plan.own, jnp.int32)
    result = jnp.zeros((lists, LANE), jnp.int32)
    for z in range(plan.nz):
        for x in range(plan.nx):
            for c in range(2):
                d = plan.index(z, x, c)
                mine = owners == d
                rank = (inner[d * lists : (d + 1) * lists, :] + outer[:, d : d + 1]).astype(jnp.int32)
                start = plan.start(my_z ^ z, my_x ^ x, my_c ^ c)
                first_norm = d * plan.norm_each
                tail = [jnp.zeros((plan.tail, LANE), jnp.float32)]
                for row in range(min(first_norm + plan.norm_each, plan.norm_rows) - 1, first_norm - 1, -1):
                    part = norm_ref[row * LANE // D : row * LANE // D + 1, row * LANE % D : row * LANE % D + LANE]
                    tail.insert(0, part.astype(jnp.float32))
                tail = jnp.concatenate(tail, 0)[: plan.tail]
                moved[pl.ds(pl.multiple_of(start + plan.own, 8), plan.tail), :] = tail
                result = jnp.where(mine, rank + start, result)
                ranks = jnp.where(mine, rank, ranks)
    position_ref[...] = result
    to_scalar = pltpu.make_async_copy(position_ref, position, sem_position)
    to_scalar.start()
    to_scalar.wait()
    fetch.wait()

    line_of = lax.broadcasted_iota(jnp.int32, (lists, LANE), 0)
    cuts = [plan.own * (i + 1) // (8 * PHASES) * 8 for i in range(PHASES - 1)] + [plan.own]
    begin = jnp.int32(0)
    copies = []
    for phase, cut in enumerate(cuts):
        end = plan.blocks // LANE
        if phase < PHASES - 1:
            end = jnp.max(jnp.where(ranks < cut, line_of + 1, 0))

        @pl.loop(begin, end)
        def _(line):
            for part in range(0, LANE, 16):
                rows = raw[pl.ds(pl.multiple_of(line * LANE + part, 16), 16), :].astype(jnp.float32)
                for u in range(16):
                    moved[pl.ds(position[line, part + u], 1), :] = rows[u : u + 1, :]

        begin = end
        low = cuts[phase - 1] if phase else 0
        high = cut if phase < PHASES - 1 else plan.block
        for i, out in enumerate(out_refs):
            start = (i // plan.nz) * plan.half + (plan.nz - 1 - i % plan.nz) * plan.group
            for x in range(plan.nx):
                rows = pl.ds(x * plan.block + low, high - low)
                source = moved.at[pl.ds(start + x * plan.block + low, high - low)]
                copies.append(pltpu.make_async_copy(source, out.at[rows], sem_out.at[len(copies)]))
                copies[-1].start()
    for copy in copies:
        copy.wait()


def place(plan, my_place, owners, norm_grads, grads):
    shapes = [(plan.group, LANE)] * (2 * plan.nz)
    outs = pl.pallas_call(
        functools.partial(place_kernel, plan),
        out_shape=[jax.ShapeDtypeStruct(s, jnp.float32) for s in shapes]
        + [jax.ShapeDtypeStruct((plan.lists, LANE), jnp.int32)],
        in_specs=[
            pl.BlockSpec(memory_space=pltpu.SMEM),
            pl.BlockSpec(memory_space=pltpu.VMEM),
            pl.BlockSpec(memory_space=pltpu.VMEM),
            pl.BlockSpec(memory_space=pl.ANY),
        ],
        out_specs=[pl.BlockSpec(memory_space=pl.ANY)] * len(shapes) + [pl.BlockSpec(memory_space=pltpu.VMEM)],
        scratch_shapes=[
            pltpu.VMEM((plan.blocks, LANE), jnp.bfloat16),
            pltpu.VMEM((2 * plan.half, LANE), jnp.float32),
            pltpu.SMEM((plan.lists, LANE), jnp.int32),
            pltpu.SemaphoreType.DMA,
            pltpu.SemaphoreType.DMA,
            pltpu.SemaphoreType.DMA((len(shapes) * plan.nx * PHASES,)),
        ],
        compiler_params=pltpu.CompilerParams(vmem_limit_bytes=58 * MIB),
        name="place_gradients",
    )(my_place, owners, norm_grads, grads)
    return list(outs[: plan.nz][::-1]), outs[plan.nz : 2 * plan.nz][::-1], outs[-1]


def owned_kernel(plan, place_ref, owner_ref, weights_ref, owned_ref, natural_ref, held, listed, order, sem_in, sem_order):
    fetch = pltpu.make_async_copy(weights_ref, held, sem_in)
    fetch.start()
    lists = plan.lists
    me = plan.index(place_ref[0], place_ref[1], place_ref[2])
    flags = (owner_ref[...] == me).astype(jnp.float32).astype(jnp.bfloat16)
    lane_in = lax.broadcasted_iota(jnp.int32, (LANE, LANE), 0)
    lane_out = lax.broadcasted_iota(jnp.int32, (LANE, LANE), 1)
    upto = (lane_in <= lane_out).astype(jnp.float32).astype(jnp.bfloat16)
    inner = jnp.dot(flags, upto, preferred_element_type=jnp.float32).astype(jnp.bfloat16)
    totals = lax.dot_general(
        jnp.ones((8, LANE), jnp.bfloat16), flags, (((1,), (1,)), ((), ())), preferred_element_type=jnp.float32
    )
    row_in = lax.broadcasted_iota(jnp.int32, (lists, lists), 0)
    row_out = lax.broadcasted_iota(jnp.int32, (lists, lists), 1)
    upto = (row_in <= row_out).astype(jnp.float32).astype(jnp.bfloat16)
    ends = jnp.dot(totals.astype(jnp.bfloat16), upto, preferred_element_type=jnp.float32)[0:1, :]
    place_of = lax.broadcasted_iota(jnp.int32, (LANE, lists), 1).astype(jnp.float32)
    rank_of = lax.broadcasted_iota(jnp.int32, (LANE, 1), 0)
    for step in range(listed.shape[0]):
        if step * LANE >= plan.own:
            break
        rank = (rank_of + step * LANE).astype(jnp.float32)
        passed = ends <= rank
        line = jnp.sum(passed.astype(jnp.float32), axis=1, keepdims=True)
        before = jnp.max(jnp.where(passed, ends, 0.0), axis=1, keepdims=True)
        chosen = (place_of == line).astype(jnp.float32).astype(jnp.bfloat16)
        counts = jnp.dot(chosen, inner, preferred_element_type=jnp.float32)
        column = jnp.sum((counts <= rank - before).astype(jnp.float32), axis=1, keepdims=True)
        block = jnp.broadcast_to((line * LANE + column).astype(jnp.int32), (LANE, LANE))
        natural_ref[step * LANE : (step + 1) * LANE, :] = block
        listed[step : step + 1, :] = jnp.sum(jnp.where(lane_in == lane_out, block, 0), axis=0, keepdims=True)
    to_scalar = pltpu.make_async_copy(listed, order, sem_order)
    to_scalar.start()
    to_scalar.wait()
    fetch.wait()

    def pick(line, count):
        for u in range(count):
            owned_ref[pl.ds(line * LANE + u, 1), :] = held[pl.ds(order[line, u], 1), :]

    @pl.loop(0, plan.own // LANE)
    def _(line):
        pick(line, LANE)

    if plan.own % LANE:
        pick(plan.own // LANE, plan.own % LANE)


def owned(plan, my_place, owners, weights):
    high_rows = -(-plan.own // (8 * LANE)) * 8
    ranks = -(-plan.own // LANE) * LANE
    vmem = pl.BlockSpec(memory_space=pltpu.VMEM)
    return pl.pallas_call(
        functools.partial(owned_kernel, plan),
        out_shape=[
            jax.ShapeDtypeStruct((plan.own, LANE), jnp.float32),
            jax.ShapeDtypeStruct((ranks, LANE), jnp.int32),
        ],
        in_specs=[pl.BlockSpec(memory_space=pltpu.SMEM), vmem, pl.BlockSpec(memory_space=pl.ANY)],
        out_specs=[vmem] * 2,
        scratch_shapes=[
            pltpu.VMEM((plan.blocks, LANE), jnp.float32),
            pltpu.VMEM((high_rows, LANE), jnp.int32),
            pltpu.SMEM((high_rows, LANE), jnp.int32),
            pltpu.SemaphoreType.DMA,
            pltpu.SemaphoreType.DMA,
        ],
        compiler_params=pltpu.CompilerParams(vmem_limit_bytes=58 * MIB),
        cost_estimate=pl.CostEstimate(flops=0, bytes_accessed=20 * MIB, transcendentals=0),
        name="owned_weights",
    )(my_place, owners, weights)


def update_kernel(plan, terms, *refs):
    parts, refs = refs[:terms], refs[terms:]
    first_ref, second_ref, weight_ref, natural_ref = refs[:4]
    new_first_ref, new_second_ref, block_ref, stats_ref = refs[4:]
    gradient = parts[0][: plan.block, :]
    for part in parts[1:]:
        gradient = gradient + part[: plan.block, :]
    block_ref[plan.own :, :] = gradient[plan.own :, :]
    gradient = gradient[: plan.own, :]
    moment_one = beta_one * first_ref[...] + (1.0 - beta_one) * gradient
    moment_two = beta_two * second_ref[...] + (1.0 - beta_two) * gradient * gradient
    new_first_ref[...] = moment_one
    new_second_ref[...] = moment_two
    step = moment_one / bias_one / (jnp.sqrt(moment_two / bias_two) + epsilon)
    block_ref[: plan.own, :] = step
    weight = weight_ref[...]
    direction = step + decay_rate * weight
    natural = natural_ref[: plan.own, :]
    limits = (0,) + plan.bounds + (plan.blocks,)
    lane = lax.broadcasted_iota(jnp.int32, (8, LANE), 1)
    rank = lax.broadcasted_iota(jnp.int32, (8, LANE), 0)
    stats = jnp.zeros((8, LANE), jnp.float32)
    for column, squares in enumerate((weight * weight, direction * direction)):
        for k in range(matrices):
            inside = (natural >= limits[k]) & (natural < limits[k + 1])
            kept = jnp.where(inside, squares, 0.0).reshape(plan.own // 8, 8, LANE)
            total = jnp.sum(jnp.sum(kept, axis=0))
            stats = jnp.where((rank == plan.norm_each + k) & (lane == column), total, stats)
    stats_ref[...] = stats


def update(plan, parts, first, second, weight, natural):
    vmem = pl.BlockSpec(memory_space=pltpu.VMEM)
    shapes = [(plan.own, LANE), (plan.own, LANE), (plan.block, LANE), (plan.tail, LANE)]
    return pl.pallas_call(
        functools.partial(update_kernel, plan, len(parts)),
        out_shape=[jax.ShapeDtypeStruct(s, jnp.float32) for s in shapes],
        in_specs=[vmem] * (len(parts) + 4),
        out_specs=[vmem] * len(shapes),
        compiler_params=pltpu.CompilerParams(vmem_limit_bytes=20 * MIB),
        name="moments",
    )(*parts, first, second, weight, natural)


def adam_rows(gradient, moment_one, moment_two, weight):
    moment_one = beta_one * moment_one + (1.0 - beta_one) * gradient
    moment_two = beta_two * moment_two + (1.0 - beta_two) * gradient * gradient
    step = moment_one / bias_one / (jnp.sqrt(moment_two / bias_two) + epsilon) + decay_rate * weight
    return (moment_one, moment_two, step)


def finish_kernel(plan, tile, slots, place_ref, position_ref, norm_ref, weights_ref, *refs):
    pieces, refs = refs[: len(slots)], refs[len(slots) :]
    out_ref, new_norm_ref, trust_ref, held, norms, rates = refs
    now = pl.program_id(0)

    @pl.when(now == 0)
    def _():
        for piece, parts in zip(pieces, slots):
            for i, slot in enumerate(parts):
                held[pl.ds(plan.start(*slot), plan.block), :] = piece[i * plan.block : (i + 1) * plan.block, :]
        total = jnp.zeros((plan.tail, LANE), jnp.float32)
        for z in range(plan.nz):
            for x in range(plan.nx):
                for c in range(2):
                    start = plan.start(place_ref[0] ^ z, place_ref[1] ^ x, place_ref[2] ^ c) + plan.own
                    tail = held[pl.ds(pl.multiple_of(start, 8), plan.tail), :]
                    total = total + tail
                    first = plan.index(z, x, c) * plan.norm_each
                    for row in range(first, min(first + plan.norm_each, plan.norm_rows)):
                        norms[row : row + 1, :] = tail[row - first : row - first + 1, :]
        for k in range(matrices):
            row = plan.norm_each + k
            weight_square, direction_square = total[row : row + 1, 0:1], total[row : row + 1, 1:2]
            ratio = jnp.sqrt(weight_square) / (jnp.sqrt(direction_square) + epsilon)
            rates[k : k + 1, :] = jnp.broadcast_to(learning * ratio, (1, LANE))
            trust_ref[k] = jnp.sum(ratio)
        each = plan.norm_rows // 2
        for i in range(2):
            gains, first, second = (
                jnp.concatenate([norm_ref[j, i : i + 1, row * LANE : (row + 1) * LANE] for row in range(each)], 0)
                for j in range(3)
            )
            one, two, step = adam_rows(norms[i * each : (i + 1) * each, :], first, second, gains)
            gain_square = jnp.sum(jnp.sum(gains * gains, axis=1, keepdims=True), axis=0, keepdims=True)
            step_square = jnp.sum(jnp.sum(step * step, axis=1, keepdims=True), axis=0, keepdims=True)
            ratio = jnp.sqrt(gain_square) / (jnp.sqrt(step_square) + epsilon)
            trust_ref[matrices + i] = jnp.sum(ratio)
            for j, value in enumerate((gains - learning * ratio * step, one, two)):
                for row in range(each):
                    new_norm_ref[j, i : i + 1, row * LANE : (row + 1) * LANE] = value[row : row + 1, :]

    lines = tile // LANE

    @pl.loop(0, lines)
    def _(line):
        matrix = jnp.int32(0)
        for bound in plan.bounds:
            matrix = matrix + (now * lines + line >= bound // LANE).astype(jnp.int32)
        rate = jnp.broadcast_to(rates[pl.ds(matrix, 1), :], (8, LANE))
        for group in range(0, LANE, 8):
            rows = [held[pl.ds(position_ref[now * lines + line, group + u], 1), :] for u in range(8)]
            here = pl.ds(pl.multiple_of(line * LANE + group, 8), 8)
            weight = weights_ref[here, :]
            direction = jnp.concatenate(rows, 0) + decay_rate * weight
            out_ref[here, :] = weight - rate * direction


def finish(plan, my_place, position, norm_state, weights, pieces, slots):
    assert all(bound % LANE == 0 for bound in plan.bounds + (plan.blocks,))
    tile = plan.blocks // next(n for n in (TILES, 4, 2, 1) if plan.blocks // LANE % n == 0)
    smem = pl.BlockSpec(memory_space=pltpu.SMEM)
    vmem = pl.BlockSpec(memory_space=pltpu.VMEM)
    return pl.pallas_call(
        functools.partial(finish_kernel, plan, tile, slots),
        grid=(plan.blocks // tile,),
        out_shape=[
            jax.ShapeDtypeStruct((plan.blocks, LANE), jnp.float32),
            jax.ShapeDtypeStruct(norm_state.shape, jnp.float32),
            jax.ShapeDtypeStruct((matrices + 2,), jnp.float32),
        ],
        in_specs=[smem, smem, vmem, pl.BlockSpec((tile, LANE), lambda i: (i, 0))]
        + [vmem] * len(pieces),
        out_specs=[pl.BlockSpec((tile, LANE), lambda i: (i, 0)), vmem, smem],
        scratch_shapes=[
            pltpu.VMEM((2 * plan.half, LANE), jnp.float32),
            pltpu.VMEM((plan.norm_rows, LANE), jnp.float32),
            pltpu.VMEM((8, LANE), jnp.float32),
        ],
        compiler_params=pltpu.CompilerParams(vmem_limit_bytes=20 * MIB),
        name="new_weights",
    )(my_place, position, norm_state, weights, *pieces)


def local(gradients, weights, first_moment, second_moment, owner_list, norm_grads, norm_state):
    plan = Plan(lax.axis_size("dp"), lax.axis_size("mp"), weights.shape[0])
    me = lax.axis_index("dp").astype(jnp.int32)
    my_place = jnp.stack([me // (2 * plan.nx), (me // 2) % plan.nx, me % 2]).astype(jnp.int32)
    owners = jnp.pad(owner_list[0], (0, plan.lists * LANE - plan.blocks), constant_values=-1)
    owners = owners.reshape(plan.lists, LANE)
    siblings, blocks, position = place(plan, my_place, owners, norm_grads[0], gradients[0])
    weight_own, natural = owned(plan, my_place, owners, weights)

    mine, theirs = [None] * plan.nz, [None] * plan.nz
    for z in reversed(range(plan.nz)):
        other = plan.swap(siblings[z])
        both = [
            blocks[z][x * plan.block : (x + 1) * plan.block] + other[x * plan.block : (x + 1) * plan.block]
            for x in range(plan.nx)
        ]
        mine[z], theirs[z] = both[0], both[1:]
        if z == 3:
            theirs[3], siblings[2], siblings[1], siblings[0] = together(theirs[3], *siblings[2::-1])
    if plan.nz == 4:
        parts = reduce(plan, mine, theirs, (weight_own, natural))
        parts, (weight_own, natural) = parts[:-2], parts[-2:]
    else:
        near = []
        for z in reversed(range(plan.nz)):
            terms = line_reduce(plan, "x", [mine[z]] + theirs[z])
            near.insert(0, sum(terms[1:], terms[0]) if z else None)
        parts = terms + line_reduce(plan, "z", near)[1:]
    new_first, new_second, block, stats = update(
        plan, parts, first_moment[0], second_moment[0], weight_own, natural
    )

    hop = 1
    while hop < plan.narrow:
        stats = stats + lax.ppermute(stats, "mp", [(i, i ^ hop) for i in range(plan.narrow)])
        hop *= 2
    block = lax.dynamic_update_slice(block, block[plan.own :] + stats, (plan.own, 0))
    found = gather(plan, block)
    pieces, slots = [piece for piece, _ in found], [parts for _, parts in found]
    new_weights, new_state, trust_ratios = finish(plan, my_place, position, norm_state, weights, pieces, slots)
    return (new_weights, new_first[None], new_second[None], new_state, trust_ratios)


def solution(mesh):
    in_specs = (
        P("dp", "mp", None),
        P("mp", None),
        P("mp", "dp", None),
        P("mp", "dp", None),
        P("mp", None),
        P("dp", None, None),
        P(),
    )
    out_specs = (P("mp", None), P("mp", "dp", None), P("mp", "dp", None), P(), P())
    return jax.shard_map(local, mesh=mesh, in_specs=in_specs, out_specs=out_specs, check_vma=False)
```

```python
import functools

import jax
import jax.numpy as jnp
from jax import lax
from jax.experimental import pallas as pl
from jax.experimental.pallas import tpu as pltpu
from jax.sharding import PartitionSpec as P

D = 1024
NTAB = 8
NKEYS = 256
KDIM = 128
LANE = 128
VROW_DEV = 512

beta_one = 0.9
beta_two = 0.99
bias_one = 1.0 - 0.9**4
bias_two = 1.0 - 0.99**4
epsilon = 1e-06
learning = 0.02
decay_rate = 0.01
matrices = 5
MIB = 1 << 20
TILES = 8
PHASES = 2


def matrix_bounds(narrow):
    query_blocks = D * D // (LANE * narrow)
    key_blocks = NTAB * NKEYS * KDIM // (LANE * narrow)
    value_blocks = VROW_DEV * D // LANE
    return (
        query_blocks,
        query_blocks + key_blocks,
        query_blocks + key_blocks + value_blocks,
        2 * query_blocks + key_blocks + value_blocks,
    )


class Plan:
    def __init__(self, replicas, narrow, blocks):
        self.replicas, self.narrow, self.blocks = replicas, narrow, blocks
        chips = replicas // 2
        self.nz = 4 if chips % 4 == 0 else chips
        self.nx = chips // self.nz
        assert self.nz in (1, 2, 4) and self.nx in (1, 2, 4)
        self.own = blocks // replicas
        self.tail = 8
        self.norm_rows = 2 * D // LANE
        self.norm_each = -(-self.norm_rows // replicas)
        self.block = self.own + self.tail
        self.group = self.nx * self.block
        self.half = self.nz * self.group
        self.lists = -(-blocks // (8 * LANE)) * 8
        self.bounds = matrix_bounds(narrow)

    def index(self, z, x, c):
        return (z * self.nx + x) * 2 + c

    def start(self, far_z, far_x, far_c):
        return (1 - far_c) * self.half + far_z * self.group + far_x * self.block

    def send(self, value, axis, pairs):
        every = []
        for z in range(self.nz):
            for x in range(self.nx):
                for c in range(2):
                    here = {"z": z, "x": x, "c": c}
                    for source, target in pairs:
                        if here[axis] == source:
                            every.append((self.index(z, x, c), self.index(**{**here, axis: target})))
        return lax.ppermute(value, "dp", every)

    def swap(self, value):
        return self.send(value, "c", PAIR)


PAIR = [(0, 1), (1, 0)]
PAIRS = [(0, 1), (1, 0), (2, 3), (3, 2)]
MIDDLE = [(1, 2), (2, 1)]
INWARD = [(0, 1), (3, 2)]
OUTWARD = [(1, 0), (2, 3)]


def line_reduce(plan, axis, blocks):
    if len(blocks) == 1:
        return [blocks[0]]
    if len(blocks) == 2:
        return [blocks[0], plan.send(blocks[1], axis, PAIR)]
    in_three = plan.send(blocks[3], axis, INWARD)
    in_two = plan.send(blocks[2], axis, INWARD)
    across_two = plan.send(blocks[2] + in_three, axis, MIDDLE)
    across_three = plan.send(blocks[3] + in_two, axis, MIDDLE)
    pair = plan.send(blocks[1] + across_two, axis, PAIRS)
    return [blocks[0], pair, across_three]


def together(*values):
    return lax.optimization_barrier(values)


def reduce(plan, mine, theirs, beside):
    def along_x(z, own):
        terms = line_reduce(plan, "x", [own] + theirs[z])
        return terms

    three = along_x(3, mine[3])
    two = along_x(2, mine[2])
    near_three = sum(three[1:], three[0])
    in_three = plan.send(near_three, "z", INWARD)
    in_three, near_two, *beside = together(in_three, sum(two[1:], two[0]), *beside)
    one = along_x(1, mine[1])
    across_two = plan.send(near_two + in_three, "z", MIDDLE)
    in_two = plan.send(near_two, "z", INWARD)
    across_two, in_two, near_one = together(across_two, in_two, sum(one[1:], one[0]))
    zero = along_x(0, mine[0])
    pair = plan.send(near_one + across_two, "z", PAIRS)
    across_three = plan.send(near_three + in_two, "z", MIDDLE)
    return zero + [pair, across_three] + beside


def gather(plan, block):
    def along_x(value):
        return line_gather(plan, "x", plan.nx, value)

    if plan.nz != 4:
        lines = [along_x(value) for value in line_gather(plan, "z", plan.nz, block)]
        mine = [(value, [(z, x)]) for z, line in enumerate(lines) for x, value in enumerate(line)]
    else:
        line = along_x(block)
        pair = plan.send(block, "z", PAIRS)
        three = plan.send(block, "z", MIDDLE)
        three, own, *line = together(three, jnp.concatenate([block, pair]), *line)
        line_pair = along_x(pair)
        two = plan.send(pair, "z", MIDDLE)
        out_two = plan.send(three, "z", OUTWARD)
        far = [jnp.concatenate([line[x], line_pair[x]]) for x in range(1, plan.nx)]
        near_two, *far = together(two + out_two, *far)
        line_two = along_x(near_two)
        out_three = plan.send(two, "z", OUTWARD)
        line_three = along_x(three + out_three)
        own, *line_two = together(own, *line_two)
        mine = [(value, [(0, x), (1, x)]) for x, value in enumerate([own] + far)]
        mine += [(value, [(2, x)]) for x, value in enumerate(line_two)]
        mine += [(value, [(3, x)]) for x, value in enumerate(line_three)]
    swapped = [plan.swap(value) for value, _ in mine]
    found = [(value, [slot + (0,) for slot in slots]) for value, slots in mine]
    return found + [(value, [slot + (1,) for slot in slots]) for value, (_, slots) in zip(swapped, mine)]


def line_gather(plan, axis, count, value):
    if count == 1:
        return [value]
    if count == 2:
        return [value, plan.send(value, axis, PAIR)]
    pair = plan.send(value, axis, PAIRS)
    across_three = plan.send(value, axis, MIDDLE)
    across_two = plan.send(pair, axis, MIDDLE)
    out_two = plan.send(across_three, axis, OUTWARD)
    out_three = plan.send(across_two, axis, OUTWARD)
    return [value, pair, across_two + out_two, across_three + out_three]


def place_kernel(plan, place_ref, owner_ref, norm_ref, grads_ref, *refs):
    out_refs, refs = refs[: 2 * plan.nz], refs[2 * plan.nz :]
    position_ref, raw, moved, position, sem_in, sem_position, sem_out = refs
    fetch = pltpu.make_async_copy(grads_ref, raw, sem_in)
    fetch.start()
    lists = plan.lists
    owners = owner_ref[...]
    my_z, my_x, my_c = place_ref[0], place_ref[1], place_ref[2]
    count = plan.replicas
    lane_in = lax.broadcasted_iota(jnp.int32, (LANE, LANE), 0)
    lane_out = lax.broadcasted_iota(jnp.int32, (LANE, LANE), 1)
    before = (lane_in < lane_out).astype(jnp.float32).astype(jnp.bfloat16)
    row_out = lax.broadcasted_iota(jnp.int32, (lists, lists), 0)
    row_in = lax.broadcasted_iota(jnp.int32, (lists, lists), 1)
    above = (row_in < row_out).astype(jnp.float32).astype(jnp.bfloat16)
    flags = [(owners == d).astype(jnp.float32).astype(jnp.bfloat16) for d in range(count)]
    inner = jnp.dot(jnp.concatenate(flags, 0), before, preferred_element_type=jnp.float32)
    owner_in = lax.broadcasted_iota(jnp.int32, (count * LANE, LANE), 0)
    owner_out = lax.broadcasted_iota(jnp.int32, (count * LANE, LANE), 1)
    pick = (owner_in // LANE == owner_out).astype(jnp.float32).astype(jnp.bfloat16)
    totals = jnp.dot(jnp.concatenate(flags, 1), pick, preferred_element_type=jnp.float32)
    outer = jnp.dot(above, totals.astype(jnp.bfloat16), preferred_element_type=jnp.float32)
    ranks = jnp.full((lists, LANE), plan.own, jnp.int32)
    result = jnp.zeros((lists, LANE), jnp.int32)
    for z in range(plan.nz):
        for x in range(plan.nx):
            for c in range(2):
                d = plan.index(z, x, c)
                mine = owners == d
                rank = (inner[d * lists : (d + 1) * lists, :] + outer[:, d : d + 1]).astype(jnp.int32)
                start = plan.start(my_z ^ z, my_x ^ x, my_c ^ c)
                first_norm = d * plan.norm_each
                tail = [jnp.zeros((plan.tail, LANE), jnp.float32)]
                for row in range(min(first_norm + plan.norm_each, plan.norm_rows) - 1, first_norm - 1, -1):
                    part = norm_ref[row * LANE // D : row * LANE // D + 1, row * LANE % D : row * LANE % D + LANE]
                    tail.insert(0, part.astype(jnp.float32))
                tail = jnp.concatenate(tail, 0)[: plan.tail]
                moved[pl.ds(pl.multiple_of(start + plan.own, 8), plan.tail), :] = tail
                result = jnp.where(mine, rank + start, result)
                ranks = jnp.where(mine, rank, ranks)
    position_ref[...] = result
    to_scalar = pltpu.make_async_copy(position_ref, position, sem_position)
    to_scalar.start()
    to_scalar.wait()
    fetch.wait()

    line_of = lax.broadcasted_iota(jnp.int32, (lists, LANE), 0)
    cuts = [plan.own * (i + 1) // (8 * PHASES) * 8 for i in range(PHASES - 1)] + [plan.own]
    begin = jnp.int32(0)
    copies = []
    for phase, cut in enumerate(cuts):
        end = plan.blocks // LANE
        if phase < PHASES - 1:
            end = jnp.max(jnp.where(ranks < cut, line_of + 1, 0))

        @pl.loop(begin, end)
        def _(line):
            for part in range(0, LANE, 16):
                rows = raw[pl.ds(pl.multiple_of(line * LANE + part, 16), 16), :].astype(jnp.float32)
                for u in range(16):
                    moved[pl.ds(position[line, part + u], 1), :] = rows[u : u + 1, :]

        begin = end
        low = cuts[phase - 1] if phase else 0
        high = cut if phase < PHASES - 1 else plan.block
        for i, out in enumerate(out_refs):
            start = (i // plan.nz) * plan.half + (plan.nz - 1 - i % plan.nz) * plan.group
            for x in range(plan.nx):
                rows = pl.ds(x * plan.block + low, high - low)
                source = moved.at[pl.ds(start + x * plan.block + low, high - low)]
                copies.append(pltpu.make_async_copy(source, out.at[rows], sem_out.at[len(copies)]))
                copies[-1].start()
    for copy in copies:
        copy.wait()


def place(plan, my_place, owners, norm_grads, grads):
    shapes = [(plan.group, LANE)] * (2 * plan.nz)
    outs = pl.pallas_call(
        functools.partial(place_kernel, plan),
        out_shape=[jax.ShapeDtypeStruct(s, jnp.float32) for s in shapes]
        + [jax.ShapeDtypeStruct((plan.lists, LANE), jnp.int32)],
        in_specs=[
            pl.BlockSpec(memory_space=pltpu.SMEM),
            pl.BlockSpec(memory_space=pltpu.VMEM),
            pl.BlockSpec(memory_space=pltpu.VMEM),
            pl.BlockSpec(memory_space=pl.ANY),
        ],
        out_specs=[pl.BlockSpec(memory_space=pl.ANY)] * len(shapes) + [pl.BlockSpec(memory_space=pltpu.VMEM)],
        scratch_shapes=[
            pltpu.VMEM((plan.blocks, LANE), jnp.bfloat16),
            pltpu.VMEM((2 * plan.half, LANE), jnp.float32),
            pltpu.SMEM((plan.lists, LANE), jnp.int32),
            pltpu.SemaphoreType.DMA,
            pltpu.SemaphoreType.DMA,
            pltpu.SemaphoreType.DMA((len(shapes) * plan.nx * PHASES,)),
        ],
        compiler_params=pltpu.CompilerParams(vmem_limit_bytes=58 * MIB),
        name="place_gradients",
    )(my_place, owners, norm_grads, grads)
    return list(outs[: plan.nz][::-1]), outs[plan.nz : 2 * plan.nz][::-1], outs[-1]


def owned_kernel(plan, place_ref, owner_ref, weights_ref, owned_ref, natural_ref, held, listed, order, sem_in, sem_order):
    fetch = pltpu.make_async_copy(weights_ref, held, sem_in)
    fetch.start()
    lists = plan.lists
    me = plan.index(place_ref[0], place_ref[1], place_ref[2])
    flags = (owner_ref[...] == me).astype(jnp.float32).astype(jnp.bfloat16)
    lane_in = lax.broadcasted_iota(jnp.int32, (LANE, LANE), 0)
    lane_out = lax.broadcasted_iota(jnp.int32, (LANE, LANE), 1)
    upto = (lane_in <= lane_out).astype(jnp.float32).astype(jnp.bfloat16)
    inner = jnp.dot(flags, upto, preferred_element_type=jnp.float32).astype(jnp.bfloat16)
    totals = lax.dot_general(
        jnp.ones((8, LANE), jnp.bfloat16), flags, (((1,), (1,)), ((), ())), preferred_element_type=jnp.float32
    )
    row_in = lax.broadcasted_iota(jnp.int32, (lists, lists), 0)
    row_out = lax.broadcasted_iota(jnp.int32, (lists, lists), 1)
    upto = (row_in <= row_out).astype(jnp.float32).astype(jnp.bfloat16)
    ends = jnp.dot(totals.astype(jnp.bfloat16), upto, preferred_element_type=jnp.float32)[0:1, :]
    place_of = lax.broadcasted_iota(jnp.int32, (LANE, lists), 1).astype(jnp.float32)
    rank_of = lax.broadcasted_iota(jnp.int32, (LANE, 1), 0)
    for step in range(listed.shape[0]):
        if step * LANE >= plan.own:
            break
        rank = (rank_of + step * LANE).astype(jnp.float32)
        passed = ends <= rank
        line = jnp.sum(passed.astype(jnp.float32), axis=1, keepdims=True)
        before = jnp.max(jnp.where(passed, ends, 0.0), axis=1, keepdims=True)
        chosen = (place_of == line).astype(jnp.float32).astype(jnp.bfloat16)
        counts = jnp.dot(chosen, inner, preferred_element_type=jnp.float32)
        column = jnp.sum((counts <= rank - before).astype(jnp.float32), axis=1, keepdims=True)
        block = jnp.broadcast_to((line * LANE + column).astype(jnp.int32), (LANE, LANE))
        natural_ref[step * LANE : (step + 1) * LANE, :] = block
        listed[step : step + 1, :] = jnp.sum(jnp.where(lane_in == lane_out, block, 0), axis=0, keepdims=True)
    to_scalar = pltpu.make_async_copy(listed, order, sem_order)
    to_scalar.start()
    to_scalar.wait()
    fetch.wait()

    def pick(line, count):
        for u in range(count):
            owned_ref[pl.ds(line * LANE + u, 1), :] = held[pl.ds(order[line, u], 1), :]

    @pl.loop(0, plan.own // LANE)
    def _(line):
        pick(line, LANE)

    if plan.own % LANE:
        pick(plan.own // LANE, plan.own % LANE)


def owned(plan, my_place, owners, weights):
    high_rows = -(-plan.own // (8 * LANE)) * 8
    ranks = -(-plan.own // LANE) * LANE
    vmem = pl.BlockSpec(memory_space=pltpu.VMEM)
    return pl.pallas_call(
        functools.partial(owned_kernel, plan),
        out_shape=[
            jax.ShapeDtypeStruct((plan.own, LANE), jnp.float32),
            jax.ShapeDtypeStruct((ranks, LANE), jnp.int32),
        ],
        in_specs=[pl.BlockSpec(memory_space=pltpu.SMEM), vmem, pl.BlockSpec(memory_space=pl.ANY)],
        out_specs=[vmem] * 2,
        scratch_shapes=[
            pltpu.VMEM((plan.blocks, LANE), jnp.float32),
            pltpu.VMEM((high_rows, LANE), jnp.int32),
            pltpu.SMEM((high_rows, LANE), jnp.int32),
            pltpu.SemaphoreType.DMA,
            pltpu.SemaphoreType.DMA,
        ],
        compiler_params=pltpu.CompilerParams(vmem_limit_bytes=58 * MIB),
        cost_estimate=pl.CostEstimate(flops=0, bytes_accessed=20 * MIB, transcendentals=0),
        name="owned_weights",
    )(my_place, owners, weights)


def update_kernel(plan, terms, *refs):
    parts, refs = refs[:terms], refs[terms:]
    first_ref, second_ref, weight_ref, natural_ref = refs[:4]
    new_first_ref, new_second_ref, block_ref, stats_ref = refs[4:]
    gradient = parts[0][: plan.block, :]
    for part in parts[1:]:
        gradient = gradient + part[: plan.block, :]
    block_ref[plan.own :, :] = gradient[plan.own :, :]
    gradient = gradient[: plan.own, :]
    moment_one = beta_one * first_ref[...] + (1.0 - beta_one) * gradient
    moment_two = beta_two * second_ref[...] + (1.0 - beta_two) * gradient * gradient
    new_first_ref[...] = moment_one
    new_second_ref[...] = moment_two
    step = moment_one / bias_one / (jnp.sqrt(moment_two / bias_two) + epsilon)
    block_ref[: plan.own, :] = step
    weight = weight_ref[...]
    direction = step + decay_rate * weight
    natural = natural_ref[: plan.own, :]
    limits = (0,) + plan.bounds + (plan.blocks,)
    lane = lax.broadcasted_iota(jnp.int32, (8, LANE), 1)
    rank = lax.broadcasted_iota(jnp.int32, (8, LANE), 0)
    stats = jnp.zeros((8, LANE), jnp.float32)
    for column, squares in enumerate((weight * weight, direction * direction)):
        for k in range(matrices):
            inside = (natural >= limits[k]) & (natural < limits[k + 1])
            kept = jnp.where(inside, squares, 0.0).reshape(plan.own // 8, 8, LANE)
            total = jnp.sum(jnp.sum(kept, axis=0))
            stats = jnp.where((rank == plan.norm_each + k) & (lane == column), total, stats)
    stats_ref[...] = stats


def update(plan, parts, first, second, weight, natural):
    vmem = pl.BlockSpec(memory_space=pltpu.VMEM)
    shapes = [(plan.own, LANE), (plan.own, LANE), (plan.block, LANE), (plan.tail, LANE)]
    return pl.pallas_call(
        functools.partial(update_kernel, plan, len(parts)),
        out_shape=[jax.ShapeDtypeStruct(s, jnp.float32) for s in shapes],
        in_specs=[vmem] * (len(parts) + 4),
        out_specs=[vmem] * len(shapes),
        compiler_params=pltpu.CompilerParams(vmem_limit_bytes=20 * MIB),
        name="moments",
    )(*parts, first, second, weight, natural)


def adam_rows(gradient, moment_one, moment_two, weight):
    moment_one = beta_one * moment_one + (1.0 - beta_one) * gradient
    moment_two = beta_two * moment_two + (1.0 - beta_two) * gradient * gradient
    step = moment_one / bias_one / (jnp.sqrt(moment_two / bias_two) + epsilon) + decay_rate * weight
    return (moment_one, moment_two, step)


def finish_kernel(plan, tile, slots, place_ref, position_ref, norm_ref, weights_ref, *refs):
    pieces, refs = refs[: len(slots)], refs[len(slots) :]
    out_ref, new_norm_ref, trust_ref, held, norms, rates = refs
    now = pl.program_id(0)

    @pl.when(now == 0)
    def _():
        for piece, parts in zip(pieces, slots):
            for i, slot in enumerate(parts):
                held[pl.ds(plan.start(*slot), plan.block), :] = piece[i * plan.block : (i + 1) * plan.block, :]
        total = jnp.zeros((plan.tail, LANE), jnp.float32)
        for z in range(plan.nz):
            for x in range(plan.nx):
                for c in range(2):
                    start = plan.start(place_ref[0] ^ z, place_ref[1] ^ x, place_ref[2] ^ c) + plan.own
                    tail = held[pl.ds(pl.multiple_of(start, 8), plan.tail), :]
                    total = total + tail
                    first = plan.index(z, x, c) * plan.norm_each
                    for row in range(first, min(first + plan.norm_each, plan.norm_rows)):
                        norms[row : row + 1, :] = tail[row - first : row - first + 1, :]
        for k in range(matrices):
            row = plan.norm_each + k
            weight_square, direction_square = total[row : row + 1, 0:1], total[row : row + 1, 1:2]
            ratio = jnp.sqrt(weight_square) / (jnp.sqrt(direction_square) + epsilon)
            rates[k : k + 1, :] = jnp.broadcast_to(learning * ratio, (1, LANE))
            trust_ref[k] = jnp.sum(ratio)
        each = plan.norm_rows // 2
        for i in range(2):
            gains, first, second = (
                jnp.concatenate([norm_ref[j, i : i + 1, row * LANE : (row + 1) * LANE] for row in range(each)], 0)
                for j in range(3)
            )
            one, two, step = adam_rows(norms[i * each : (i + 1) * each, :], first, second, gains)
            gain_square = jnp.sum(jnp.sum(gains * gains, axis=1, keepdims=True), axis=0, keepdims=True)
            step_square = jnp.sum(jnp.sum(step * step, axis=1, keepdims=True), axis=0, keepdims=True)
            ratio = jnp.sqrt(gain_square) / (jnp.sqrt(step_square) + epsilon)
            trust_ref[matrices + i] = jnp.sum(ratio)
            for j, value in enumerate((gains - learning * ratio * step, one, two)):
                for row in range(each):
                    new_norm_ref[j, i : i + 1, row * LANE : (row + 1) * LANE] = value[row : row + 1, :]

    lines = tile // LANE

    @pl.loop(0, lines)
    def _(line):
        matrix = jnp.int32(0)
        for bound in plan.bounds:
            matrix = matrix + (now * lines + line >= bound // LANE).astype(jnp.int32)
        rate = jnp.broadcast_to(rates[pl.ds(matrix, 1), :], (8, LANE))
        for group in range(0, LANE, 8):
            rows = [held[pl.ds(position_ref[now * lines + line, group + u], 1), :] for u in range(8)]
            here = pl.ds(pl.multiple_of(line * LANE + group, 8), 8)
            weight = weights_ref[here, :]
            direction = jnp.concatenate(rows, 0) + decay_rate * weight
            out_ref[here, :] = weight - rate * direction


def finish(plan, my_place, position, norm_state, weights, pieces, slots):
    assert all(bound % LANE == 0 for bound in plan.bounds + (plan.blocks,))
    tile = plan.blocks // next(n for n in (TILES, 4, 2, 1) if plan.blocks // LANE % n == 0)
    smem = pl.BlockSpec(memory_space=pltpu.SMEM)
    vmem = pl.BlockSpec(memory_space=pltpu.VMEM)
    return pl.pallas_call(
        functools.partial(finish_kernel, plan, tile, slots),
        grid=(plan.blocks // tile,),
        out_shape=[
            jax.ShapeDtypeStruct((plan.blocks, LANE), jnp.float32),
            jax.ShapeDtypeStruct(norm_state.shape, jnp.float32),
            jax.ShapeDtypeStruct((matrices + 2,), jnp.float32),
        ],
        in_specs=[smem, smem, vmem, pl.BlockSpec((tile, LANE), lambda i: (i, 0))]
        + [vmem] * len(pieces),
        out_specs=[pl.BlockSpec((tile, LANE), lambda i: (i, 0)), vmem, smem],
        scratch_shapes=[
            pltpu.VMEM((2 * plan.half, LANE), jnp.float32),
            pltpu.VMEM((plan.norm_rows, LANE), jnp.float32),
            pltpu.VMEM((8, LANE), jnp.float32),
        ],
        compiler_params=pltpu.CompilerParams(vmem_limit_bytes=20 * MIB),
        name="new_weights",
    )(my_place, position, norm_state, weights, *pieces)


def local(gradients, weights, first_moment, second_moment, owner_list, norm_grads, norm_state):
    plan = Plan(lax.axis_size("dp"), lax.axis_size("mp"), weights.shape[0])
    me = lax.axis_index("dp").astype(jnp.int32)
    my_place = jnp.stack([me // (2 * plan.nx), (me // 2) % plan.nx, me % 2]).astype(jnp.int32)
    owners = jnp.pad(owner_list[0], (0, plan.lists * LANE - plan.blocks), constant_values=-1)
    owners = owners.reshape(plan.lists, LANE)
    siblings, blocks, position = place(plan, my_place, owners, norm_grads[0], gradients[0])
    weight_own, natural = owned(plan, my_place, owners, weights)

    mine, theirs = [None] * plan.nz, [None] * plan.nz
    for z in reversed(range(plan.nz)):
        other = plan.swap(siblings[z])
        both = [
            blocks[z][x * plan.block : (x + 1) * plan.block] + other[x * plan.block : (x + 1) * plan.block]
            for x in range(plan.nx)
        ]
        mine[z], theirs[z] = both[0], both[1:]
        if z == 3:
            theirs[3], siblings[2], siblings[1], siblings[0] = together(theirs[3], *siblings[2::-1])
    if plan.nz == 4:
        parts = reduce(plan, mine, theirs, (weight_own, natural))
        parts, (weight_own, natural) = parts[:-2], parts[-2:]
    else:
        near = []
        for z in reversed(range(plan.nz)):
            terms = line_reduce(plan, "x", [mine[z]] + theirs[z])
            near.insert(0, sum(terms[1:], terms[0]) if z else None)
        parts = terms + line_reduce(plan, "z", near)[1:]
    new_first, new_second, block, stats = update(
        plan, parts, first_moment[0], second_moment[0], weight_own, natural
    )

    hop = 1
    while hop < plan.narrow:
        stats = stats + lax.ppermute(stats, "mp", [(i, i ^ hop) for i in range(plan.narrow)])
        hop *= 2
    block = lax.dynamic_update_slice(block, block[plan.own :] + stats, (plan.own, 0))
    found = gather(plan, block)
    pieces, slots = [piece for piece, _ in found], [parts for _, parts in found]
    new_weights, new_state, trust_ratios = finish(plan, my_place, position, norm_state, weights, pieces, slots)
    return (new_weights, new_first[None], new_second[None], new_state, trust_ratios)


def solution(mesh):
    in_specs = (
        P("dp", "mp", None),
        P("mp", None),
        P("mp", "dp", None),
        P("mp", "dp", None),
        P("mp", None),
        P("dp", None, None),
        P(),
    )
    out_specs = (P("mp", None), P("mp", "dp", None), P("mp", "dp", None), P(), P())
    return jax.shard_map(local, mesh=mesh, in_specs=in_specs, out_specs=out_specs, check_vma=False)
```

```python
import functools

import jax
import jax.numpy as jnp
from jax import lax
from jax.experimental import pallas as pl
from jax.experimental.pallas import tpu as pltpu
from jax.sharding import PartitionSpec as P

D = 1024
NTAB = 8
NKEYS = 256
KDIM = 128
LANE = 128
VROW_DEV = 512

beta_one = 0.9
beta_two = 0.99
bias_one = 1.0 - 0.9**4
bias_two = 1.0 - 0.99**4
epsilon = 1e-06
learning = 0.02
decay_rate = 0.01
matrices = 5
MIB = 1 << 20
TILES = 8
PHASES = 2


def matrix_bounds(narrow):
    query_blocks = D * D // (LANE * narrow)
    key_blocks = NTAB * NKEYS * KDIM // (LANE * narrow)
    value_blocks = VROW_DEV * D // LANE
    return (
        query_blocks,
        query_blocks + key_blocks,
        query_blocks + key_blocks + value_blocks,
        2 * query_blocks + key_blocks + value_blocks,
    )


class Plan:
    def __init__(self, replicas, narrow, blocks):
        self.replicas, self.narrow, self.blocks = replicas, narrow, blocks
        chips = replicas // 2
        self.nz = 4 if chips % 4 == 0 else chips
        self.nx = chips // self.nz
        assert self.nz in (1, 2, 4) and self.nx in (1, 2, 4)
        self.own = blocks // replicas
        self.tail = 8
        self.norm_rows = 2 * D // LANE
        self.norm_each = -(-self.norm_rows // replicas)
        self.block = self.own + self.tail
        self.group = self.nx * self.block
        self.half = self.nz * self.group
        self.lists = -(-blocks // (8 * LANE)) * 8
        self.bounds = matrix_bounds(narrow)

    def index(self, z, x, c):
        return (z * self.nx + x) * 2 + c

    def start(self, far_z, far_x, far_c):
        return (1 - far_c) * self.half + far_z * self.group + far_x * self.block

    def send(self, value, axis, pairs):
        every = []
        for z in range(self.nz):
            for x in range(self.nx):
                for c in range(2):
                    here = {"z": z, "x": x, "c": c}
                    for source, target in pairs:
                        if here[axis] == source:
                            every.append((self.index(z, x, c), self.index(**{**here, axis: target})))
        return lax.ppermute(value, "dp", every)

    def swap(self, value):
        return self.send(value, "c", PAIR)


PAIR = [(0, 1), (1, 0)]
PAIRS = [(0, 1), (1, 0), (2, 3), (3, 2)]
MIDDLE = [(1, 2), (2, 1)]
INWARD = [(0, 1), (3, 2)]
OUTWARD = [(1, 0), (2, 3)]
SECOND = [(0, 2), (2, 0), (1, 3), (3, 1)]


def line_reduce(plan, axis, blocks):
    if len(blocks) == 1:
        return [blocks[0]]
    if len(blocks) == 2:
        return [blocks[0], plan.send(blocks[1], axis, PAIR)]
    in_three = plan.send(blocks[3], axis, INWARD)
    second = plan.send(blocks[2] + in_three, axis, SECOND)
    return [blocks[0], plan.send(blocks[1], axis, PAIRS), second, plan.send(blocks[3], axis, MIDDLE)]


def together(*values):
    return lax.optimization_barrier(values)


def reduce(plan, mine, theirs, beside):
    def along_x(z, own):
        terms = line_reduce(plan, "x", [own] + theirs[z])
        return terms

    three = along_x(3, mine[3])
    near_three = sum(three[1:], three[0])
    in_three = plan.send(near_three, "z", INWARD)
    middle = plan.send(near_three, "z", MIDDLE)
    two = along_x(2, mine[2])
    in_three, middle, near_two, *beside = together(in_three, middle, sum(two[1:], two[0]), *beside)
    second = plan.send(near_two + in_three, "z", SECOND)
    one = along_x(1, mine[1])
    pair = plan.send(sum(one[1:], one[0]), "z", PAIRS)
    zero = along_x(0, mine[0])
    return [add_early(zero[0], second, middle)] + zero[1:] + [pair] + beside


def add_early(*terms):
    def kernel(*refs):
        total = refs[0][...]
        for ref in refs[1:-1]:
            total = total + ref[...]
        refs[-1][...] = total

    vmem = pl.BlockSpec(memory_space=pltpu.VMEM)
    return pl.pallas_call(
        kernel,
        out_shape=jax.ShapeDtypeStruct(terms[0].shape, jnp.float32),
        in_specs=[vmem] * len(terms),
        out_specs=vmem,
        compiler_params=pltpu.CompilerParams(vmem_limit_bytes=8 * MIB),
        cost_estimate=pl.CostEstimate(flops=0, bytes_accessed=36 * MIB, transcendentals=0),
        name="add_early",
    )(*terms)


def gather(plan, block):
    def along_x(value):
        return line_gather(plan, "x", plan.nx, value)

    if plan.nz != 4:
        lines = [along_x(value) for value in line_gather(plan, "z", plan.nz, block)]
        mine = [(value, [(z, x)]) for z, line in enumerate(lines) for x, value in enumerate(line)]
    else:
        line = along_x(block)
        pair = plan.send(block, "z", PAIRS)
        second = plan.send(block, "z", SECOND)
        line_pair = along_x(pair)
        tail, own, *line = together(
            add_early(second[plan.own :], block[plan.own :]), jnp.concatenate([block, pair]), *line
        )
        far = [jnp.concatenate([line[x], line_pair[x]]) for x in range(1, plan.nx)]
        same, tail, *far = together(block, tail, *far)
        middle = plan.send(same, "z", MIDDLE)
        line_two = along_x(second)
        out_three = plan.send(second, "z", OUTWARD)
        line_three = along_x(middle + out_three)
        own, *line_two = together(own, *line_two)
        mine = [(value, [(0, x), (1, x)]) for x, value in enumerate([own] + far)]
        mine += [(value, [(2, x)]) for x, value in enumerate(line_two)]
        mine += [(value, [(3, x)]) for x, value in enumerate(line_three)]
    swapped = [plan.swap(value) for value, _ in mine]
    found = [(value, [slot + (0,) for slot in slots]) for value, slots in mine]
    return found + [(value, [slot + (1,) for slot in slots]) for value, (_, slots) in zip(swapped, mine)]


def line_gather(plan, axis, count, value):
    if count == 1:
        return [value]
    if count == 2:
        return [value, plan.send(value, axis, PAIR)]
    second = plan.send(value, axis, SECOND)
    third = plan.send(value, axis, MIDDLE) + plan.send(second, axis, OUTWARD)
    return [value, plan.send(value, axis, PAIRS), second, third]


def place_kernel(plan, place_ref, owner_ref, norm_ref, grads_ref, *refs):
    out_refs, refs = refs[: 2 * plan.nz], refs[2 * plan.nz :]
    position_ref, raw, moved, position, sem_in, sem_position, sem_out = refs
    fetch = pltpu.make_async_copy(grads_ref, raw, sem_in)
    fetch.start()
    lists = plan.lists
    owners = owner_ref[...]
    my_z, my_x, my_c = place_ref[0], place_ref[1], place_ref[2]
    count = plan.replicas
    lane_in = lax.broadcasted_iota(jnp.int32, (LANE, LANE), 0)
    lane_out = lax.broadcasted_iota(jnp.int32, (LANE, LANE), 1)
    before = (lane_in < lane_out).astype(jnp.float32).astype(jnp.bfloat16)
    row_out = lax.broadcasted_iota(jnp.int32, (lists, lists), 0)
    row_in = lax.broadcasted_iota(jnp.int32, (lists, lists), 1)
    above = (row_in < row_out).astype(jnp.float32).astype(jnp.bfloat16)
    flags = [(owners == d).astype(jnp.float32).astype(jnp.bfloat16) for d in range(count)]
    inner = jnp.dot(jnp.concatenate(flags, 0), before, preferred_element_type=jnp.float32)
    owner_in = lax.broadcasted_iota(jnp.int32, (count * LANE, LANE), 0)
    owner_out = lax.broadcasted_iota(jnp.int32, (count * LANE, LANE), 1)
    pick = (owner_in // LANE == owner_out).astype(jnp.float32).astype(jnp.bfloat16)
    totals = jnp.dot(jnp.concatenate(flags, 1), pick, preferred_element_type=jnp.float32)
    outer = jnp.dot(above, totals.astype(jnp.bfloat16), preferred_element_type=jnp.float32)
    ranks = jnp.full((lists, LANE), plan.own, jnp.int32)
    result = jnp.zeros((lists, LANE), jnp.int32)
    for z in range(plan.nz):
        for x in range(plan.nx):
            for c in range(2):
                d = plan.index(z, x, c)
                mine = owners == d
                rank = (inner[d * lists : (d + 1) * lists, :] + outer[:, d : d + 1]).astype(jnp.int32)
                start = plan.start(my_z ^ z, my_x ^ x, my_c ^ c)
                first_norm = d * plan.norm_each
                tail = [jnp.zeros((plan.tail, LANE), jnp.float32)]
                for row in range(min(first_norm + plan.norm_each, plan.norm_rows) - 1, first_norm - 1, -1):
                    part = norm_ref[row * LANE // D : row * LANE // D + 1, row * LANE % D : row * LANE % D + LANE]
                    tail.insert(0, part.astype(jnp.float32))
                tail = jnp.concatenate(tail, 0)[: plan.tail]
                moved[pl.ds(pl.multiple_of(start + plan.own, 8), plan.tail), :] = tail
                result = jnp.where(mine, rank + start, result)
                ranks = jnp.where(mine, rank, ranks)
    position_ref[...] = result
    to_scalar = pltpu.make_async_copy(position_ref, position, sem_position)
    to_scalar.start()
    to_scalar.wait()
    fetch.wait()

    line_of = lax.broadcasted_iota(jnp.int32, (lists, LANE), 0)
    cuts = [plan.own * (i + 1) // (8 * PHASES) * 8 for i in range(PHASES - 1)] + [plan.own]
    begin = jnp.int32(0)
    copies = []
    for phase, cut in enumerate(cuts):
        end = plan.blocks // LANE
        if phase < PHASES - 1:
            end = jnp.max(jnp.where(ranks < cut, line_of + 1, 0))

        @pl.loop(begin, end)
        def _(line):
            for part in range(0, LANE, 16):
                rows = raw[pl.ds(pl.multiple_of(line * LANE + part, 16), 16), :].astype(jnp.float32)
                for u in range(16):
                    moved[pl.ds(position[line, part + u], 1), :] = rows[u : u + 1, :]

        begin = end
        low = cuts[phase - 1] if phase else 0
        high = cut if phase < PHASES - 1 else plan.block
        for i, out in enumerate(out_refs):
            start = (i // plan.nz) * plan.half + (plan.nz - 1 - i % plan.nz) * plan.group
            for x in range(plan.nx):
                rows = pl.ds(x * plan.block + low, high - low)
                source = moved.at[pl.ds(start + x * plan.block + low, high - low)]
                copies.append(pltpu.make_async_copy(source, out.at[rows], sem_out.at[len(copies)]))
                copies[-1].start()
    for copy in copies:
        copy.wait()


def place(plan, my_place, owners, norm_grads, grads):
    shapes = [(plan.group, LANE)] * (2 * plan.nz)
    outs = pl.pallas_call(
        functools.partial(place_kernel, plan),
        out_shape=[jax.ShapeDtypeStruct(s, jnp.float32) for s in shapes]
        + [jax.ShapeDtypeStruct((plan.lists, LANE), jnp.int32)],
        in_specs=[
            pl.BlockSpec(memory_space=pltpu.SMEM),
            pl.BlockSpec(memory_space=pltpu.VMEM),
            pl.BlockSpec(memory_space=pltpu.VMEM),
            pl.BlockSpec(memory_space=pl.ANY),
        ],
        out_specs=[pl.BlockSpec(memory_space=pl.ANY)] * len(shapes) + [pl.BlockSpec(memory_space=pltpu.VMEM)],
        scratch_shapes=[
            pltpu.VMEM((plan.blocks, LANE), jnp.bfloat16),
            pltpu.VMEM((2 * plan.half, LANE), jnp.float32),
            pltpu.SMEM((plan.lists, LANE), jnp.int32),
            pltpu.SemaphoreType.DMA,
            pltpu.SemaphoreType.DMA,
            pltpu.SemaphoreType.DMA((len(shapes) * plan.nx * PHASES,)),
        ],
        compiler_params=pltpu.CompilerParams(vmem_limit_bytes=58 * MIB),
        name="place_gradients",
    )(my_place, owners, norm_grads, grads)
    return list(outs[: plan.nz][::-1]), outs[plan.nz : 2 * plan.nz][::-1], outs[-1]


def owned_kernel(plan, place_ref, owner_ref, weights_ref, owned_ref, natural_ref, held, listed, order, sem_in, sem_order):
    fetch = pltpu.make_async_copy(weights_ref, held, sem_in)
    fetch.start()
    lists = plan.lists
    me = plan.index(place_ref[0], place_ref[1], place_ref[2])
    flags = (owner_ref[...] == me).astype(jnp.float32).astype(jnp.bfloat16)
    lane_in = lax.broadcasted_iota(jnp.int32, (LANE, LANE), 0)
    lane_out = lax.broadcasted_iota(jnp.int32, (LANE, LANE), 1)
    upto = (lane_in <= lane_out).astype(jnp.float32).astype(jnp.bfloat16)
    inner = jnp.dot(flags, upto, preferred_element_type=jnp.float32).astype(jnp.bfloat16)
    totals = lax.dot_general(
        jnp.ones((8, LANE), jnp.bfloat16), flags, (((1,), (1,)), ((), ())), preferred_element_type=jnp.float32
    )
    row_in = lax.broadcasted_iota(jnp.int32, (lists, lists), 0)
    row_out = lax.broadcasted_iota(jnp.int32, (lists, lists), 1)
    upto = (row_in <= row_out).astype(jnp.float32).astype(jnp.bfloat16)
    ends = jnp.dot(totals.astype(jnp.bfloat16), upto, preferred_element_type=jnp.float32)[0:1, :]
    place_of = lax.broadcasted_iota(jnp.int32, (LANE, lists), 1).astype(jnp.float32)
    rank_of = lax.broadcasted_iota(jnp.int32, (LANE, 1), 0)
    for step in range(listed.shape[0]):
        if step * LANE >= plan.own:
            break
        rank = (rank_of + step * LANE).astype(jnp.float32)
        passed = ends <= rank
        line = jnp.sum(passed.astype(jnp.float32), axis=1, keepdims=True)
        before = jnp.max(jnp.where(passed, ends, 0.0), axis=1, keepdims=True)
        chosen = (place_of == line).astype(jnp.float32).astype(jnp.bfloat16)
        counts = jnp.dot(chosen, inner, preferred_element_type=jnp.float32)
        column = jnp.sum((counts <= rank - before).astype(jnp.float32), axis=1, keepdims=True)
        block = jnp.broadcast_to((line * LANE + column).astype(jnp.int32), (LANE, LANE))
        natural_ref[step * LANE : (step + 1) * LANE, :] = block
        listed[step : step + 1, :] = jnp.sum(jnp.where(lane_in == lane_out, block, 0), axis=0, keepdims=True)
    to_scalar = pltpu.make_async_copy(listed, order, sem_order)
    to_scalar.start()
    to_scalar.wait()
    fetch.wait()

    def pick(line, count):
        for u in range(count):
            owned_ref[pl.ds(line * LANE + u, 1), :] = held[pl.ds(order[line, u], 1), :]

    @pl.loop(0, plan.own // LANE)
    def _(line):
        pick(line, LANE)

    if plan.own % LANE:
        pick(plan.own // LANE, plan.own % LANE)


def owned(plan, my_place, owners, weights):
    high_rows = -(-plan.own // (8 * LANE)) * 8
    ranks = -(-plan.own // LANE) * LANE
    vmem = pl.BlockSpec(memory_space=pltpu.VMEM)
    return pl.pallas_call(
        functools.partial(owned_kernel, plan),
        out_shape=[
            jax.ShapeDtypeStruct((plan.own, LANE), jnp.float32),
            jax.ShapeDtypeStruct((ranks, LANE), jnp.int32),
        ],
        in_specs=[pl.BlockSpec(memory_space=pltpu.SMEM), vmem, pl.BlockSpec(memory_space=pl.ANY)],
        out_specs=[vmem] * 2,
        scratch_shapes=[
            pltpu.VMEM((plan.blocks, LANE), jnp.float32),
            pltpu.VMEM((high_rows, LANE), jnp.int32),
            pltpu.SMEM((high_rows, LANE), jnp.int32),
            pltpu.SemaphoreType.DMA,
            pltpu.SemaphoreType.DMA,
        ],
        compiler_params=pltpu.CompilerParams(vmem_limit_bytes=58 * MIB),
        cost_estimate=pl.CostEstimate(flops=0, bytes_accessed=20 * MIB, transcendentals=0),
        name="owned_weights",
    )(my_place, owners, weights)


def update_kernel(plan, terms, *refs):
    parts, refs = refs[:terms], refs[terms:]
    first_ref, second_ref, weight_ref, natural_ref = refs[:4]
    new_first_ref, new_second_ref, block_ref, stats_ref = refs[4:]
    gradient = parts[0][: plan.block, :]
    for part in parts[1:]:
        gradient = gradient + part[: plan.block, :]
    block_ref[plan.own :, :] = gradient[plan.own :, :]
    gradient = gradient[: plan.own, :]
    moment_one = beta_one * first_ref[...] + (1.0 - beta_one) * gradient
    moment_two = beta_two * second_ref[...] + (1.0 - beta_two) * gradient * gradient
    new_first_ref[...] = moment_one
    new_second_ref[...] = moment_two
    step = moment_one / bias_one / (jnp.sqrt(moment_two / bias_two) + epsilon)
    block_ref[: plan.own, :] = step
    weight = weight_ref[...]
    direction = step + decay_rate * weight
    natural = natural_ref[: plan.own, :]
    limits = (0,) + plan.bounds + (plan.blocks,)
    lane = lax.broadcasted_iota(jnp.int32, (8, LANE), 1)
    rank = lax.broadcasted_iota(jnp.int32, (8, LANE), 0)
    stats = jnp.zeros((8, LANE), jnp.float32)
    for column, squares in enumerate((weight * weight, direction * direction)):
        for k in range(matrices):
            inside = (natural >= limits[k]) & (natural < limits[k + 1])
            kept = jnp.where(inside, squares, 0.0).reshape(plan.own // 8, 8, LANE)
            total = jnp.sum(jnp.sum(kept, axis=0))
            stats = jnp.where((rank == plan.norm_each + k) & (lane == column), total, stats)
    stats_ref[...] = stats


def update(plan, parts, first, second, weight, natural):
    vmem = pl.BlockSpec(memory_space=pltpu.VMEM)
    shapes = [(plan.own, LANE), (plan.own, LANE), (plan.block, LANE), (plan.tail, LANE)]
    return pl.pallas_call(
        functools.partial(update_kernel, plan, len(parts)),
        out_shape=[jax.ShapeDtypeStruct(s, jnp.float32) for s in shapes],
        in_specs=[vmem] * (len(parts) + 4),
        out_specs=[vmem] * len(shapes),
        compiler_params=pltpu.CompilerParams(vmem_limit_bytes=20 * MIB),
        name="moments",
    )(*parts, first, second, weight, natural)


def adam_rows(gradient, moment_one, moment_two, weight):
    moment_one = beta_one * moment_one + (1.0 - beta_one) * gradient
    moment_two = beta_two * moment_two + (1.0 - beta_two) * gradient * gradient
    step = moment_one / bias_one / (jnp.sqrt(moment_two / bias_two) + epsilon) + decay_rate * weight
    return (moment_one, moment_two, step)


def finish_kernel(plan, tile, slots, place_ref, position_ref, norm_ref, weights_ref, *refs):
    pieces, refs = refs[: len(slots)], refs[len(slots) :]
    out_ref, new_norm_ref, trust_ref, held, norms, rates = refs
    now = pl.program_id(0)

    @pl.when(now == 0)
    def _():
        for piece, parts in zip(pieces, slots):
            for i, slot in enumerate(parts):
                held[pl.ds(plan.start(*slot), plan.block), :] = piece[i * plan.block : (i + 1) * plan.block, :]
        total = jnp.zeros((plan.tail, LANE), jnp.float32)
        for z in range(plan.nz):
            for x in range(plan.nx):
                for c in range(2):
                    start = plan.start(place_ref[0] ^ z, place_ref[1] ^ x, place_ref[2] ^ c) + plan.own
                    tail = held[pl.ds(pl.multiple_of(start, 8), plan.tail), :]
                    total = total + tail
                    first = plan.index(z, x, c) * plan.norm_each
                    for row in range(first, min(first + plan.norm_each, plan.norm_rows)):
                        norms[row : row + 1, :] = tail[row - first : row - first + 1, :]
        for k in range(matrices):
            row = plan.norm_each + k
            weight_square, direction_square = total[row : row + 1, 0:1], total[row : row + 1, 1:2]
            ratio = jnp.sqrt(weight_square) / (jnp.sqrt(direction_square) + epsilon)
            rates[k : k + 1, :] = jnp.broadcast_to(learning * ratio, (1, LANE))
            trust_ref[k] = jnp.sum(ratio)
        each = plan.norm_rows // 2
        for i in range(2):
            gains, first, second = (
                jnp.concatenate([norm_ref[j, i : i + 1, row * LANE : (row + 1) * LANE] for row in range(each)], 0)
                for j in range(3)
            )
            one, two, step = adam_rows(norms[i * each : (i + 1) * each, :], first, second, gains)
            gain_square = jnp.sum(jnp.sum(gains * gains, axis=1, keepdims=True), axis=0, keepdims=True)
            step_square = jnp.sum(jnp.sum(step * step, axis=1, keepdims=True), axis=0, keepdims=True)
            ratio = jnp.sqrt(gain_square) / (jnp.sqrt(step_square) + epsilon)
            trust_ref[matrices + i] = jnp.sum(ratio)
            for j, value in enumerate((gains - learning * ratio * step, one, two)):
                for row in range(each):
                    new_norm_ref[j, i : i + 1, row * LANE : (row + 1) * LANE] = value[row : row + 1, :]

    lines = tile // LANE

    @pl.loop(0, lines)
    def _(line):
        matrix = jnp.int32(0)
        for bound in plan.bounds:
            matrix = matrix + (now * lines + line >= bound // LANE).astype(jnp.int32)
        rate = jnp.broadcast_to(rates[pl.ds(matrix, 1), :], (8, LANE))
        for group in range(0, LANE, 8):
            rows = [held[pl.ds(position_ref[now * lines + line, group + u], 1), :] for u in range(8)]
            here = pl.ds(pl.multiple_of(line * LANE + group, 8), 8)
            weight = weights_ref[here, :]
            direction = jnp.concatenate(rows, 0) + decay_rate * weight
            out_ref[here, :] = weight - rate * direction


def finish(plan, my_place, position, norm_state, weights, pieces, slots):
    assert all(bound % LANE == 0 for bound in plan.bounds + (plan.blocks,))
    tile = plan.blocks // next(n for n in (TILES, 4, 2, 1) if plan.blocks // LANE % n == 0)
    smem = pl.BlockSpec(memory_space=pltpu.SMEM)
    vmem = pl.BlockSpec(memory_space=pltpu.VMEM)
    return pl.pallas_call(
        functools.partial(finish_kernel, plan, tile, slots),
        grid=(plan.blocks // tile,),
        out_shape=[
            jax.ShapeDtypeStruct((plan.blocks, LANE), jnp.float32),
            jax.ShapeDtypeStruct(norm_state.shape, jnp.float32),
            jax.ShapeDtypeStruct((matrices + 2,), jnp.float32),
        ],
        in_specs=[smem, smem, vmem, pl.BlockSpec((tile, LANE), lambda i: (i, 0))]
        + [vmem] * len(pieces),
        out_specs=[pl.BlockSpec((tile, LANE), lambda i: (i, 0)), vmem, smem],
        scratch_shapes=[
            pltpu.VMEM((2 * plan.half, LANE), jnp.float32),
            pltpu.VMEM((plan.norm_rows, LANE), jnp.float32),
            pltpu.VMEM((8, LANE), jnp.float32),
        ],
        compiler_params=pltpu.CompilerParams(vmem_limit_bytes=20 * MIB),
        name="new_weights",
    )(my_place, position, norm_state, weights, *pieces)


def local(gradients, weights, first_moment, second_moment, owner_list, norm_grads, norm_state):
    plan = Plan(lax.axis_size("dp"), lax.axis_size("mp"), weights.shape[0])
    me = lax.axis_index("dp").astype(jnp.int32)
    my_place = jnp.stack([me // (2 * plan.nx), (me // 2) % plan.nx, me % 2]).astype(jnp.int32)
    owners = jnp.pad(owner_list[0], (0, plan.lists * LANE - plan.blocks), constant_values=-1)
    owners = owners.reshape(plan.lists, LANE)
    siblings, blocks, position = place(plan, my_place, owners, norm_grads[0], gradients[0])
    weight_own, natural = owned(plan, my_place, owners, weights)

    mine, theirs = [None] * plan.nz, [None] * plan.nz
    for z in reversed(range(plan.nz)):
        other = plan.swap(siblings[z])
        both = [
            blocks[z][x * plan.block : (x + 1) * plan.block] + other[x * plan.block : (x + 1) * plan.block]
            for x in range(plan.nx)
        ]
        mine[z], theirs[z] = both[0], both[1:]
        if z == 3:
            theirs[3], siblings[2], siblings[1], siblings[0] = together(theirs[3], *siblings[2::-1])
    if plan.nz == 4:
        parts = reduce(plan, mine, theirs, (weight_own, natural))
        parts, (weight_own, natural) = parts[:-2], parts[-2:]
    else:
        near = []
        for z in reversed(range(plan.nz)):
            terms = line_reduce(plan, "x", [mine[z]] + theirs[z])
            near.insert(0, sum(terms[1:], terms[0]) if z else None)
        parts = terms + line_reduce(plan, "z", near)[1:]
    new_first, new_second, block, stats = update(
        plan, parts, first_moment[0], second_moment[0], weight_own, natural
    )

    hop = 1
    while hop < plan.narrow:
        stats = stats + lax.ppermute(stats, "mp", [(i, i ^ hop) for i in range(plan.narrow)])
        hop *= 2
    block = lax.dynamic_update_slice(block, block[plan.own :] + stats, (plan.own, 0))
    found = gather(plan, block)
    pieces, slots = [piece for piece, _ in found], [parts for _, parts in found]
    new_weights, new_state, trust_ratios = finish(plan, my_place, position, norm_state, weights, pieces, slots)
    return (new_weights, new_first[None], new_second[None], new_state, trust_ratios)


def solution(mesh):
    in_specs = (
        P("dp", "mp", None),
        P("mp", None),
        P("mp", "dp", None),
        P("mp", "dp", None),
        P("mp", None),
        P("dp", None, None),
        P(),
    )
    out_specs = (P("mp", None), P("mp", "dp", None), P("mp", "dp", None), P(), P())
    return jax.shard_map(local, mesh=mesh, in_specs=in_specs, out_specs=out_specs, check_vma=False)
```

```python
import functools

import jax
import jax.numpy as jnp
from jax import lax
from jax.experimental import pallas as pl
from jax.experimental.pallas import tpu as pltpu
from jax.sharding import PartitionSpec as P

D = 1024
NTAB = 8
NKEYS = 256
KDIM = 128
LANE = 128
VROW_DEV = 512

beta_one = 0.9
beta_two = 0.99
bias_one = 1.0 - 0.9**4
bias_two = 1.0 - 0.99**4
epsilon = 1e-06
learning = 0.02
decay_rate = 0.01
matrices = 5
MIB = 1 << 20
PHASES = 2
EARLY = 0.5


def matrix_bounds(narrow):
    query_blocks = D * D // (LANE * narrow)
    key_blocks = NTAB * NKEYS * KDIM // (LANE * narrow)
    value_blocks = VROW_DEV * D // LANE
    return (
        query_blocks,
        query_blocks + key_blocks,
        query_blocks + key_blocks + value_blocks,
        2 * query_blocks + key_blocks + value_blocks,
    )


class Plan:
    def __init__(self, replicas, narrow, blocks):
        self.replicas, self.narrow, self.blocks = replicas, narrow, blocks
        chips = replicas // 2
        self.nz = 4 if chips % 4 == 0 else chips
        self.nx = chips // self.nz
        assert self.nz in (1, 2, 4) and self.nx in (1, 2, 4)
        self.own = blocks // replicas
        self.tail = 8
        self.norm_rows = 2 * D // LANE
        self.norm_each = -(-self.norm_rows // replicas)
        self.block = self.tail + self.own
        self.early = int(self.own * EARLY / 8 + 0.5) * 8
        self.cut = self.tail + self.early
        self.group = self.nx * self.block
        self.half = self.nz * self.group
        self.lists = -(-blocks // (8 * LANE)) * 8
        self.bounds = matrix_bounds(narrow)

    def index(self, z, x, c):
        return (z * self.nx + x) * 2 + c

    def start(self, far_z, far_x, far_c):
        return (1 - far_c) * self.half + far_z * self.group + far_x * self.block

    def send(self, value, axis, pairs):
        every = []
        for z in range(self.nz):
            for x in range(self.nx):
                for c in range(2):
                    here = {"z": z, "x": x, "c": c}
                    for source, target in pairs:
                        if here[axis] == source:
                            every.append((self.index(z, x, c), self.index(**{**here, axis: target})))
        return lax.ppermute(value, "dp", every)

    def swap(self, value):
        return self.send(value, "c", PAIR)


PAIR = [(0, 1), (1, 0)]
PAIRS = [(0, 1), (1, 0), (2, 3), (3, 2)]
MIDDLE = [(1, 2), (2, 1)]
INWARD = [(0, 1), (3, 2)]
OUTWARD = [(1, 0), (2, 3)]


def line_reduce(plan, axis, blocks):
    if len(blocks) == 1:
        return [blocks[0]]
    if len(blocks) == 2:
        return [blocks[0], plan.send(blocks[1], axis, PAIR)]
    in_three = plan.send(blocks[3], axis, INWARD)
    in_two = plan.send(blocks[2], axis, INWARD)
    across_two = plan.send(blocks[2] + in_three, axis, MIDDLE)
    across_three = plan.send(blocks[3] + in_two, axis, MIDDLE)
    pair = plan.send(blocks[1] + across_two, axis, PAIRS)
    return [blocks[0], pair, across_three]


def together(*values):
    return lax.optimization_barrier(values)


def reduce(plan, mine, theirs, beside):
    def along_x(z, own):
        terms = line_reduce(plan, "x", [own] + theirs[z])
        return terms

    three = along_x(3, mine[3])
    two = along_x(2, mine[2])
    near_three = sum(three[1:], three[0])
    in_three = plan.send(near_three, "z", INWARD)
    in_three, near_two, *beside = together(in_three, sum(two[1:], two[0]), *beside)
    one = along_x(1, mine[1])
    across_two = plan.send(near_two + in_three, "z", MIDDLE)
    in_two = plan.send(near_two, "z", INWARD)
    across_two, in_two, near_one = together(across_two, in_two, sum(one[1:], one[0]))
    zero = along_x(0, mine[0])
    pair = plan.send(near_one + across_two, "z", PAIRS)
    across_three = plan.send(near_three + in_two, "z", MIDDLE)
    return zero + [pair, across_three] + beside


def gather(plan, block):
    def along_x(value):
        return line_gather(plan, "x", plan.nx, value)

    def parts(x, *zs):
        return [((z, x), 0, plan.block) for z in zs]

    if plan.nz != 4:
        lines = [along_x(value) for value in line_gather(plan, "z", plan.nz, block)]
        return [(value, parts(x, z)) for z, line in enumerate(lines) for x, value in enumerate(line)], []
    line = along_x(block)
    pair = plan.send(block, "z", PAIRS)
    three = plan.send(block, "z", MIDDLE)
    three, own, *line = together(three, jnp.concatenate([block, pair]), *line)
    line_pair = along_x(pair)
    two = plan.send(pair, "z", MIDDLE)
    out_two = plan.send(three, "z", OUTWARD)
    far = [jnp.concatenate([line[x], line_pair[x]]) for x in range(1, plan.nx)]
    near_two, *far = together(two + out_two, *far)
    line_two = along_x(near_two)
    out_three = plan.send(two, "z", OUTWARD)
    line_early = along_x(three[: plan.cut] + out_three[: plan.cut])
    line_late = along_x(three[plan.cut :] + out_three[plan.cut :])
    own, *line_two = together(own, *line_two)
    found = [(value, parts(x, 0, 1)) for x, value in enumerate([own] + far)]
    found += [(value, parts(x, 2)) for x, value in enumerate(line_two)]
    found += [(value, [((3, x), 0, plan.cut)]) for x, value in enumerate(line_early)]
    late = [(value, [((3, x), plan.cut, plan.block - plan.cut)]) for x, value in enumerate(line_late)]
    return found, late


def both_cores(plan, found):
    swapped = [(plan.swap(value), parts) for value, parts in found]
    return [(value, [(slot + (0,), low, rows) for slot, low, rows in parts]) for value, parts in found] + [
        (value, [(slot + (1,), low, rows) for slot, low, rows in parts]) for value, parts in swapped
    ]


def line_gather(plan, axis, count, value):
    if count == 1:
        return [value]
    if count == 2:
        return [value, plan.send(value, axis, PAIR)]
    pair = plan.send(value, axis, PAIRS)
    across_three = plan.send(value, axis, MIDDLE)
    across_two = plan.send(pair, axis, MIDDLE)
    out_two = plan.send(across_three, axis, OUTWARD)
    out_three = plan.send(across_two, axis, OUTWARD)
    return [value, pair, across_two + out_two, across_three + out_three]


def place_kernel(plan, place_ref, owner_ref, norm_ref, grads_ref, *refs):
    out_refs, refs = refs[: 2 * plan.nz], refs[2 * plan.nz :]
    position_ref, limit_ref, raw, moved, position, sem_in, sem_position, sem_out = refs
    fetch = pltpu.make_async_copy(grads_ref, raw, sem_in)
    fetch.start()
    lists = plan.lists
    owners = owner_ref[...]
    my_z, my_x, my_c = place_ref[0], place_ref[1], place_ref[2]
    count = plan.replicas
    lane_in = lax.broadcasted_iota(jnp.int32, (LANE, LANE), 0)
    lane_out = lax.broadcasted_iota(jnp.int32, (LANE, LANE), 1)
    before = (lane_in < lane_out).astype(jnp.float32).astype(jnp.bfloat16)
    row_out = lax.broadcasted_iota(jnp.int32, (lists, lists), 0)
    row_in = lax.broadcasted_iota(jnp.int32, (lists, lists), 1)
    above = (row_in < row_out).astype(jnp.float32).astype(jnp.bfloat16)
    flags = [(owners == d).astype(jnp.float32).astype(jnp.bfloat16) for d in range(count)]
    inner = jnp.dot(jnp.concatenate(flags, 0), before, preferred_element_type=jnp.float32)
    owner_in = lax.broadcasted_iota(jnp.int32, (count * LANE, LANE), 0)
    owner_out = lax.broadcasted_iota(jnp.int32, (count * LANE, LANE), 1)
    pick = (owner_in // LANE == owner_out).astype(jnp.float32).astype(jnp.bfloat16)
    totals = jnp.dot(jnp.concatenate(flags, 1), pick, preferred_element_type=jnp.float32)
    outer = jnp.dot(above, totals.astype(jnp.bfloat16), preferred_element_type=jnp.float32)
    ranks = jnp.full((lists, LANE), plan.own, jnp.int32)
    result = jnp.zeros((lists, LANE), jnp.int32)
    for z in range(plan.nz):
        for x in range(plan.nx):
            for c in range(2):
                d = plan.index(z, x, c)
                mine = owners == d
                rank = (inner[d * lists : (d + 1) * lists, :] + outer[:, d : d + 1]).astype(jnp.int32)
                start = plan.start(my_z ^ z, my_x ^ x, my_c ^ c)
                first_norm = d * plan.norm_each
                tail = [jnp.zeros((plan.tail, LANE), jnp.float32)]
                for row in range(min(first_norm + plan.norm_each, plan.norm_rows) - 1, first_norm - 1, -1):
                    part = norm_ref[row * LANE // D : row * LANE // D + 1, row * LANE % D : row * LANE % D + LANE]
                    tail.insert(0, part.astype(jnp.float32))
                tail = jnp.concatenate(tail, 0)[: plan.tail]
                moved[pl.ds(pl.multiple_of(start, 8), plan.tail), :] = tail
                result = jnp.where(mine, rank + (start + plan.tail), result)
                ranks = jnp.where(mine, rank, ranks)
    position_ref[...] = result
    natural = lax.broadcasted_iota(jnp.int32, (lists, LANE), 0) * LANE + lax.broadcasted_iota(jnp.int32, (lists, LANE), 1)
    limit_ref[0] = jnp.min(jnp.where((owners >= 0) & (ranks >= plan.early), natural, plan.blocks))
    to_scalar = pltpu.make_async_copy(position_ref, position, sem_position)
    to_scalar.start()
    to_scalar.wait()
    fetch.wait()

    line_of = lax.broadcasted_iota(jnp.int32, (lists, LANE), 0)
    cuts = [plan.own * (i + 1) // (8 * PHASES) * 8 for i in range(PHASES - 1)] + [plan.own]
    begin = jnp.int32(0)
    copies = []
    for phase, cut in enumerate(cuts):
        end = plan.blocks // LANE
        if phase < PHASES - 1:
            end = jnp.max(jnp.where(ranks < cut, line_of + 1, 0))

        @pl.loop(begin, end)
        def _(line):
            for part in range(0, LANE, 16):
                rows = raw[pl.ds(pl.multiple_of(line * LANE + part, 16), 16), :].astype(jnp.float32)
                for u in range(16):
                    moved[pl.ds(position[line, part + u], 1), :] = rows[u : u + 1, :]

        begin = end
        low = plan.tail + cuts[phase - 1] if phase else 0
        high = plan.tail + cut
        for i, out in enumerate(out_refs):
            start = (i // plan.nz) * plan.half + (plan.nz - 1 - i % plan.nz) * plan.group
            for x in range(plan.nx):
                rows = pl.ds(x * plan.block + low, high - low)
                source = moved.at[pl.ds(start + x * plan.block + low, high - low)]
                copies.append(pltpu.make_async_copy(source, out.at[rows], sem_out.at[len(copies)]))
                copies[-1].start()
    for copy in copies:
        copy.wait()


def place(plan, my_place, owners, norm_grads, grads):
    shapes = [(plan.group, LANE)] * (2 * plan.nz)
    outs = pl.pallas_call(
        functools.partial(place_kernel, plan),
        out_shape=[jax.ShapeDtypeStruct(s, jnp.float32) for s in shapes]
        + [jax.ShapeDtypeStruct((plan.lists, LANE), jnp.int32), jax.ShapeDtypeStruct((1,), jnp.int32)],
        in_specs=[
            pl.BlockSpec(memory_space=pltpu.SMEM),
            pl.BlockSpec(memory_space=pltpu.VMEM),
            pl.BlockSpec(memory_space=pltpu.VMEM),
            pl.BlockSpec(memory_space=pl.ANY),
        ],
        out_specs=[pl.BlockSpec(memory_space=pl.ANY)] * len(shapes)
        + [pl.BlockSpec(memory_space=pltpu.VMEM), pl.BlockSpec(memory_space=pltpu.SMEM)],
        scratch_shapes=[
            pltpu.VMEM((plan.blocks, LANE), jnp.bfloat16),
            pltpu.VMEM((2 * plan.half, LANE), jnp.float32),
            pltpu.SMEM((plan.lists, LANE), jnp.int32),
            pltpu.SemaphoreType.DMA,
            pltpu.SemaphoreType.DMA,
            pltpu.SemaphoreType.DMA((len(shapes) * plan.nx * PHASES,)),
        ],
        compiler_params=pltpu.CompilerParams(vmem_limit_bytes=58 * MIB),
        name="place_gradients",
    )(my_place, owners, norm_grads, grads)
    return list(outs[: plan.nz][::-1]), outs[plan.nz : 2 * plan.nz][::-1], outs[-2], outs[-1]


def owned_kernel(plan, place_ref, owner_ref, weights_ref, owned_ref, natural_ref, held, listed, order, sem_in, sem_order):
    fetch = pltpu.make_async_copy(weights_ref, held, sem_in)
    fetch.start()
    lists = plan.lists
    me = plan.index(place_ref[0], place_ref[1], place_ref[2])
    flags = (owner_ref[...] == me).astype(jnp.float32).astype(jnp.bfloat16)
    lane_in = lax.broadcasted_iota(jnp.int32, (LANE, LANE), 0)
    lane_out = lax.broadcasted_iota(jnp.int32, (LANE, LANE), 1)
    upto = (lane_in <= lane_out).astype(jnp.float32).astype(jnp.bfloat16)
    inner = jnp.dot(flags, upto, preferred_element_type=jnp.float32).astype(jnp.bfloat16)
    totals = lax.dot_general(
        jnp.ones((8, LANE), jnp.bfloat16), flags, (((1,), (1,)), ((), ())), preferred_element_type=jnp.float32
    )
    row_in = lax.broadcasted_iota(jnp.int32, (lists, lists), 0)
    row_out = lax.broadcasted_iota(jnp.int32, (lists, lists), 1)
    upto = (row_in <= row_out).astype(jnp.float32).astype(jnp.bfloat16)
    ends = jnp.dot(totals.astype(jnp.bfloat16), upto, preferred_element_type=jnp.float32)[0:1, :]
    place_of = lax.broadcasted_iota(jnp.int32, (LANE, lists), 1).astype(jnp.float32)
    rank_of = lax.broadcasted_iota(jnp.int32, (LANE, 1), 0)
    for step in range(listed.shape[0]):
        if step * LANE >= plan.own:
            break
        rank = (rank_of + step * LANE).astype(jnp.float32)
        passed = ends <= rank
        line = jnp.sum(passed.astype(jnp.float32), axis=1, keepdims=True)
        before = jnp.max(jnp.where(passed, ends, 0.0), axis=1, keepdims=True)
        chosen = (place_of == line).astype(jnp.float32).astype(jnp.bfloat16)
        counts = jnp.dot(chosen, inner, preferred_element_type=jnp.float32)
        column = jnp.sum((counts <= rank - before).astype(jnp.float32), axis=1, keepdims=True)
        block = jnp.broadcast_to((line * LANE + column).astype(jnp.int32), (LANE, LANE))
        natural_ref[step * LANE : (step + 1) * LANE, :] = block
        listed[step : step + 1, :] = jnp.sum(jnp.where(lane_in == lane_out, block, 0), axis=0, keepdims=True)
    to_scalar = pltpu.make_async_copy(listed, order, sem_order)
    to_scalar.start()
    to_scalar.wait()
    fetch.wait()

    def pick(line, count):
        for u in range(count):
            owned_ref[pl.ds(line * LANE + u, 1), :] = held[pl.ds(order[line, u], 1), :]

    @pl.loop(0, plan.own // LANE)
    def _(line):
        pick(line, LANE)

    if plan.own % LANE:
        pick(plan.own // LANE, plan.own % LANE)


def owned(plan, my_place, owners, weights):
    high_rows = -(-plan.own // (8 * LANE)) * 8
    ranks = -(-plan.own // LANE) * LANE
    vmem = pl.BlockSpec(memory_space=pltpu.VMEM)
    return pl.pallas_call(
        functools.partial(owned_kernel, plan),
        out_shape=[
            jax.ShapeDtypeStruct((plan.own, LANE), jnp.float32),
            jax.ShapeDtypeStruct((ranks, LANE), jnp.int32),
        ],
        in_specs=[pl.BlockSpec(memory_space=pltpu.SMEM), vmem, pl.BlockSpec(memory_space=pl.ANY)],
        out_specs=[vmem] * 2,
        scratch_shapes=[
            pltpu.VMEM((plan.blocks, LANE), jnp.float32),
            pltpu.VMEM((high_rows, LANE), jnp.int32),
            pltpu.SMEM((high_rows, LANE), jnp.int32),
            pltpu.SemaphoreType.DMA,
            pltpu.SemaphoreType.DMA,
        ],
        compiler_params=pltpu.CompilerParams(vmem_limit_bytes=58 * MIB),
        cost_estimate=pl.CostEstimate(flops=0, bytes_accessed=20 * MIB, transcendentals=0),
        name="owned_weights",
    )(my_place, owners, weights)


def update_kernel(plan, terms, *refs):
    parts, refs = refs[:terms], refs[terms:]
    first_ref, second_ref, weight_ref, natural_ref = refs[:4]
    new_first_ref, new_second_ref, block_ref, stats_ref = refs[4:]
    gradient = parts[0][: plan.block, :]
    for part in parts[1:]:
        gradient = gradient + part[: plan.block, :]
    block_ref[: plan.tail, :] = gradient[: plan.tail, :]
    gradient = gradient[plan.tail :, :]
    moment_one = beta_one * first_ref[...] + (1.0 - beta_one) * gradient
    moment_two = beta_two * second_ref[...] + (1.0 - beta_two) * gradient * gradient
    new_first_ref[...] = moment_one
    new_second_ref[...] = moment_two
    step = moment_one / bias_one / (jnp.sqrt(moment_two / bias_two) + epsilon)
    block_ref[plan.tail :, :] = step
    weight = weight_ref[...]
    direction = step + decay_rate * weight
    natural = natural_ref[: plan.own, :]
    limits = (0,) + plan.bounds + (plan.blocks,)
    lane = lax.broadcasted_iota(jnp.int32, (8, LANE), 1)
    rank = lax.broadcasted_iota(jnp.int32, (8, LANE), 0)
    stats = jnp.zeros((8, LANE), jnp.float32)
    for column, squares in enumerate((weight * weight, direction * direction)):
        for k in range(matrices):
            inside = (natural >= limits[k]) & (natural < limits[k + 1])
            kept = jnp.where(inside, squares, 0.0).reshape(plan.own // 8, 8, LANE)
            total = jnp.sum(jnp.sum(kept, axis=0))
            stats = jnp.where((rank == plan.norm_each + k) & (lane == column), total, stats)
    stats_ref[...] = stats


def update(plan, parts, first, second, weight, natural):
    vmem = pl.BlockSpec(memory_space=pltpu.VMEM)
    shapes = [(plan.own, LANE), (plan.own, LANE), (plan.block, LANE), (plan.tail, LANE)]
    return pl.pallas_call(
        functools.partial(update_kernel, plan, len(parts)),
        out_shape=[jax.ShapeDtypeStruct(s, jnp.float32) for s in shapes],
        in_specs=[vmem] * (len(parts) + 4),
        out_specs=[vmem] * len(shapes),
        compiler_params=pltpu.CompilerParams(vmem_limit_bytes=20 * MIB),
        name="moments",
    )(*parts, first, second, weight, natural)


def adam_rows(gradient, moment_one, moment_two, weight):
    moment_one = beta_one * moment_one + (1.0 - beta_one) * gradient
    moment_two = beta_two * moment_two + (1.0 - beta_two) * gradient * gradient
    step = moment_one / bias_one / (jnp.sqrt(moment_two / bias_two) + epsilon) + decay_rate * weight
    return (moment_one, moment_two, step)


def lay(plan, pieces, parts, held):
    for piece, own_parts in zip(pieces, parts):
        first = 0
        for slot, low, rows in own_parts:
            held[pl.ds(plan.start(*slot) + low, rows), :] = piece[first : first + rows, :]
            first += rows


def tile_of(plan):
    assert all(bound % LANE == 0 for bound in plan.bounds + (plan.blocks,))
    return next(n * LANE for n in (8, 4, 2, 1) if plan.blocks // LANE % n == 0)


def new_tile(plan, now, position_ref, rates, weights_ref, held, out_ref):
    lines = tile_of(plan) // LANE

    @pl.loop(0, lines)
    def _(line):
        matrix = jnp.int32(0)
        for bound in plan.bounds:
            matrix = matrix + (now * lines + line >= bound // LANE).astype(jnp.int32)
        rate = jnp.broadcast_to(rates[pl.ds(matrix, 1), :], (8, LANE))
        for group in range(0, LANE, 8):
            rows = [held[pl.ds(position_ref[now * lines + line, group + u], 1), :] for u in range(8)]
            here = pl.ds(pl.multiple_of(line * LANE + group, 8), 8)
            weight = weights_ref[here, :]
            direction = jnp.concatenate(rows, 0) + decay_rate * weight
            out_ref[here, :] = weight - rate * direction


def early_kernel(plan, parts, limit_ref, place_ref, position_ref, norm_ref, weights_ref, *refs):
    pieces, refs = refs[: len(parts)], refs[len(parts) :]
    out_ref, rates, new_norm_ref, trust_ref, held, norms = refs
    now = pl.program_id(0)

    @pl.when(now == 0)
    def _():
        lay(plan, pieces, parts, held)
        total = jnp.zeros((plan.tail, LANE), jnp.float32)
        for z in range(plan.nz):
            for x in range(plan.nx):
                for c in range(2):
                    start = plan.start(place_ref[0] ^ z, place_ref[1] ^ x, place_ref[2] ^ c)
                    tail = held[pl.ds(pl.multiple_of(start, 8), plan.tail), :]
                    total = total + tail
                    first = plan.index(z, x, c) * plan.norm_each
                    for row in range(first, min(first + plan.norm_each, plan.norm_rows)):
                        norms[row : row + 1, :] = tail[row - first : row - first + 1, :]
        rates[...] = jnp.zeros_like(rates)
        for k in range(matrices):
            row = plan.norm_each + k
            weight_square, direction_square = total[row : row + 1, 0:1], total[row : row + 1, 1:2]
            ratio = jnp.sqrt(weight_square) / (jnp.sqrt(direction_square) + epsilon)
            rates[k : k + 1, :] = jnp.broadcast_to(learning * ratio, (1, LANE))
            trust_ref[k] = jnp.sum(ratio)
        each = plan.norm_rows // 2
        for i in range(2):
            gains, first, second = (
                jnp.concatenate([norm_ref[j, i : i + 1, row * LANE : (row + 1) * LANE] for row in range(each)], 0)
                for j in range(3)
            )
            one, two, step = adam_rows(norms[i * each : (i + 1) * each, :], first, second, gains)
            gain_square = jnp.sum(jnp.sum(gains * gains, axis=1, keepdims=True), axis=0, keepdims=True)
            step_square = jnp.sum(jnp.sum(step * step, axis=1, keepdims=True), axis=0, keepdims=True)
            ratio = jnp.sqrt(gain_square) / (jnp.sqrt(step_square) + epsilon)
            trust_ref[matrices + i] = jnp.sum(ratio)
            for j, value in enumerate((gains - learning * ratio * step, one, two)):
                for row in range(each):
                    new_norm_ref[j, i : i + 1, row * LANE : (row + 1) * LANE] = value[row : row + 1, :]

    @pl.when((now + 1) * tile_of(plan) <= limit_ref[0])
    def _():
        new_tile(plan, now, position_ref, rates, weights_ref, held, out_ref)


def late_kernel(plan, parts, limit_ref, position_ref, rates_ref, weights_ref, early_ref, *refs):
    pieces, (out_ref, held) = refs[: len(parts)], refs[len(parts) :]
    now = pl.program_id(0)

    @pl.when(now == 0)
    def _():
        lay(plan, pieces, parts, held)

    @pl.when((now + 1) * tile_of(plan) > limit_ref[0])
    def _():
        new_tile(plan, now, position_ref, rates_ref, weights_ref, held, out_ref)


def finish(plan, my_place, limit, position, norm_state, weights, early, late):
    tile = tile_of(plan)
    count = plan.blocks // tile
    smem = pl.BlockSpec(memory_space=pltpu.SMEM)
    vmem = pl.BlockSpec(memory_space=pltpu.VMEM)
    params = pltpu.CompilerParams(vmem_limit_bytes=16 * MIB)

    def early_tile(i, limit_ref):
        return (jnp.maximum(jnp.minimum(i, limit_ref[0] // tile - 1), 0), 0)

    def late_tile(i, limit_ref):
        return (jnp.minimum(jnp.maximum(i, limit_ref[0] // tile), count - 1), 0)

    early = both_cores(plan, early)
    shape = jax.ShapeDtypeStruct((plan.blocks, LANE), jnp.float32)
    new_weights, rates, new_norm, trust = pl.pallas_call(
        functools.partial(early_kernel, plan, [parts for _, parts in early]),
        grid_spec=pltpu.PrefetchScalarGridSpec(
            num_scalar_prefetch=1,
            grid=(count,),
            in_specs=[smem, smem, vmem, pl.BlockSpec((tile, LANE), early_tile)] + [vmem] * len(early),
            out_specs=[pl.BlockSpec((tile, LANE), early_tile), vmem, vmem, smem],
            scratch_shapes=[
                pltpu.VMEM((2 * plan.half, LANE), jnp.float32),
                pltpu.VMEM((plan.norm_rows, LANE), jnp.float32),
            ],
        ),
        out_shape=[
            shape,
            jax.ShapeDtypeStruct((8, LANE), jnp.float32),
            jax.ShapeDtypeStruct(norm_state.shape, jnp.float32),
            jax.ShapeDtypeStruct((matrices + 2,), jnp.float32),
        ],
        compiler_params=params,
        cost_estimate=pl.CostEstimate(flops=0, bytes_accessed=36 * MIB, transcendentals=0),
        name="new_weights_early",
    )(limit, my_place, position, norm_state, weights, *(value for value, _ in early))
    if late:
        rates, *values = together(rates, *(value for value, _ in late))
        late = [(value, parts) for value, (_, parts) in zip(values, late)]
    pieces = early + both_cores(plan, late)
    new_weights = pl.pallas_call(
        functools.partial(late_kernel, plan, [parts for _, parts in pieces]),
        grid_spec=pltpu.PrefetchScalarGridSpec(
            num_scalar_prefetch=1,
            grid=(count,),
            in_specs=[smem, vmem, pl.BlockSpec((tile, LANE), late_tile), pl.BlockSpec(memory_space=pl.ANY)]
            + [vmem] * len(pieces),
            out_specs=pl.BlockSpec((tile, LANE), late_tile),
            scratch_shapes=[pltpu.VMEM((2 * plan.half, LANE), jnp.float32)],
        ),
        out_shape=shape,
        input_output_aliases={4: 0},
        compiler_params=params,
        name="new_weights_late",
    )(limit, position, rates, weights, new_weights, *(value for value, _ in pieces))
    return new_weights, new_norm, trust


def local(gradients, weights, first_moment, second_moment, owner_list, norm_grads, norm_state):
    plan = Plan(lax.axis_size("dp"), lax.axis_size("mp"), weights.shape[0])
    me = lax.axis_index("dp").astype(jnp.int32)
    my_place = jnp.stack([me // (2 * plan.nx), (me // 2) % plan.nx, me % 2]).astype(jnp.int32)
    owners = jnp.pad(owner_list[0], (0, plan.lists * LANE - plan.blocks), constant_values=-1)
    owners = owners.reshape(plan.lists, LANE)
    siblings, blocks, position, limit = place(plan, my_place, owners, norm_grads[0], gradients[0])
    weight_own, natural = owned(plan, my_place, owners, weights)

    mine, theirs = [None] * plan.nz, [None] * plan.nz
    for z in reversed(range(plan.nz)):
        other = plan.swap(siblings[z])
        both = [
            blocks[z][x * plan.block : (x + 1) * plan.block] + other[x * plan.block : (x + 1) * plan.block]
            for x in range(plan.nx)
        ]
        mine[z], theirs[z] = both[0], both[1:]
        if z == 3:
            theirs[3], siblings[2], siblings[1], siblings[0] = together(theirs[3], *siblings[2::-1])
    if plan.nz == 4:
        parts = reduce(plan, mine, theirs, (weight_own, natural))
        parts, (weight_own, natural) = parts[:-2], parts[-2:]
    else:
        near = []
        for z in reversed(range(plan.nz)):
            terms = line_reduce(plan, "x", [mine[z]] + theirs[z])
            near.insert(0, sum(terms[1:], terms[0]) if z else None)
        parts = terms + line_reduce(plan, "z", near)[1:]
    new_first, new_second, block, stats = update(
        plan, parts, first_moment[0], second_moment[0], weight_own, natural
    )

    hop = 1
    while hop < plan.narrow:
        stats = stats + lax.ppermute(stats, "mp", [(i, i ^ hop) for i in range(plan.narrow)])
        hop *= 2
    block = lax.dynamic_update_slice(block, block[: plan.tail] + stats, (0, 0))
    early, late = gather(plan, block)
    new_weights, new_state, trust_ratios = finish(
        plan, my_place, limit, position, norm_state, weights, early, late
    )
    return (new_weights, new_first[None], new_second[None], new_state, trust_ratios)


def solution(mesh):
    in_specs = (
        P("dp", "mp", None),
        P("mp", None),
        P("mp", "dp", None),
        P("mp", "dp", None),
        P("mp", None),
        P("dp", None, None),
        P(),
    )
    out_specs = (P("mp", None), P("mp", "dp", None), P("mp", "dp", None), P(), P())
    return jax.shard_map(local, mesh=mesh, in_specs=in_specs, out_specs=out_specs, check_vma=False)
```

```python
import functools

import jax
import jax.numpy as jnp
from jax import lax
from jax.experimental import pallas as pl
from jax.experimental.pallas import tpu as pltpu
from jax.sharding import PartitionSpec as P

D = 1024
NTAB = 8
NKEYS = 256
KDIM = 128
LANE = 128
VROW_DEV = 512

beta_one = 0.9
beta_two = 0.99
bias_one = 1.0 - 0.9**4
bias_two = 1.0 - 0.99**4
epsilon = 1e-06
learning = 0.02
decay_rate = 0.01
matrices = 5
MIB = 1 << 20
TILES = 8
PHASES = 2


def matrix_bounds(narrow):
    query_blocks = D * D // (LANE * narrow)
    key_blocks = NTAB * NKEYS * KDIM // (LANE * narrow)
    value_blocks = VROW_DEV * D // LANE
    return (
        query_blocks,
        query_blocks + key_blocks,
        query_blocks + key_blocks + value_blocks,
        2 * query_blocks + key_blocks + value_blocks,
    )


class Plan:
    def __init__(self, replicas, narrow, blocks):
        self.replicas, self.narrow, self.blocks = replicas, narrow, blocks
        chips = replicas // 2
        self.nz = 4 if chips % 4 == 0 else chips
        self.nx = chips // self.nz
        assert self.nz in (1, 2, 4) and self.nx in (1, 2, 4)
        self.own = blocks // replicas
        self.tail = 8
        self.norm_rows = 2 * D // LANE
        self.norm_each = -(-self.norm_rows // replicas)
        self.block = self.own + self.tail
        self.group = self.nx * self.block
        self.half = self.nz * self.group
        self.lists = -(-blocks // (8 * LANE)) * 8
        self.bounds = matrix_bounds(narrow)

    def index(self, z, x, c):
        return (z * self.nx + x) * 2 + c

    def start(self, far_z, far_x, far_c):
        return (1 - far_c) * self.half + far_z * self.group + far_x * self.block

    def send(self, value, axis, pairs):
        every = []
        for z in range(self.nz):
            for x in range(self.nx):
                for c in range(2):
                    here = {"z": z, "x": x, "c": c}
                    for source, target in pairs:
                        if here[axis] == source:
                            every.append((self.index(z, x, c), self.index(**{**here, axis: target})))
        return lax.ppermute(value, "dp", every)

    def swap(self, value):
        return self.send(value, "c", PAIR)


PAIR = [(0, 1), (1, 0)]
PAIRS = [(0, 1), (1, 0), (2, 3), (3, 2)]
MIDDLE = [(1, 2), (2, 1)]
INWARD = [(0, 1), (3, 2)]
OUTWARD = [(1, 0), (2, 3)]


def line_reduce(plan, axis, blocks):
    if len(blocks) == 1:
        return [blocks[0]]
    if len(blocks) == 2:
        return [blocks[0], plan.send(blocks[1], axis, PAIR)]
    in_three = plan.send(blocks[3], axis, INWARD)
    in_two = plan.send(blocks[2], axis, INWARD)
    across_two = plan.send(blocks[2] + in_three, axis, MIDDLE)
    across_three = plan.send(blocks[3] + in_two, axis, MIDDLE)
    pair = plan.send(blocks[1] + across_two, axis, PAIRS)
    return [blocks[0], pair, across_three]


def together(*values):
    return lax.optimization_barrier(values)


def reduce(plan, mine, theirs, beside):
    def along_x(z, own):
        terms = line_reduce(plan, "x", [own] + theirs[z])
        return terms

    three = along_x(3, mine[3])
    two = along_x(2, mine[2])
    near_three = sum(three[1:], three[0])
    in_three = plan.send(near_three, "z", INWARD)
    in_three, near_two, *beside = together(in_three, sum(two[1:], two[0]), *beside)
    one = along_x(1, mine[1])
    across_two = plan.send(near_two + in_three, "z", MIDDLE)
    in_two = plan.send(near_two, "z", INWARD)
    across_two, in_two, near_one = together(across_two, in_two, sum(one[1:], one[0]))
    zero = along_x(0, mine[0])
    pair = plan.send(near_one + across_two, "z", PAIRS)
    across_three = plan.send(near_three + in_two, "z", MIDDLE)
    return zero + [pair, across_three] + beside


def sums_kernel(plan, place_ref, *refs):
    tails, (out_ref, held) = refs[: plan.nz], refs[plan.nz :]
    for far_z, tail in enumerate(tails):
        held[place_ref[0] ^ far_z] = tail[...]
    total = held[0]
    for z in range(1, plan.nz):
        total = total + held[z]
    out_ref[...] = total


def all_sums(plan, my_place, blocks):
    def tail_of(row):
        return pl.BlockSpec((plan.tail, LANE), lambda i: ((row + plan.own) // plan.tail, 0))

    specs = [tail_of(row) for _, row in blocks]
    total = pl.pallas_call(
        functools.partial(sums_kernel, plan),
        grid=(1,),
        out_shape=jax.ShapeDtypeStruct((plan.tail, LANE), jnp.float32),
        in_specs=[pl.BlockSpec(memory_space=pltpu.SMEM)] + specs,
        out_specs=pl.BlockSpec(memory_space=pltpu.VMEM),
        scratch_shapes=[pltpu.VMEM((plan.nz, plan.tail, LANE), jnp.float32)],
        compiler_params=pltpu.CompilerParams(vmem_limit_bytes=4 * MIB),
        name="sums",
    )(my_place, *(value for value, _ in blocks))
    hop = 1
    while hop < plan.nx:
        total = total + plan.send(total, "x", [(i, i ^ hop) for i in range(plan.nx)])
        hop *= 2
    total = total + plan.swap(total)
    hop = 1
    while hop < plan.narrow:
        total = total + lax.ppermute(total, "mp", [(i, i ^ hop) for i in range(plan.narrow)])
        hop *= 2
    return total


def gather(plan, my_place, block):
    def along_x(value):
        return line_gather(plan, "x", plan.nx, value)

    if plan.nz != 4:
        lines = [along_x(value) for value in line_gather(plan, "z", plan.nz, block)]
        total = all_sums(plan, my_place, [(line[0], 0) for line in lines])
        mine = [(value, [(z, x)]) for z, line in enumerate(lines) for x, value in enumerate(line)]
    else:
        line = along_x(block)
        pair = plan.send(block, "z", PAIRS)
        three = plan.send(block, "z", MIDDLE)
        three, own, *line = together(three, jnp.concatenate([block, pair]), *line)
        line_pair = along_x(pair)
        two = plan.send(pair, "z", MIDDLE)
        out_two = plan.send(three, "z", OUTWARD)
        far = [jnp.concatenate([line[x], line_pair[x]]) for x in range(1, plan.nx)]
        near_two, *far = together(two + out_two, *far)
        line_two = along_x(near_two)
        out_three = plan.send(two, "z", OUTWARD)
        near_three = three + out_three
        line_three = along_x(near_three)
        total = all_sums(plan, my_place, [(own, 0), (own, plan.block), (near_two, 0), (near_three, 0)])
        own, *line_two = together(own, *line_two)
        total, *line_three = together(total, *line_three)
        mine = [(value, [(0, x), (1, x)]) for x, value in enumerate([own] + far)]
        mine += [(value, [(2, x)]) for x, value in enumerate(line_two)]
        mine += [(value, [(3, x)]) for x, value in enumerate(line_three)]
    swapped = [plan.swap(value) for value, _ in mine]
    found = [(value, [slot + (0,) for slot in slots]) for value, slots in mine]
    found += [(value, [slot + (1,) for slot in slots]) for value, (_, slots) in zip(swapped, mine)]
    return found, total


def line_gather(plan, axis, count, value):
    if count == 1:
        return [value]
    if count == 2:
        return [value, plan.send(value, axis, PAIR)]
    pair = plan.send(value, axis, PAIRS)
    across_three = plan.send(value, axis, MIDDLE)
    across_two = plan.send(pair, axis, MIDDLE)
    out_two = plan.send(across_three, axis, OUTWARD)
    out_three = plan.send(across_two, axis, OUTWARD)
    return [value, pair, across_two + out_two, across_three + out_three]


def place_kernel(plan, place_ref, owner_ref, norm_ref, grads_ref, *refs):
    out_refs, refs = refs[: 2 * plan.nz], refs[2 * plan.nz :]
    position_ref, raw, moved, position, sem_in, sem_position, sem_out = refs
    fetch = pltpu.make_async_copy(grads_ref, raw, sem_in)
    fetch.start()
    lists = plan.lists
    owners = owner_ref[...]
    my_z, my_x, my_c = place_ref[0], place_ref[1], place_ref[2]
    count = plan.replicas
    lane_in = lax.broadcasted_iota(jnp.int32, (LANE, LANE), 0)
    lane_out = lax.broadcasted_iota(jnp.int32, (LANE, LANE), 1)
    before = (lane_in < lane_out).astype(jnp.float32).astype(jnp.bfloat16)
    row_out = lax.broadcasted_iota(jnp.int32, (lists, lists), 0)
    row_in = lax.broadcasted_iota(jnp.int32, (lists, lists), 1)
    above = (row_in < row_out).astype(jnp.float32).astype(jnp.bfloat16)
    flags = [(owners == d).astype(jnp.float32).astype(jnp.bfloat16) for d in range(count)]
    inner = jnp.dot(jnp.concatenate(flags, 0), before, preferred_element_type=jnp.float32)
    owner_in = lax.broadcasted_iota(jnp.int32, (count * LANE, LANE), 0)
    owner_out = lax.broadcasted_iota(jnp.int32, (count * LANE, LANE), 1)
    pick = (owner_in // LANE == owner_out).astype(jnp.float32).astype(jnp.bfloat16)
    totals = jnp.dot(jnp.concatenate(flags, 1), pick, preferred_element_type=jnp.float32)
    outer = jnp.dot(above, totals.astype(jnp.bfloat16), preferred_element_type=jnp.float32)
    ranks = jnp.full((lists, LANE), plan.own, jnp.int32)
    result = jnp.zeros((lists, LANE), jnp.int32)
    for z in range(plan.nz):
        for x in range(plan.nx):
            for c in range(2):
                d = plan.index(z, x, c)
                mine = owners == d
                rank = (inner[d * lists : (d + 1) * lists, :] + outer[:, d : d + 1]).astype(jnp.int32)
                start = plan.start(my_z ^ z, my_x ^ x, my_c ^ c)
                first_norm = d * plan.norm_each
                tail = [jnp.zeros((plan.tail, LANE), jnp.float32)]
                for row in range(min(first_norm + plan.norm_each, plan.norm_rows) - 1, first_norm - 1, -1):
                    part = norm_ref[row * LANE // D : row * LANE // D + 1, row * LANE % D : row * LANE % D + LANE]
                    tail.insert(0, part.astype(jnp.float32))
                tail = jnp.concatenate(tail, 0)[: plan.tail]
                moved[pl.ds(pl.multiple_of(start + plan.own, 8), plan.tail), :] = tail
                result = jnp.where(mine, rank + start, result)
                ranks = jnp.where(mine, rank, ranks)
    position_ref[...] = result
    to_scalar = pltpu.make_async_copy(position_ref, position, sem_position)
    to_scalar.start()
    to_scalar.wait()
    fetch.wait()

    line_of = lax.broadcasted_iota(jnp.int32, (lists, LANE), 0)
    cuts = [plan.own * (i + 1) // (8 * PHASES) * 8 for i in range(PHASES - 1)] + [plan.own]
    begin = jnp.int32(0)
    copies = []
    for phase, cut in enumerate(cuts):
        end = plan.blocks // LANE
        if phase < PHASES - 1:
            end = jnp.max(jnp.where(ranks < cut, line_of + 1, 0))

        @pl.loop(begin, end)
        def _(line):
            for part in range(0, LANE, 16):
                rows = raw[pl.ds(pl.multiple_of(line * LANE + part, 16), 16), :].astype(jnp.float32)
                for u in range(16):
                    moved[pl.ds(position[line, part + u], 1), :] = rows[u : u + 1, :]

        begin = end
        low = cuts[phase - 1] if phase else 0
        high = cut if phase < PHASES - 1 else plan.block
        for i, out in enumerate(out_refs):
            start = (i // plan.nz) * plan.half + (plan.nz - 1 - i % plan.nz) * plan.group
            for x in range(plan.nx):
                rows = pl.ds(x * plan.block + low, high - low)
                source = moved.at[pl.ds(start + x * plan.block + low, high - low)]
                copies.append(pltpu.make_async_copy(source, out.at[rows], sem_out.at[len(copies)]))
                copies[-1].start()
    for copy in copies:
        copy.wait()


def place(plan, my_place, owners, norm_grads, grads):
    shapes = [(plan.group, LANE)] * (2 * plan.nz)
    outs = pl.pallas_call(
        functools.partial(place_kernel, plan),
        out_shape=[jax.ShapeDtypeStruct(s, jnp.float32) for s in shapes]
        + [jax.ShapeDtypeStruct((plan.lists, LANE), jnp.int32)],
        in_specs=[
            pl.BlockSpec(memory_space=pltpu.SMEM),
            pl.BlockSpec(memory_space=pltpu.VMEM),
            pl.BlockSpec(memory_space=pltpu.VMEM),
            pl.BlockSpec(memory_space=pl.ANY),
        ],
        out_specs=[pl.BlockSpec(memory_space=pl.ANY)] * len(shapes) + [pl.BlockSpec(memory_space=pltpu.VMEM)],
        scratch_shapes=[
            pltpu.VMEM((plan.blocks, LANE), jnp.bfloat16),
            pltpu.VMEM((2 * plan.half, LANE), jnp.float32),
            pltpu.SMEM((plan.lists, LANE), jnp.int32),
            pltpu.SemaphoreType.DMA,
            pltpu.SemaphoreType.DMA,
            pltpu.SemaphoreType.DMA((len(shapes) * plan.nx * PHASES,)),
        ],
        compiler_params=pltpu.CompilerParams(vmem_limit_bytes=58 * MIB),
        name="place_gradients",
    )(my_place, owners, norm_grads, grads)
    return list(outs[: plan.nz][::-1]), outs[plan.nz : 2 * plan.nz][::-1], outs[-1]


def owned_kernel(plan, place_ref, owner_ref, weights_ref, owned_ref, natural_ref, held, listed, order, sem_in, sem_order):
    fetch = pltpu.make_async_copy(weights_ref, held, sem_in)
    fetch.start()
    lists = plan.lists
    me = plan.index(place_ref[0], place_ref[1], place_ref[2])
    flags = (owner_ref[...] == me).astype(jnp.float32).astype(jnp.bfloat16)
    lane_in = lax.broadcasted_iota(jnp.int32, (LANE, LANE), 0)
    lane_out = lax.broadcasted_iota(jnp.int32, (LANE, LANE), 1)
    upto = (lane_in <= lane_out).astype(jnp.float32).astype(jnp.bfloat16)
    inner = jnp.dot(flags, upto, preferred_element_type=jnp.float32).astype(jnp.bfloat16)
    totals = lax.dot_general(
        jnp.ones((8, LANE), jnp.bfloat16), flags, (((1,), (1,)), ((), ())), preferred_element_type=jnp.float32
    )
    row_in = lax.broadcasted_iota(jnp.int32, (lists, lists), 0)
    row_out = lax.broadcasted_iota(jnp.int32, (lists, lists), 1)
    upto = (row_in <= row_out).astype(jnp.float32).astype(jnp.bfloat16)
    ends = jnp.dot(totals.astype(jnp.bfloat16), upto, preferred_element_type=jnp.float32)[0:1, :]
    place_of = lax.broadcasted_iota(jnp.int32, (LANE, lists), 1).astype(jnp.float32)
    rank_of = lax.broadcasted_iota(jnp.int32, (LANE, 1), 0)
    for step in range(listed.shape[0]):
        if step * LANE >= plan.own:
            break
        rank = (rank_of + step * LANE).astype(jnp.float32)
        passed = ends <= rank
        line = jnp.sum(passed.astype(jnp.float32), axis=1, keepdims=True)
        before = jnp.max(jnp.where(passed, ends, 0.0), axis=1, keepdims=True)
        chosen = (place_of == line).astype(jnp.float32).astype(jnp.bfloat16)
        counts = jnp.dot(chosen, inner, preferred_element_type=jnp.float32)
        column = jnp.sum((counts <= rank - before).astype(jnp.float32), axis=1, keepdims=True)
        block = jnp.broadcast_to((line * LANE + column).astype(jnp.int32), (LANE, LANE))
        natural_ref[step * LANE : (step + 1) * LANE, :] = block
        listed[step : step + 1, :] = jnp.sum(jnp.where(lane_in == lane_out, block, 0), axis=0, keepdims=True)
    to_scalar = pltpu.make_async_copy(listed, order, sem_order)
    to_scalar.start()
    to_scalar.wait()
    fetch.wait()

    def pick(line, count):
        for u in range(count):
            owned_ref[pl.ds(line * LANE + u, 1), :] = held[pl.ds(order[line, u], 1), :]

    @pl.loop(0, plan.own // LANE)
    def _(line):
        pick(line, LANE)

    if plan.own % LANE:
        pick(plan.own // LANE, plan.own % LANE)


def owned(plan, my_place, owners, weights):
    high_rows = -(-plan.own // (8 * LANE)) * 8
    ranks = -(-plan.own // LANE) * LANE
    vmem = pl.BlockSpec(memory_space=pltpu.VMEM)
    return pl.pallas_call(
        functools.partial(owned_kernel, plan),
        out_shape=[
            jax.ShapeDtypeStruct((plan.own, LANE), jnp.float32),
            jax.ShapeDtypeStruct((ranks, LANE), jnp.int32),
        ],
        in_specs=[pl.BlockSpec(memory_space=pltpu.SMEM), vmem, pl.BlockSpec(memory_space=pl.ANY)],
        out_specs=[vmem] * 2,
        scratch_shapes=[
            pltpu.VMEM((plan.blocks, LANE), jnp.float32),
            pltpu.VMEM((high_rows, LANE), jnp.int32),
            pltpu.SMEM((high_rows, LANE), jnp.int32),
            pltpu.SemaphoreType.DMA,
            pltpu.SemaphoreType.DMA,
        ],
        compiler_params=pltpu.CompilerParams(vmem_limit_bytes=58 * MIB),
        cost_estimate=pl.CostEstimate(flops=0, bytes_accessed=20 * MIB, transcendentals=0),
        name="owned_weights",
    )(my_place, owners, weights)


def update_kernel(plan, terms, *refs):
    parts, refs = refs[:terms], refs[terms:]
    first_ref, second_ref, weight_ref, natural_ref = refs[:4]
    new_first_ref, new_second_ref, block_ref = refs[4:]
    gradient = parts[0][: plan.block, :]
    for part in parts[1:]:
        gradient = gradient + part[: plan.block, :]
    tail, gradient = gradient[plan.own :, :], gradient[: plan.own, :]
    moment_one = beta_one * first_ref[...] + (1.0 - beta_one) * gradient
    moment_two = beta_two * second_ref[...] + (1.0 - beta_two) * gradient * gradient
    new_first_ref[...] = moment_one
    new_second_ref[...] = moment_two
    step = moment_one / bias_one / (jnp.sqrt(moment_two / bias_two) + epsilon)
    block_ref[: plan.own, :] = step
    weight = weight_ref[...]
    direction = step + decay_rate * weight
    natural = natural_ref[: plan.own, :]
    limits = (0,) + plan.bounds + (plan.blocks,)
    lane = lax.broadcasted_iota(jnp.int32, (8, LANE), 1)
    rank = lax.broadcasted_iota(jnp.int32, (8, LANE), 0)
    stats = jnp.zeros((8, LANE), jnp.float32)
    for column, squares in enumerate((weight * weight, direction * direction)):
        for k in range(matrices):
            inside = (natural >= limits[k]) & (natural < limits[k + 1])
            kept = jnp.where(inside, squares, 0.0).reshape(plan.own // 8, 8, LANE)
            total = jnp.sum(jnp.sum(kept, axis=0))
            stats = jnp.where((rank == plan.norm_each + k) & (lane == column), total, stats)
    block_ref[plan.own :, :] = tail + stats


def update(plan, parts, first, second, weight, natural):
    vmem = pl.BlockSpec(memory_space=pltpu.VMEM)
    shapes = [(plan.own, LANE), (plan.own, LANE), (plan.block, LANE)]
    return pl.pallas_call(
        functools.partial(update_kernel, plan, len(parts)),
        out_shape=[jax.ShapeDtypeStruct(s, jnp.float32) for s in shapes],
        in_specs=[vmem] * (len(parts) + 4),
        out_specs=[vmem] * len(shapes),
        compiler_params=pltpu.CompilerParams(vmem_limit_bytes=20 * MIB),
        name="moments",
    )(*parts, first, second, weight, natural)


def adam_rows(gradient, moment_one, moment_two, weight):
    moment_one = beta_one * moment_one + (1.0 - beta_one) * gradient
    moment_two = beta_two * moment_two + (1.0 - beta_two) * gradient * gradient
    step = moment_one / bias_one / (jnp.sqrt(moment_two / bias_two) + epsilon) + decay_rate * weight
    return (moment_one, moment_two, step)


def finish_kernel(plan, tile, slots, place_ref, position_ref, total_ref, norm_ref, weights_ref, *refs):
    pieces, refs = refs[: len(slots)], refs[len(slots) :]
    out_ref, new_norm_ref, trust_ref, held, norms, rates = refs
    now = pl.program_id(0)

    @pl.when(now == 0)
    def _():
        for piece, parts in zip(pieces, slots):
            for i, slot in enumerate(parts):
                held[pl.ds(plan.start(*slot), plan.block), :] = piece[i * plan.block : (i + 1) * plan.block, :]
        total = total_ref[...]
        for z in range(plan.nz):
            for x in range(plan.nx):
                for c in range(2):
                    start = plan.start(place_ref[0] ^ z, place_ref[1] ^ x, place_ref[2] ^ c) + plan.own
                    tail = held[pl.ds(pl.multiple_of(start, 8), plan.tail), :]
                    first = plan.index(z, x, c) * plan.norm_each
                    for row in range(first, min(first + plan.norm_each, plan.norm_rows)):
                        norms[row : row + 1, :] = tail[row - first : row - first + 1, :]
        for k in range(matrices):
            row = plan.norm_each + k
            weight_square, direction_square = total[row : row + 1, 0:1], total[row : row + 1, 1:2]
            ratio = jnp.sqrt(weight_square) / (jnp.sqrt(direction_square) + epsilon)
            rates[k : k + 1, :] = jnp.broadcast_to(learning * ratio, (1, LANE))
            trust_ref[k] = jnp.sum(ratio)
        each = plan.norm_rows // 2
        for i in range(2):
            gains, first, second = (
                jnp.concatenate([norm_ref[j, i : i + 1, row * LANE : (row + 1) * LANE] for row in range(each)], 0)
                for j in range(3)
            )
            one, two, step = adam_rows(norms[i * each : (i + 1) * each, :], first, second, gains)
            gain_square = jnp.sum(jnp.sum(gains * gains, axis=1, keepdims=True), axis=0, keepdims=True)
            step_square = jnp.sum(jnp.sum(step * step, axis=1, keepdims=True), axis=0, keepdims=True)
            ratio = jnp.sqrt(gain_square) / (jnp.sqrt(step_square) + epsilon)
            trust_ref[matrices + i] = jnp.sum(ratio)
            for j, value in enumerate((gains - learning * ratio * step, one, two)):
                for row in range(each):
                    new_norm_ref[j, i : i + 1, row * LANE : (row + 1) * LANE] = value[row : row + 1, :]

    lines = tile // LANE

    @pl.loop(0, lines)
    def _(line):
        matrix = jnp.int32(0)
        for bound in plan.bounds:
            matrix = matrix + (now * lines + line >= bound // LANE).astype(jnp.int32)
        rate = jnp.broadcast_to(rates[pl.ds(matrix, 1), :], (8, LANE))
        for group in range(0, LANE, 8):
            rows = [held[pl.ds(position_ref[now * lines + line, group + u], 1), :] for u in range(8)]
            here = pl.ds(pl.multiple_of(line * LANE + group, 8), 8)
            weight = weights_ref[here, :]
            direction = jnp.concatenate(rows, 0) + decay_rate * weight
            out_ref[here, :] = weight - rate * direction


def finish(plan, my_place, position, total, norm_state, weights, pieces, slots):
    assert all(bound % LANE == 0 for bound in plan.bounds + (plan.blocks,))
    tile = plan.blocks // next(n for n in (TILES, 4, 2, 1) if plan.blocks // LANE % n == 0)
    smem = pl.BlockSpec(memory_space=pltpu.SMEM)
    vmem = pl.BlockSpec(memory_space=pltpu.VMEM)
    return pl.pallas_call(
        functools.partial(finish_kernel, plan, tile, slots),
        grid=(plan.blocks // tile,),
        out_shape=[
            jax.ShapeDtypeStruct((plan.blocks, LANE), jnp.float32),
            jax.ShapeDtypeStruct(norm_state.shape, jnp.float32),
            jax.ShapeDtypeStruct((matrices + 2,), jnp.float32),
        ],
        in_specs=[smem, smem, vmem, vmem, pl.BlockSpec((tile, LANE), lambda i: (i, 0))]
        + [vmem] * len(pieces),
        out_specs=[pl.BlockSpec((tile, LANE), lambda i: (i, 0)), vmem, smem],
        scratch_shapes=[
            pltpu.VMEM((2 * plan.half, LANE), jnp.float32),
            pltpu.VMEM((plan.norm_rows, LANE), jnp.float32),
            pltpu.VMEM((8, LANE), jnp.float32),
        ],
        compiler_params=pltpu.CompilerParams(vmem_limit_bytes=20 * MIB),
        name="new_weights",
    )(my_place, position, total, norm_state, weights, *pieces)


def local(gradients, weights, first_moment, second_moment, owner_list, norm_grads, norm_state):
    plan = Plan(lax.axis_size("dp"), lax.axis_size("mp"), weights.shape[0])
    me = lax.axis_index("dp").astype(jnp.int32)
    my_place = jnp.stack([me // (2 * plan.nx), (me // 2) % plan.nx, me % 2]).astype(jnp.int32)
    owners = jnp.pad(owner_list[0], (0, plan.lists * LANE - plan.blocks), constant_values=-1)
    owners = owners.reshape(plan.lists, LANE)
    siblings, blocks, position = place(plan, my_place, owners, norm_grads[0], gradients[0])
    weight_own, natural = owned(plan, my_place, owners, weights)

    mine, theirs = [None] * plan.nz, [None] * plan.nz
    for z in reversed(range(plan.nz)):
        other = plan.swap(siblings[z])
        both = [
            blocks[z][x * plan.block : (x + 1) * plan.block] + other[x * plan.block : (x + 1) * plan.block]
            for x in range(plan.nx)
        ]
        mine[z], theirs[z] = both[0], both[1:]
        if z == 3:
            theirs[3], siblings[2], siblings[1], siblings[0] = together(theirs[3], *siblings[2::-1])
    if plan.nz == 4:
        parts = reduce(plan, mine, theirs, (weight_own, natural))
        parts, (weight_own, natural) = parts[:-2], parts[-2:]
    else:
        near = []
        for z in reversed(range(plan.nz)):
            terms = line_reduce(plan, "x", [mine[z]] + theirs[z])
            near.insert(0, sum(terms[1:], terms[0]) if z else None)
        parts = terms + line_reduce(plan, "z", near)[1:]
    new_first, new_second, block = update(
        plan, parts, first_moment[0], second_moment[0], weight_own, natural
    )

    found, total = gather(plan, my_place, block)
    pieces, slots = [piece for piece, _ in found], [parts for _, parts in found]
    new_weights, new_state, trust_ratios = finish(
        plan, my_place, position, total, norm_state, weights, pieces, slots
    )
    return (new_weights, new_first[None], new_second[None], new_state, trust_ratios)


def solution(mesh):
    in_specs = (
        P("dp", "mp", None),
        P("mp", None),
        P("mp", "dp", None),
        P("mp", "dp", None),
        P("mp", None),
        P("dp", None, None),
        P(),
    )
    out_specs = (P("mp", None), P("mp", "dp", None), P("mp", "dp", None), P(), P())
    return jax.shard_map(local, mesh=mesh, in_specs=in_specs, out_specs=out_specs, check_vma=False)
```

```python
import functools

import jax
import jax.numpy as jnp
from jax import lax
from jax.experimental import pallas as pl
from jax.experimental.pallas import tpu as pltpu
from jax.sharding import PartitionSpec as P

D = 1024
NTAB = 8
NKEYS = 256
KDIM = 128
LANE = 128
VROW_DEV = 512

beta_one = 0.9
beta_two = 0.99
bias_one = 1.0 - 0.9**4
bias_two = 1.0 - 0.99**4
epsilon = 1e-06
learning = 0.02
decay_rate = 0.01
matrices = 5
MIB = 1 << 20
TILES = 8
PHASES = 2


def matrix_bounds(narrow):
    query_blocks = D * D // (LANE * narrow)
    key_blocks = NTAB * NKEYS * KDIM // (LANE * narrow)
    value_blocks = VROW_DEV * D // LANE
    return (
        query_blocks,
        query_blocks + key_blocks,
        query_blocks + key_blocks + value_blocks,
        2 * query_blocks + key_blocks + value_blocks,
    )


class Plan:
    def __init__(self, replicas, narrow, blocks):
        self.replicas, self.narrow, self.blocks = replicas, narrow, blocks
        chips = replicas // 2
        self.nz = 4 if chips % 4 == 0 else chips
        self.nx = chips // self.nz
        assert self.nz in (1, 2, 4) and self.nx in (1, 2, 4)
        self.own = blocks // replicas
        self.tail = 8
        self.norm_rows = 2 * D // LANE
        self.norm_each = -(-self.norm_rows // replicas)
        self.block = self.own + self.tail
        self.group = self.nx * self.block
        self.half = self.nz * self.group
        self.lists = -(-blocks // (8 * LANE)) * 8
        self.bounds = matrix_bounds(narrow)

    def index(self, z, x, c):
        return (z * self.nx + x) * 2 + c

    def start(self, far_z, far_x, far_c):
        return (1 - far_c) * self.half + far_z * self.group + far_x * self.block

    def send(self, value, axis, pairs):
        every = []
        for z in range(self.nz):
            for x in range(self.nx):
                for c in range(2):
                    here = {"z": z, "x": x, "c": c}
                    for source, target in pairs:
                        if here[axis] == source:
                            every.append((self.index(z, x, c), self.index(**{**here, axis: target})))
        return lax.ppermute(value, "dp", every)

    def swap(self, value):
        return self.send(value, "c", PAIR)


PAIR = [(0, 1), (1, 0)]
PAIRS = [(0, 1), (1, 0), (2, 3), (3, 2)]
MIDDLE = [(1, 2), (2, 1)]
INWARD = [(0, 1), (3, 2)]
OUTWARD = [(1, 0), (2, 3)]


def line_reduce(plan, axis, blocks):
    if len(blocks) == 1:
        return [blocks[0]]
    if len(blocks) == 2:
        return [blocks[0], plan.send(blocks[1], axis, PAIR)]
    in_three = plan.send(blocks[3], axis, INWARD)
    in_two = plan.send(blocks[2], axis, INWARD)
    across_two = plan.send(blocks[2] + in_three, axis, MIDDLE)
    across_three = plan.send(blocks[3] + in_two, axis, MIDDLE)
    pair = plan.send(blocks[1] + across_two, axis, PAIRS)
    return [blocks[0], pair, across_three]


def together(*values):
    return lax.optimization_barrier(values)


def reduce(plan, mine, theirs, beside):
    def along_x(z, own):
        terms = line_reduce(plan, "x", [own] + theirs[z])
        return terms

    three = along_x(3, mine[3])
    two = along_x(2, mine[2])
    near_three = sum(three[1:], three[0])
    in_three = plan.send(near_three, "z", INWARD)
    in_three, near_two, *beside = together(in_three, sum(two[1:], two[0]), *beside)
    one = along_x(1, mine[1])
    across_two = plan.send(near_two + in_three, "z", MIDDLE)
    in_two = plan.send(near_two, "z", INWARD)
    across_two, in_two, near_one = together(across_two, in_two, sum(one[1:], one[0]))
    zero = along_x(0, mine[0])
    pair = plan.send(near_one + across_two, "z", PAIRS)
    across_three = plan.send(near_three + in_two, "z", MIDDLE)
    return zero + [pair, across_three] + beside


def sums_kernel(plan, place_ref, *refs):
    tails, (out_ref, held) = refs[: plan.nz], refs[plan.nz :]
    for far_z, tail in enumerate(tails):
        held[place_ref[0] ^ far_z] = tail[...]
    total = held[0]
    for z in range(1, plan.nz):
        total = total + held[z]
    out_ref[...] = total


def all_sums(plan, my_place, blocks):
    def tail_of(row):
        return pl.BlockSpec((plan.tail, LANE), lambda i: ((row + plan.own) // plan.tail, 0))

    specs = [tail_of(row) for _, row in blocks]
    total = pl.pallas_call(
        functools.partial(sums_kernel, plan),
        grid=(1,),
        out_shape=jax.ShapeDtypeStruct((plan.tail, LANE), jnp.float32),
        in_specs=[pl.BlockSpec(memory_space=pltpu.SMEM)] + specs,
        out_specs=pl.BlockSpec(memory_space=pltpu.VMEM),
        scratch_shapes=[pltpu.VMEM((plan.nz, plan.tail, LANE), jnp.float32)],
        compiler_params=pltpu.CompilerParams(vmem_limit_bytes=4 * MIB),
        name="sums",
    )(my_place, *(value for value, _ in blocks))
    hop = 1
    while hop < plan.nx:
        total = total + plan.send(total, "x", [(i, i ^ hop) for i in range(plan.nx)])
        hop *= 2
    return total


def all_cores(plan, total):
    total = total + plan.swap(total)
    hop = 1
    while hop < plan.narrow:
        total = total + lax.ppermute(total, "mp", [(i, i ^ hop) for i in range(plan.narrow)])
        hop *= 2
    return total


def gather(plan, my_place, block):
    def along_x(value):
        return line_gather(plan, "x", plan.nx, value)

    if plan.nz != 4:
        lines = [along_x(value) for value in line_gather(plan, "z", plan.nz, block)]
        total = all_cores(plan, all_sums(plan, my_place, [(line[0], 0) for line in lines]))
        mine = [(value, [(z, x)]) for z, line in enumerate(lines) for x, value in enumerate(line)]
    else:
        line = along_x(block)
        pair = plan.send(block, "z", PAIRS)
        three = plan.send(block, "z", MIDDLE)
        three, own, *line = together(three, jnp.concatenate([block, pair]), *line)
        line_pair = along_x(pair)
        two = plan.send(pair, "z", MIDDLE)
        out_two = plan.send(three, "z", OUTWARD)
        _, *line_pair = together(two, *line_pair)
        far = [jnp.concatenate([line[x], line_pair[x]]) for x in range(1, plan.nx)]
        near_two, *far = together(two + out_two, *far)
        line_two = along_x(near_two)
        out_three = plan.send(two, "z", OUTWARD)
        near_three = three + out_three
        line_three = along_x(near_three)
        total = all_sums(plan, my_place, [(own, 0), (own, plan.block), (near_two, 0), (near_three, 0)])
        total, *line_two = together(total, *line_two)
        early = plan.swap(near_three)
        early, total, *line_three = together(early, all_cores(plan, total), *line_three)
        mine = [(value, [(0, x), (1, x)]) for x, value in enumerate([own] + far)]
        mine += [(value, [(2, x)]) for x, value in enumerate(line_two)]
        mine += [(value, [(3, x)]) for x, value in enumerate(line_three)]
    swapped = [early if plan.nz == 4 and slots == [(3, 0)] else plan.swap(value) for value, slots in mine]
    found = [(value, [slot + (0,) for slot in slots]) for value, slots in mine]
    found += [(value, [slot + (1,) for slot in slots]) for value, (_, slots) in zip(swapped, mine)]
    return found, total


def line_gather(plan, axis, count, value):
    if count == 1:
        return [value]
    if count == 2:
        return [value, plan.send(value, axis, PAIR)]
    pair = plan.send(value, axis, PAIRS)
    across_three = plan.send(value, axis, MIDDLE)
    across_two = plan.send(pair, axis, MIDDLE)
    out_two = plan.send(across_three, axis, OUTWARD)
    out_three = plan.send(across_two, axis, OUTWARD)
    return [value, pair, across_two + out_two, across_three + out_three]


def place_kernel(plan, place_ref, owner_ref, norm_ref, grads_ref, *refs):
    out_refs, refs = refs[: 2 * plan.nz], refs[2 * plan.nz :]
    position_ref, raw, moved, position, sem_in, sem_position, sem_out = refs
    fetch = pltpu.make_async_copy(grads_ref, raw, sem_in)
    fetch.start()
    lists = plan.lists
    owners = owner_ref[...]
    my_z, my_x, my_c = place_ref[0], place_ref[1], place_ref[2]
    count = plan.replicas
    lane_in = lax.broadcasted_iota(jnp.int32, (LANE, LANE), 0)
    lane_out = lax.broadcasted_iota(jnp.int32, (LANE, LANE), 1)
    before = (lane_in < lane_out).astype(jnp.float32).astype(jnp.bfloat16)
    row_out = lax.broadcasted_iota(jnp.int32, (lists, lists), 0)
    row_in = lax.broadcasted_iota(jnp.int32, (lists, lists), 1)
    above = (row_in < row_out).astype(jnp.float32).astype(jnp.bfloat16)
    flags = [(owners == d).astype(jnp.float32).astype(jnp.bfloat16) for d in range(count)]
    inner = jnp.dot(jnp.concatenate(flags, 0), before, preferred_element_type=jnp.float32)
    owner_in = lax.broadcasted_iota(jnp.int32, (count * LANE, LANE), 0)
    owner_out = lax.broadcasted_iota(jnp.int32, (count * LANE, LANE), 1)
    pick = (owner_in // LANE == owner_out).astype(jnp.float32).astype(jnp.bfloat16)
    totals = jnp.dot(jnp.concatenate(flags, 1), pick, preferred_element_type=jnp.float32)
    outer = jnp.dot(above, totals.astype(jnp.bfloat16), preferred_element_type=jnp.float32)
    ranks = jnp.full((lists, LANE), plan.own, jnp.int32)
    result = jnp.zeros((lists, LANE), jnp.int32)
    for z in range(plan.nz):
        for x in range(plan.nx):
            for c in range(2):
                d = plan.index(z, x, c)
                mine = owners == d
                rank = (inner[d * lists : (d + 1) * lists, :] + outer[:, d : d + 1]).astype(jnp.int32)
                start = plan.start(my_z ^ z, my_x ^ x, my_c ^ c)
                first_norm = d * plan.norm_each
                tail = [jnp.zeros((plan.tail, LANE), jnp.float32)]
                for row in range(min(first_norm + plan.norm_each, plan.norm_rows) - 1, first_norm - 1, -1):
                    part = norm_ref[row * LANE // D : row * LANE // D + 1, row * LANE % D : row * LANE % D + LANE]
                    tail.insert(0, part.astype(jnp.float32))
                tail = jnp.concatenate(tail, 0)[: plan.tail]
                moved[pl.ds(pl.multiple_of(start + plan.own, 8), plan.tail), :] = tail
                result = jnp.where(mine, rank + start, result)
                ranks = jnp.where(mine, rank, ranks)
    position_ref[...] = result
    to_scalar = pltpu.make_async_copy(position_ref, position, sem_position)
    to_scalar.start()
    to_scalar.wait()
    fetch.wait()

    line_of = lax.broadcasted_iota(jnp.int32, (lists, LANE), 0)
    cuts = [plan.own * (i + 1) // (8 * PHASES) * 8 for i in range(PHASES - 1)] + [plan.own]
    begin = jnp.int32(0)
    copies = []
    for phase, cut in enumerate(cuts):
        end = plan.blocks // LANE
        if phase < PHASES - 1:
            end = jnp.max(jnp.where(ranks < cut, line_of + 1, 0))

        @pl.loop(begin, end)
        def _(line):
            for part in range(0, LANE, 16):
                rows = raw[pl.ds(pl.multiple_of(line * LANE + part, 16), 16), :].astype(jnp.float32)
                for u in range(16):
                    moved[pl.ds(position[line, part + u], 1), :] = rows[u : u + 1, :]

        begin = end
        low = cuts[phase - 1] if phase else 0
        high = cut if phase < PHASES - 1 else plan.block
        for i, out in enumerate(out_refs):
            start = (i // plan.nz) * plan.half + (plan.nz - 1 - i % plan.nz) * plan.group
            for x in range(plan.nx):
                rows = pl.ds(x * plan.block + low, high - low)
                source = moved.at[pl.ds(start + x * plan.block + low, high - low)]
                copies.append(pltpu.make_async_copy(source, out.at[rows], sem_out.at[len(copies)]))
                copies[-1].start()
    for copy in copies:
        copy.wait()


def place(plan, my_place, owners, norm_grads, grads):
    shapes = [(plan.group, LANE)] * (2 * plan.nz)
    outs = pl.pallas_call(
        functools.partial(place_kernel, plan),
        out_shape=[jax.ShapeDtypeStruct(s, jnp.float32) for s in shapes]
        + [jax.ShapeDtypeStruct((plan.lists, LANE), jnp.int32)],
        in_specs=[
            pl.BlockSpec(memory_space=pltpu.SMEM),
            pl.BlockSpec(memory_space=pltpu.VMEM),
            pl.BlockSpec(memory_space=pltpu.VMEM),
            pl.BlockSpec(memory_space=pl.ANY),
        ],
        out_specs=[pl.BlockSpec(memory_space=pl.ANY)] * len(shapes) + [pl.BlockSpec(memory_space=pltpu.VMEM)],
        scratch_shapes=[
            pltpu.VMEM((plan.blocks, LANE), jnp.bfloat16),
            pltpu.VMEM((2 * plan.half, LANE), jnp.float32),
            pltpu.SMEM((plan.lists, LANE), jnp.int32),
            pltpu.SemaphoreType.DMA,
            pltpu.SemaphoreType.DMA,
            pltpu.SemaphoreType.DMA((len(shapes) * plan.nx * PHASES,)),
        ],
        compiler_params=pltpu.CompilerParams(vmem_limit_bytes=58 * MIB),
        name="place_gradients",
    )(my_place, owners, norm_grads, grads)
    return list(outs[: plan.nz][::-1]), outs[plan.nz : 2 * plan.nz][::-1], outs[-1]


def owned_kernel(plan, place_ref, owner_ref, weights_ref, owned_ref, natural_ref, held, listed, order, sem_in, sem_order):
    fetch = pltpu.make_async_copy(weights_ref, held, sem_in)
    fetch.start()
    lists = plan.lists
    me = plan.index(place_ref[0], place_ref[1], place_ref[2])
    flags = (owner_ref[...] == me).astype(jnp.float32).astype(jnp.bfloat16)
    lane_in = lax.broadcasted_iota(jnp.int32, (LANE, LANE), 0)
    lane_out = lax.broadcasted_iota(jnp.int32, (LANE, LANE), 1)
    upto = (lane_in <= lane_out).astype(jnp.float32).astype(jnp.bfloat16)
    inner = jnp.dot(flags, upto, preferred_element_type=jnp.float32).astype(jnp.bfloat16)
    totals = lax.dot_general(
        jnp.ones((8, LANE), jnp.bfloat16), flags, (((1,), (1,)), ((), ())), preferred_element_type=jnp.float32
    )
    row_in = lax.broadcasted_iota(jnp.int32, (lists, lists), 0)
    row_out = lax.broadcasted_iota(jnp.int32, (lists, lists), 1)
    upto = (row_in <= row_out).astype(jnp.float32).astype(jnp.bfloat16)
    ends = jnp.dot(totals.astype(jnp.bfloat16), upto, preferred_element_type=jnp.float32)[0:1, :]
    place_of = lax.broadcasted_iota(jnp.int32, (LANE, lists), 1).astype(jnp.float32)
    rank_of = lax.broadcasted_iota(jnp.int32, (LANE, 1), 0)
    for step in range(listed.shape[0]):
        if step * LANE >= plan.own:
            break
        rank = (rank_of + step * LANE).astype(jnp.float32)
        passed = ends <= rank
        line = jnp.sum(passed.astype(jnp.float32), axis=1, keepdims=True)
        before = jnp.max(jnp.where(passed, ends, 0.0), axis=1, keepdims=True)
        chosen = (place_of == line).astype(jnp.float32).astype(jnp.bfloat16)
        counts = jnp.dot(chosen, inner, preferred_element_type=jnp.float32)
        column = jnp.sum((counts <= rank - before).astype(jnp.float32), axis=1, keepdims=True)
        block = jnp.broadcast_to((line * LANE + column).astype(jnp.int32), (LANE, LANE))
        natural_ref[step * LANE : (step + 1) * LANE, :] = block
        listed[step : step + 1, :] = jnp.sum(jnp.where(lane_in == lane_out, block, 0), axis=0, keepdims=True)
    to_scalar = pltpu.make_async_copy(listed, order, sem_order)
    to_scalar.start()
    to_scalar.wait()
    fetch.wait()

    def pick(line, count):
        for u in range(count):
            owned_ref[pl.ds(line * LANE + u, 1), :] = held[pl.ds(order[line, u], 1), :]

    @pl.loop(0, plan.own // LANE)
    def _(line):
        pick(line, LANE)

    if plan.own % LANE:
        pick(plan.own // LANE, plan.own % LANE)


def owned(plan, my_place, owners, weights):
    high_rows = -(-plan.own // (8 * LANE)) * 8
    ranks = -(-plan.own // LANE) * LANE
    vmem = pl.BlockSpec(memory_space=pltpu.VMEM)
    return pl.pallas_call(
        functools.partial(owned_kernel, plan),
        out_shape=[
            jax.ShapeDtypeStruct((plan.own, LANE), jnp.float32),
            jax.ShapeDtypeStruct((ranks, LANE), jnp.int32),
        ],
        in_specs=[pl.BlockSpec(memory_space=pltpu.SMEM), vmem, pl.BlockSpec(memory_space=pl.ANY)],
        out_specs=[vmem] * 2,
        scratch_shapes=[
            pltpu.VMEM((plan.blocks, LANE), jnp.float32),
            pltpu.VMEM((high_rows, LANE), jnp.int32),
            pltpu.SMEM((high_rows, LANE), jnp.int32),
            pltpu.SemaphoreType.DMA,
            pltpu.SemaphoreType.DMA,
        ],
        compiler_params=pltpu.CompilerParams(vmem_limit_bytes=58 * MIB),
        cost_estimate=pl.CostEstimate(flops=0, bytes_accessed=20 * MIB, transcendentals=0),
        name="owned_weights",
    )(my_place, owners, weights)


def update_kernel(plan, terms, *refs):
    parts, refs = refs[:terms], refs[terms:]
    first_ref, second_ref, weight_ref, natural_ref = refs[:4]
    new_first_ref, new_second_ref, block_ref = refs[4:]
    gradient = parts[0][: plan.block, :]
    for part in parts[1:]:
        gradient = gradient + part[: plan.block, :]
    tail, gradient = gradient[plan.own :, :], gradient[: plan.own, :]
    moment_one = beta_one * first_ref[...] + (1.0 - beta_one) * gradient
    moment_two = beta_two * second_ref[...] + (1.0 - beta_two) * gradient * gradient
    new_first_ref[...] = moment_one
    new_second_ref[...] = moment_two
    step = moment_one / bias_one / (jnp.sqrt(moment_two / bias_two) + epsilon)
    block_ref[: plan.own, :] = step
    weight = weight_ref[...]
    direction = step + decay_rate * weight
    natural = natural_ref[: plan.own, :]
    limits = (0,) + plan.bounds + (plan.blocks,)
    lane = lax.broadcasted_iota(jnp.int32, (8, LANE), 1)
    rank = lax.broadcasted_iota(jnp.int32, (8, LANE), 0)
    stats = jnp.zeros((8, LANE), jnp.float32)
    for column, squares in enumerate((weight * weight, direction * direction)):
        for k in range(matrices):
            inside = (natural >= limits[k]) & (natural < limits[k + 1])
            kept = jnp.where(inside, squares, 0.0).reshape(plan.own // 8, 8, LANE)
            total = jnp.sum(jnp.sum(kept, axis=0))
            stats = jnp.where((rank == plan.norm_each + k) & (lane == column), total, stats)
    block_ref[plan.own :, :] = tail + stats


def update(plan, parts, first, second, weight, natural):
    vmem = pl.BlockSpec(memory_space=pltpu.VMEM)
    shapes = [(plan.own, LANE), (plan.own, LANE), (plan.block, LANE)]
    return pl.pallas_call(
        functools.partial(update_kernel, plan, len(parts)),
        out_shape=[jax.ShapeDtypeStruct(s, jnp.float32) for s in shapes],
        in_specs=[vmem] * (len(parts) + 4),
        out_specs=[vmem] * len(shapes),
        compiler_params=pltpu.CompilerParams(vmem_limit_bytes=20 * MIB),
        name="moments",
    )(*parts, first, second, weight, natural)


def adam_rows(gradient, moment_one, moment_two, weight):
    moment_one = beta_one * moment_one + (1.0 - beta_one) * gradient
    moment_two = beta_two * moment_two + (1.0 - beta_two) * gradient * gradient
    step = moment_one / bias_one / (jnp.sqrt(moment_two / bias_two) + epsilon) + decay_rate * weight
    return (moment_one, moment_two, step)


def finish_kernel(plan, tile, slots, place_ref, position_ref, total_ref, norm_ref, weights_ref, *refs):
    pieces, refs = refs[: len(slots)], refs[len(slots) :]
    out_ref, new_norm_ref, trust_ref, held, norms, rates = refs
    now = pl.program_id(0)

    @pl.when(now == 0)
    def _():
        for piece, parts in zip(pieces, slots):
            for i, slot in enumerate(parts):
                held[pl.ds(plan.start(*slot), plan.block), :] = piece[i * plan.block : (i + 1) * plan.block, :]
        total = total_ref[...]
        for z in range(plan.nz):
            for x in range(plan.nx):
                for c in range(2):
                    start = plan.start(place_ref[0] ^ z, place_ref[1] ^ x, place_ref[2] ^ c) + plan.own
                    tail = held[pl.ds(pl.multiple_of(start, 8), plan.tail), :]
                    first = plan.index(z, x, c) * plan.norm_each
                    for row in range(first, min(first + plan.norm_each, plan.norm_rows)):
                        norms[row : row + 1, :] = tail[row - first : row - first + 1, :]
        for k in range(matrices):
            row = plan.norm_each + k
            weight_square, direction_square = total[row : row + 1, 0:1], total[row : row + 1, 1:2]
            ratio = jnp.sqrt(weight_square) / (jnp.sqrt(direction_square) + epsilon)
            rates[k : k + 1, :] = jnp.broadcast_to(learning * ratio, (1, LANE))
            trust_ref[k] = jnp.sum(ratio)
        each = plan.norm_rows // 2
        for i in range(2):
            gains, first, second = (
                jnp.concatenate([norm_ref[j, i : i + 1, row * LANE : (row + 1) * LANE] for row in range(each)], 0)
                for j in range(3)
            )
            one, two, step = adam_rows(norms[i * each : (i + 1) * each, :], first, second, gains)
            gain_square = jnp.sum(jnp.sum(gains * gains, axis=1, keepdims=True), axis=0, keepdims=True)
            step_square = jnp.sum(jnp.sum(step * step, axis=1, keepdims=True), axis=0, keepdims=True)
            ratio = jnp.sqrt(gain_square) / (jnp.sqrt(step_square) + epsilon)
            trust_ref[matrices + i] = jnp.sum(ratio)
            for j, value in enumerate((gains - learning * ratio * step, one, two)):
                for row in range(each):
                    new_norm_ref[j, i : i + 1, row * LANE : (row + 1) * LANE] = value[row : row + 1, :]

    lines = tile // LANE

    @pl.loop(0, lines)
    def _(line):
        matrix = jnp.int32(0)
        for bound in plan.bounds:
            matrix = matrix + (now * lines + line >= bound // LANE).astype(jnp.int32)
        rate = jnp.broadcast_to(rates[pl.ds(matrix, 1), :], (8, LANE))
        for group in range(0, LANE, 8):
            rows = [held[pl.ds(position_ref[now * lines + line, group + u], 1), :] for u in range(8)]
            here = pl.ds(pl.multiple_of(line * LANE + group, 8), 8)
            weight = weights_ref[here, :]
            direction = jnp.concatenate(rows, 0) + decay_rate * weight
            out_ref[here, :] = weight - rate * direction


def finish(plan, my_place, position, total, norm_state, weights, pieces, slots):
    assert all(bound % LANE == 0 for bound in plan.bounds + (plan.blocks,))
    tile = plan.blocks // next(n for n in (TILES, 4, 2, 1) if plan.blocks // LANE % n == 0)
    smem = pl.BlockSpec(memory_space=pltpu.SMEM)
    vmem = pl.BlockSpec(memory_space=pltpu.VMEM)
    return pl.pallas_call(
        functools.partial(finish_kernel, plan, tile, slots),
        grid=(plan.blocks // tile,),
        out_shape=[
            jax.ShapeDtypeStruct((plan.blocks, LANE), jnp.float32),
            jax.ShapeDtypeStruct(norm_state.shape, jnp.float32),
            jax.ShapeDtypeStruct((matrices + 2,), jnp.float32),
        ],
        in_specs=[smem, smem, vmem, vmem, pl.BlockSpec((tile, LANE), lambda i: (i, 0))]
        + [vmem] * len(pieces),
        out_specs=[pl.BlockSpec((tile, LANE), lambda i: (i, 0)), vmem, smem],
        scratch_shapes=[
            pltpu.VMEM((2 * plan.half, LANE), jnp.float32),
            pltpu.VMEM((plan.norm_rows, LANE), jnp.float32),
            pltpu.VMEM((8, LANE), jnp.float32),
        ],
        compiler_params=pltpu.CompilerParams(vmem_limit_bytes=20 * MIB),
        name="new_weights",
    )(my_place, position, total, norm_state, weights, *pieces)


def local(gradients, weights, first_moment, second_moment, owner_list, norm_grads, norm_state):
    plan = Plan(lax.axis_size("dp"), lax.axis_size("mp"), weights.shape[0])
    me = lax.axis_index("dp").astype(jnp.int32)
    my_place = jnp.stack([me // (2 * plan.nx), (me // 2) % plan.nx, me % 2]).astype(jnp.int32)
    owners = jnp.pad(owner_list[0], (0, plan.lists * LANE - plan.blocks), constant_values=-1)
    owners = owners.reshape(plan.lists, LANE)
    siblings, blocks, position = place(plan, my_place, owners, norm_grads[0], gradients[0])
    weight_own, natural = owned(plan, my_place, owners, weights)

    mine, theirs = [None] * plan.nz, [None] * plan.nz
    for z in reversed(range(plan.nz)):
        other = plan.swap(siblings[z])
        both = [
            blocks[z][x * plan.block : (x + 1) * plan.block] + other[x * plan.block : (x + 1) * plan.block]
            for x in range(plan.nx)
        ]
        mine[z], theirs[z] = both[0], both[1:]
        if z == 3:
            theirs[3], siblings[2], siblings[1], siblings[0] = together(theirs[3], *siblings[2::-1])
    if plan.nz == 4:
        parts = reduce(plan, mine, theirs, (weight_own, natural))
        parts, (weight_own, natural) = parts[:-2], parts[-2:]
    else:
        near = []
        for z in reversed(range(plan.nz)):
            terms = line_reduce(plan, "x", [mine[z]] + theirs[z])
            near.insert(0, sum(terms[1:], terms[0]) if z else None)
        parts = terms + line_reduce(plan, "z", near)[1:]
    new_first, new_second, block = update(
        plan, parts, first_moment[0], second_moment[0], weight_own, natural
    )

    found, total = gather(plan, my_place, block)
    pieces, slots = [piece for piece, _ in found], [parts for _, parts in found]
    new_weights, new_state, trust_ratios = finish(
        plan, my_place, position, total, norm_state, weights, pieces, slots
    )
    return (new_weights, new_first[None], new_second[None], new_state, trust_ratios)


def solution(mesh):
    in_specs = (
        P("dp", "mp", None),
        P("mp", None),
        P("mp", "dp", None),
        P("mp", "dp", None),
        P("mp", None),
        P("dp", None, None),
        P(),
    )
    out_specs = (P("mp", None), P("mp", "dp", None), P("mp", "dp", None), P(), P())
    return jax.shard_map(local, mesh=mesh, in_specs=in_specs, out_specs=out_specs, check_vma=False)
```

```python
import functools

import jax
import jax.numpy as jnp
from jax import lax
from jax.experimental import pallas as pl
from jax.experimental.pallas import tpu as pltpu
from jax.sharding import PartitionSpec as P

D = 1024
NTAB = 8
NKEYS = 256
KDIM = 128
LANE = 128
VROW_DEV = 512

beta_one = 0.9
beta_two = 0.99
bias_one = 1.0 - 0.9**4
bias_two = 1.0 - 0.99**4
epsilon = 1e-06
learning = 0.02
decay_rate = 0.01
matrices = 5
MIB = 1 << 20
TILES = 8
FETCHES = 4
EARLY = 0.7


def matrix_bounds(narrow):
    query_blocks = D * D // (LANE * narrow)
    key_blocks = NTAB * NKEYS * KDIM // (LANE * narrow)
    value_blocks = VROW_DEV * D // LANE
    return (
        query_blocks,
        query_blocks + key_blocks,
        query_blocks + key_blocks + value_blocks,
        2 * query_blocks + key_blocks + value_blocks,
    )


class Plan:
    def __init__(self, replicas, narrow, blocks):
        self.replicas, self.narrow, self.blocks = replicas, narrow, blocks
        chips = replicas // 2
        self.nz = 4 if chips % 4 == 0 else chips
        self.nx = chips // self.nz
        assert self.nz in (1, 2, 4) and self.nx in (1, 2, 4)
        self.own = blocks // replicas
        self.tail = 8
        self.norm_rows = 2 * D // LANE
        self.norm_each = -(-self.norm_rows // replicas)
        self.block = self.own + self.tail
        self.group = self.nx * self.block
        self.half = self.nz * self.group
        self.lists = -(-blocks // (8 * LANE)) * 8
        self.bounds = matrix_bounds(narrow)

    def index(self, z, x, c):
        return (z * self.nx + x) * 2 + c

    def start(self, far_z, far_x, far_c):
        return (1 - far_c) * self.half + far_z * self.group + far_x * self.block

    def order(self):
        zs, xs = range(self.nz - 1, -1, -1), range(self.nx - 1, -1, -1)
        return [(z, x, far_c) for far_c in (1, 0) for z in zs for x in xs]

    def send(self, value, axis, pairs):
        every = []
        for z in range(self.nz):
            for x in range(self.nx):
                for c in range(2):
                    here = {"z": z, "x": x, "c": c}
                    for source, target in pairs:
                        if here[axis] == source:
                            every.append((self.index(z, x, c), self.index(**{**here, axis: target})))
        return lax.ppermute(value, "dp", every)

    def swap(self, value):
        return self.send(value, "c", PAIR)


PAIR = [(0, 1), (1, 0)]
PAIRS = [(0, 1), (1, 0), (2, 3), (3, 2)]
MIDDLE = [(1, 2), (2, 1)]
INWARD = [(0, 1), (3, 2)]
OUTWARD = [(1, 0), (2, 3)]


def line_reduce(plan, axis, blocks):
    if len(blocks) == 1:
        return [blocks[0]]
    if len(blocks) == 2:
        return [blocks[0], plan.send(blocks[1], axis, PAIR)]
    in_three = plan.send(blocks[3], axis, INWARD)
    in_two = plan.send(blocks[2], axis, INWARD)
    across_two = plan.send(blocks[2] + in_three, axis, MIDDLE)
    across_three = plan.send(blocks[3] + in_two, axis, MIDDLE)
    pair = plan.send(blocks[1] + across_two, axis, PAIRS)
    return [blocks[0], pair, across_three]


def together(*values):
    return lax.optimization_barrier(values)


def reduce(plan, mine, theirs, beside):
    def along_x(z, own):
        terms = line_reduce(plan, "x", [own] + theirs[z])
        return terms

    three = along_x(3, mine[3])
    two = along_x(2, mine[2])
    near_three = sum(three[1:], three[0])
    in_three = plan.send(near_three, "z", INWARD)
    in_three, near_two, *beside = together(in_three, sum(two[1:], two[0]), *beside)
    one = along_x(1, mine[1])
    near_two, onward = together(near_two, near_two + in_three)
    across_two = plan.send(onward, "z", MIDDLE)
    in_two = plan.send(near_two, "z", INWARD)
    across_two, in_two, near_one = together(across_two, in_two, sum(one[1:], one[0]))
    zero = along_x(0, mine[0])
    pair = plan.send(near_one + across_two, "z", PAIRS)
    across_three = plan.send(near_three + in_two, "z", MIDDLE)
    return zero + [pair, across_three] + beside


def sums_kernel(plan, place_ref, *refs):
    tails, (out_ref, held) = refs[: plan.nz], refs[plan.nz :]
    for far_z, tail in enumerate(tails):
        held[place_ref[0] ^ far_z] = tail[...]
    total = held[0]
    for z in range(1, plan.nz):
        total = total + held[z]
    out_ref[...] = total


def all_sums(plan, my_place, blocks):
    def tail_of(row):
        return pl.BlockSpec((plan.tail, LANE), lambda i: ((row + plan.own) // plan.tail, 0))

    specs = [tail_of(row) for _, row in blocks]
    total = pl.pallas_call(
        functools.partial(sums_kernel, plan),
        grid=(1,),
        out_shape=jax.ShapeDtypeStruct((plan.tail, LANE), jnp.float32),
        in_specs=[pl.BlockSpec(memory_space=pltpu.SMEM)] + specs,
        out_specs=pl.BlockSpec(memory_space=pltpu.VMEM),
        scratch_shapes=[pltpu.VMEM((plan.nz, plan.tail, LANE), jnp.float32)],
        compiler_params=pltpu.CompilerParams(vmem_limit_bytes=4 * MIB),
        name="sums",
    )(my_place, *(value for value, _ in blocks))
    hop = 1
    while hop < plan.nx:
        total = total + plan.send(total, "x", [(i, i ^ hop) for i in range(plan.nx)])
        hop *= 2
    return total


def all_cores(plan, total):
    total = total + plan.swap(total)
    hop = 1
    while hop < plan.narrow:
        total = total + lax.ppermute(total, "mp", [(i, i ^ hop) for i in range(plan.narrow)])
        hop *= 2
    return total


def gather(plan, my_place, block):
    def along_x(value):
        return line_gather(plan, "x", plan.nx, value)

    if plan.nz != 4:
        lines = [along_x(value) for value in line_gather(plan, "z", plan.nz, block)]
        total = all_cores(plan, all_sums(plan, my_place, [(line[0], 0) for line in lines]))
        mine = [(value, [(z, x)]) for z, line in enumerate(lines) for x, value in enumerate(line)]
    else:
        line = along_x(block)
        pair = plan.send(block, "z", PAIRS)
        three = plan.send(block, "z", MIDDLE)
        three, own, *line = together(three, jnp.concatenate([block, pair]), *line)
        line_pair = along_x(pair)
        two = plan.send(pair, "z", MIDDLE)
        out_two = plan.send(three, "z", OUTWARD)
        _, *line_pair = together(two, *line_pair)
        far = [jnp.concatenate([line[x], line_pair[x]]) for x in range(1, plan.nx)]
        near_two, *far = together(two + out_two, *far)
        line_two = along_x(near_two)
        out_three = plan.send(two, "z", OUTWARD)
        near_three = three + out_three
        line_three = along_x(near_three)
        total = all_sums(plan, my_place, [(own, 0), (own, plan.block), (near_two, 0), (near_three, 0)])
        total, *line_two = together(total, *line_two)
        early = plan.swap(near_three)
        early, total, *line_three = together(early, all_cores(plan, total), *line_three)
        mine = [(value, [(0, x), (1, x)]) for x, value in enumerate([own] + far)]
        mine += [(value, [(2, x)]) for x, value in enumerate(line_two)]
        mine += [(value, [(3, x)]) for x, value in enumerate(line_three)]
    swapped = [early if plan.nz == 4 and slots == [(3, 0)] else plan.swap(value) for value, slots in mine]
    found = [(value, [slot + (0,) for slot in slots]) for value, slots in mine]
    found += [(value, [slot + (1,) for slot in slots]) for value, (_, slots) in zip(swapped, mine)]
    return found, total


def line_gather(plan, axis, count, value):
    if count == 1:
        return [value]
    if count == 2:
        return [value, plan.send(value, axis, PAIR)]
    pair = plan.send(value, axis, PAIRS)
    across_three = plan.send(value, axis, MIDDLE)
    across_two = plan.send(pair, axis, MIDDLE)
    out_two = plan.send(across_three, axis, OUTWARD)
    out_three = plan.send(across_two, axis, OUTWARD)
    return [value, pair, across_two + out_two, across_three + out_three]


def place_kernel(plan, place_ref, owner_ref, norm_ref, grads_ref, *refs):
    out_refs, refs = refs[: plan.replicas], refs[plan.replicas :]
    position_ref, raw, moved, position, sem_in, sem_position, sem_out = refs
    lines = plan.blocks // LANE
    ends = [lines * (i + 1) // FETCHES for i in range(FETCHES)]
    fetches = []
    for i, end in enumerate(ends):
        low = ends[i - 1] * LANE if i else 0
        rows = pl.ds(low, end * LANE - low)
        fetches.append(pltpu.make_async_copy(grads_ref.at[rows], raw.at[rows], sem_in.at[i]))
        fetches[-1].start()
    lists = plan.lists
    owners = owner_ref[...]
    my_z, my_x, my_c = place_ref[0], place_ref[1], place_ref[2]
    count = plan.replicas
    lane_in = lax.broadcasted_iota(jnp.int32, (LANE, LANE), 0)
    lane_out = lax.broadcasted_iota(jnp.int32, (LANE, LANE), 1)
    before = (lane_in < lane_out).astype(jnp.float32).astype(jnp.bfloat16)
    row_out = lax.broadcasted_iota(jnp.int32, (lists, lists), 0)
    row_in = lax.broadcasted_iota(jnp.int32, (lists, lists), 1)
    above = (row_in < row_out).astype(jnp.float32).astype(jnp.bfloat16)
    flags = [(owners == d).astype(jnp.float32).astype(jnp.bfloat16) for d in range(count)]
    inner = jnp.dot(jnp.concatenate(flags, 0), before, preferred_element_type=jnp.float32)
    owner_in = lax.broadcasted_iota(jnp.int32, (count * LANE, LANE), 0)
    owner_out = lax.broadcasted_iota(jnp.int32, (count * LANE, LANE), 1)
    pick = (owner_in // LANE == owner_out).astype(jnp.float32).astype(jnp.bfloat16)
    totals = jnp.dot(jnp.concatenate(flags, 1), pick, preferred_element_type=jnp.float32)
    outer = jnp.dot(above, totals.astype(jnp.bfloat16), preferred_element_type=jnp.float32)
    ranks = jnp.full((lists, LANE), plan.own, jnp.int32)
    result = jnp.zeros((lists, LANE), jnp.int32)
    for z in range(plan.nz):
        for x in range(plan.nx):
            for c in range(2):
                d = plan.index(z, x, c)
                mine = owners == d
                rank = (inner[d * lists : (d + 1) * lists, :] + outer[:, d : d + 1]).astype(jnp.int32)
                start = plan.start(my_z ^ z, my_x ^ x, my_c ^ c)
                first_norm = d * plan.norm_each
                tail = [jnp.zeros((plan.tail, LANE), jnp.float32)]
                for row in range(min(first_norm + plan.norm_each, plan.norm_rows) - 1, first_norm - 1, -1):
                    part = norm_ref[row * LANE // D : row * LANE // D + 1, row * LANE % D : row * LANE % D + LANE]
                    tail.insert(0, part.astype(jnp.float32))
                tail = jnp.concatenate(tail, 0)[: plan.tail]
                moved[pl.ds(pl.multiple_of(start + plan.own, 8), plan.tail), :] = tail
                result = jnp.where(mine, rank + start, result)
                ranks = jnp.where(mine, rank, ranks)
    position_ref[...] = result
    to_scalar = pltpu.make_async_copy(position_ref, position, sem_position)
    to_scalar.start()
    to_scalar.wait()

    def copies(part, low, high):
        found = []
        for i, (out, slot) in enumerate(zip(out_refs, plan.order())):
            source = moved.at[pl.ds(plan.start(*slot) + low, high - low)]
            found.append(pltpu.make_async_copy(source, out.at[pl.ds(low, high - low)], sem_out.at[part, i]))
        return found

    cut = int(plan.own * EARLY / 8) * 8
    line_of = lax.broadcasted_iota(jnp.int32, (lists, LANE), 0)
    complete = jnp.max(jnp.where(ranks < cut, line_of + 1, 0))
    early = copies(0, 0, cut)
    late = copies(1, cut, plan.block)

    for i, end in enumerate(ends):
        fetches[i].wait()

        @pl.loop(ends[i - 1] if i else 0, end)
        def _(line):
            for part in range(0, LANE, 16):
                rows = raw[pl.ds(pl.multiple_of(line * LANE + part, 16), 16), :].astype(jnp.float32)
                for u in range(16):
                    moved[pl.ds(position[line, part + u], 1), :] = rows[u : u + 1, :]

        if i == FETCHES - 2:

            @pl.when(complete <= end)
            def _():
                for copy in early:
                    copy.start()

    @pl.when(complete > ends[FETCHES - 2])
    def _():
        for copy in early:
            copy.start()

    for copy in late:
        copy.start()
    for copy in early + late:
        copy.wait()


def place(plan, my_place, owners, norm_grads, grads):
    shapes = [(plan.block, LANE)] * plan.replicas
    outs = pl.pallas_call(
        functools.partial(place_kernel, plan),
        out_shape=[jax.ShapeDtypeStruct(s, jnp.float32) for s in shapes]
        + [jax.ShapeDtypeStruct((plan.lists, LANE), jnp.int32)],
        in_specs=[
            pl.BlockSpec(memory_space=pltpu.SMEM),
            pl.BlockSpec(memory_space=pltpu.VMEM),
            pl.BlockSpec(memory_space=pltpu.VMEM),
            pl.BlockSpec(memory_space=pl.ANY),
        ],
        out_specs=[pl.BlockSpec(memory_space=pl.ANY)] * len(shapes) + [pl.BlockSpec(memory_space=pltpu.VMEM)],
        scratch_shapes=[
            pltpu.VMEM((plan.blocks, LANE), jnp.bfloat16),
            pltpu.VMEM((2 * plan.half, LANE), jnp.float32),
            pltpu.SMEM((plan.lists, LANE), jnp.int32),
            pltpu.SemaphoreType.DMA((FETCHES,)),
            pltpu.SemaphoreType.DMA,
            pltpu.SemaphoreType.DMA((2, len(shapes))),
        ],
        compiler_params=pltpu.CompilerParams(vmem_limit_bytes=58 * MIB),
        name="place_gradients",
    )(my_place, owners, norm_grads, grads)
    return dict(zip(plan.order(), outs)), outs[-1]


def owned_kernel(plan, place_ref, owner_ref, weights_ref, owned_ref, natural_ref, held, listed, order, sem_in, sem_order):
    fetch = pltpu.make_async_copy(weights_ref, held, sem_in)
    fetch.start()
    lists = plan.lists
    me = plan.index(place_ref[0], place_ref[1], place_ref[2])
    flags = (owner_ref[...] == me).astype(jnp.float32).astype(jnp.bfloat16)
    lane_in = lax.broadcasted_iota(jnp.int32, (LANE, LANE), 0)
    lane_out = lax.broadcasted_iota(jnp.int32, (LANE, LANE), 1)
    upto = (lane_in <= lane_out).astype(jnp.float32).astype(jnp.bfloat16)
    inner = jnp.dot(flags, upto, preferred_element_type=jnp.float32).astype(jnp.bfloat16)
    totals = lax.dot_general(
        jnp.ones((8, LANE), jnp.bfloat16), flags, (((1,), (1,)), ((), ())), preferred_element_type=jnp.float32
    )
    row_in = lax.broadcasted_iota(jnp.int32, (lists, lists), 0)
    row_out = lax.broadcasted_iota(jnp.int32, (lists, lists), 1)
    upto = (row_in <= row_out).astype(jnp.float32).astype(jnp.bfloat16)
    ends = jnp.dot(totals.astype(jnp.bfloat16), upto, preferred_element_type=jnp.float32)[0:1, :]
    place_of = lax.broadcasted_iota(jnp.int32, (LANE, lists), 1).astype(jnp.float32)
    rank_of = lax.broadcasted_iota(jnp.int32, (LANE, 1), 0)
    for step in range(listed.shape[0]):
        if step * LANE >= plan.own:
            break
        rank = (rank_of + step * LANE).astype(jnp.float32)
        passed = ends <= rank
        line = jnp.sum(passed.astype(jnp.float32), axis=1, keepdims=True)
        before = jnp.max(jnp.where(passed, ends, 0.0), axis=1, keepdims=True)
        chosen = (place_of == line).astype(jnp.float32).astype(jnp.bfloat16)
        counts = jnp.dot(chosen, inner, preferred_element_type=jnp.float32)
        column = jnp.sum((counts <= rank - before).astype(jnp.float32), axis=1, keepdims=True)
        block = jnp.broadcast_to((line * LANE + column).astype(jnp.int32), (LANE, LANE))
        natural_ref[step * LANE : (step + 1) * LANE, :] = block
        listed[step : step + 1, :] = jnp.sum(jnp.where(lane_in == lane_out, block, 0), axis=0, keepdims=True)
    to_scalar = pltpu.make_async_copy(listed, order, sem_order)
    to_scalar.start()
    to_scalar.wait()
    fetch.wait()

    def pick(line, count):
        for u in range(count):
            owned_ref[pl.ds(line * LANE + u, 1), :] = held[pl.ds(order[line, u], 1), :]

    @pl.loop(0, plan.own // LANE)
    def _(line):
        pick(line, LANE)

    if plan.own % LANE:
        pick(plan.own // LANE, plan.own % LANE)


def owned(plan, my_place, owners, weights):
    high_rows = -(-plan.own // (8 * LANE)) * 8
    ranks = -(-plan.own // LANE) * LANE
    vmem = pl.BlockSpec(memory_space=pltpu.VMEM)
    return pl.pallas_call(
        functools.partial(owned_kernel, plan),
        out_shape=[
            jax.ShapeDtypeStruct((plan.own, LANE), jnp.float32),
            jax.ShapeDtypeStruct((ranks, LANE), jnp.int32),
        ],
        in_specs=[pl.BlockSpec(memory_space=pltpu.SMEM), vmem, pl.BlockSpec(memory_space=pl.ANY)],
        out_specs=[vmem] * 2,
        scratch_shapes=[
            pltpu.VMEM((plan.blocks, LANE), jnp.float32),
            pltpu.VMEM((high_rows, LANE), jnp.int32),
            pltpu.SMEM((high_rows, LANE), jnp.int32),
            pltpu.SemaphoreType.DMA,
            pltpu.SemaphoreType.DMA,
        ],
        compiler_params=pltpu.CompilerParams(vmem_limit_bytes=58 * MIB),
        cost_estimate=pl.CostEstimate(flops=0, bytes_accessed=20 * MIB, transcendentals=0),
        name="owned_weights",
    )(my_place, owners, weights)


def update_kernel(plan, terms, *refs):
    parts, refs = refs[:terms], refs[terms:]
    first_ref, second_ref, weight_ref, natural_ref = refs[:4]
    new_first_ref, new_second_ref, block_ref = refs[4:]
    gradient = parts[0][: plan.block, :]
    for part in parts[1:]:
        gradient = gradient + part[: plan.block, :]
    tail, gradient = gradient[plan.own :, :], gradient[: plan.own, :]
    moment_one = beta_one * first_ref[...] + (1.0 - beta_one) * gradient
    moment_two = beta_two * second_ref[...] + (1.0 - beta_two) * gradient * gradient
    new_first_ref[...] = moment_one
    new_second_ref[...] = moment_two
    step = moment_one / bias_one / (jnp.sqrt(moment_two / bias_two) + epsilon)
    block_ref[: plan.own, :] = step
    weight = weight_ref[...]
    direction = step + decay_rate * weight
    natural = natural_ref[: plan.own, :]
    limits = (0,) + plan.bounds + (plan.blocks,)
    lane = lax.broadcasted_iota(jnp.int32, (8, LANE), 1)
    rank = lax.broadcasted_iota(jnp.int32, (8, LANE), 0)
    stats = jnp.zeros((8, LANE), jnp.float32)
    for column, squares in enumerate((weight * weight, direction * direction)):
        for k in range(matrices):
            inside = (natural >= limits[k]) & (natural < limits[k + 1])
            kept = jnp.where(inside, squares, 0.0).reshape(plan.own // 8, 8, LANE)
            total = jnp.sum(jnp.sum(kept, axis=0))
            stats = jnp.where((rank == plan.norm_each + k) & (lane == column), total, stats)
    block_ref[plan.own :, :] = tail + stats


def update(plan, parts, first, second, weight, natural):
    vmem = pl.BlockSpec(memory_space=pltpu.VMEM)
    shapes = [(plan.own, LANE), (plan.own, LANE), (plan.block, LANE)]
    return pl.pallas_call(
        functools.partial(update_kernel, plan, len(parts)),
        out_shape=[jax.ShapeDtypeStruct(s, jnp.float32) for s in shapes],
        in_specs=[vmem] * (len(parts) + 4),
        out_specs=[vmem] * len(shapes),
        compiler_params=pltpu.CompilerParams(vmem_limit_bytes=20 * MIB),
        name="moments",
    )(*parts, first, second, weight, natural)


def adam_rows(gradient, moment_one, moment_two, weight):
    moment_one = beta_one * moment_one + (1.0 - beta_one) * gradient
    moment_two = beta_two * moment_two + (1.0 - beta_two) * gradient * gradient
    step = moment_one / bias_one / (jnp.sqrt(moment_two / bias_two) + epsilon) + decay_rate * weight
    return (moment_one, moment_two, step)


def finish_kernel(plan, tile, slots, place_ref, position_ref, total_ref, norm_ref, weights_ref, *refs):
    pieces, refs = refs[: len(slots)], refs[len(slots) :]
    out_ref, new_norm_ref, trust_ref, held, norms, rates = refs
    now = pl.program_id(0)

    @pl.when(now == 0)
    def _():
        for piece, parts in zip(pieces, slots):
            for i, slot in enumerate(parts):
                held[pl.ds(plan.start(*slot), plan.block), :] = piece[i * plan.block : (i + 1) * plan.block, :]
        total = total_ref[...]
        for z in range(plan.nz):
            for x in range(plan.nx):
                for c in range(2):
                    start = plan.start(place_ref[0] ^ z, place_ref[1] ^ x, place_ref[2] ^ c) + plan.own
                    tail = held[pl.ds(pl.multiple_of(start, 8), plan.tail), :]
                    first = plan.index(z, x, c) * plan.norm_each
                    for row in range(first, min(first + plan.norm_each, plan.norm_rows)):
                        norms[row : row + 1, :] = tail[row - first : row - first + 1, :]
        for k in range(matrices):
            row = plan.norm_each + k
            weight_square, direction_square = total[row : row + 1, 0:1], total[row : row + 1, 1:2]
            ratio = jnp.sqrt(weight_square) / (jnp.sqrt(direction_square) + epsilon)
            rates[k : k + 1, :] = jnp.broadcast_to(learning * ratio, (1, LANE))
            trust_ref[k] = jnp.sum(ratio)
        each = plan.norm_rows // 2
        for i in range(2):
            gains, first, second = (
                jnp.concatenate([norm_ref[j, i : i + 1, row * LANE : (row + 1) * LANE] for row in range(each)], 0)
                for j in range(3)
            )
            one, two, step = adam_rows(norms[i * each : (i + 1) * each, :], first, second, gains)
            gain_square = jnp.sum(jnp.sum(gains * gains, axis=1, keepdims=True), axis=0, keepdims=True)
            step_square = jnp.sum(jnp.sum(step * step, axis=1, keepdims=True), axis=0, keepdims=True)
            ratio = jnp.sqrt(gain_square) / (jnp.sqrt(step_square) + epsilon)
            trust_ref[matrices + i] = jnp.sum(ratio)
            for j, value in enumerate((gains - learning * ratio * step, one, two)):
                for row in range(each):
                    new_norm_ref[j, i : i + 1, row * LANE : (row + 1) * LANE] = value[row : row + 1, :]

    lines = tile // LANE

    @pl.loop(0, lines)
    def _(line):
        matrix = jnp.int32(0)
        for bound in plan.bounds:
            matrix = matrix + (now * lines + line >= bound // LANE).astype(jnp.int32)
        rate = jnp.broadcast_to(rates[pl.ds(matrix, 1), :], (8, LANE))
        for group in range(0, LANE, 8):
            rows = [held[pl.ds(position_ref[now * lines + line, group + u], 1), :] for u in range(8)]
            here = pl.ds(pl.multiple_of(line * LANE + group, 8), 8)
            weight = weights_ref[here, :]
            direction = jnp.concatenate(rows, 0) + decay_rate * weight
            out_ref[here, :] = weight - rate * direction


def finish(plan, my_place, position, total, norm_state, weights, pieces, slots):
    assert all(bound % LANE == 0 for bound in plan.bounds + (plan.blocks,))
    tile = plan.blocks // next(n for n in (TILES, 4, 2, 1) if plan.blocks // LANE % n == 0)
    smem = pl.BlockSpec(memory_space=pltpu.SMEM)
    vmem = pl.BlockSpec(memory_space=pltpu.VMEM)
    return pl.pallas_call(
        functools.partial(finish_kernel, plan, tile, slots),
        grid=(plan.blocks // tile,),
        out_shape=[
            jax.ShapeDtypeStruct((plan.blocks, LANE), jnp.float32),
            jax.ShapeDtypeStruct(norm_state.shape, jnp.float32),
            jax.ShapeDtypeStruct((matrices + 2,), jnp.float32),
        ],
        in_specs=[smem, smem, vmem, vmem, pl.BlockSpec((tile, LANE), lambda i: (i, 0))]
        + [vmem] * len(pieces),
        out_specs=[pl.BlockSpec((tile, LANE), lambda i: (i, 0)), vmem, smem],
        scratch_shapes=[
            pltpu.VMEM((2 * plan.half, LANE), jnp.float32),
            pltpu.VMEM((plan.norm_rows, LANE), jnp.float32),
            pltpu.VMEM((8, LANE), jnp.float32),
        ],
        compiler_params=pltpu.CompilerParams(vmem_limit_bytes=20 * MIB),
        name="new_weights",
    )(my_place, position, total, norm_state, weights, *pieces)


def local(gradients, weights, first_moment, second_moment, owner_list, norm_grads, norm_state):
    plan = Plan(lax.axis_size("dp"), lax.axis_size("mp"), weights.shape[0])
    me = lax.axis_index("dp").astype(jnp.int32)
    my_place = jnp.stack([me // (2 * plan.nx), (me // 2) % plan.nx, me % 2]).astype(jnp.int32)
    owners = jnp.pad(owner_list[0], (0, plan.lists * LANE - plan.blocks), constant_values=-1)
    owners = owners.reshape(plan.lists, LANE)
    placed, position = place(plan, my_place, owners, norm_grads[0], gradients[0])
    weight_own, natural = owned(plan, my_place, owners, weights)

    mine, theirs = [None] * plan.nz, [None] * plan.nz
    for z in reversed(range(plan.nz)):
        both = [None] * plan.nx
        for x in reversed(range(plan.nx)):
            both[x] = placed[z, x, 0] + plan.swap(placed[z, x, 1])
            if (z, x) == (3, plan.nx - 1):
                later = [slot for slot in plan.order() if slot[2] and slot[:2] != (z, x)]
                both[x], *values = together(both[x], *(placed[slot] for slot in later))
                placed.update(zip(later, values))
        mine[z], theirs[z] = both[0], both[1:]
    if plan.nz == 4:
        parts = reduce(plan, mine, theirs, (weight_own, natural))
        parts, (weight_own, natural) = parts[:-2], parts[-2:]
    else:
        near = []
        for z in reversed(range(plan.nz)):
            terms = line_reduce(plan, "x", [mine[z]] + theirs[z])
            near.insert(0, sum(terms[1:], terms[0]) if z else None)
        parts = terms + line_reduce(plan, "z", near)[1:]
    new_first, new_second, block = update(
        plan, parts, first_moment[0], second_moment[0], weight_own, natural
    )

    found, total = gather(plan, my_place, block)
    pieces, slots = [piece for piece, _ in found], [parts for _, parts in found]
    new_weights, new_state, trust_ratios = finish(
        plan, my_place, position, total, norm_state, weights, pieces, slots
    )
    return (new_weights, new_first[None], new_second[None], new_state, trust_ratios)


def solution(mesh):
    in_specs = (
        P("dp", "mp", None),
        P("mp", None),
        P("mp", "dp", None),
        P("mp", "dp", None),
        P("mp", None),
        P("dp", None, None),
        P(),
    )
    out_specs = (P("mp", None), P("mp", "dp", None), P("mp", "dp", None), P(), P())
    return jax.shard_map(local, mesh=mesh, in_specs=in_specs, out_specs=out_specs, check_vma=False)
```

```python
import functools

import jax
import jax.numpy as jnp
from jax import lax
from jax.experimental import pallas as pl
from jax.experimental.pallas import tpu as pltpu
from jax.sharding import PartitionSpec as P

D = 1024
NTAB = 8
NKEYS = 256
KDIM = 128
LANE = 128
VROW_DEV = 512

beta_one = 0.9
beta_two = 0.99
bias_one = 1.0 - 0.9**4
bias_two = 1.0 - 0.99**4
epsilon = 1e-06
learning = 0.02
decay_rate = 0.01
matrices = 5
MIB = 1 << 20
TILES = 8
FETCHES = 4
EARLY = 0.7


def matrix_bounds(narrow):
    query_blocks = D * D // (LANE * narrow)
    key_blocks = NTAB * NKEYS * KDIM // (LANE * narrow)
    value_blocks = VROW_DEV * D // LANE
    return (
        query_blocks,
        query_blocks + key_blocks,
        query_blocks + key_blocks + value_blocks,
        2 * query_blocks + key_blocks + value_blocks,
    )


class Plan:
    def __init__(self, replicas, narrow, blocks):
        self.replicas, self.narrow, self.blocks = replicas, narrow, blocks
        chips = replicas // 2
        self.nz = 4 if chips % 4 == 0 else chips
        self.nx = chips // self.nz
        assert self.nz in (1, 2, 4) and self.nx in (1, 2, 4)
        self.own = blocks // replicas
        self.tail = 8
        self.norm_rows = 2 * D // LANE
        self.norm_each = -(-self.norm_rows // replicas)
        self.block = self.own + self.tail
        self.group = self.nx * self.block
        self.half = self.nz * self.group
        self.lists = -(-blocks // (8 * LANE)) * 8
        self.bounds = matrix_bounds(narrow)

    def index(self, z, x, c):
        return (z * self.nx + x) * 2 + c

    def start(self, far_z, far_x, far_c):
        return (1 - far_c) * self.half + far_z * self.group + far_x * self.block

    def order(self):
        zs, xs = range(self.nz - 1, -1, -1), range(self.nx - 1, -1, -1)
        return [(z, x, far_c) for far_c in (1, 0) for z in zs for x in xs]

    def send(self, value, axis, pairs):
        every = []
        for z in range(self.nz):
            for x in range(self.nx):
                for c in range(2):
                    here = {"z": z, "x": x, "c": c}
                    for source, target in pairs:
                        if here[axis] == source:
                            every.append((self.index(z, x, c), self.index(**{**here, axis: target})))
        return lax.ppermute(value, "dp", every)

    def swap(self, value):
        return self.send(value, "c", PAIR)


PAIR = [(0, 1), (1, 0)]
PAIRS = [(0, 1), (1, 0), (2, 3), (3, 2)]
MIDDLE = [(1, 2), (2, 1)]
INWARD = [(0, 1), (3, 2)]
OUTWARD = [(1, 0), (2, 3)]


def line_reduce(plan, axis, blocks):
    if len(blocks) == 1:
        return [blocks[0]]
    if len(blocks) == 2:
        return [blocks[0], plan.send(blocks[1], axis, PAIR)]
    in_three = plan.send(blocks[3], axis, INWARD)
    in_two = plan.send(blocks[2], axis, INWARD)
    across_two = plan.send(blocks[2] + in_three, axis, MIDDLE)
    across_three = plan.send(blocks[3] + in_two, axis, MIDDLE)
    pair = plan.send(blocks[1] + across_two, axis, PAIRS)
    return [blocks[0], pair, across_three]


def together(*values):
    return lax.optimization_barrier(values)


def reduce(plan, mine, theirs, beside):
    def along_x(z, own):
        terms = line_reduce(plan, "x", [own] + theirs[z])
        return terms

    three = along_x(3, mine[3])
    two = along_x(2, mine[2])
    near_three = sum(three[1:], three[0])
    in_three = plan.send(near_three, "z", INWARD)
    in_three, near_two, *beside = together(in_three, sum(two[1:], two[0]), *beside)
    one = along_x(1, mine[1])
    across_two = plan.send(near_two + in_three, "z", MIDDLE)
    in_two = plan.send(near_two, "z", INWARD)
    across_two, in_two, near_one = together(across_two, in_two, sum(one[1:], one[0]))
    zero = along_x(0, mine[0])
    pair = plan.send(near_one + across_two, "z", PAIRS)
    across_three = plan.send(near_three + in_two, "z", MIDDLE)
    return zero + [pair, across_three] + beside


def sums_kernel(plan, place_ref, *refs):
    tails, (out_ref, held) = refs[: plan.nz], refs[plan.nz :]
    for far_z, tail in enumerate(tails):
        held[place_ref[0] ^ far_z] = tail[...]
    total = held[0]
    for z in range(1, plan.nz):
        total = total + held[z]
    out_ref[...] = total


def all_sums(plan, my_place, blocks):
    def tail_of(row):
        return pl.BlockSpec((plan.tail, LANE), lambda i: ((row + plan.own) // plan.tail, 0))

    specs = [tail_of(row) for _, row in blocks]
    total = pl.pallas_call(
        functools.partial(sums_kernel, plan),
        grid=(1,),
        out_shape=jax.ShapeDtypeStruct((plan.tail, LANE), jnp.float32),
        in_specs=[pl.BlockSpec(memory_space=pltpu.SMEM)] + specs,
        out_specs=pl.BlockSpec(memory_space=pltpu.VMEM),
        scratch_shapes=[pltpu.VMEM((plan.nz, plan.tail, LANE), jnp.float32)],
        compiler_params=pltpu.CompilerParams(vmem_limit_bytes=4 * MIB),
        name="sums",
    )(my_place, *(value for value, _ in blocks))
    hop = 1
    while hop < plan.nx:
        total = total + plan.send(total, "x", [(i, i ^ hop) for i in range(plan.nx)])
        hop *= 2
    return total


def all_cores(plan, total):
    total = total + plan.swap(total)
    hop = 1
    while hop < plan.narrow:
        total = total + lax.ppermute(total, "mp", [(i, i ^ hop) for i in range(plan.narrow)])
        hop *= 2
    return total


def gather(plan, my_place, block):
    def along_x(value):
        return line_gather(plan, "x", plan.nx, value)

    if plan.nz != 4:
        lines = [along_x(value) for value in line_gather(plan, "z", plan.nz, block)]
        total = all_cores(plan, all_sums(plan, my_place, [(line[0], 0) for line in lines]))
        mine = [(value, [(z, x)]) for z, line in enumerate(lines) for x, value in enumerate(line)]
    else:
        line = along_x(block)
        pair = plan.send(block, "z", PAIRS)
        three = plan.send(block, "z", MIDDLE)
        three, own, *line = together(three, jnp.concatenate([block, pair]), *line)
        line_pair = along_x(pair)
        two = plan.send(pair, "z", MIDDLE)
        out_two = plan.send(three, "z", OUTWARD)
        _, *line_pair = together(two, *line_pair)
        far = [jnp.concatenate([line[x], line_pair[x]]) for x in range(1, plan.nx)]
        near_two, *far = together(two + out_two, *far)
        line_two = along_x(near_two)
        out_three = plan.send(two, "z", OUTWARD)
        near_three = three + out_three
        line_three = along_x(near_three)
        total = all_sums(plan, my_place, [(own, 0), (own, plan.block), (near_two, 0), (near_three, 0)])
        total, *line_two = together(total, *line_two)
        early = plan.swap(near_three)
        early, total, *line_three = together(early, all_cores(plan, total), *line_three)
        mine = [(value, [(0, x), (1, x)]) for x, value in enumerate([own] + far)]
        mine += [(value, [(2, x)]) for x, value in enumerate(line_two)]
        mine += [(value, [(3, x)]) for x, value in enumerate(line_three)]
    swapped = [early if plan.nz == 4 and slots == [(3, 0)] else plan.swap(value) for value, slots in mine]
    found = [(value, [slot + (0,) for slot in slots]) for value, slots in mine]
    found += [(value, [slot + (1,) for slot in slots]) for value, (_, slots) in zip(swapped, mine)]
    return found, total


def line_gather(plan, axis, count, value):
    if count == 1:
        return [value]
    if count == 2:
        return [value, plan.send(value, axis, PAIR)]
    pair = plan.send(value, axis, PAIRS)
    across_three = plan.send(value, axis, MIDDLE)
    across_two = plan.send(pair, axis, MIDDLE)
    out_two = plan.send(across_three, axis, OUTWARD)
    out_three = plan.send(across_two, axis, OUTWARD)
    return [value, pair, across_two + out_two, across_three + out_three]


def place_kernel(plan, place_ref, owner_ref, norm_ref, grads_ref, *refs):
    out_refs, refs = refs[: plan.replicas], refs[plan.replicas :]
    position_ref, raw, moved, position, sem_in, sem_position, sem_out = refs
    lines = plan.blocks // LANE
    ends = [lines * (i + 1) // FETCHES for i in range(FETCHES)]
    fetches = []
    for i, end in enumerate(ends):
        low = ends[i - 1] * LANE if i else 0
        rows = pl.ds(low, end * LANE - low)
        fetches.append(pltpu.make_async_copy(grads_ref.at[rows], raw.at[rows], sem_in.at[i]))
        fetches[-1].start()
    lists = plan.lists
    owners = owner_ref[...]
    my_z, my_x, my_c = place_ref[0], place_ref[1], place_ref[2]
    count = plan.replicas
    lane_in = lax.broadcasted_iota(jnp.int32, (LANE, LANE), 0)
    lane_out = lax.broadcasted_iota(jnp.int32, (LANE, LANE), 1)
    before = (lane_in < lane_out).astype(jnp.float32).astype(jnp.bfloat16)
    row_out = lax.broadcasted_iota(jnp.int32, (lists, lists), 0)
    row_in = lax.broadcasted_iota(jnp.int32, (lists, lists), 1)
    above = (row_in < row_out).astype(jnp.float32).astype(jnp.bfloat16)
    flags = [(owners == d).astype(jnp.float32).astype(jnp.bfloat16) for d in range(count)]
    inner = jnp.dot(jnp.concatenate(flags, 0), before, preferred_element_type=jnp.float32)
    owner_in = lax.broadcasted_iota(jnp.int32, (count * LANE, LANE), 0)
    owner_out = lax.broadcasted_iota(jnp.int32, (count * LANE, LANE), 1)
    pick = (owner_in // LANE == owner_out).astype(jnp.float32).astype(jnp.bfloat16)
    totals = jnp.dot(jnp.concatenate(flags, 1), pick, preferred_element_type=jnp.float32)
    outer = jnp.dot(above, totals.astype(jnp.bfloat16), preferred_element_type=jnp.float32)
    ranks = jnp.full((lists, LANE), plan.own, jnp.int32)
    result = jnp.zeros((lists, LANE), jnp.int32)
    for z in range(plan.nz):
        for x in range(plan.nx):
            for c in range(2):
                d = plan.index(z, x, c)
                mine = owners == d
                rank = (inner[d * lists : (d + 1) * lists, :] + outer[:, d : d + 1]).astype(jnp.int32)
                start = plan.start(my_z ^ z, my_x ^ x, my_c ^ c)
                first_norm = d * plan.norm_each
                tail = [jnp.zeros((plan.tail, LANE), jnp.float32)]
                for row in range(min(first_norm + plan.norm_each, plan.norm_rows) - 1, first_norm - 1, -1):
                    part = norm_ref[row * LANE // D : row * LANE // D + 1, row * LANE % D : row * LANE % D + LANE]
                    tail.insert(0, part.astype(jnp.float32))
                tail = jnp.concatenate(tail, 0)[: plan.tail]
                moved[pl.ds(pl.multiple_of(start + plan.own, 8), plan.tail), :] = tail
                result = jnp.where(mine, rank + start, result)
                ranks = jnp.where(mine, rank, ranks)
    position_ref[...] = result
    to_scalar = pltpu.make_async_copy(position_ref, position, sem_position)
    to_scalar.start()
    to_scalar.wait()

    def copies(part, low, high):
        found = []
        for i, (out, slot) in enumerate(zip(out_refs, plan.order())):
            source = moved.at[pl.ds(plan.start(*slot) + low, high - low)]
            found.append(pltpu.make_async_copy(source, out.at[pl.ds(low, high - low)], sem_out.at[part, i]))
        return found

    cut = int(plan.own * EARLY / 8) * 8
    line_of = lax.broadcasted_iota(jnp.int32, (lists, LANE), 0)
    complete = jnp.max(jnp.where(ranks < cut, line_of + 1, 0))
    early = copies(0, 0, cut)
    late = copies(1, cut, plan.block)

    for i, end in enumerate(ends):
        fetches[i].wait()

        @pl.loop(ends[i - 1] if i else 0, end)
        def _(line):
            for part in range(0, LANE, 16):
                rows = raw[pl.ds(pl.multiple_of(line * LANE + part, 16), 16), :].astype(jnp.float32)
                for u in range(16):
                    moved[pl.ds(position[line, part + u], 1), :] = rows[u : u + 1, :]

        if i == FETCHES - 2:

            @pl.when(complete <= end)
            def _():
                for copy in early:
                    copy.start()

    @pl.when(complete > ends[FETCHES - 2])
    def _():
        for copy in early:
            copy.start()

    for copy in late:
        copy.start()
    for copy in early + late:
        copy.wait()


def place(plan, my_place, owners, norm_grads, grads):
    shapes = [(plan.block, LANE)] * plan.replicas
    outs = pl.pallas_call(
        functools.partial(place_kernel, plan),
        out_shape=[jax.ShapeDtypeStruct(s, jnp.float32) for s in shapes]
        + [jax.ShapeDtypeStruct((plan.lists, LANE), jnp.int32)],
        in_specs=[
            pl.BlockSpec(memory_space=pltpu.SMEM),
            pl.BlockSpec(memory_space=pltpu.VMEM),
            pl.BlockSpec(memory_space=pltpu.VMEM),
            pl.BlockSpec(memory_space=pl.ANY),
        ],
        out_specs=[pl.BlockSpec(memory_space=pl.ANY)] * len(shapes) + [pl.BlockSpec(memory_space=pltpu.VMEM)],
        scratch_shapes=[
            pltpu.VMEM((plan.blocks, LANE), jnp.bfloat16),
            pltpu.VMEM((2 * plan.half, LANE), jnp.float32),
            pltpu.SMEM((plan.lists, LANE), jnp.int32),
            pltpu.SemaphoreType.DMA((FETCHES,)),
            pltpu.SemaphoreType.DMA,
            pltpu.SemaphoreType.DMA((2, len(shapes))),
        ],
        compiler_params=pltpu.CompilerParams(vmem_limit_bytes=58 * MIB),
        name="place_gradients",
    )(my_place, owners, norm_grads, grads)
    return dict(zip(plan.order(), outs)), outs[-1]


def owned_kernel(plan, place_ref, owner_ref, weights_ref, owned_ref, natural_ref, held, listed, order, sem_in, sem_order):
    fetch = pltpu.make_async_copy(weights_ref, held, sem_in)
    fetch.start()
    lists = plan.lists
    me = plan.index(place_ref[0], place_ref[1], place_ref[2])
    flags = (owner_ref[...] == me).astype(jnp.float32).astype(jnp.bfloat16)
    lane_in = lax.broadcasted_iota(jnp.int32, (LANE, LANE), 0)
    lane_out = lax.broadcasted_iota(jnp.int32, (LANE, LANE), 1)
    upto = (lane_in <= lane_out).astype(jnp.float32).astype(jnp.bfloat16)
    inner = jnp.dot(flags, upto, preferred_element_type=jnp.float32).astype(jnp.bfloat16)
    totals = lax.dot_general(
        jnp.ones((8, LANE), jnp.bfloat16), flags, (((1,), (1,)), ((), ())), preferred_element_type=jnp.float32
    )
    row_in = lax.broadcasted_iota(jnp.int32, (lists, lists), 0)
    row_out = lax.broadcasted_iota(jnp.int32, (lists, lists), 1)
    upto = (row_in <= row_out).astype(jnp.float32).astype(jnp.bfloat16)
    ends = jnp.dot(totals.astype(jnp.bfloat16), upto, preferred_element_type=jnp.float32)[0:1, :]
    place_of = lax.broadcasted_iota(jnp.int32, (LANE, lists), 1).astype(jnp.float32)
    rank_of = lax.broadcasted_iota(jnp.int32, (LANE, 1), 0)
    for step in range(listed.shape[0]):
        if step * LANE >= plan.own:
            break
        rank = (rank_of + step * LANE).astype(jnp.float32)
        passed = ends <= rank
        line = jnp.sum(passed.astype(jnp.float32), axis=1, keepdims=True)
        before = jnp.max(jnp.where(passed, ends, 0.0), axis=1, keepdims=True)
        chosen = (place_of == line).astype(jnp.float32).astype(jnp.bfloat16)
        counts = jnp.dot(chosen, inner, preferred_element_type=jnp.float32)
        column = jnp.sum((counts <= rank - before).astype(jnp.float32), axis=1, keepdims=True)
        block = jnp.broadcast_to((line * LANE + column).astype(jnp.int32), (LANE, LANE))
        natural_ref[step * LANE : (step + 1) * LANE, :] = block
        listed[step : step + 1, :] = jnp.sum(jnp.where(lane_in == lane_out, block, 0), axis=0, keepdims=True)
    to_scalar = pltpu.make_async_copy(listed, order, sem_order)
    to_scalar.start()
    to_scalar.wait()
    fetch.wait()

    def pick(line, count):
        for u in range(count):
            owned_ref[pl.ds(line * LANE + u, 1), :] = held[pl.ds(order[line, u], 1), :]

    @pl.loop(0, plan.own // LANE)
    def _(line):
        pick(line, LANE)

    if plan.own % LANE:
        pick(plan.own // LANE, plan.own % LANE)


def owned(plan, my_place, owners, weights):
    high_rows = -(-plan.own // (8 * LANE)) * 8
    ranks = -(-plan.own // LANE) * LANE
    vmem = pl.BlockSpec(memory_space=pltpu.VMEM)
    return pl.pallas_call(
        functools.partial(owned_kernel, plan),
        out_shape=[
            jax.ShapeDtypeStruct((plan.own, LANE), jnp.float32),
            jax.ShapeDtypeStruct((ranks, LANE), jnp.int32),
        ],
        in_specs=[pl.BlockSpec(memory_space=pltpu.SMEM), vmem, pl.BlockSpec(memory_space=pl.ANY)],
        out_specs=[vmem] * 2,
        scratch_shapes=[
            pltpu.VMEM((plan.blocks, LANE), jnp.float32),
            pltpu.VMEM((high_rows, LANE), jnp.int32),
            pltpu.SMEM((high_rows, LANE), jnp.int32),
            pltpu.SemaphoreType.DMA,
            pltpu.SemaphoreType.DMA,
        ],
        compiler_params=pltpu.CompilerParams(vmem_limit_bytes=58 * MIB),
        cost_estimate=pl.CostEstimate(flops=0, bytes_accessed=20 * MIB, transcendentals=0),
        name="owned_weights",
    )(my_place, owners, weights)


def update_kernel(plan, terms, *refs):
    parts, refs = refs[:terms], refs[terms:]
    first_ref, second_ref, weight_ref, natural_ref = refs[:4]
    new_first_ref, new_second_ref, block_ref = refs[4:]
    gradient = parts[0][: plan.block, :]
    for part in parts[1:]:
        gradient = gradient + part[: plan.block, :]
    tail, gradient = gradient[plan.own :, :], gradient[: plan.own, :]
    moment_one = beta_one * first_ref[...] + (1.0 - beta_one) * gradient
    moment_two = beta_two * second_ref[...] + (1.0 - beta_two) * gradient * gradient
    new_first_ref[...] = moment_one
    new_second_ref[...] = moment_two
    step = moment_one / bias_one / (jnp.sqrt(moment_two / bias_two) + epsilon)
    block_ref[: plan.own, :] = step
    weight = weight_ref[...]
    direction = step + decay_rate * weight
    natural = natural_ref[: plan.own, :]
    limits = (0,) + plan.bounds + (plan.blocks,)
    lane = lax.broadcasted_iota(jnp.int32, (8, LANE), 1)
    rank = lax.broadcasted_iota(jnp.int32, (8, LANE), 0)
    stats = jnp.zeros((8, LANE), jnp.float32)
    for column, squares in enumerate((weight * weight, direction * direction)):
        for k in range(matrices):
            inside = (natural >= limits[k]) & (natural < limits[k + 1])
            kept = jnp.where(inside, squares, 0.0).reshape(plan.own // 8, 8, LANE)
            total = jnp.sum(jnp.sum(kept, axis=0))
            stats = jnp.where((rank == plan.norm_each + k) & (lane == column), total, stats)
    block_ref[plan.own :, :] = tail + stats


def update(plan, parts, first, second, weight, natural):
    vmem = pl.BlockSpec(memory_space=pltpu.VMEM)
    shapes = [(plan.own, LANE), (plan.own, LANE), (plan.block, LANE)]
    return pl.pallas_call(
        functools.partial(update_kernel, plan, len(parts)),
        out_shape=[jax.ShapeDtypeStruct(s, jnp.float32) for s in shapes],
        in_specs=[vmem] * (len(parts) + 4),
        out_specs=[vmem] * len(shapes),
        compiler_params=pltpu.CompilerParams(vmem_limit_bytes=20 * MIB),
        name="moments",
    )(*parts, first, second, weight, natural)


def adam_rows(gradient, moment_one, moment_two, weight):
    moment_one = beta_one * moment_one + (1.0 - beta_one) * gradient
    moment_two = beta_two * moment_two + (1.0 - beta_two) * gradient * gradient
    step = moment_one / bias_one / (jnp.sqrt(moment_two / bias_two) + epsilon) + decay_rate * weight
    return (moment_one, moment_two, step)


def finish_kernel(plan, tile, slots, place_ref, position_ref, total_ref, norm_ref, weights_ref, *refs):
    pieces, refs = refs[: len(slots)], refs[len(slots) :]
    out_ref, new_norm_ref, trust_ref, held, norms, rates = refs
    now = pl.program_id(0)

    @pl.when(now == 0)
    def _():
        for piece, parts in zip(pieces, slots):
            for i, slot in enumerate(parts):
                held[pl.ds(plan.start(*slot), plan.block), :] = piece[i * plan.block : (i + 1) * plan.block, :]
        total = total_ref[...]
        for z in range(plan.nz):
            for x in range(plan.nx):
                for c in range(2):
                    start = plan.start(place_ref[0] ^ z, place_ref[1] ^ x, place_ref[2] ^ c) + plan.own
                    tail = held[pl.ds(pl.multiple_of(start, 8), plan.tail), :]
                    first = plan.index(z, x, c) * plan.norm_each
                    for row in range(first, min(first + plan.norm_each, plan.norm_rows)):
                        norms[row : row + 1, :] = tail[row - first : row - first + 1, :]
        for k in range(matrices):
            row = plan.norm_each + k
            weight_square, direction_square = total[row : row + 1, 0:1], total[row : row + 1, 1:2]
            ratio = jnp.sqrt(weight_square) / (jnp.sqrt(direction_square) + epsilon)
            rates[k : k + 1, :] = jnp.broadcast_to(learning * ratio, (1, LANE))
            trust_ref[k] = jnp.sum(ratio)
        each = plan.norm_rows // 2
        for i in range(2):
            gains, first, second = (
                jnp.concatenate([norm_ref[j, i : i + 1, row * LANE : (row + 1) * LANE] for row in range(each)], 0)
                for j in range(3)
            )
            one, two, step = adam_rows(norms[i * each : (i + 1) * each, :], first, second, gains)
            gain_square = jnp.sum(jnp.sum(gains * gains, axis=1, keepdims=True), axis=0, keepdims=True)
            step_square = jnp.sum(jnp.sum(step * step, axis=1, keepdims=True), axis=0, keepdims=True)
            ratio = jnp.sqrt(gain_square) / (jnp.sqrt(step_square) + epsilon)
            trust_ref[matrices + i] = jnp.sum(ratio)
            for j, value in enumerate((gains - learning * ratio * step, one, two)):
                for row in range(each):
                    new_norm_ref[j, i : i + 1, row * LANE : (row + 1) * LANE] = value[row : row + 1, :]

    lines = tile // LANE

    @pl.loop(0, lines)
    def _(line):
        matrix = jnp.int32(0)
        for bound in plan.bounds:
            matrix = matrix + (now * lines + line >= bound // LANE).astype(jnp.int32)
        rate = jnp.broadcast_to(rates[pl.ds(matrix, 1), :], (8, LANE))
        for group in range(0, LANE, 8):
            rows = [held[pl.ds(position_ref[now * lines + line, group + u], 1), :] for u in range(8)]
            here = pl.ds(pl.multiple_of(line * LANE + group, 8), 8)
            weight = weights_ref[here, :]
            direction = jnp.concatenate(rows, 0) + decay_rate * weight
            out_ref[here, :] = weight - rate * direction


def finish(plan, my_place, position, total, norm_state, weights, pieces, slots):
    assert all(bound % LANE == 0 for bound in plan.bounds + (plan.blocks,))
    tile = plan.blocks // next(n for n in (TILES, 4, 2, 1) if plan.blocks // LANE % n == 0)
    smem = pl.BlockSpec(memory_space=pltpu.SMEM)
    vmem = pl.BlockSpec(memory_space=pltpu.VMEM)
    return pl.pallas_call(
        functools.partial(finish_kernel, plan, tile, slots),
        grid=(plan.blocks // tile,),
        out_shape=[
            jax.ShapeDtypeStruct((plan.blocks, LANE), jnp.float32),
            jax.ShapeDtypeStruct(norm_state.shape, jnp.float32),
            jax.ShapeDtypeStruct((matrices + 2,), jnp.float32),
        ],
        in_specs=[smem, smem, vmem, vmem, pl.BlockSpec((tile, LANE), lambda i: (i, 0))]
        + [vmem] * len(pieces),
        out_specs=[pl.BlockSpec((tile, LANE), lambda i: (i, 0)), vmem, smem],
        scratch_shapes=[
            pltpu.VMEM((2 * plan.half, LANE), jnp.float32),
            pltpu.VMEM((plan.norm_rows, LANE), jnp.float32),
            pltpu.VMEM((8, LANE), jnp.float32),
        ],
        compiler_params=pltpu.CompilerParams(vmem_limit_bytes=20 * MIB),
        name="new_weights",
    )(my_place, position, total, norm_state, weights, *pieces)


def local(gradients, weights, first_moment, second_moment, owner_list, norm_grads, norm_state):
    plan = Plan(lax.axis_size("dp"), lax.axis_size("mp"), weights.shape[0])
    me = lax.axis_index("dp").astype(jnp.int32)
    my_place = jnp.stack([me // (2 * plan.nx), (me // 2) % plan.nx, me % 2]).astype(jnp.int32)
    owners = jnp.pad(owner_list[0], (0, plan.lists * LANE - plan.blocks), constant_values=-1)
    owners = owners.reshape(plan.lists, LANE)
    placed, position = place(plan, my_place, owners, norm_grads[0], gradients[0])
    weight_own, natural = owned(plan, my_place, owners, weights)

    mine, theirs = [None] * plan.nz, [None] * plan.nz
    for z in reversed(range(plan.nz)):
        both = [None] * plan.nx
        for x in reversed(range(plan.nx)):
            both[x] = placed[z, x, 0] + plan.swap(placed[z, x, 1])
            if (z, x) == (3, plan.nx - 1):
                later = [slot for slot in plan.order() if slot[2] and slot[:2] != (z, x)]
                both[x], *values = together(both[x], *(placed[slot] for slot in later))
                placed.update(zip(later, values))
        mine[z], theirs[z] = both[0], both[1:]
    if plan.nz == 4:
        parts = reduce(plan, mine, theirs, (weight_own, natural))
        parts, (weight_own, natural) = parts[:-2], parts[-2:]
    else:
        near = []
        for z in reversed(range(plan.nz)):
            terms = line_reduce(plan, "x", [mine[z]] + theirs[z])
            near.insert(0, sum(terms[1:], terms[0]) if z else None)
        parts = terms + line_reduce(plan, "z", near)[1:]
    new_first, new_second, block = update(
        plan, parts, first_moment[0], second_moment[0], weight_own, natural
    )

    found, total = gather(plan, my_place, block)
    pieces, slots = [piece for piece, _ in found], [parts for _, parts in found]
    new_weights, new_state, trust_ratios = finish(
        plan, my_place, position, total, norm_state, weights, pieces, slots
    )
    return (new_weights, new_first[None], new_second[None], new_state, trust_ratios)


def solution(mesh):
    in_specs = (
        P("dp", "mp", None),
        P("mp", None),
        P("mp", "dp", None),
        P("mp", "dp", None),
        P("mp", None),
        P("dp", None, None),
        P(),
    )
    out_specs = (P("mp", None), P("mp", "dp", None), P("mp", "dp", None), P(), P())
    return jax.shard_map(local, mesh=mesh, in_specs=in_specs, out_specs=out_specs, check_vma=False)
```

```python
import functools

import jax
import jax.numpy as jnp
from jax import lax
from jax.experimental import pallas as pl
from jax.experimental.pallas import tpu as pltpu
from jax.sharding import PartitionSpec as P

D = 1024
NTAB = 8
NKEYS = 256
KDIM = 128
LANE = 128
VROW_DEV = 512

beta_one = 0.9
beta_two = 0.99
bias_one = 1.0 - 0.9**4
bias_two = 1.0 - 0.99**4
epsilon = 1e-06
learning = 0.02
decay_rate = 0.01
matrices = 5
MIB = 1 << 20
TILES = 8
FETCHES = 4
EARLY = 0.7


def matrix_bounds(narrow):
    query_blocks = D * D // (LANE * narrow)
    key_blocks = NTAB * NKEYS * KDIM // (LANE * narrow)
    value_blocks = VROW_DEV * D // LANE
    return (
        query_blocks,
        query_blocks + key_blocks,
        query_blocks + key_blocks + value_blocks,
        2 * query_blocks + key_blocks + value_blocks,
    )


class Plan:
    def __init__(self, replicas, narrow, blocks):
        self.replicas, self.narrow, self.blocks = replicas, narrow, blocks
        chips = replicas // 2
        self.nz = 4 if chips % 4 == 0 else chips
        self.nx = chips // self.nz
        assert self.nz in (1, 2, 4) and self.nx in (1, 2, 4)
        self.own = blocks // replicas
        self.tail = 8
        self.norm_rows = 2 * D // LANE
        self.norm_each = -(-self.norm_rows // replicas)
        self.block = self.own + self.tail
        self.group = self.nx * self.block
        self.half = self.nz * self.group
        self.lists = -(-blocks // (8 * LANE)) * 8
        self.bounds = matrix_bounds(narrow)

    def index(self, z, x, c):
        return (z * self.nx + x) * 2 + c

    def start(self, far_z, far_x, far_c):
        return (1 - far_c) * self.half + far_z * self.group + far_x * self.block

    def order(self):
        zs, xs = range(self.nz - 1, -1, -1), range(self.nx - 1, -1, -1)
        return [(z, x, far_c) for far_c in (1, 0) for z in zs for x in xs]

    def send(self, value, axis, pairs):
        every = []
        for z in range(self.nz):
            for x in range(self.nx):
                for c in range(2):
                    here = {"z": z, "x": x, "c": c}
                    for source, target in pairs:
                        if here[axis] == source:
                            every.append((self.index(z, x, c), self.index(**{**here, axis: target})))
        return lax.ppermute(value, "dp", every)

    def swap(self, value):
        return self.send(value, "c", PAIR)


PAIR = [(0, 1), (1, 0)]
PAIRS = [(0, 1), (1, 0), (2, 3), (3, 2)]
MIDDLE = [(1, 2), (2, 1)]
INWARD = [(0, 1), (3, 2)]
OUTWARD = [(1, 0), (2, 3)]


def line_reduce(plan, axis, blocks):
    if len(blocks) == 1:
        return [blocks[0]]
    if len(blocks) == 2:
        return [blocks[0], plan.send(blocks[1], axis, PAIR)]
    in_three = plan.send(blocks[3], axis, INWARD)
    in_two = plan.send(blocks[2], axis, INWARD)
    across_two = plan.send(blocks[2] + in_three, axis, MIDDLE)
    across_three = plan.send(blocks[3] + in_two, axis, MIDDLE)
    pair = plan.send(blocks[1] + across_two, axis, PAIRS)
    return [blocks[0], pair, across_three]


def together(*values):
    return lax.optimization_barrier(values)


def reduce(plan, mine, theirs, beside):
    def along_x(z, own):
        terms = line_reduce(plan, "x", [own] + theirs[z])
        return terms

    three = along_x(3, mine[3])
    two = along_x(2, mine[2])
    near_three = sum(three[1:], three[0])
    in_three = plan.send(near_three, "z", INWARD)
    in_three, near_two, *beside = together(in_three, sum(two[1:], two[0]), *beside)
    one = along_x(1, mine[1])
    across_two = plan.send(near_two + in_three, "z", MIDDLE)
    in_two = plan.send(near_two, "z", INWARD)
    across_two, onward, near_one = together(across_two, near_three + in_two, sum(one[1:], one[0]))
    zero = along_x(0, mine[0])
    pair = plan.send(near_one + across_two, "z", PAIRS)
    across_three = plan.send(onward, "z", MIDDLE)
    return zero + [pair, across_three] + beside


def sums_kernel(plan, place_ref, *refs):
    tails, (out_ref, held) = refs[: plan.nz], refs[plan.nz :]
    for far_z, tail in enumerate(tails):
        held[place_ref[0] ^ far_z] = tail[...]
    total = held[0]
    for z in range(1, plan.nz):
        total = total + held[z]
    out_ref[...] = total


def all_sums(plan, my_place, blocks):
    def tail_of(row):
        return pl.BlockSpec((plan.tail, LANE), lambda i: ((row + plan.own) // plan.tail, 0))

    specs = [tail_of(row) for _, row in blocks]
    total = pl.pallas_call(
        functools.partial(sums_kernel, plan),
        grid=(1,),
        out_shape=jax.ShapeDtypeStruct((plan.tail, LANE), jnp.float32),
        in_specs=[pl.BlockSpec(memory_space=pltpu.SMEM)] + specs,
        out_specs=pl.BlockSpec(memory_space=pltpu.VMEM),
        scratch_shapes=[pltpu.VMEM((plan.nz, plan.tail, LANE), jnp.float32)],
        compiler_params=pltpu.CompilerParams(vmem_limit_bytes=4 * MIB),
        name="sums",
    )(my_place, *(value for value, _ in blocks))
    hop = 1
    while hop < plan.nx:
        total = total + plan.send(total, "x", [(i, i ^ hop) for i in range(plan.nx)])
        hop *= 2
    return total


def all_cores(plan, total):
    total = total + plan.swap(total)
    hop = 1
    while hop < plan.narrow:
        total = total + lax.ppermute(total, "mp", [(i, i ^ hop) for i in range(plan.narrow)])
        hop *= 2
    return total


def gather(plan, my_place, block):
    def along_x(value):
        return line_gather(plan, "x", plan.nx, value)

    if plan.nz != 4:
        lines = [along_x(value) for value in line_gather(plan, "z", plan.nz, block)]
        total = all_cores(plan, all_sums(plan, my_place, [(line[0], 0) for line in lines]))
        mine = [(value, [(z, x)]) for z, line in enumerate(lines) for x, value in enumerate(line)]
    else:
        line = along_x(block)
        pair = plan.send(block, "z", PAIRS)
        three = plan.send(block, "z", MIDDLE)
        three, own, *line = together(three, jnp.concatenate([block, pair]), *line)
        line_pair = along_x(pair)
        two = plan.send(pair, "z", MIDDLE)
        out_two = plan.send(three, "z", OUTWARD)
        _, *line_pair = together(two, *line_pair)
        far = [jnp.concatenate([line[x], line_pair[x]]) for x in range(1, plan.nx)]
        near_two, *far = together(two + out_two, *far)
        line_two = along_x(near_two)
        out_three = plan.send(two, "z", OUTWARD)
        near_three = three + out_three
        line_three = along_x(near_three)
        total = all_sums(plan, my_place, [(own, 0), (own, plan.block), (near_two, 0), (near_three, 0)])
        total, *line_two = together(total, *line_two)
        early = plan.swap(near_three)
        early, total, *line_three = together(early, all_cores(plan, total), *line_three)
        mine = [(value, [(0, x), (1, x)]) for x, value in enumerate([own] + far)]
        mine += [(value, [(2, x)]) for x, value in enumerate(line_two)]
        mine += [(value, [(3, x)]) for x, value in enumerate(line_three)]
    swapped = [early if plan.nz == 4 and slots == [(3, 0)] else plan.swap(value) for value, slots in mine]
    found = [(value, [slot + (0,) for slot in slots]) for value, slots in mine]
    found += [(value, [slot + (1,) for slot in slots]) for value, (_, slots) in zip(swapped, mine)]
    return found, total


def line_gather(plan, axis, count, value):
    if count == 1:
        return [value]
    if count == 2:
        return [value, plan.send(value, axis, PAIR)]
    pair = plan.send(value, axis, PAIRS)
    across_three = plan.send(value, axis, MIDDLE)
    across_two = plan.send(pair, axis, MIDDLE)
    out_two = plan.send(across_three, axis, OUTWARD)
    out_three = plan.send(across_two, axis, OUTWARD)
    return [value, pair, across_two + out_two, across_three + out_three]


def place_kernel(plan, place_ref, owner_ref, norm_ref, grads_ref, *refs):
    out_refs, refs = refs[: plan.replicas], refs[plan.replicas :]
    position_ref, raw, moved, position, sem_in, sem_position, sem_out = refs
    lines = plan.blocks // LANE
    ends = [lines * (i + 1) // FETCHES for i in range(FETCHES)]
    fetches = []
    for i, end in enumerate(ends):
        low = ends[i - 1] * LANE if i else 0
        rows = pl.ds(low, end * LANE - low)
        fetches.append(pltpu.make_async_copy(grads_ref.at[rows], raw.at[rows], sem_in.at[i]))
        fetches[-1].start()
    lists = plan.lists
    owners = owner_ref[...]
    my_z, my_x, my_c = place_ref[0], place_ref[1], place_ref[2]
    count = plan.replicas
    lane_in = lax.broadcasted_iota(jnp.int32, (LANE, LANE), 0)
    lane_out = lax.broadcasted_iota(jnp.int32, (LANE, LANE), 1)
    before = (lane_in < lane_out).astype(jnp.float32).astype(jnp.bfloat16)
    row_out = lax.broadcasted_iota(jnp.int32, (lists, lists), 0)
    row_in = lax.broadcasted_iota(jnp.int32, (lists, lists), 1)
    above = (row_in < row_out).astype(jnp.float32).astype(jnp.bfloat16)
    flags = [(owners == d).astype(jnp.float32).astype(jnp.bfloat16) for d in range(count)]
    inner = jnp.dot(jnp.concatenate(flags, 0), before, preferred_element_type=jnp.float32)
    owner_in = lax.broadcasted_iota(jnp.int32, (count * LANE, LANE), 0)
    owner_out = lax.broadcasted_iota(jnp.int32, (count * LANE, LANE), 1)
    pick = (owner_in // LANE == owner_out).astype(jnp.float32).astype(jnp.bfloat16)
    totals = jnp.dot(jnp.concatenate(flags, 1), pick, preferred_element_type=jnp.float32)
    outer = jnp.dot(above, totals.astype(jnp.bfloat16), preferred_element_type=jnp.float32)
    ranks = jnp.full((lists, LANE), plan.own, jnp.int32)
    result = jnp.zeros((lists, LANE), jnp.int32)
    for z in range(plan.nz):
        for x in range(plan.nx):
            for c in range(2):
                d = plan.index(z, x, c)
                mine = owners == d
                rank = (inner[d * lists : (d + 1) * lists, :] + outer[:, d : d + 1]).astype(jnp.int32)
                start = plan.start(my_z ^ z, my_x ^ x, my_c ^ c)
                first_norm = d * plan.norm_each
                tail = [jnp.zeros((plan.tail, LANE), jnp.float32)]
                for row in range(min(first_norm + plan.norm_each, plan.norm_rows) - 1, first_norm - 1, -1):
                    part = norm_ref[row * LANE // D : row * LANE // D + 1, row * LANE % D : row * LANE % D + LANE]
                    tail.insert(0, part.astype(jnp.float32))
                tail = jnp.concatenate(tail, 0)[: plan.tail]
                moved[pl.ds(pl.multiple_of(start + plan.own, 8), plan.tail), :] = tail
                result = jnp.where(mine, rank + start, result)
                ranks = jnp.where(mine, rank, ranks)
    position_ref[...] = result
    to_scalar = pltpu.make_async_copy(position_ref, position, sem_position)
    to_scalar.start()
    to_scalar.wait()

    def copies(part, low, high):
        found = []
        for i, (out, slot) in enumerate(zip(out_refs, plan.order())):
            source = moved.at[pl.ds(plan.start(*slot) + low, high - low)]
            found.append(pltpu.make_async_copy(source, out.at[pl.ds(low, high - low)], sem_out.at[part, i]))
        return found

    cut = int(plan.own * EARLY / 8) * 8
    line_of = lax.broadcasted_iota(jnp.int32, (lists, LANE), 0)
    complete = jnp.max(jnp.where(ranks < cut, line_of + 1, 0))
    early = copies(0, 0, cut)
    late = copies(1, cut, plan.block)

    for i, end in enumerate(ends):
        fetches[i].wait()

        @pl.loop(ends[i - 1] if i else 0, end)
        def _(line):
            for part in range(0, LANE, 16):
                rows = raw[pl.ds(pl.multiple_of(line * LANE + part, 16), 16), :].astype(jnp.float32)
                for u in range(16):
                    moved[pl.ds(position[line, part + u], 1), :] = rows[u : u + 1, :]

        if i == FETCHES - 2:

            @pl.when(complete <= end)
            def _():
                for copy in early:
                    copy.start()

    @pl.when(complete > ends[FETCHES - 2])
    def _():
        for copy in early:
            copy.start()

    for copy in late:
        copy.start()
    for copy in early + late:
        copy.wait()


def place(plan, my_place, owners, norm_grads, grads):
    shapes = [(plan.block, LANE)] * plan.replicas
    outs = pl.pallas_call(
        functools.partial(place_kernel, plan),
        out_shape=[jax.ShapeDtypeStruct(s, jnp.float32) for s in shapes]
        + [jax.ShapeDtypeStruct((plan.lists, LANE), jnp.int32)],
        in_specs=[
            pl.BlockSpec(memory_space=pltpu.SMEM),
            pl.BlockSpec(memory_space=pltpu.VMEM),
            pl.BlockSpec(memory_space=pltpu.VMEM),
            pl.BlockSpec(memory_space=pl.ANY),
        ],
        out_specs=[pl.BlockSpec(memory_space=pl.ANY)] * len(shapes) + [pl.BlockSpec(memory_space=pltpu.VMEM)],
        scratch_shapes=[
            pltpu.VMEM((plan.blocks, LANE), jnp.bfloat16),
            pltpu.VMEM((2 * plan.half, LANE), jnp.float32),
            pltpu.SMEM((plan.lists, LANE), jnp.int32),
            pltpu.SemaphoreType.DMA((FETCHES,)),
            pltpu.SemaphoreType.DMA,
            pltpu.SemaphoreType.DMA((2, len(shapes))),
        ],
        compiler_params=pltpu.CompilerParams(vmem_limit_bytes=58 * MIB),
        name="place_gradients",
    )(my_place, owners, norm_grads, grads)
    return dict(zip(plan.order(), outs)), outs[-1]


def owned_kernel(plan, place_ref, owner_ref, weights_ref, owned_ref, natural_ref, held, listed, order, sem_in, sem_order):
    fetch = pltpu.make_async_copy(weights_ref, held, sem_in)
    fetch.start()
    lists = plan.lists
    me = plan.index(place_ref[0], place_ref[1], place_ref[2])
    flags = (owner_ref[...] == me).astype(jnp.float32).astype(jnp.bfloat16)
    lane_in = lax.broadcasted_iota(jnp.int32, (LANE, LANE), 0)
    lane_out = lax.broadcasted_iota(jnp.int32, (LANE, LANE), 1)
    upto = (lane_in <= lane_out).astype(jnp.float32).astype(jnp.bfloat16)
    inner = jnp.dot(flags, upto, preferred_element_type=jnp.float32).astype(jnp.bfloat16)
    totals = lax.dot_general(
        jnp.ones((8, LANE), jnp.bfloat16), flags, (((1,), (1,)), ((), ())), preferred_element_type=jnp.float32
    )
    row_in = lax.broadcasted_iota(jnp.int32, (lists, lists), 0)
    row_out = lax.broadcasted_iota(jnp.int32, (lists, lists), 1)
    upto = (row_in <= row_out).astype(jnp.float32).astype(jnp.bfloat16)
    ends = jnp.dot(totals.astype(jnp.bfloat16), upto, preferred_element_type=jnp.float32)[0:1, :]
    place_of = lax.broadcasted_iota(jnp.int32, (LANE, lists), 1).astype(jnp.float32)
    rank_of = lax.broadcasted_iota(jnp.int32, (LANE, 1), 0)
    for step in range(listed.shape[0]):
        if step * LANE >= plan.own:
            break
        rank = (rank_of + step * LANE).astype(jnp.float32)
        passed = ends <= rank
        line = jnp.sum(passed.astype(jnp.float32), axis=1, keepdims=True)
        before = jnp.max(jnp.where(passed, ends, 0.0), axis=1, keepdims=True)
        chosen = (place_of == line).astype(jnp.float32).astype(jnp.bfloat16)
        counts = jnp.dot(chosen, inner, preferred_element_type=jnp.float32)
        column = jnp.sum((counts <= rank - before).astype(jnp.float32), axis=1, keepdims=True)
        block = jnp.broadcast_to((line * LANE + column).astype(jnp.int32), (LANE, LANE))
        natural_ref[step * LANE : (step + 1) * LANE, :] = block
        listed[step : step + 1, :] = jnp.sum(jnp.where(lane_in == lane_out, block, 0), axis=0, keepdims=True)
    to_scalar = pltpu.make_async_copy(listed, order, sem_order)
    to_scalar.start()
    to_scalar.wait()
    fetch.wait()

    def pick(line, count):
        for u in range(count):
            owned_ref[pl.ds(line * LANE + u, 1), :] = held[pl.ds(order[line, u], 1), :]

    @pl.loop(0, plan.own // LANE)
    def _(line):
        pick(line, LANE)

    if plan.own % LANE:
        pick(plan.own // LANE, plan.own % LANE)


def owned(plan, my_place, owners, weights):
    high_rows = -(-plan.own // (8 * LANE)) * 8
    ranks = -(-plan.own // LANE) * LANE
    vmem = pl.BlockSpec(memory_space=pltpu.VMEM)
    return pl.pallas_call(
        functools.partial(owned_kernel, plan),
        out_shape=[
            jax.ShapeDtypeStruct((plan.own, LANE), jnp.float32),
            jax.ShapeDtypeStruct((ranks, LANE), jnp.int32),
        ],
        in_specs=[pl.BlockSpec(memory_space=pltpu.SMEM), vmem, pl.BlockSpec(memory_space=pl.ANY)],
        out_specs=[vmem] * 2,
        scratch_shapes=[
            pltpu.VMEM((plan.blocks, LANE), jnp.float32),
            pltpu.VMEM((high_rows, LANE), jnp.int32),
            pltpu.SMEM((high_rows, LANE), jnp.int32),
            pltpu.SemaphoreType.DMA,
            pltpu.SemaphoreType.DMA,
        ],
        compiler_params=pltpu.CompilerParams(vmem_limit_bytes=58 * MIB),
        cost_estimate=pl.CostEstimate(flops=0, bytes_accessed=20 * MIB, transcendentals=0),
        name="owned_weights",
    )(my_place, owners, weights)


def update_kernel(plan, terms, *refs):
    parts, refs = refs[:terms], refs[terms:]
    first_ref, second_ref, weight_ref, natural_ref = refs[:4]
    new_first_ref, new_second_ref, block_ref = refs[4:]
    gradient = parts[0][: plan.block, :]
    for part in parts[1:]:
        gradient = gradient + part[: plan.block, :]
    tail, gradient = gradient[plan.own :, :], gradient[: plan.own, :]
    moment_one = beta_one * first_ref[...] + (1.0 - beta_one) * gradient
    moment_two = beta_two * second_ref[...] + (1.0 - beta_two) * gradient * gradient
    new_first_ref[...] = moment_one
    new_second_ref[...] = moment_two
    step = moment_one / bias_one / (jnp.sqrt(moment_two / bias_two) + epsilon)
    block_ref[: plan.own, :] = step
    weight = weight_ref[...]
    direction = step + decay_rate * weight
    natural = natural_ref[: plan.own, :]
    limits = (0,) + plan.bounds + (plan.blocks,)
    lane = lax.broadcasted_iota(jnp.int32, (8, LANE), 1)
    rank = lax.broadcasted_iota(jnp.int32, (8, LANE), 0)
    stats = jnp.zeros((8, LANE), jnp.float32)
    for column, squares in enumerate((weight * weight, direction * direction)):
        for k in range(matrices):
            inside = (natural >= limits[k]) & (natural < limits[k + 1])
            kept = jnp.where(inside, squares, 0.0).reshape(plan.own // 8, 8, LANE)
            total = jnp.sum(jnp.sum(kept, axis=0))
            stats = jnp.where((rank == plan.norm_each + k) & (lane == column), total, stats)
    block_ref[plan.own :, :] = tail + stats


def update(plan, parts, first, second, weight, natural):
    vmem = pl.BlockSpec(memory_space=pltpu.VMEM)
    shapes = [(plan.own, LANE), (plan.own, LANE), (plan.block, LANE)]
    return pl.pallas_call(
        functools.partial(update_kernel, plan, len(parts)),
        out_shape=[jax.ShapeDtypeStruct(s, jnp.float32) for s in shapes],
        in_specs=[vmem] * (len(parts) + 4),
        out_specs=[vmem] * len(shapes),
        compiler_params=pltpu.CompilerParams(vmem_limit_bytes=20 * MIB),
        name="moments",
    )(*parts, first, second, weight, natural)


def adam_rows(gradient, moment_one, moment_two, weight):
    moment_one = beta_one * moment_one + (1.0 - beta_one) * gradient
    moment_two = beta_two * moment_two + (1.0 - beta_two) * gradient * gradient
    step = moment_one / bias_one / (jnp.sqrt(moment_two / bias_two) + epsilon) + decay_rate * weight
    return (moment_one, moment_two, step)


def finish_kernel(plan, tile, slots, place_ref, position_ref, total_ref, norm_ref, weights_ref, *refs):
    pieces, refs = refs[: len(slots)], refs[len(slots) :]
    out_ref, new_norm_ref, trust_ref, held, norms, rates = refs
    now = pl.program_id(0)

    @pl.when(now == 0)
    def _():
        for piece, parts in zip(pieces, slots):
            for i, slot in enumerate(parts):
                held[pl.ds(plan.start(*slot), plan.block), :] = piece[i * plan.block : (i + 1) * plan.block, :]
        total = total_ref[...]
        for z in range(plan.nz):
            for x in range(plan.nx):
                for c in range(2):
                    start = plan.start(place_ref[0] ^ z, place_ref[1] ^ x, place_ref[2] ^ c) + plan.own
                    tail = held[pl.ds(pl.multiple_of(start, 8), plan.tail), :]
                    first = plan.index(z, x, c) * plan.norm_each
                    for row in range(first, min(first + plan.norm_each, plan.norm_rows)):
                        norms[row : row + 1, :] = tail[row - first : row - first + 1, :]
        for k in range(matrices):
            row = plan.norm_each + k
            weight_square, direction_square = total[row : row + 1, 0:1], total[row : row + 1, 1:2]
            ratio = jnp.sqrt(weight_square) / (jnp.sqrt(direction_square) + epsilon)
            rates[k : k + 1, :] = jnp.broadcast_to(learning * ratio, (1, LANE))
            trust_ref[k] = jnp.sum(ratio)
        each = plan.norm_rows // 2
        for i in range(2):
            gains, first, second = (
                jnp.concatenate([norm_ref[j, i : i + 1, row * LANE : (row + 1) * LANE] for row in range(each)], 0)
                for j in range(3)
            )
            one, two, step = adam_rows(norms[i * each : (i + 1) * each, :], first, second, gains)
            gain_square = jnp.sum(jnp.sum(gains * gains, axis=1, keepdims=True), axis=0, keepdims=True)
            step_square = jnp.sum(jnp.sum(step * step, axis=1, keepdims=True), axis=0, keepdims=True)
            ratio = jnp.sqrt(gain_square) / (jnp.sqrt(step_square) + epsilon)
            trust_ref[matrices + i] = jnp.sum(ratio)
            for j, value in enumerate((gains - learning * ratio * step, one, two)):
                for row in range(each):
                    new_norm_ref[j, i : i + 1, row * LANE : (row + 1) * LANE] = value[row : row + 1, :]

    lines = tile // LANE

    @pl.loop(0, lines)
    def _(line):
        matrix = jnp.int32(0)
        for bound in plan.bounds:
            matrix = matrix + (now * lines + line >= bound // LANE).astype(jnp.int32)
        rate = jnp.broadcast_to(rates[pl.ds(matrix, 1), :], (8, LANE))
        for group in range(0, LANE, 8):
            rows = [held[pl.ds(position_ref[now * lines + line, group + u], 1), :] for u in range(8)]
            here = pl.ds(pl.multiple_of(line * LANE + group, 8), 8)
            weight = weights_ref[here, :]
            direction = jnp.concatenate(rows, 0) + decay_rate * weight
            out_ref[here, :] = weight - rate * direction


def finish(plan, my_place, position, total, norm_state, weights, pieces, slots):
    assert all(bound % LANE == 0 for bound in plan.bounds + (plan.blocks,))
    tile = plan.blocks // next(n for n in (TILES, 4, 2, 1) if plan.blocks // LANE % n == 0)
    smem = pl.BlockSpec(memory_space=pltpu.SMEM)
    vmem = pl.BlockSpec(memory_space=pltpu.VMEM)
    return pl.pallas_call(
        functools.partial(finish_kernel, plan, tile, slots),
        grid=(plan.blocks // tile,),
        out_shape=[
            jax.ShapeDtypeStruct((plan.blocks, LANE), jnp.float32),
            jax.ShapeDtypeStruct(norm_state.shape, jnp.float32),
            jax.ShapeDtypeStruct((matrices + 2,), jnp.float32),
        ],
        in_specs=[smem, smem, vmem, vmem, pl.BlockSpec((tile, LANE), lambda i: (i, 0))]
        + [vmem] * len(pieces),
        out_specs=[pl.BlockSpec((tile, LANE), lambda i: (i, 0)), vmem, smem],
        scratch_shapes=[
            pltpu.VMEM((2 * plan.half, LANE), jnp.float32),
            pltpu.VMEM((plan.norm_rows, LANE), jnp.float32),
            pltpu.VMEM((8, LANE), jnp.float32),
        ],
        compiler_params=pltpu.CompilerParams(vmem_limit_bytes=20 * MIB),
        name="new_weights",
    )(my_place, position, total, norm_state, weights, *pieces)


def local(gradients, weights, first_moment, second_moment, owner_list, norm_grads, norm_state):
    plan = Plan(lax.axis_size("dp"), lax.axis_size("mp"), weights.shape[0])
    me = lax.axis_index("dp").astype(jnp.int32)
    my_place = jnp.stack([me // (2 * plan.nx), (me // 2) % plan.nx, me % 2]).astype(jnp.int32)
    owners = jnp.pad(owner_list[0], (0, plan.lists * LANE - plan.blocks), constant_values=-1)
    owners = owners.reshape(plan.lists, LANE)
    placed, position = place(plan, my_place, owners, norm_grads[0], gradients[0])
    weight_own, natural = owned(plan, my_place, owners, weights)

    mine, theirs = [None] * plan.nz, [None] * plan.nz
    for z in reversed(range(plan.nz)):
        both = [None] * plan.nx
        for x in reversed(range(plan.nx)):
            both[x] = placed[z, x, 0] + plan.swap(placed[z, x, 1])
            if (z, x) == (3, plan.nx - 1):
                later = [slot for slot in plan.order() if slot[2] and slot[:2] != (z, x)]
                both[x], *values = together(both[x], *(placed[slot] for slot in later))
                placed.update(zip(later, values))
        mine[z], theirs[z] = both[0], both[1:]
    if plan.nz == 4:
        parts = reduce(plan, mine, theirs, (weight_own, natural))
        parts, (weight_own, natural) = parts[:-2], parts[-2:]
    else:
        near = []
        for z in reversed(range(plan.nz)):
            terms = line_reduce(plan, "x", [mine[z]] + theirs[z])
            near.insert(0, sum(terms[1:], terms[0]) if z else None)
        parts = terms + line_reduce(plan, "z", near)[1:]
    new_first, new_second, block = update(
        plan, parts, first_moment[0], second_moment[0], weight_own, natural
    )

    found, total = gather(plan, my_place, block)
    pieces, slots = [piece for piece, _ in found], [parts for _, parts in found]
    new_weights, new_state, trust_ratios = finish(
        plan, my_place, position, total, norm_state, weights, pieces, slots
    )
    return (new_weights, new_first[None], new_second[None], new_state, trust_ratios)


def solution(mesh):
    in_specs = (
        P("dp", "mp", None),
        P("mp", None),
        P("mp", "dp", None),
        P("mp", "dp", None),
        P("mp", None),
        P("dp", None, None),
        P(),
    )
    out_specs = (P("mp", None), P("mp", "dp", None), P("mp", "dp", None), P(), P())
    return jax.shard_map(local, mesh=mesh, in_specs=in_specs, out_specs=out_specs, check_vma=False)
```

```python
import functools

import jax
import jax.numpy as jnp
from jax import lax
from jax.experimental import pallas as pl
from jax.experimental.pallas import tpu as pltpu
from jax.sharding import PartitionSpec as P

D = 1024
NTAB = 8
NKEYS = 256
KDIM = 128
LANE = 128
VROW_DEV = 512

beta_one = 0.9
beta_two = 0.99
bias_one = 1.0 - 0.9**4
bias_two = 1.0 - 0.99**4
epsilon = 1e-06
learning = 0.02
decay_rate = 0.01
matrices = 5
MIB = 1 << 20
TILES = 8
FETCHES = 4
EARLY = 0.7


def matrix_bounds(narrow):
    query_blocks = D * D // (LANE * narrow)
    key_blocks = NTAB * NKEYS * KDIM // (LANE * narrow)
    value_blocks = VROW_DEV * D // LANE
    return (
        query_blocks,
        query_blocks + key_blocks,
        query_blocks + key_blocks + value_blocks,
        2 * query_blocks + key_blocks + value_blocks,
    )


class Plan:
    def __init__(self, replicas, narrow, blocks):
        self.replicas, self.narrow, self.blocks = replicas, narrow, blocks
        chips = replicas // 2
        self.nz = 4 if chips % 4 == 0 else chips
        self.nx = chips // self.nz
        assert self.nz in (1, 2, 4) and self.nx in (1, 2, 4)
        self.own = blocks // replicas
        self.tail = 8
        self.norm_rows = 2 * D // LANE
        self.norm_each = -(-self.norm_rows // replicas)
        self.block = self.own + self.tail
        self.group = self.nx * self.block
        self.half = self.nz * self.group
        self.lists = -(-blocks // (8 * LANE)) * 8
        self.bounds = matrix_bounds(narrow)

    def index(self, z, x, c):
        return (z * self.nx + x) * 2 + c

    def start(self, far_z, far_x, far_c):
        return (1 - far_c) * self.half + far_z * self.group + far_x * self.block

    def order(self):
        zs, xs = range(self.nz - 1, -1, -1), range(self.nx - 1, -1, -1)
        return [(z, x, far_c) for far_c in (1, 0) for z in zs for x in xs]

    def send(self, value, axis, pairs):
        every = []
        for z in range(self.nz):
            for x in range(self.nx):
                for c in range(2):
                    here = {"z": z, "x": x, "c": c}
                    for source, target in pairs:
                        if here[axis] == source:
                            every.append((self.index(z, x, c), self.index(**{**here, axis: target})))
        return lax.ppermute(value, "dp", every)

    def swap(self, value):
        return self.send(value, "c", PAIR)


PAIR = [(0, 1), (1, 0)]
PAIRS = [(0, 1), (1, 0), (2, 3), (3, 2)]
MIDDLE = [(1, 2), (2, 1)]
INWARD = [(0, 1), (3, 2)]
OUTWARD = [(1, 0), (2, 3)]


def line_reduce(plan, axis, blocks):
    if len(blocks) == 1:
        return [blocks[0]]
    if len(blocks) == 2:
        return [blocks[0], plan.send(blocks[1], axis, PAIR)]
    in_three = plan.send(blocks[3], axis, INWARD)
    in_two = plan.send(blocks[2], axis, INWARD)
    across_two = plan.send(blocks[2] + in_three, axis, MIDDLE)
    across_three = plan.send(blocks[3] + in_two, axis, MIDDLE)
    pair = plan.send(blocks[1] + across_two, axis, PAIRS)
    return [blocks[0], pair, across_three]


def together(*values):
    return lax.optimization_barrier(values)


def reduce(plan, mine, theirs, beside):
    def along_x(z, own):
        terms = line_reduce(plan, "x", [own] + theirs[z])
        return terms

    three = along_x(3, mine[3])
    two = along_x(2, mine[2])
    near_three = sum(three[1:], three[0])
    in_three = plan.send(near_three, "z", INWARD)
    in_three, near_two, *beside = together(in_three, sum(two[1:], two[0]), *beside)
    one = along_x(1, mine[1])
    across_two = plan.send(near_two + in_three, "z", MIDDLE)
    in_two = plan.send(near_two, "z", INWARD)
    across_two, onward, near_one = together(across_two, near_three + in_two, sum(one[1:], one[0]))
    zero = along_x(0, mine[0])
    pair = plan.send(near_one + across_two, "z", PAIRS)
    across_three = plan.send(onward, "z", MIDDLE)
    return zero + [pair, across_three] + beside


def sums_kernel(plan, place_ref, *refs):
    tails, (out_ref, held) = refs[: plan.nz], refs[plan.nz :]
    for far_z, tail in enumerate(tails):
        held[place_ref[0] ^ far_z] = tail[...]
    total = held[0]
    for z in range(1, plan.nz):
        total = total + held[z]
    out_ref[...] = total


def all_sums(plan, my_place, blocks):
    def tail_of(row):
        return pl.BlockSpec((plan.tail, LANE), lambda i: ((row + plan.own) // plan.tail, 0))

    specs = [tail_of(row) for _, row in blocks]
    total = pl.pallas_call(
        functools.partial(sums_kernel, plan),
        grid=(1,),
        out_shape=jax.ShapeDtypeStruct((plan.tail, LANE), jnp.float32),
        in_specs=[pl.BlockSpec(memory_space=pltpu.SMEM)] + specs,
        out_specs=pl.BlockSpec(memory_space=pltpu.VMEM),
        scratch_shapes=[pltpu.VMEM((plan.nz, plan.tail, LANE), jnp.float32)],
        compiler_params=pltpu.CompilerParams(vmem_limit_bytes=4 * MIB),
        name="sums",
    )(my_place, *(value for value, _ in blocks))
    hop = 1
    while hop < plan.nx:
        total = total + plan.send(total, "x", [(i, i ^ hop) for i in range(plan.nx)])
        hop *= 2
    return total


def all_cores(plan, total):
    total = total + plan.swap(total)
    hop = 1
    while hop < plan.narrow:
        total = total + lax.ppermute(total, "mp", [(i, i ^ hop) for i in range(plan.narrow)])
        hop *= 2
    return total


def gather(plan, my_place, block):
    def along_x(value):
        return line_gather(plan, "x", plan.nx, value)

    if plan.nz != 4:
        ready = {}
        lines = [along_x(value) for value in line_gather(plan, "z", plan.nz, block)]
        total = all_cores(plan, all_sums(plan, my_place, [(line[0], 0) for line in lines]))
        mine = [(value, [(z, x)]) for z, line in enumerate(lines) for x, value in enumerate(line)]
    else:
        line = along_x(block)
        pair = plan.send(block, "z", PAIRS)
        three = plan.send(block, "z", MIDDLE)
        three, own, *line = together(three, jnp.concatenate([block, pair]), *line)
        line_pair = along_x(pair)
        two = plan.send(pair, "z", MIDDLE)
        out_two = plan.send(three, "z", OUTWARD)
        _, *line_pair = together(two, *line_pair)
        far = [jnp.concatenate([line[x], line_pair[x]]) for x in range(1, plan.nx)]
        near_two, *far = together(two + out_two, *far)
        line_two = along_x(near_two)
        out_three = plan.send(two, "z", OUTWARD)
        near_three = three + out_three
        line_three = along_x(near_three)
        total = all_sums(plan, my_place, [(own, 0), (own, plan.block), (near_two, 0), (near_three, 0)])
        total, *line_two = together(total, *line_two)
        early = plan.swap(near_three)
        early, total, *line_three = together(early, all_cores(plan, total), *line_three)
        ready = {(3, 0): early}
        mine = [(value, [(0, x), (1, x)]) for x, value in enumerate([own] + far)]
        mine += [(value, [(2, x)]) for x, value in enumerate(line_two)]
        mine += [(value, [(3, x)]) for x, value in enumerate(line_three)]
    swapped = [ready[slots[0]] if slots[0] in ready else plan.swap(value) for value, slots in mine]
    found = [(value, [slot + (0,) for slot in slots]) for value, slots in mine]
    found += [(value, [slot + (1,) for slot in slots]) for value, (_, slots) in zip(swapped, mine)]
    return found, total


def line_gather(plan, axis, count, value):
    if count == 1:
        return [value]
    if count == 2:
        return [value, plan.send(value, axis, PAIR)]
    pair = plan.send(value, axis, PAIRS)
    across_three = plan.send(value, axis, MIDDLE)
    across_two = plan.send(pair, axis, MIDDLE)
    out_two = plan.send(across_three, axis, OUTWARD)
    out_three = plan.send(across_two, axis, OUTWARD)
    return [value, pair, across_two + out_two, across_three + out_three]


def place_kernel(plan, owner_ref, norm_ref, grads_ref, *refs):
    out_refs, refs = refs[: plan.replicas], refs[plan.replicas :]
    position_ref, raw, moved, position, sem_in, sem_position, sem_out = refs
    lines = plan.blocks // LANE
    ends = [lines * (i + 1) // FETCHES for i in range(FETCHES)]
    fetches = []
    for i, end in enumerate(ends):
        low = ends[i - 1] * LANE if i else 0
        rows = pl.ds(low, end * LANE - low)
        fetches.append(pltpu.make_async_copy(grads_ref.at[rows], raw.at[rows], sem_in.at[i]))
        fetches[-1].start()
    lists = plan.lists
    owners = owner_ref[...]
    me = lax.axis_index("dp").astype(jnp.int32)
    my_z, my_x, my_c = me // (2 * plan.nx), me // 2 % plan.nx, me % 2
    count = plan.replicas
    lane_in = lax.broadcasted_iota(jnp.int32, (LANE, LANE), 0)
    lane_out = lax.broadcasted_iota(jnp.int32, (LANE, LANE), 1)
    before = (lane_in < lane_out).astype(jnp.float32).astype(jnp.bfloat16)
    row_out = lax.broadcasted_iota(jnp.int32, (lists, lists), 0)
    row_in = lax.broadcasted_iota(jnp.int32, (lists, lists), 1)
    above = (row_in < row_out).astype(jnp.float32).astype(jnp.bfloat16)
    flags = [(owners == d).astype(jnp.float32).astype(jnp.bfloat16) for d in range(count)]
    inner = jnp.dot(jnp.concatenate(flags, 0), before, preferred_element_type=jnp.float32)
    owner_in = lax.broadcasted_iota(jnp.int32, (count * LANE, LANE), 0)
    owner_out = lax.broadcasted_iota(jnp.int32, (count * LANE, LANE), 1)
    pick = (owner_in // LANE == owner_out).astype(jnp.float32).astype(jnp.bfloat16)
    totals = jnp.dot(jnp.concatenate(flags, 1), pick, preferred_element_type=jnp.float32)
    outer = jnp.dot(above, totals.astype(jnp.bfloat16), preferred_element_type=jnp.float32)
    ranks = jnp.full((lists, LANE), plan.own, jnp.int32)
    result = jnp.zeros((lists, LANE), jnp.int32)
    for z in range(plan.nz):
        for x in range(plan.nx):
            for c in range(2):
                d = plan.index(z, x, c)
                mine = owners == d
                rank = (inner[d * lists : (d + 1) * lists, :] + outer[:, d : d + 1]).astype(jnp.int32)
                start = plan.start(my_z ^ z, my_x ^ x, my_c ^ c)
                first_norm = d * plan.norm_each
                tail = [jnp.zeros((plan.tail, LANE), jnp.float32)]
                for row in range(min(first_norm + plan.norm_each, plan.norm_rows) - 1, first_norm - 1, -1):
                    part = norm_ref[row * LANE // D : row * LANE // D + 1, row * LANE % D : row * LANE % D + LANE]
                    tail.insert(0, part.astype(jnp.float32))
                tail = jnp.concatenate(tail, 0)[: plan.tail]
                moved[pl.ds(pl.multiple_of(start + plan.own, 8), plan.tail), :] = tail
                result = jnp.where(mine, rank + start, result)
                ranks = jnp.where(mine, rank, ranks)
    position_ref[...] = result
    to_scalar = pltpu.make_async_copy(position_ref, position, sem_position)
    to_scalar.start()
    to_scalar.wait()

    def copies(part, low, high):
        found = []
        for i, (out, slot) in enumerate(zip(out_refs, plan.order())):
            source = moved.at[pl.ds(plan.start(*slot) + low, high - low)]
            found.append(pltpu.make_async_copy(source, out.at[pl.ds(low, high - low)], sem_out.at[part, i]))
        return found

    cut = int(plan.own * EARLY / 8) * 8
    line_of = lax.broadcasted_iota(jnp.int32, (lists, LANE), 0)
    complete = jnp.max(jnp.where(ranks < cut, line_of + 1, 0))
    early = copies(0, 0, cut)
    late = copies(1, cut, plan.block)

    for i, end in enumerate(ends):
        fetches[i].wait()

        @pl.loop(ends[i - 1] if i else 0, end)
        def _(line):
            for part in range(0, LANE, 16):
                rows = raw[pl.ds(pl.multiple_of(line * LANE + part, 16), 16), :].astype(jnp.float32)
                for u in range(16):
                    moved[pl.ds(position[line, part + u], 1), :] = rows[u : u + 1, :]

        if i == FETCHES - 2:

            @pl.when(complete <= end)
            def _():
                for copy in early:
                    copy.start()

    @pl.when(complete > ends[FETCHES - 2])
    def _():
        for copy in early:
            copy.start()

    for copy in late:
        copy.start()
    for copy in early + late:
        copy.wait()


def place(plan, owners, norm_grads, grads):
    shapes = [(plan.block, LANE)] * plan.replicas
    outs = pl.pallas_call(
        functools.partial(place_kernel, plan),
        out_shape=[jax.ShapeDtypeStruct(s, jnp.float32) for s in shapes]
        + [jax.ShapeDtypeStruct((plan.lists, LANE), jnp.int32)],
        in_specs=[
            pl.BlockSpec(memory_space=pltpu.VMEM),
            pl.BlockSpec(memory_space=pltpu.VMEM),
            pl.BlockSpec(memory_space=pl.ANY),
        ],
        out_specs=[pl.BlockSpec(memory_space=pl.ANY)] * len(shapes) + [pl.BlockSpec(memory_space=pltpu.VMEM)],
        scratch_shapes=[
            pltpu.VMEM((plan.blocks, LANE), jnp.bfloat16),
            pltpu.VMEM((2 * plan.half, LANE), jnp.float32),
            pltpu.SMEM((plan.lists, LANE), jnp.int32),
            pltpu.SemaphoreType.DMA((FETCHES,)),
            pltpu.SemaphoreType.DMA,
            pltpu.SemaphoreType.DMA((2, len(shapes))),
        ],
        compiler_params=pltpu.CompilerParams(vmem_limit_bytes=58 * MIB),
        name="place_gradients",
    )(owners, norm_grads, grads)
    return dict(zip(plan.order(), outs)), outs[-1]


def owned_kernel(plan, place_ref, owner_ref, weights_ref, owned_ref, natural_ref, held, listed, order, sem_in, sem_order):
    fetch = pltpu.make_async_copy(weights_ref, held, sem_in)
    fetch.start()
    lists = plan.lists
    me = plan.index(place_ref[0], place_ref[1], place_ref[2])
    flags = (owner_ref[...] == me).astype(jnp.float32).astype(jnp.bfloat16)
    lane_in = lax.broadcasted_iota(jnp.int32, (LANE, LANE), 0)
    lane_out = lax.broadcasted_iota(jnp.int32, (LANE, LANE), 1)
    upto = (lane_in <= lane_out).astype(jnp.float32).astype(jnp.bfloat16)
    inner = jnp.dot(flags, upto, preferred_element_type=jnp.float32).astype(jnp.bfloat16)
    totals = lax.dot_general(
        jnp.ones((8, LANE), jnp.bfloat16), flags, (((1,), (1,)), ((), ())), preferred_element_type=jnp.float32
    )
    row_in = lax.broadcasted_iota(jnp.int32, (lists, lists), 0)
    row_out = lax.broadcasted_iota(jnp.int32, (lists, lists), 1)
    upto = (row_in <= row_out).astype(jnp.float32).astype(jnp.bfloat16)
    ends = jnp.dot(totals.astype(jnp.bfloat16), upto, preferred_element_type=jnp.float32)[0:1, :]
    place_of = lax.broadcasted_iota(jnp.int32, (LANE, lists), 1).astype(jnp.float32)
    rank_of = lax.broadcasted_iota(jnp.int32, (LANE, 1), 0)
    for step in range(listed.shape[0]):
        if step * LANE >= plan.own:
            break
        rank = (rank_of + step * LANE).astype(jnp.float32)
        passed = ends <= rank
        line = jnp.sum(passed.astype(jnp.float32), axis=1, keepdims=True)
        before = jnp.max(jnp.where(passed, ends, 0.0), axis=1, keepdims=True)
        chosen = (place_of == line).astype(jnp.float32).astype(jnp.bfloat16)
        counts = jnp.dot(chosen, inner, preferred_element_type=jnp.float32)
        column = jnp.sum((counts <= rank - before).astype(jnp.float32), axis=1, keepdims=True)
        block = jnp.broadcast_to((line * LANE + column).astype(jnp.int32), (LANE, LANE))
        natural_ref[step * LANE : (step + 1) * LANE, :] = block
        listed[step : step + 1, :] = jnp.sum(jnp.where(lane_in == lane_out, block, 0), axis=0, keepdims=True)
    to_scalar = pltpu.make_async_copy(listed, order, sem_order)
    to_scalar.start()
    to_scalar.wait()
    fetch.wait()

    def pick(line, count):
        for u in range(count):
            owned_ref[pl.ds(line * LANE + u, 1), :] = held[pl.ds(order[line, u], 1), :]

    @pl.loop(0, plan.own // LANE)
    def _(line):
        pick(line, LANE)

    if plan.own % LANE:
        pick(plan.own // LANE, plan.own % LANE)


def owned(plan, my_place, owners, weights):
    high_rows = -(-plan.own // (8 * LANE)) * 8
    ranks = -(-plan.own // LANE) * LANE
    vmem = pl.BlockSpec(memory_space=pltpu.VMEM)
    return pl.pallas_call(
        functools.partial(owned_kernel, plan),
        out_shape=[
            jax.ShapeDtypeStruct((plan.own, LANE), jnp.float32),
            jax.ShapeDtypeStruct((ranks, LANE), jnp.int32),
        ],
        in_specs=[pl.BlockSpec(memory_space=pltpu.SMEM), vmem, pl.BlockSpec(memory_space=pl.ANY)],
        out_specs=[vmem] * 2,
        scratch_shapes=[
            pltpu.VMEM((plan.blocks, LANE), jnp.float32),
            pltpu.VMEM((high_rows, LANE), jnp.int32),
            pltpu.SMEM((high_rows, LANE), jnp.int32),
            pltpu.SemaphoreType.DMA,
            pltpu.SemaphoreType.DMA,
        ],
        compiler_params=pltpu.CompilerParams(vmem_limit_bytes=58 * MIB),
        cost_estimate=pl.CostEstimate(flops=0, bytes_accessed=20 * MIB, transcendentals=0),
        name="owned_weights",
    )(my_place, owners, weights)


def update_kernel(plan, terms, *refs):
    parts, refs = refs[:terms], refs[terms:]
    first_ref, second_ref, weight_ref, natural_ref = refs[:4]
    new_first_ref, new_second_ref, block_ref = refs[4:]
    gradient = parts[0][: plan.block, :]
    for part in parts[1:]:
        gradient = gradient + part[: plan.block, :]
    tail, gradient = gradient[plan.own :, :], gradient[: plan.own, :]
    moment_one = beta_one * first_ref[...] + (1.0 - beta_one) * gradient
    moment_two = beta_two * second_ref[...] + (1.0 - beta_two) * gradient * gradient
    new_first_ref[...] = moment_one
    new_second_ref[...] = moment_two
    step = moment_one / bias_one / (jnp.sqrt(moment_two / bias_two) + epsilon)
    block_ref[: plan.own, :] = step
    weight = weight_ref[...]
    direction = step + decay_rate * weight
    natural = natural_ref[: plan.own, :]
    limits = (0,) + plan.bounds + (plan.blocks,)
    lane = lax.broadcasted_iota(jnp.int32, (8, LANE), 1)
    rank = lax.broadcasted_iota(jnp.int32, (8, LANE), 0)
    stats = jnp.zeros((8, LANE), jnp.float32)
    for column, squares in enumerate((weight * weight, direction * direction)):
        for k in range(matrices):
            inside = (natural >= limits[k]) & (natural < limits[k + 1])
            kept = jnp.where(inside, squares, 0.0).reshape(plan.own // 8, 8, LANE)
            total = jnp.sum(jnp.sum(kept, axis=0))
            stats = jnp.where((rank == plan.norm_each + k) & (lane == column), total, stats)
    block_ref[plan.own :, :] = tail + stats


def update(plan, parts, first, second, weight, natural):
    vmem = pl.BlockSpec(memory_space=pltpu.VMEM)
    shapes = [(plan.own, LANE), (plan.own, LANE), (plan.block, LANE)]
    return pl.pallas_call(
        functools.partial(update_kernel, plan, len(parts)),
        out_shape=[jax.ShapeDtypeStruct(s, jnp.float32) for s in shapes],
        in_specs=[vmem] * (len(parts) + 4),
        out_specs=[vmem] * len(shapes),
        compiler_params=pltpu.CompilerParams(vmem_limit_bytes=20 * MIB),
        name="moments",
    )(*parts, first, second, weight, natural)


def adam_rows(gradient, moment_one, moment_two, weight):
    moment_one = beta_one * moment_one + (1.0 - beta_one) * gradient
    moment_two = beta_two * moment_two + (1.0 - beta_two) * gradient * gradient
    step = moment_one / bias_one / (jnp.sqrt(moment_two / bias_two) + epsilon) + decay_rate * weight
    return (moment_one, moment_two, step)


def finish_kernel(plan, tile, slots, place_ref, position_ref, total_ref, norm_ref, weights_ref, *refs):
    pieces, refs = refs[: len(slots)], refs[len(slots) :]
    out_ref, new_norm_ref, trust_ref, held, norms, rates = refs
    now = pl.program_id(0)

    @pl.when(now == 0)
    def _():
        for piece, parts in zip(pieces, slots):
            for i, slot in enumerate(parts):
                held[pl.ds(plan.start(*slot), plan.block), :] = piece[i * plan.block : (i + 1) * plan.block, :]
        total = total_ref[...]
        for z in range(plan.nz):
            for x in range(plan.nx):
                for c in range(2):
                    start = plan.start(place_ref[0] ^ z, place_ref[1] ^ x, place_ref[2] ^ c) + plan.own
                    tail = held[pl.ds(pl.multiple_of(start, 8), plan.tail), :]
                    first = plan.index(z, x, c) * plan.norm_each
                    for row in range(first, min(first + plan.norm_each, plan.norm_rows)):
                        norms[row : row + 1, :] = tail[row - first : row - first + 1, :]
        for k in range(matrices):
            row = plan.norm_each + k
            weight_square, direction_square = total[row : row + 1, 0:1], total[row : row + 1, 1:2]
            ratio = jnp.sqrt(weight_square) / (jnp.sqrt(direction_square) + epsilon)
            rates[k : k + 1, :] = jnp.broadcast_to(learning * ratio, (1, LANE))
            trust_ref[k] = jnp.sum(ratio)
        each = plan.norm_rows // 2
        for i in range(2):
            gains, first, second = (
                jnp.concatenate([norm_ref[j, i : i + 1, row * LANE : (row + 1) * LANE] for row in range(each)], 0)
                for j in range(3)
            )
            one, two, step = adam_rows(norms[i * each : (i + 1) * each, :], first, second, gains)
            gain_square = jnp.sum(jnp.sum(gains * gains, axis=1, keepdims=True), axis=0, keepdims=True)
            step_square = jnp.sum(jnp.sum(step * step, axis=1, keepdims=True), axis=0, keepdims=True)
            ratio = jnp.sqrt(gain_square) / (jnp.sqrt(step_square) + epsilon)
            trust_ref[matrices + i] = jnp.sum(ratio)
            for j, value in enumerate((gains - learning * ratio * step, one, two)):
                for row in range(each):
                    new_norm_ref[j, i : i + 1, row * LANE : (row + 1) * LANE] = value[row : row + 1, :]

    lines = tile // LANE

    @pl.loop(0, lines)
    def _(line):
        matrix = jnp.int32(0)
        for bound in plan.bounds:
            matrix = matrix + (now * lines + line >= bound // LANE).astype(jnp.int32)
        rate = jnp.broadcast_to(rates[pl.ds(matrix, 1), :], (8, LANE))
        for group in range(0, LANE, 8):
            rows = [held[pl.ds(position_ref[now * lines + line, group + u], 1), :] for u in range(8)]
            here = pl.ds(pl.multiple_of(line * LANE + group, 8), 8)
            weight = weights_ref[here, :]
            direction = jnp.concatenate(rows, 0) + decay_rate * weight
            out_ref[here, :] = weight - rate * direction


def finish(plan, my_place, position, total, norm_state, weights, pieces, slots):
    assert all(bound % LANE == 0 for bound in plan.bounds + (plan.blocks,))
    tile = plan.blocks // next(n for n in (TILES, 4, 2, 1) if plan.blocks // LANE % n == 0)
    smem = pl.BlockSpec(memory_space=pltpu.SMEM)
    vmem = pl.BlockSpec(memory_space=pltpu.VMEM)
    return pl.pallas_call(
        functools.partial(finish_kernel, plan, tile, slots),
        grid=(plan.blocks // tile,),
        out_shape=[
            jax.ShapeDtypeStruct((plan.blocks, LANE), jnp.float32),
            jax.ShapeDtypeStruct(norm_state.shape, jnp.float32),
            jax.ShapeDtypeStruct((matrices + 2,), jnp.float32),
        ],
        in_specs=[smem, smem, vmem, vmem, pl.BlockSpec((tile, LANE), lambda i: (i, 0))]
        + [vmem] * len(pieces),
        out_specs=[pl.BlockSpec((tile, LANE), lambda i: (i, 0)), vmem, smem],
        scratch_shapes=[
            pltpu.VMEM((2 * plan.half, LANE), jnp.float32),
            pltpu.VMEM((plan.norm_rows, LANE), jnp.float32),
            pltpu.VMEM((8, LANE), jnp.float32),
        ],
        compiler_params=pltpu.CompilerParams(vmem_limit_bytes=20 * MIB),
        name="new_weights",
    )(my_place, position, total, norm_state, weights, *pieces)


def local(gradients, weights, first_moment, second_moment, owner_list, norm_grads, norm_state):
    plan = Plan(lax.axis_size("dp"), lax.axis_size("mp"), weights.shape[0])
    me = lax.axis_index("dp").astype(jnp.int32)
    my_place = jnp.stack([me // (2 * plan.nx), (me // 2) % plan.nx, me % 2]).astype(jnp.int32)
    owners = jnp.pad(owner_list[0], (0, plan.lists * LANE - plan.blocks), constant_values=-1)
    owners = owners.reshape(plan.lists, LANE)
    placed, position = place(plan, owners, norm_grads[0], gradients[0])
    weight_own, natural = owned(plan, my_place, owners, weights)

    mine, theirs = [None] * plan.nz, [None] * plan.nz
    for z in reversed(range(plan.nz)):
        both = [None] * plan.nx
        for x in reversed(range(plan.nx)):
            both[x] = placed[z, x, 0] + plan.swap(placed[z, x, 1])
            if (z, x) == (3, plan.nx - 1):
                later = [slot for slot in plan.order() if slot[2] and slot[:2] != (z, x)]
                both[x], *values = together(both[x], *(placed[slot] for slot in later))
                placed.update(zip(later, values))
        mine[z], theirs[z] = both[0], both[1:]
    if plan.nz == 4:
        parts = reduce(plan, mine, theirs, (weight_own, natural))
        parts, (weight_own, natural) = parts[:-2], parts[-2:]
    else:
        near = []
        for z in reversed(range(plan.nz)):
            terms = line_reduce(plan, "x", [mine[z]] + theirs[z])
            near.insert(0, sum(terms[1:], terms[0]) if z else None)
        parts = terms + line_reduce(plan, "z", near)[1:]
    new_first, new_second, block = update(
        plan, parts, first_moment[0], second_moment[0], weight_own, natural
    )

    found, total = gather(plan, my_place, block)
    pieces, slots = [piece for piece, _ in found], [parts for _, parts in found]
    new_weights, new_state, trust_ratios = finish(
        plan, my_place, position, total, norm_state, weights, pieces, slots
    )
    return (new_weights, new_first[None], new_second[None], new_state, trust_ratios)


def solution(mesh):
    in_specs = (
        P("dp", "mp", None),
        P("mp", None),
        P("mp", "dp", None),
        P("mp", "dp", None),
        P("mp", None),
        P("dp", None, None),
        P(),
    )
    out_specs = (P("mp", None), P("mp", "dp", None), P("mp", "dp", None), P(), P())
    return jax.shard_map(local, mesh=mesh, in_specs=in_specs, out_specs=out_specs, check_vma=False)
```

```python
import functools

import jax
import jax.numpy as jnp
from jax import lax
from jax.experimental import pallas as pl
from jax.experimental.pallas import tpu as pltpu
from jax.sharding import PartitionSpec as P

D = 1024
NTAB = 8
NKEYS = 256
KDIM = 128
LANE = 128
VROW_DEV = 512

beta_one = 0.9
beta_two = 0.99
bias_one = 1.0 - 0.9**4
bias_two = 1.0 - 0.99**4
epsilon = 1e-06
learning = 0.02
decay_rate = 0.01
matrices = 5
MIB = 1 << 20
TILES = 8
FETCHES = 4
EARLY = 0.7


def matrix_bounds(narrow):
    query_blocks = D * D // (LANE * narrow)
    key_blocks = NTAB * NKEYS * KDIM // (LANE * narrow)
    value_blocks = VROW_DEV * D // LANE
    return (
        query_blocks,
        query_blocks + key_blocks,
        query_blocks + key_blocks + value_blocks,
        2 * query_blocks + key_blocks + value_blocks,
    )


class Plan:
    def __init__(self, replicas, narrow, blocks):
        self.replicas, self.narrow, self.blocks = replicas, narrow, blocks
        chips = replicas // 2
        self.nz = 4 if chips % 4 == 0 else chips
        self.nx = chips // self.nz
        assert self.nz in (1, 2, 4) and self.nx in (1, 2, 4)
        self.own = blocks // replicas
        self.tail = 8
        self.norm_rows = 2 * D // LANE
        self.norm_each = -(-self.norm_rows // replicas)
        self.block = self.own + self.tail
        self.group = self.nx * self.block
        self.half = self.nz * self.group
        self.lists = -(-blocks // (8 * LANE)) * 8
        self.bounds = matrix_bounds(narrow)

    def index(self, z, x, c):
        return (z * self.nx + x) * 2 + c

    def start(self, far_z, far_x, far_c):
        return (1 - far_c) * self.half + far_z * self.group + far_x * self.block

    def order(self):
        zs, xs = range(self.nz - 1, -1, -1), range(self.nx - 1, -1, -1)
        return [(z, x, far_c) for far_c in (1, 0) for z in zs for x in xs]

    def send(self, value, axis, pairs):
        every = []
        for z in range(self.nz):
            for x in range(self.nx):
                for c in range(2):
                    here = {"z": z, "x": x, "c": c}
                    for source, target in pairs:
                        if here[axis] == source:
                            every.append((self.index(z, x, c), self.index(**{**here, axis: target})))
        return lax.ppermute(value, "dp", every)

    def swap(self, value):
        return self.send(value, "c", PAIR)


PAIR = [(0, 1), (1, 0)]
PAIRS = [(0, 1), (1, 0), (2, 3), (3, 2)]
MIDDLE = [(1, 2), (2, 1)]
INWARD = [(0, 1), (3, 2)]
OUTWARD = [(1, 0), (2, 3)]


def line_reduce(plan, axis, blocks):
    if len(blocks) == 1:
        return [blocks[0]]
    if len(blocks) == 2:
        return [blocks[0], plan.send(blocks[1], axis, PAIR)]
    in_three = plan.send(blocks[3], axis, INWARD)
    in_two = plan.send(blocks[2], axis, INWARD)
    across_two = plan.send(blocks[2] + in_three, axis, MIDDLE)
    across_three = plan.send(blocks[3] + in_two, axis, MIDDLE)
    pair = plan.send(blocks[1] + across_two, axis, PAIRS)
    return [blocks[0], pair, across_three]


def together(*values):
    return lax.optimization_barrier(values)


def reduce(plan, mine, theirs, beside):
    def along_x(z, own):
        terms = line_reduce(plan, "x", [own] + theirs[z])
        return terms

    three = along_x(3, mine[3])
    two = along_x(2, mine[2])
    near_three = sum(three[1:], three[0])
    in_three = plan.send(near_three, "z", INWARD)
    in_three, near_two, *beside = together(in_three, sum(two[1:], two[0]), *beside)
    one = along_x(1, mine[1])
    across_two = plan.send(near_two + in_three, "z", MIDDLE)
    in_two = plan.send(near_two, "z", INWARD)
    across_two, onward, near_one = together(across_two, near_three + in_two, sum(one[1:], one[0]))
    zero = along_x(0, mine[0])
    pair = plan.send(near_one + across_two, "z", PAIRS)
    across_three = plan.send(onward, "z", MIDDLE)
    return zero + [pair, across_three] + beside


def sums_kernel(plan, place_ref, *refs):
    tails, (out_ref, held) = refs[: plan.nz], refs[plan.nz :]
    for far_z, tail in enumerate(tails):
        held[place_ref[0] ^ far_z] = tail[...]
    total = held[0]
    for z in range(1, plan.nz):
        total = total + held[z]
    out_ref[...] = total


def all_sums(plan, my_place, blocks):
    def tail_of(row):
        return pl.BlockSpec((plan.tail, LANE), lambda i: ((row + plan.own) // plan.tail, 0))

    specs = [tail_of(row) for _, row in blocks]
    total = pl.pallas_call(
        functools.partial(sums_kernel, plan),
        grid=(1,),
        out_shape=jax.ShapeDtypeStruct((plan.tail, LANE), jnp.float32),
        in_specs=[pl.BlockSpec(memory_space=pltpu.SMEM)] + specs,
        out_specs=pl.BlockSpec(memory_space=pltpu.VMEM),
        scratch_shapes=[pltpu.VMEM((plan.nz, plan.tail, LANE), jnp.float32)],
        compiler_params=pltpu.CompilerParams(vmem_limit_bytes=4 * MIB),
        name="sums",
    )(my_place, *(value for value, _ in blocks))
    hop = 1
    while hop < plan.nx:
        total = total + plan.send(total, "x", [(i, i ^ hop) for i in range(plan.nx)])
        hop *= 2
    return total


def all_cores(plan, total):
    total = total + plan.swap(total)
    hop = 1
    while hop < plan.narrow:
        total = total + lax.ppermute(total, "mp", [(i, i ^ hop) for i in range(plan.narrow)])
        hop *= 2
    return total


def gather(plan, my_place, block):
    def along_x(value):
        return line_gather(plan, "x", plan.nx, value)

    if plan.nz != 4:
        ready = {}
        lines = [along_x(value) for value in line_gather(plan, "z", plan.nz, block)]
        total = all_cores(plan, all_sums(plan, my_place, [(line[0], 0) for line in lines]))
        mine = [(value, [(z, x)]) for z, line in enumerate(lines) for x, value in enumerate(line)]
    else:
        line = along_x(block)
        pair = plan.send(block, "z", PAIRS)
        three = plan.send(block, "z", MIDDLE)
        three, own, *line = together(three, jnp.concatenate([block, pair]), *line)
        line_pair = along_x(pair)
        two = plan.send(pair, "z", MIDDLE)
        out_two = plan.send(three, "z", OUTWARD)
        _, *line_pair = together(two, *line_pair)
        far = [jnp.concatenate([line[x], line_pair[x]]) for x in range(1, plan.nx)]
        near_two, *far = together(two + out_two, *far)
        line_two = along_x(near_two)
        out_three = plan.send(two, "z", OUTWARD)
        near_three = three + out_three
        line_three = along_x(near_three)
        total = all_sums(plan, my_place, [(own, 0), (own, plan.block), (near_two, 0), (near_three, 0)])
        total, *line_two = together(total, *line_two)
        early = plan.swap(near_three)
        early, total, *line_three = together(early, all_cores(plan, total), *line_three)
        ready = {(3, 0): early}
        mine = [(value, [(0, x), (1, x)]) for x, value in enumerate([own] + far)]
        mine += [(value, [(2, x)]) for x, value in enumerate(line_two)]
        mine += [(value, [(3, x)]) for x, value in enumerate(line_three)]
    swapped = [ready[slots[0]] if slots[0] in ready else plan.swap(value) for value, slots in mine]
    found = [(value, [slot + (0,) for slot in slots]) for value, slots in mine]
    found += [(value, [slot + (1,) for slot in slots]) for value, (_, slots) in zip(swapped, mine)]
    return found, total


def line_gather(plan, axis, count, value):
    if count == 1:
        return [value]
    if count == 2:
        return [value, plan.send(value, axis, PAIR)]
    pair = plan.send(value, axis, PAIRS)
    across_three = plan.send(value, axis, MIDDLE)
    across_two = plan.send(pair, axis, MIDDLE)
    out_two = plan.send(across_three, axis, OUTWARD)
    out_three = plan.send(across_two, axis, OUTWARD)
    return [value, pair, across_two + out_two, across_three + out_three]


def place_kernel(plan, owner_ref, norm_ref, grads_ref, *refs):
    out_refs, refs = refs[: plan.replicas], refs[plan.replicas :]
    position_ref, raw, moved, position, sem_in, sem_position, sem_out = refs
    lines = plan.blocks // LANE
    ends = [lines * (i + 1) // FETCHES for i in range(FETCHES)]
    fetches = []
    for i, end in enumerate(ends):
        low = ends[i - 1] * LANE if i else 0
        rows = pl.ds(low, end * LANE - low)
        fetches.append(pltpu.make_async_copy(grads_ref.at[rows], raw.at[rows], sem_in.at[i]))
        fetches[-1].start()
    lists = plan.lists
    owners = owner_ref[...]
    me = lax.axis_index("dp").astype(jnp.int32)
    my_z, my_x, my_c = me // (2 * plan.nx), me // 2 % plan.nx, me % 2
    count = plan.replicas
    lane_in = lax.broadcasted_iota(jnp.int32, (LANE, LANE), 0)
    lane_out = lax.broadcasted_iota(jnp.int32, (LANE, LANE), 1)
    before = (lane_in < lane_out).astype(jnp.float32).astype(jnp.bfloat16)
    row_out = lax.broadcasted_iota(jnp.int32, (lists, lists), 0)
    row_in = lax.broadcasted_iota(jnp.int32, (lists, lists), 1)
    above = (row_in < row_out).astype(jnp.float32).astype(jnp.bfloat16)
    flags = [(owners == d).astype(jnp.float32).astype(jnp.bfloat16) for d in range(count)]
    inner = jnp.dot(jnp.concatenate(flags, 0), before, preferred_element_type=jnp.float32)
    owner_in = lax.broadcasted_iota(jnp.int32, (count * LANE, LANE), 0)
    owner_out = lax.broadcasted_iota(jnp.int32, (count * LANE, LANE), 1)
    pick = (owner_in // LANE == owner_out).astype(jnp.float32).astype(jnp.bfloat16)
    totals = jnp.dot(jnp.concatenate(flags, 1), pick, preferred_element_type=jnp.float32)
    outer = jnp.dot(above, totals.astype(jnp.bfloat16), preferred_element_type=jnp.float32)
    ranks = jnp.full((lists, LANE), plan.own, jnp.int32)
    result = jnp.zeros((lists, LANE), jnp.int32)
    for z in range(plan.nz):
        for x in range(plan.nx):
            for c in range(2):
                d = plan.index(z, x, c)
                mine = owners == d
                rank = (inner[d * lists : (d + 1) * lists, :] + outer[:, d : d + 1]).astype(jnp.int32)
                start = plan.start(my_z ^ z, my_x ^ x, my_c ^ c)
                first_norm = d * plan.norm_each
                tail = [jnp.zeros((plan.tail, LANE), jnp.float32)]
                for row in range(min(first_norm + plan.norm_each, plan.norm_rows) - 1, first_norm - 1, -1):
                    part = norm_ref[row * LANE // D : row * LANE // D + 1, row * LANE % D : row * LANE % D + LANE]
                    tail.insert(0, part.astype(jnp.float32))
                tail = jnp.concatenate(tail, 0)[: plan.tail]
                moved[pl.ds(pl.multiple_of(start + plan.own, 8), plan.tail), :] = tail
                result = jnp.where(mine, rank + start, result)
                ranks = jnp.where(mine, rank, ranks)
    position_ref[...] = result
    to_scalar = pltpu.make_async_copy(position_ref, position, sem_position)
    to_scalar.start()
    to_scalar.wait()

    def copies(part, low, high):
        found = []
        for i, (out, slot) in enumerate(zip(out_refs, plan.order())):
            source = moved.at[pl.ds(plan.start(*slot) + low, high - low)]
            found.append(pltpu.make_async_copy(source, out.at[pl.ds(low, high - low)], sem_out.at[part, i]))
        return found

    cut = int(plan.own * EARLY / 8) * 8
    line_of = lax.broadcasted_iota(jnp.int32, (lists, LANE), 0)
    complete = jnp.max(jnp.where(ranks < cut, line_of + 1, 0))
    early = copies(0, 0, cut)
    late = copies(1, cut, plan.block)

    for i, end in enumerate(ends):
        fetches[i].wait()

        @pl.loop(ends[i - 1] if i else 0, end)
        def _(line):
            for part in range(0, LANE, 16):
                rows = raw[pl.ds(pl.multiple_of(line * LANE + part, 16), 16), :].astype(jnp.float32)
                for u in range(16):
                    moved[pl.ds(position[line, part + u], 1), :] = rows[u : u + 1, :]

        if i == FETCHES - 2:

            @pl.when(complete <= end)
            def _():
                for copy in early:
                    copy.start()

    @pl.when(complete > ends[FETCHES - 2])
    def _():
        for copy in early:
            copy.start()

    for copy in late:
        copy.start()
    for copy in early + late:
        copy.wait()


def place(plan, owners, norm_grads, grads):
    shapes = [(plan.block, LANE)] * plan.replicas
    outs = pl.pallas_call(
        functools.partial(place_kernel, plan),
        out_shape=[jax.ShapeDtypeStruct(s, jnp.float32) for s in shapes]
        + [jax.ShapeDtypeStruct((plan.lists, LANE), jnp.int32)],
        in_specs=[
            pl.BlockSpec(memory_space=pltpu.VMEM),
            pl.BlockSpec(memory_space=pltpu.VMEM),
            pl.BlockSpec(memory_space=pl.ANY),
        ],
        out_specs=[pl.BlockSpec(memory_space=pl.ANY)] * len(shapes) + [pl.BlockSpec(memory_space=pltpu.VMEM)],
        scratch_shapes=[
            pltpu.VMEM((plan.blocks, LANE), jnp.bfloat16),
            pltpu.VMEM((2 * plan.half, LANE), jnp.float32),
            pltpu.SMEM((plan.lists, LANE), jnp.int32),
            pltpu.SemaphoreType.DMA((FETCHES,)),
            pltpu.SemaphoreType.DMA,
            pltpu.SemaphoreType.DMA((2, len(shapes))),
        ],
        compiler_params=pltpu.CompilerParams(vmem_limit_bytes=58 * MIB),
        name="place_gradients",
    )(owners, norm_grads, grads)
    return dict(zip(plan.order(), outs)), outs[-1]


def owned_kernel(plan, place_ref, owner_ref, weights_ref, owned_ref, natural_ref, held, listed, order, sem_in, sem_order):
    fetch = pltpu.make_async_copy(weights_ref, held, sem_in)
    fetch.start()
    lists = plan.lists
    me = plan.index(place_ref[0], place_ref[1], place_ref[2])
    flags = (owner_ref[...] == me).astype(jnp.float32).astype(jnp.bfloat16)
    lane_in = lax.broadcasted_iota(jnp.int32, (LANE, LANE), 0)
    lane_out = lax.broadcasted_iota(jnp.int32, (LANE, LANE), 1)
    upto = (lane_in <= lane_out).astype(jnp.float32).astype(jnp.bfloat16)
    inner = jnp.dot(flags, upto, preferred_element_type=jnp.float32).astype(jnp.bfloat16)
    totals = lax.dot_general(
        jnp.ones((8, LANE), jnp.bfloat16), flags, (((1,), (1,)), ((), ())), preferred_element_type=jnp.float32
    )
    row_in = lax.broadcasted_iota(jnp.int32, (lists, lists), 0)
    row_out = lax.broadcasted_iota(jnp.int32, (lists, lists), 1)
    upto = (row_in <= row_out).astype(jnp.float32).astype(jnp.bfloat16)
    ends = jnp.dot(totals.astype(jnp.bfloat16), upto, preferred_element_type=jnp.float32)[0:1, :]
    place_of = lax.broadcasted_iota(jnp.int32, (LANE, lists), 1).astype(jnp.float32)
    rank_of = lax.broadcasted_iota(jnp.int32, (LANE, 1), 0)
    for step in range(listed.shape[0]):
        if step * LANE >= plan.own:
            break
        rank = (rank_of + step * LANE).astype(jnp.float32)
        passed = ends <= rank
        line = jnp.sum(passed.astype(jnp.float32), axis=1, keepdims=True)
        before = jnp.max(jnp.where(passed, ends, 0.0), axis=1, keepdims=True)
        chosen = (place_of == line).astype(jnp.float32).astype(jnp.bfloat16)
        counts = jnp.dot(chosen, inner, preferred_element_type=jnp.float32)
        column = jnp.sum((counts <= rank - before).astype(jnp.float32), axis=1, keepdims=True)
        block = jnp.broadcast_to((line * LANE + column).astype(jnp.int32), (LANE, LANE))
        natural_ref[step * LANE : (step + 1) * LANE, :] = block
        listed[step : step + 1, :] = jnp.sum(jnp.where(lane_in == lane_out, block, 0), axis=0, keepdims=True)
    to_scalar = pltpu.make_async_copy(listed, order, sem_order)
    to_scalar.start()
    to_scalar.wait()
    fetch.wait()

    def pick(line, count):
        for u in range(count):
            owned_ref[pl.ds(line * LANE + u, 1), :] = held[pl.ds(order[line, u], 1), :]

    @pl.loop(0, plan.own // LANE)
    def _(line):
        pick(line, LANE)

    if plan.own % LANE:
        pick(plan.own // LANE, plan.own % LANE)


def owned(plan, my_place, owners, weights):
    high_rows = -(-plan.own // (8 * LANE)) * 8
    ranks = -(-plan.own // LANE) * LANE
    vmem = pl.BlockSpec(memory_space=pltpu.VMEM)
    return pl.pallas_call(
        functools.partial(owned_kernel, plan),
        out_shape=[
            jax.ShapeDtypeStruct((plan.own, LANE), jnp.float32),
            jax.ShapeDtypeStruct((ranks, LANE), jnp.int32),
        ],
        in_specs=[pl.BlockSpec(memory_space=pltpu.SMEM), vmem, pl.BlockSpec(memory_space=pl.ANY)],
        out_specs=[vmem] * 2,
        scratch_shapes=[
            pltpu.VMEM((plan.blocks, LANE), jnp.float32),
            pltpu.VMEM((high_rows, LANE), jnp.int32),
            pltpu.SMEM((high_rows, LANE), jnp.int32),
            pltpu.SemaphoreType.DMA,
            pltpu.SemaphoreType.DMA,
        ],
        compiler_params=pltpu.CompilerParams(vmem_limit_bytes=58 * MIB),
        cost_estimate=pl.CostEstimate(flops=0, bytes_accessed=20 * MIB, transcendentals=0),
        name="owned_weights",
    )(my_place, owners, weights)


def update_kernel(plan, terms, *refs):
    parts, refs = refs[:terms], refs[terms:]
    first_ref, second_ref, weight_ref, natural_ref = refs[:4]
    new_first_ref, new_second_ref, block_ref = refs[4:]
    gradient = parts[0][: plan.block, :]
    for part in parts[1:]:
        gradient = gradient + part[: plan.block, :]
    tail, gradient = gradient[plan.own :, :], gradient[: plan.own, :]
    moment_one = beta_one * first_ref[...] + (1.0 - beta_one) * gradient
    moment_two = beta_two * second_ref[...] + (1.0 - beta_two) * gradient * gradient
    new_first_ref[...] = moment_one
    new_second_ref[...] = moment_two
    step = moment_one / bias_one / (jnp.sqrt(moment_two / bias_two) + epsilon)
    block_ref[: plan.own, :] = step
    weight = weight_ref[...]
    direction = step + decay_rate * weight
    natural = natural_ref[: plan.own, :]
    limits = (0,) + plan.bounds + (plan.blocks,)
    lane = lax.broadcasted_iota(jnp.int32, (8, LANE), 1)
    rank = lax.broadcasted_iota(jnp.int32, (8, LANE), 0)
    stats = jnp.zeros((8, LANE), jnp.float32)
    for column, squares in enumerate((weight * weight, direction * direction)):
        for k in range(matrices):
            inside = (natural >= limits[k]) & (natural < limits[k + 1])
            kept = jnp.where(inside, squares, 0.0).reshape(plan.own // 8, 8, LANE)
            total = jnp.sum(jnp.sum(kept, axis=0))
            stats = jnp.where((rank == plan.norm_each + k) & (lane == column), total, stats)
    block_ref[plan.own :, :] = tail + stats


def update(plan, parts, first, second, weight, natural):
    vmem = pl.BlockSpec(memory_space=pltpu.VMEM)
    shapes = [(plan.own, LANE), (plan.own, LANE), (plan.block, LANE)]
    return pl.pallas_call(
        functools.partial(update_kernel, plan, len(parts)),
        out_shape=[jax.ShapeDtypeStruct(s, jnp.float32) for s in shapes],
        in_specs=[vmem] * (len(parts) + 4),
        out_specs=[vmem] * len(shapes),
        compiler_params=pltpu.CompilerParams(vmem_limit_bytes=20 * MIB),
        name="moments",
    )(*parts, first, second, weight, natural)


def adam_rows(gradient, moment_one, moment_two, weight):
    moment_one = beta_one * moment_one + (1.0 - beta_one) * gradient
    moment_two = beta_two * moment_two + (1.0 - beta_two) * gradient * gradient
    step = moment_one / bias_one / (jnp.sqrt(moment_two / bias_two) + epsilon) + decay_rate * weight
    return (moment_one, moment_two, step)


def finish_kernel(plan, tile, slots, place_ref, position_ref, total_ref, norm_ref, weights_ref, *refs):
    pieces, refs = refs[: len(slots)], refs[len(slots) :]
    out_ref, new_norm_ref, trust_ref, held, norms, rates = refs
    now = pl.program_id(0)

    @pl.when(now == 0)
    def _():
        for piece, parts in zip(pieces, slots):
            for i, slot in enumerate(parts):
                held[pl.ds(plan.start(*slot), plan.block), :] = piece[i * plan.block : (i + 1) * plan.block, :]
        total = total_ref[...]
        for z in range(plan.nz):
            for x in range(plan.nx):
                for c in range(2):
                    start = plan.start(place_ref[0] ^ z, place_ref[1] ^ x, place_ref[2] ^ c) + plan.own
                    tail = held[pl.ds(pl.multiple_of(start, 8), plan.tail), :]
                    first = plan.index(z, x, c) * plan.norm_each
                    for row in range(first, min(first + plan.norm_each, plan.norm_rows)):
                        norms[row : row + 1, :] = tail[row - first : row - first + 1, :]
        for k in range(matrices):
            row = plan.norm_each + k
            weight_square, direction_square = total[row : row + 1, 0:1], total[row : row + 1, 1:2]
            ratio = jnp.sqrt(weight_square) / (jnp.sqrt(direction_square) + epsilon)
            rates[k : k + 1, :] = jnp.broadcast_to(learning * ratio, (1, LANE))
            trust_ref[k] = jnp.sum(ratio)
        each = plan.norm_rows // 2
        for i in range(2):
            gains, first, second = (
                jnp.concatenate([norm_ref[j, i : i + 1, row * LANE : (row + 1) * LANE] for row in range(each)], 0)
                for j in range(3)
            )
            one, two, step = adam_rows(norms[i * each : (i + 1) * each, :], first, second, gains)
            gain_square = jnp.sum(jnp.sum(gains * gains, axis=1, keepdims=True), axis=0, keepdims=True)
            step_square = jnp.sum(jnp.sum(step * step, axis=1, keepdims=True), axis=0, keepdims=True)
            ratio = jnp.sqrt(gain_square) / (jnp.sqrt(step_square) + epsilon)
            trust_ref[matrices + i] = jnp.sum(ratio)
            for j, value in enumerate((gains - learning * ratio * step, one, two)):
                for row in range(each):
                    new_norm_ref[j, i : i + 1, row * LANE : (row + 1) * LANE] = value[row : row + 1, :]

    lines = tile // LANE

    @pl.loop(0, lines)
    def _(line):
        matrix = jnp.int32(0)
        for bound in plan.bounds:
            matrix = matrix + (now * lines + line >= bound // LANE).astype(jnp.int32)
        rate = jnp.broadcast_to(rates[pl.ds(matrix, 1), :], (8, LANE))
        for group in range(0, LANE, 8):
            rows = [held[pl.ds(position_ref[now * lines + line, group + u], 1), :] for u in range(8)]
            here = pl.ds(pl.multiple_of(line * LANE + group, 8), 8)
            weight = weights_ref[pl.ds(pl.multiple_of((now * lines + line) * LANE + group, 8), 8), :]
            direction = jnp.concatenate(rows, 0) + decay_rate * weight
            out_ref[here, :] = weight - rate * direction


def finish(plan, my_place, position, total, norm_state, weights, pieces, slots):
    assert all(bound % LANE == 0 for bound in plan.bounds + (plan.blocks,))
    tile = plan.blocks // next(n for n in (TILES, 4, 2, 1) if plan.blocks // LANE % n == 0)
    smem = pl.BlockSpec(memory_space=pltpu.SMEM)
    vmem = pl.BlockSpec(memory_space=pltpu.VMEM)
    return pl.pallas_call(
        functools.partial(finish_kernel, plan, tile, slots),
        grid=(plan.blocks // tile,),
        out_shape=[
            jax.ShapeDtypeStruct((plan.blocks, LANE), jnp.float32),
            jax.ShapeDtypeStruct(norm_state.shape, jnp.float32),
            jax.ShapeDtypeStruct((matrices + 2,), jnp.float32),
        ],
        in_specs=[smem, smem, vmem, vmem, vmem]
        + [vmem] * len(pieces),
        out_specs=[pl.BlockSpec((tile, LANE), lambda i: (i, 0)), vmem, smem],
        scratch_shapes=[
            pltpu.VMEM((2 * plan.half, LANE), jnp.float32),
            pltpu.VMEM((plan.norm_rows, LANE), jnp.float32),
            pltpu.VMEM((8, LANE), jnp.float32),
        ],
        compiler_params=pltpu.CompilerParams(vmem_limit_bytes=20 * MIB),
        name="new_weights",
    )(my_place, position, total, norm_state, weights, *pieces)


def local(gradients, weights, first_moment, second_moment, owner_list, norm_grads, norm_state):
    plan = Plan(lax.axis_size("dp"), lax.axis_size("mp"), weights.shape[0])
    me = lax.axis_index("dp").astype(jnp.int32)
    my_place = jnp.stack([me // (2 * plan.nx), (me // 2) % plan.nx, me % 2]).astype(jnp.int32)
    owners = jnp.pad(owner_list[0], (0, plan.lists * LANE - plan.blocks), constant_values=-1)
    owners = owners.reshape(plan.lists, LANE)
    placed, position = place(plan, owners, norm_grads[0], gradients[0])
    weight_own, natural = owned(plan, my_place, owners, weights)

    mine, theirs = [None] * plan.nz, [None] * plan.nz
    for z in reversed(range(plan.nz)):
        both = [None] * plan.nx
        for x in reversed(range(plan.nx)):
            both[x] = placed[z, x, 0] + plan.swap(placed[z, x, 1])
            if (z, x) == (3, plan.nx - 1):
                later = [slot for slot in plan.order() if slot[2] and slot[:2] != (z, x)]
                both[x], *values = together(both[x], *(placed[slot] for slot in later))
                placed.update(zip(later, values))
        mine[z], theirs[z] = both[0], both[1:]
    if plan.nz == 4:
        parts = reduce(plan, mine, theirs, (weight_own, natural))
        parts, (weight_own, natural) = parts[:-2], parts[-2:]
    else:
        near = []
        for z in reversed(range(plan.nz)):
            terms = line_reduce(plan, "x", [mine[z]] + theirs[z])
            near.insert(0, sum(terms[1:], terms[0]) if z else None)
        parts = terms + line_reduce(plan, "z", near)[1:]
    new_first, new_second, block = update(
        plan, parts, first_moment[0], second_moment[0], weight_own, natural
    )

    found, total = gather(plan, my_place, block)
    pieces, slots = [piece for piece, _ in found], [parts for _, parts in found]
    new_weights, new_state, trust_ratios = finish(
        plan, my_place, position, total, norm_state, weights, pieces, slots
    )
    return (new_weights, new_first[None], new_second[None], new_state, trust_ratios)


def solution(mesh):
    in_specs = (
        P("dp", "mp", None),
        P("mp", None),
        P("mp", "dp", None),
        P("mp", "dp", None),
        P("mp", None),
        P("dp", None, None),
        P(),
    )
    out_specs = (P("mp", None), P("mp", "dp", None), P("mp", "dp", None), P(), P())
    return jax.shard_map(local, mesh=mesh, in_specs=in_specs, out_specs=out_specs, check_vma=False)
```

```python
import functools

import jax
import jax.numpy as jnp
from jax import lax
from jax.experimental import pallas as pl
from jax.experimental.pallas import tpu as pltpu
from jax.sharding import PartitionSpec as P

D = 1024
NTAB = 8
NKEYS = 256
KDIM = 128
LANE = 128
VROW_DEV = 512

beta_one = 0.9
beta_two = 0.99
bias_one = 1.0 - 0.9**4
bias_two = 1.0 - 0.99**4
epsilon = 1e-06
learning = 0.02
decay_rate = 0.01
matrices = 5
MIB = 1 << 20
TILES = 8
FETCHES = 4
EARLY = 0.7


def matrix_bounds(narrow):
    query_blocks = D * D // (LANE * narrow)
    key_blocks = NTAB * NKEYS * KDIM // (LANE * narrow)
    value_blocks = VROW_DEV * D // LANE
    return (
        query_blocks,
        query_blocks + key_blocks,
        query_blocks + key_blocks + value_blocks,
        2 * query_blocks + key_blocks + value_blocks,
    )


class Plan:
    def __init__(self, replicas, narrow, blocks):
        self.replicas, self.narrow, self.blocks = replicas, narrow, blocks
        chips = replicas // 2
        self.nz = 4 if chips % 4 == 0 else chips
        self.nx = chips // self.nz
        assert self.nz in (1, 2, 4) and self.nx in (1, 2, 4)
        self.own = blocks // replicas
        self.tail = 8
        self.norm_rows = 2 * D // LANE
        self.norm_each = -(-self.norm_rows // replicas)
        self.block = self.own + self.tail
        self.group = self.nx * self.block
        self.half = self.nz * self.group
        self.lists = -(-blocks // (8 * LANE)) * 8
        self.bounds = matrix_bounds(narrow)

    def index(self, z, x, c):
        return (z * self.nx + x) * 2 + c

    def start(self, far_z, far_x, far_c):
        return (1 - far_c) * self.half + far_z * self.group + far_x * self.block

    def order(self):
        zs, xs = range(self.nz - 1, -1, -1), range(self.nx - 1, -1, -1)
        return [(z, x, far_c) for far_c in (1, 0) for z in zs for x in xs]

    def send(self, value, axis, pairs):
        every = []
        for z in range(self.nz):
            for x in range(self.nx):
                for c in range(2):
                    here = {"z": z, "x": x, "c": c}
                    for source, target in pairs:
                        if here[axis] == source:
                            every.append((self.index(z, x, c), self.index(**{**here, axis: target})))
        return lax.ppermute(value, "dp", every)

    def swap(self, value):
        return self.send(value, "c", PAIR)


PAIR = [(0, 1), (1, 0)]
PAIRS = [(0, 1), (1, 0), (2, 3), (3, 2)]
MIDDLE = [(1, 2), (2, 1)]
INWARD = [(0, 1), (3, 2)]
OUTWARD = [(1, 0), (2, 3)]


def line_reduce(plan, axis, blocks):
    if len(blocks) == 1:
        return [blocks[0]]
    if len(blocks) == 2:
        return [blocks[0], plan.send(blocks[1], axis, PAIR)]
    in_three = plan.send(blocks[3], axis, INWARD)
    in_two = plan.send(blocks[2], axis, INWARD)
    across_two = plan.send(blocks[2] + in_three, axis, MIDDLE)
    across_three = plan.send(blocks[3] + in_two, axis, MIDDLE)
    pair = plan.send(blocks[1] + across_two, axis, PAIRS)
    return [blocks[0], pair, across_three]


def together(*values):
    return lax.optimization_barrier(values)


def reduce(plan, mine, theirs, beside):
    def along_x(z, own):
        terms = line_reduce(plan, "x", [own] + theirs[z])
        return terms

    three = along_x(3, mine[3])
    two = along_x(2, mine[2])
    near_three = sum(three[1:], three[0])
    in_three = plan.send(near_three, "z", INWARD)
    in_three, near_two, *beside = together(in_three, sum(two[1:], two[0]), *beside)
    one = along_x(1, mine[1])
    across_two = plan.send(near_two + in_three, "z", MIDDLE)
    in_two = plan.send(near_two, "z", INWARD)
    across_two, onward, near_one = together(across_two, near_three + in_two, sum(one[1:], one[0]))
    zero = along_x(0, mine[0])
    pair = plan.send(near_one + across_two, "z", PAIRS)
    across_three = plan.send(onward, "z", MIDDLE)
    return zero + [pair, across_three] + beside


def sums_kernel(plan, place_ref, *refs):
    tails, (out_ref, held) = refs[: plan.nz], refs[plan.nz :]
    for far_z, tail in enumerate(tails):
        held[place_ref[0] ^ far_z] = tail[...]
    total = held[0]
    for z in range(1, plan.nz):
        total = total + held[z]
    out_ref[...] = total


def all_sums(plan, my_place, blocks):
    def tail_of(row):
        return pl.BlockSpec((plan.tail, LANE), lambda i: ((row + plan.own) // plan.tail, 0))

    specs = [tail_of(row) for _, row in blocks]
    total = pl.pallas_call(
        functools.partial(sums_kernel, plan),
        grid=(1,),
        out_shape=jax.ShapeDtypeStruct((plan.tail, LANE), jnp.float32),
        in_specs=[pl.BlockSpec(memory_space=pltpu.SMEM)] + specs,
        out_specs=pl.BlockSpec(memory_space=pltpu.VMEM),
        scratch_shapes=[pltpu.VMEM((plan.nz, plan.tail, LANE), jnp.float32)],
        compiler_params=pltpu.CompilerParams(vmem_limit_bytes=4 * MIB),
        name="sums",
    )(my_place, *(value for value, _ in blocks))
    hop = 1
    while hop < plan.nx:
        total = total + plan.send(total, "x", [(i, i ^ hop) for i in range(plan.nx)])
        hop *= 2
    return total


def all_cores(plan, total):
    total = total + plan.swap(total)
    hop = 1
    while hop < plan.narrow:
        total = total + lax.ppermute(total, "mp", [(i, i ^ hop) for i in range(plan.narrow)])
        hop *= 2
    return total


def gather(plan, my_place, block):
    def along_x(value):
        return line_gather(plan, "x", plan.nx, value)

    if plan.nz != 4:
        ready = {}
        lines = [along_x(value) for value in line_gather(plan, "z", plan.nz, block)]
        total = all_cores(plan, all_sums(plan, my_place, [(line[0], 0) for line in lines]))
        mine = [(value, [(z, x)]) for z, line in enumerate(lines) for x, value in enumerate(line)]
    else:
        line = along_x(block)
        pair = plan.send(block, "z", PAIRS)
        three = plan.send(block, "z", MIDDLE)
        three, own, *line = together(three, jnp.concatenate([block, pair]), *line)
        line_pair = along_x(pair)
        two = plan.send(pair, "z", MIDDLE)
        out_two = plan.send(three, "z", OUTWARD)
        _, *line_pair = together(two, *line_pair)
        far = [jnp.concatenate([line[x], line_pair[x]]) for x in range(1, plan.nx)]
        near_two, *far = together(two + out_two, *far)
        line_two = along_x(near_two)
        out_three = plan.send(two, "z", OUTWARD)
        near_three = three + out_three
        line_three = along_x(near_three)
        total = all_sums(plan, my_place, [(own, 0), (own, plan.block), (near_two, 0), (near_three, 0)])
        total, *line_two = together(total, *line_two)
        early = plan.swap(near_three)
        early, total, *line_three = together(early, all_cores(plan, total), *line_three)
        ready = {(3, 0): early}
        mine = [(value, [(0, x), (1, x)]) for x, value in enumerate([own] + far)]
        mine.append((jnp.concatenate(line_two), [(2, x) for x in range(plan.nx)]))
        mine += [(value, [(3, x)]) for x, value in enumerate(line_three)]
    swapped = [ready[slots[0]] if slots[0] in ready else plan.swap(value) for value, slots in mine]
    found = [(value, [slot + (0,) for slot in slots]) for value, slots in mine]
    found += [(value, [slot + (1,) for slot in slots]) for value, (_, slots) in zip(swapped, mine)]
    return found, total


def line_gather(plan, axis, count, value):
    if count == 1:
        return [value]
    if count == 2:
        return [value, plan.send(value, axis, PAIR)]
    pair = plan.send(value, axis, PAIRS)
    across_three = plan.send(value, axis, MIDDLE)
    across_two = plan.send(pair, axis, MIDDLE)
    out_two = plan.send(across_three, axis, OUTWARD)
    out_three = plan.send(across_two, axis, OUTWARD)
    return [value, pair, across_two + out_two, across_three + out_three]


def place_kernel(plan, owner_ref, norm_ref, grads_ref, *refs):
    out_refs, refs = refs[: plan.replicas], refs[plan.replicas :]
    position_ref, raw, moved, position, sem_in, sem_position, sem_out = refs
    lines = plan.blocks // LANE
    ends = [lines * (i + 1) // FETCHES for i in range(FETCHES)]
    fetches = []
    for i, end in enumerate(ends):
        low = ends[i - 1] * LANE if i else 0
        rows = pl.ds(low, end * LANE - low)
        fetches.append(pltpu.make_async_copy(grads_ref.at[rows], raw.at[rows], sem_in.at[i]))
        fetches[-1].start()
    lists = plan.lists
    owners = owner_ref[...]
    me = lax.axis_index("dp").astype(jnp.int32)
    my_z, my_x, my_c = me // (2 * plan.nx), me // 2 % plan.nx, me % 2
    count = plan.replicas
    lane_in = lax.broadcasted_iota(jnp.int32, (LANE, LANE), 0)
    lane_out = lax.broadcasted_iota(jnp.int32, (LANE, LANE), 1)
    before = (lane_in < lane_out).astype(jnp.float32).astype(jnp.bfloat16)
    row_out = lax.broadcasted_iota(jnp.int32, (lists, lists), 0)
    row_in = lax.broadcasted_iota(jnp.int32, (lists, lists), 1)
    above = (row_in < row_out).astype(jnp.float32).astype(jnp.bfloat16)
    flags = [(owners == d).astype(jnp.float32).astype(jnp.bfloat16) for d in range(count)]
    inner = jnp.dot(jnp.concatenate(flags, 0), before, preferred_element_type=jnp.float32)
    owner_in = lax.broadcasted_iota(jnp.int32, (count * LANE, LANE), 0)
    owner_out = lax.broadcasted_iota(jnp.int32, (count * LANE, LANE), 1)
    pick = (owner_in // LANE == owner_out).astype(jnp.float32).astype(jnp.bfloat16)
    totals = jnp.dot(jnp.concatenate(flags, 1), pick, preferred_element_type=jnp.float32)
    outer = jnp.dot(above, totals.astype(jnp.bfloat16), preferred_element_type=jnp.float32)
    ranks = jnp.full((lists, LANE), plan.own, jnp.int32)
    result = jnp.zeros((lists, LANE), jnp.int32)
    for z in range(plan.nz):
        for x in range(plan.nx):
            for c in range(2):
                d = plan.index(z, x, c)
                mine = owners == d
                rank = (inner[d * lists : (d + 1) * lists, :] + outer[:, d : d + 1]).astype(jnp.int32)
                start = plan.start(my_z ^ z, my_x ^ x, my_c ^ c)
                first_norm = d * plan.norm_each
                tail = [jnp.zeros((plan.tail, LANE), jnp.float32)]
                for row in range(min(first_norm + plan.norm_each, plan.norm_rows) - 1, first_norm - 1, -1):
                    part = norm_ref[row * LANE // D : row * LANE // D + 1, row * LANE % D : row * LANE % D + LANE]
                    tail.insert(0, part.astype(jnp.float32))
                tail = jnp.concatenate(tail, 0)[: plan.tail]
                moved[pl.ds(pl.multiple_of(start + plan.own, 8), plan.tail), :] = tail
                result = jnp.where(mine, rank + start, result)
                ranks = jnp.where(mine, rank, ranks)
    position_ref[...] = result
    to_scalar = pltpu.make_async_copy(position_ref, position, sem_position)
    to_scalar.start()
    to_scalar.wait()

    def copies(part, low, high):
        found = []
        for i, (out, slot) in enumerate(zip(out_refs, plan.order())):
            source = moved.at[pl.ds(plan.start(*slot) + low, high - low)]
            found.append(pltpu.make_async_copy(source, out.at[pl.ds(low, high - low)], sem_out.at[part, i]))
        return found

    cut = int(plan.own * EARLY / 8) * 8
    line_of = lax.broadcasted_iota(jnp.int32, (lists, LANE), 0)
    complete = jnp.max(jnp.where(ranks < cut, line_of + 1, 0))
    early = copies(0, 0, cut)
    late = copies(1, cut, plan.block)

    for i, end in enumerate(ends):
        fetches[i].wait()

        @pl.loop(ends[i - 1] if i else 0, end)
        def _(line):
            for part in range(0, LANE, 16):
                rows = raw[pl.ds(pl.multiple_of(line * LANE + part, 16), 16), :].astype(jnp.float32)
                for u in range(16):
                    moved[pl.ds(position[line, part + u], 1), :] = rows[u : u + 1, :]

        if i == FETCHES - 2:

            @pl.when(complete <= end)
            def _():
                for copy in early:
                    copy.start()

    @pl.when(complete > ends[FETCHES - 2])
    def _():
        for copy in early:
            copy.start()

    for copy in late:
        copy.start()
    for copy in early + late:
        copy.wait()


def place(plan, owners, norm_grads, grads):
    shapes = [(plan.block, LANE)] * plan.replicas
    outs = pl.pallas_call(
        functools.partial(place_kernel, plan),
        out_shape=[jax.ShapeDtypeStruct(s, jnp.float32) for s in shapes]
        + [jax.ShapeDtypeStruct((plan.lists, LANE), jnp.int32)],
        in_specs=[
            pl.BlockSpec(memory_space=pltpu.VMEM),
            pl.BlockSpec(memory_space=pltpu.VMEM),
            pl.BlockSpec(memory_space=pl.ANY),
        ],
        out_specs=[pl.BlockSpec(memory_space=pl.ANY)] * len(shapes) + [pl.BlockSpec(memory_space=pltpu.VMEM)],
        scratch_shapes=[
            pltpu.VMEM((plan.blocks, LANE), jnp.bfloat16),
            pltpu.VMEM((2 * plan.half, LANE), jnp.float32),
            pltpu.SMEM((plan.lists, LANE), jnp.int32),
            pltpu.SemaphoreType.DMA((FETCHES,)),
            pltpu.SemaphoreType.DMA,
            pltpu.SemaphoreType.DMA((2, len(shapes))),
        ],
        compiler_params=pltpu.CompilerParams(vmem_limit_bytes=58 * MIB),
        name="place_gradients",
    )(owners, norm_grads, grads)
    return dict(zip(plan.order(), outs)), outs[-1]


def owned_kernel(plan, place_ref, owner_ref, weights_ref, owned_ref, natural_ref, held, listed, order, sem_in, sem_order):
    fetch = pltpu.make_async_copy(weights_ref, held, sem_in)
    fetch.start()
    lists = plan.lists
    me = plan.index(place_ref[0], place_ref[1], place_ref[2])
    flags = (owner_ref[...] == me).astype(jnp.float32).astype(jnp.bfloat16)
    lane_in = lax.broadcasted_iota(jnp.int32, (LANE, LANE), 0)
    lane_out = lax.broadcasted_iota(jnp.int32, (LANE, LANE), 1)
    upto = (lane_in <= lane_out).astype(jnp.float32).astype(jnp.bfloat16)
    inner = jnp.dot(flags, upto, preferred_element_type=jnp.float32).astype(jnp.bfloat16)
    totals = lax.dot_general(
        jnp.ones((8, LANE), jnp.bfloat16), flags, (((1,), (1,)), ((), ())), preferred_element_type=jnp.float32
    )
    row_in = lax.broadcasted_iota(jnp.int32, (lists, lists), 0)
    row_out = lax.broadcasted_iota(jnp.int32, (lists, lists), 1)
    upto = (row_in <= row_out).astype(jnp.float32).astype(jnp.bfloat16)
    ends = jnp.dot(totals.astype(jnp.bfloat16), upto, preferred_element_type=jnp.float32)[0:1, :]
    place_of = lax.broadcasted_iota(jnp.int32, (LANE, lists), 1).astype(jnp.float32)
    rank_of = lax.broadcasted_iota(jnp.int32, (LANE, 1), 0)
    for step in range(listed.shape[0]):
        if step * LANE >= plan.own:
            break
        rank = (rank_of + step * LANE).astype(jnp.float32)
        passed = ends <= rank
        line = jnp.sum(passed.astype(jnp.float32), axis=1, keepdims=True)
        before = jnp.max(jnp.where(passed, ends, 0.0), axis=1, keepdims=True)
        chosen = (place_of == line).astype(jnp.float32).astype(jnp.bfloat16)
        counts = jnp.dot(chosen, inner, preferred_element_type=jnp.float32)
        column = jnp.sum((counts <= rank - before).astype(jnp.float32), axis=1, keepdims=True)
        block = jnp.broadcast_to((line * LANE + column).astype(jnp.int32), (LANE, LANE))
        natural_ref[step * LANE : (step + 1) * LANE, :] = block
        listed[step : step + 1, :] = jnp.sum(jnp.where(lane_in == lane_out, block, 0), axis=0, keepdims=True)
    to_scalar = pltpu.make_async_copy(listed, order, sem_order)
    to_scalar.start()
    to_scalar.wait()
    fetch.wait()

    def pick(line, count):
        for u in range(count):
            owned_ref[pl.ds(line * LANE + u, 1), :] = held[pl.ds(order[line, u], 1), :]

    @pl.loop(0, plan.own // LANE)
    def _(line):
        pick(line, LANE)

    if plan.own % LANE:
        pick(plan.own // LANE, plan.own % LANE)


def owned(plan, my_place, owners, weights):
    high_rows = -(-plan.own // (8 * LANE)) * 8
    ranks = -(-plan.own // LANE) * LANE
    vmem = pl.BlockSpec(memory_space=pltpu.VMEM)
    return pl.pallas_call(
        functools.partial(owned_kernel, plan),
        out_shape=[
            jax.ShapeDtypeStruct((plan.own, LANE), jnp.float32),
            jax.ShapeDtypeStruct((ranks, LANE), jnp.int32),
        ],
        in_specs=[pl.BlockSpec(memory_space=pltpu.SMEM), vmem, pl.BlockSpec(memory_space=pl.ANY)],
        out_specs=[vmem] * 2,
        scratch_shapes=[
            pltpu.VMEM((plan.blocks, LANE), jnp.float32),
            pltpu.VMEM((high_rows, LANE), jnp.int32),
            pltpu.SMEM((high_rows, LANE), jnp.int32),
            pltpu.SemaphoreType.DMA,
            pltpu.SemaphoreType.DMA,
        ],
        compiler_params=pltpu.CompilerParams(vmem_limit_bytes=58 * MIB),
        cost_estimate=pl.CostEstimate(flops=0, bytes_accessed=20 * MIB, transcendentals=0),
        name="owned_weights",
    )(my_place, owners, weights)


def update_kernel(plan, terms, *refs):
    parts, refs = refs[:terms], refs[terms:]
    first_ref, second_ref, weight_ref, natural_ref = refs[:4]
    new_first_ref, new_second_ref, block_ref = refs[4:]
    gradient = parts[0][: plan.block, :]
    for part in parts[1:]:
        gradient = gradient + part[: plan.block, :]
    tail, gradient = gradient[plan.own :, :], gradient[: plan.own, :]
    moment_one = beta_one * first_ref[...] + (1.0 - beta_one) * gradient
    moment_two = beta_two * second_ref[...] + (1.0 - beta_two) * gradient * gradient
    new_first_ref[...] = moment_one
    new_second_ref[...] = moment_two
    step = moment_one / bias_one / (jnp.sqrt(moment_two / bias_two) + epsilon)
    block_ref[: plan.own, :] = step
    weight = weight_ref[...]
    direction = step + decay_rate * weight
    natural = natural_ref[: plan.own, :]
    limits = (0,) + plan.bounds + (plan.blocks,)
    lane = lax.broadcasted_iota(jnp.int32, (8, LANE), 1)
    rank = lax.broadcasted_iota(jnp.int32, (8, LANE), 0)
    stats = jnp.zeros((8, LANE), jnp.float32)
    for column, squares in enumerate((weight * weight, direction * direction)):
        for k in range(matrices):
            inside = (natural >= limits[k]) & (natural < limits[k + 1])
            kept = jnp.where(inside, squares, 0.0).reshape(plan.own // 8, 8, LANE)
            total = jnp.sum(jnp.sum(kept, axis=0))
            stats = jnp.where((rank == plan.norm_each + k) & (lane == column), total, stats)
    block_ref[plan.own :, :] = tail + stats


def update(plan, parts, first, second, weight, natural):
    vmem = pl.BlockSpec(memory_space=pltpu.VMEM)
    shapes = [(plan.own, LANE), (plan.own, LANE), (plan.block, LANE)]
    return pl.pallas_call(
        functools.partial(update_kernel, plan, len(parts)),
        out_shape=[jax.ShapeDtypeStruct(s, jnp.float32) for s in shapes],
        in_specs=[vmem] * (len(parts) + 4),
        out_specs=[vmem] * len(shapes),
        compiler_params=pltpu.CompilerParams(vmem_limit_bytes=20 * MIB),
        name="moments",
    )(*parts, first, second, weight, natural)


def adam_rows(gradient, moment_one, moment_two, weight):
    moment_one = beta_one * moment_one + (1.0 - beta_one) * gradient
    moment_two = beta_two * moment_two + (1.0 - beta_two) * gradient * gradient
    step = moment_one / bias_one / (jnp.sqrt(moment_two / bias_two) + epsilon) + decay_rate * weight
    return (moment_one, moment_two, step)


def finish_kernel(plan, tile, slots, place_ref, position_ref, total_ref, norm_ref, weights_ref, *refs):
    pieces, refs = refs[: len(slots)], refs[len(slots) :]
    out_ref, new_norm_ref, trust_ref, held, norms, rates = refs
    now = pl.program_id(0)

    @pl.when(now == 0)
    def _():
        for piece, parts in zip(pieces, slots):
            for i, slot in enumerate(parts):
                held[pl.ds(plan.start(*slot), plan.block), :] = piece[i * plan.block : (i + 1) * plan.block, :]
        total = total_ref[...]
        for z in range(plan.nz):
            for x in range(plan.nx):
                for c in range(2):
                    start = plan.start(place_ref[0] ^ z, place_ref[1] ^ x, place_ref[2] ^ c) + plan.own
                    tail = held[pl.ds(pl.multiple_of(start, 8), plan.tail), :]
                    first = plan.index(z, x, c) * plan.norm_each
                    for row in range(first, min(first + plan.norm_each, plan.norm_rows)):
                        norms[row : row + 1, :] = tail[row - first : row - first + 1, :]
        for k in range(matrices):
            row = plan.norm_each + k
            weight_square, direction_square = total[row : row + 1, 0:1], total[row : row + 1, 1:2]
            ratio = jnp.sqrt(weight_square) / (jnp.sqrt(direction_square) + epsilon)
            rates[k : k + 1, :] = jnp.broadcast_to(learning * ratio, (1, LANE))
            trust_ref[k] = jnp.sum(ratio)
        each = plan.norm_rows // 2
        for i in range(2):
            gains, first, second = (
                jnp.concatenate([norm_ref[j, i : i + 1, row * LANE : (row + 1) * LANE] for row in range(each)], 0)
                for j in range(3)
            )
            one, two, step = adam_rows(norms[i * each : (i + 1) * each, :], first, second, gains)
            gain_square = jnp.sum(jnp.sum(gains * gains, axis=1, keepdims=True), axis=0, keepdims=True)
            step_square = jnp.sum(jnp.sum(step * step, axis=1, keepdims=True), axis=0, keepdims=True)
            ratio = jnp.sqrt(gain_square) / (jnp.sqrt(step_square) + epsilon)
            trust_ref[matrices + i] = jnp.sum(ratio)
            for j, value in enumerate((gains - learning * ratio * step, one, two)):
                for row in range(each):
                    new_norm_ref[j, i : i + 1, row * LANE : (row + 1) * LANE] = value[row : row + 1, :]

    lines = tile // LANE

    @pl.loop(0, lines)
    def _(line):
        matrix = jnp.int32(0)
        for bound in plan.bounds:
            matrix = matrix + (now * lines + line >= bound // LANE).astype(jnp.int32)
        rate = jnp.broadcast_to(rates[pl.ds(matrix, 1), :], (8, LANE))
        for group in range(0, LANE, 8):
            rows = [held[pl.ds(position_ref[now * lines + line, group + u], 1), :] for u in range(8)]
            here = pl.ds(pl.multiple_of(line * LANE + group, 8), 8)
            weight = weights_ref[pl.ds(pl.multiple_of((now * lines + line) * LANE + group, 8), 8), :]
            direction = jnp.concatenate(rows, 0) + decay_rate * weight
            out_ref[here, :] = weight - rate * direction


def finish(plan, my_place, position, total, norm_state, weights, pieces, slots):
    assert all(bound % LANE == 0 for bound in plan.bounds + (plan.blocks,))
    tile = plan.blocks // next(n for n in (TILES, 4, 2, 1) if plan.blocks // LANE % n == 0)
    smem = pl.BlockSpec(memory_space=pltpu.SMEM)
    vmem = pl.BlockSpec(memory_space=pltpu.VMEM)
    return pl.pallas_call(
        functools.partial(finish_kernel, plan, tile, slots),
        grid=(plan.blocks // tile,),
        out_shape=[
            jax.ShapeDtypeStruct((plan.blocks, LANE), jnp.float32),
            jax.ShapeDtypeStruct(norm_state.shape, jnp.float32),
            jax.ShapeDtypeStruct((matrices + 2,), jnp.float32),
        ],
        in_specs=[smem, smem, vmem, vmem, vmem]
        + [vmem] * len(pieces),
        out_specs=[pl.BlockSpec((tile, LANE), lambda i: (i, 0)), vmem, smem],
        scratch_shapes=[
            pltpu.VMEM((2 * plan.half, LANE), jnp.float32),
            pltpu.VMEM((plan.norm_rows, LANE), jnp.float32),
            pltpu.VMEM((8, LANE), jnp.float32),
        ],
        compiler_params=pltpu.CompilerParams(vmem_limit_bytes=20 * MIB),
        name="new_weights",
    )(my_place, position, total, norm_state, weights, *pieces)


def local(gradients, weights, first_moment, second_moment, owner_list, norm_grads, norm_state):
    plan = Plan(lax.axis_size("dp"), lax.axis_size("mp"), weights.shape[0])
    me = lax.axis_index("dp").astype(jnp.int32)
    my_place = jnp.stack([me // (2 * plan.nx), (me // 2) % plan.nx, me % 2]).astype(jnp.int32)
    owners = jnp.pad(owner_list[0], (0, plan.lists * LANE - plan.blocks), constant_values=-1)
    owners = owners.reshape(plan.lists, LANE)
    placed, position = place(plan, owners, norm_grads[0], gradients[0])
    weight_own, natural = owned(plan, my_place, owners, weights)

    mine, theirs = [None] * plan.nz, [None] * plan.nz
    for z in reversed(range(plan.nz)):
        both = [None] * plan.nx
        for x in reversed(range(plan.nx)):
            both[x] = placed[z, x, 0] + plan.swap(placed[z, x, 1])
            if (z, x) == (3, plan.nx - 1):
                later = [slot for slot in plan.order() if slot[2] and slot[:2] != (z, x)]
                both[x], *values = together(both[x], *(placed[slot] for slot in later))
                placed.update(zip(later, values))
        mine[z], theirs[z] = both[0], both[1:]
    if plan.nz == 4:
        parts = reduce(plan, mine, theirs, (weight_own, natural))
        parts, (weight_own, natural) = parts[:-2], parts[-2:]
    else:
        near = []
        for z in reversed(range(plan.nz)):
            terms = line_reduce(plan, "x", [mine[z]] + theirs[z])
            near.insert(0, sum(terms[1:], terms[0]) if z else None)
        parts = terms + line_reduce(plan, "z", near)[1:]
    new_first, new_second, block = update(
        plan, parts, first_moment[0], second_moment[0], weight_own, natural
    )

    found, total = gather(plan, my_place, block)
    pieces, slots = [piece for piece, _ in found], [parts for _, parts in found]
    new_weights, new_state, trust_ratios = finish(
        plan, my_place, position, total, norm_state, weights, pieces, slots
    )
    return (new_weights, new_first[None], new_second[None], new_state, trust_ratios)


def solution(mesh):
    in_specs = (
        P("dp", "mp", None),
        P("mp", None),
        P("mp", "dp", None),
        P("mp", "dp", None),
        P("mp", None),
        P("dp", None, None),
        P(),
    )
    out_specs = (P("mp", None), P("mp", "dp", None), P("mp", "dp", None), P(), P())
    return jax.shard_map(local, mesh=mesh, in_specs=in_specs, out_specs=out_specs, check_vma=False)
```

```python
import functools

import jax
import jax.numpy as jnp
from jax import lax
from jax.experimental import pallas as pl
from jax.experimental.pallas import tpu as pltpu
from jax.sharding import PartitionSpec as P

D = 1024
NTAB = 8
NKEYS = 256
KDIM = 128
LANE = 128
VROW_DEV = 512

beta_one = 0.9
beta_two = 0.99
bias_one = 1.0 - 0.9**4
bias_two = 1.0 - 0.99**4
epsilon = 1e-06
learning = 0.02
decay_rate = 0.01
matrices = 5
MIB = 1 << 20
TILES = 8
FETCHES = 5
EARLY = 0.74


def matrix_bounds(narrow):
    query_blocks = D * D // (LANE * narrow)
    key_blocks = NTAB * NKEYS * KDIM // (LANE * narrow)
    value_blocks = VROW_DEV * D // LANE
    return (
        query_blocks,
        query_blocks + key_blocks,
        query_blocks + key_blocks + value_blocks,
        2 * query_blocks + key_blocks + value_blocks,
    )


class Plan:
    def __init__(self, replicas, narrow, blocks):
        self.replicas, self.narrow, self.blocks = replicas, narrow, blocks
        chips = replicas // 2
        self.nz = 4 if chips % 4 == 0 else chips
        self.nx = chips // self.nz
        assert self.nz in (1, 2, 4) and self.nx in (1, 2, 4)
        self.own = blocks // replicas
        self.tail = 8
        self.norm_rows = 2 * D // LANE
        self.norm_each = -(-self.norm_rows // replicas)
        self.block = self.own + self.tail
        self.group = self.nx * self.block
        self.half = self.nz * self.group
        self.lists = -(-blocks // (8 * LANE)) * 8
        self.bounds = matrix_bounds(narrow)

    def index(self, z, x, c):
        return (z * self.nx + x) * 2 + c

    def start(self, far_z, far_x, far_c):
        return (1 - far_c) * self.half + far_z * self.group + far_x * self.block

    def order(self):
        zs, xs = range(self.nz - 1, -1, -1), range(self.nx - 1, -1, -1)
        return [(z, x, far_c) for far_c in (1, 0) for z in zs for x in xs]

    def send(self, value, axis, pairs):
        every = []
        for z in range(self.nz):
            for x in range(self.nx):
                for c in range(2):
                    here = {"z": z, "x": x, "c": c}
                    for source, target in pairs:
                        if here[axis] == source:
                            every.append((self.index(z, x, c), self.index(**{**here, axis: target})))
        return lax.ppermute(value, "dp", every)

    def swap(self, value):
        return self.send(value, "c", PAIR)


PAIR = [(0, 1), (1, 0)]
PAIRS = [(0, 1), (1, 0), (2, 3), (3, 2)]
MIDDLE = [(1, 2), (2, 1)]
INWARD = [(0, 1), (3, 2)]
OUTWARD = [(1, 0), (2, 3)]


def line_reduce(plan, axis, blocks):
    if len(blocks) == 1:
        return [blocks[0]]
    if len(blocks) == 2:
        return [blocks[0], plan.send(blocks[1], axis, PAIR)]
    in_three = plan.send(blocks[3], axis, INWARD)
    in_two = plan.send(blocks[2], axis, INWARD)
    across_two = plan.send(blocks[2] + in_three, axis, MIDDLE)
    across_three = plan.send(blocks[3] + in_two, axis, MIDDLE)
    pair = plan.send(blocks[1] + across_two, axis, PAIRS)
    return [blocks[0], pair, across_three]


def together(*values):
    return lax.optimization_barrier(values)


def reduce(plan, mine, theirs, beside):
    def along_x(z, own):
        terms = line_reduce(plan, "x", [own] + theirs[z])
        return terms

    three = along_x(3, mine[3])
    two = along_x(2, mine[2])
    near_three = sum(three[1:], three[0])
    in_three = plan.send(near_three, "z", INWARD)
    in_three, near_two, *beside = together(in_three, sum(two[1:], two[0]), *beside)
    one = along_x(1, mine[1])
    across_two = plan.send(near_two + in_three, "z", MIDDLE)
    in_two = plan.send(near_two, "z", INWARD)
    across_two, onward, near_one = together(across_two, near_three + in_two, sum(one[1:], one[0]))
    zero = along_x(0, mine[0])
    pair = plan.send(near_one + across_two, "z", PAIRS)
    across_three = plan.send(onward, "z", MIDDLE)
    return zero + [pair, across_three] + beside


def sums_kernel(plan, place_ref, *refs):
    tails, (out_ref, held) = refs[: plan.nz], refs[plan.nz :]
    for far_z, tail in enumerate(tails):
        held[place_ref[0] ^ far_z] = tail[...]
    total = held[0]
    for z in range(1, plan.nz):
        total = total + held[z]
    out_ref[...] = total


def all_sums(plan, my_place, blocks):
    def tail_of(row):
        return pl.BlockSpec((plan.tail, LANE), lambda i: ((row + plan.own) // plan.tail, 0))

    specs = [tail_of(row) for _, row in blocks]
    total = pl.pallas_call(
        functools.partial(sums_kernel, plan),
        grid=(1,),
        out_shape=jax.ShapeDtypeStruct((plan.tail, LANE), jnp.float32),
        in_specs=[pl.BlockSpec(memory_space=pltpu.SMEM)] + specs,
        out_specs=pl.BlockSpec(memory_space=pltpu.VMEM),
        scratch_shapes=[pltpu.VMEM((plan.nz, plan.tail, LANE), jnp.float32)],
        compiler_params=pltpu.CompilerParams(vmem_limit_bytes=4 * MIB),
        name="sums",
    )(my_place, *(value for value, _ in blocks))
    hop = 1
    while hop < plan.nx:
        total = total + plan.send(total, "x", [(i, i ^ hop) for i in range(plan.nx)])
        hop *= 2
    return total


def all_cores(plan, total):
    total = total + plan.swap(total)
    hop = 1
    while hop < plan.narrow:
        total = total + lax.ppermute(total, "mp", [(i, i ^ hop) for i in range(plan.narrow)])
        hop *= 2
    return total


def gather(plan, my_place, block):
    def along_x(value):
        return line_gather(plan, "x", plan.nx, value)

    if plan.nz != 4:
        ready = {}
        lines = [along_x(value) for value in line_gather(plan, "z", plan.nz, block)]
        total = all_cores(plan, all_sums(plan, my_place, [(line[0], 0) for line in lines]))
        mine = [(value, [(z, x)]) for z, line in enumerate(lines) for x, value in enumerate(line)]
    else:
        line = along_x(block)
        pair = plan.send(block, "z", PAIRS)
        three = plan.send(block, "z", MIDDLE)
        three, own, *line = together(three, jnp.concatenate([block, pair]), *line)
        line_pair = along_x(pair)
        two = plan.send(pair, "z", MIDDLE)
        out_two = plan.send(three, "z", OUTWARD)
        _, *line_pair = together(two, *line_pair)
        far = [jnp.concatenate([line[x], line_pair[x]]) for x in range(1, plan.nx)]
        near_two, *far = together(two + out_two, *far)
        line_two = along_x(near_two)
        out_three = plan.send(two, "z", OUTWARD)
        near_three = three + out_three
        line_three = along_x(near_three)
        total = all_sums(plan, my_place, [(own, 0), (own, plan.block), (near_two, 0), (near_three, 0)])
        total, *line_two = together(total, *line_two)
        early = plan.swap(near_three)
        early, total, *line_three = together(early, all_cores(plan, total), *line_three)
        ready = {(3, 0): early}
        mine = [(value, [(0, x), (1, x)]) for x, value in enumerate([own] + far)]
        mine.append((jnp.concatenate(line_two), [(2, x) for x in range(plan.nx)]))
        mine += [(value, [(3, x)]) for x, value in enumerate(line_three)]
    swapped = [ready[slots[0]] if slots[0] in ready else plan.swap(value) for value, slots in mine]
    found = [(value, [slot + (0,) for slot in slots]) for value, slots in mine]
    found += [(value, [slot + (1,) for slot in slots]) for value, (_, slots) in zip(swapped, mine)]
    return found, total


def line_gather(plan, axis, count, value):
    if count == 1:
        return [value]
    if count == 2:
        return [value, plan.send(value, axis, PAIR)]
    pair = plan.send(value, axis, PAIRS)
    across_three = plan.send(value, axis, MIDDLE)
    across_two = plan.send(pair, axis, MIDDLE)
    out_two = plan.send(across_three, axis, OUTWARD)
    out_three = plan.send(across_two, axis, OUTWARD)
    return [value, pair, across_two + out_two, across_three + out_three]


def place_kernel(plan, owner_ref, norm_ref, grads_ref, *refs):
    out_refs, refs = refs[: plan.replicas], refs[plan.replicas :]
    position_ref, raw, moved, position, sem_in, sem_position, sem_out = refs
    lines = plan.blocks // LANE
    ends = [lines * (i + 1) // FETCHES for i in range(FETCHES)]
    fetches = []
    for i, end in enumerate(ends):
        low = ends[i - 1] * LANE if i else 0
        rows = pl.ds(low, end * LANE - low)
        fetches.append(pltpu.make_async_copy(grads_ref.at[rows], raw.at[rows], sem_in.at[i]))
        fetches[-1].start()
    lists = plan.lists
    owners = owner_ref[...]
    me = lax.axis_index("dp").astype(jnp.int32)
    my_z, my_x, my_c = me // (2 * plan.nx), me // 2 % plan.nx, me % 2
    count = plan.replicas
    lane_in = lax.broadcasted_iota(jnp.int32, (LANE, LANE), 0)
    lane_out = lax.broadcasted_iota(jnp.int32, (LANE, LANE), 1)
    before = (lane_in < lane_out).astype(jnp.float32).astype(jnp.bfloat16)
    row_out = lax.broadcasted_iota(jnp.int32, (lists, lists), 0)
    row_in = lax.broadcasted_iota(jnp.int32, (lists, lists), 1)
    above = (row_in < row_out).astype(jnp.float32).astype(jnp.bfloat16)
    flags = [(owners == d).astype(jnp.float32).astype(jnp.bfloat16) for d in range(count)]
    inner = jnp.dot(jnp.concatenate(flags, 0), before, preferred_element_type=jnp.float32)
    owner_in = lax.broadcasted_iota(jnp.int32, (count * LANE, LANE), 0)
    owner_out = lax.broadcasted_iota(jnp.int32, (count * LANE, LANE), 1)
    pick = (owner_in // LANE == owner_out).astype(jnp.float32).astype(jnp.bfloat16)
    totals = jnp.dot(jnp.concatenate(flags, 1), pick, preferred_element_type=jnp.float32)
    outer = jnp.dot(above, totals.astype(jnp.bfloat16), preferred_element_type=jnp.float32)
    ranks = jnp.full((lists, LANE), plan.own, jnp.int32)
    result = jnp.zeros((lists, LANE), jnp.int32)
    for z in range(plan.nz):
        for x in range(plan.nx):
            for c in range(2):
                d = plan.index(z, x, c)
                mine = owners == d
                rank = (inner[d * lists : (d + 1) * lists, :] + outer[:, d : d + 1]).astype(jnp.int32)
                start = plan.start(my_z ^ z, my_x ^ x, my_c ^ c)
                first_norm = d * plan.norm_each
                tail = [jnp.zeros((plan.tail, LANE), jnp.float32)]
                for row in range(min(first_norm + plan.norm_each, plan.norm_rows) - 1, first_norm - 1, -1):
                    part = norm_ref[row * LANE // D : row * LANE // D + 1, row * LANE % D : row * LANE % D + LANE]
                    tail.insert(0, part.astype(jnp.float32))
                tail = jnp.concatenate(tail, 0)[: plan.tail]
                moved[pl.ds(pl.multiple_of(start + plan.own, 8), plan.tail), :] = tail
                result = jnp.where(mine, rank + start, result)
                ranks = jnp.where(mine, rank, ranks)
    position_ref[...] = result
    to_scalar = pltpu.make_async_copy(position_ref, position, sem_position)
    to_scalar.start()
    to_scalar.wait()

    def copies(part, low, high):
        found = []
        for i, (out, slot) in enumerate(zip(out_refs, plan.order())):
            source = moved.at[pl.ds(plan.start(*slot) + low, high - low)]
            found.append(pltpu.make_async_copy(source, out.at[pl.ds(low, high - low)], sem_out.at[part, i]))
        return found

    cut = int(plan.own * EARLY / 8) * 8
    line_of = lax.broadcasted_iota(jnp.int32, (lists, LANE), 0)
    complete = jnp.max(jnp.where(ranks < cut, line_of + 1, 0))
    early = copies(0, 0, cut)
    late = copies(1, cut, plan.block)

    for i, end in enumerate(ends):
        fetches[i].wait()

        @pl.loop(ends[i - 1] if i else 0, end)
        def _(line):
            for part in range(0, LANE, 16):
                rows = raw[pl.ds(pl.multiple_of(line * LANE + part, 16), 16), :].astype(jnp.float32)
                for u in range(16):
                    moved[pl.ds(position[line, part + u], 1), :] = rows[u : u + 1, :]

        if i == FETCHES - 2:

            @pl.when(complete <= end)
            def _():
                for copy in early:
                    copy.start()

    @pl.when(complete > ends[FETCHES - 2])
    def _():
        for copy in early:
            copy.start()

    for copy in late:
        copy.start()
    for copy in early + late:
        copy.wait()


def place(plan, owners, norm_grads, grads):
    shapes = [(plan.block, LANE)] * plan.replicas
    outs = pl.pallas_call(
        functools.partial(place_kernel, plan),
        out_shape=[jax.ShapeDtypeStruct(s, jnp.float32) for s in shapes]
        + [jax.ShapeDtypeStruct((plan.lists, LANE), jnp.int32)],
        in_specs=[
            pl.BlockSpec(memory_space=pltpu.VMEM),
            pl.BlockSpec(memory_space=pltpu.VMEM),
            pl.BlockSpec(memory_space=pl.ANY),
        ],
        out_specs=[pl.BlockSpec(memory_space=pl.ANY)] * len(shapes) + [pl.BlockSpec(memory_space=pltpu.VMEM)],
        scratch_shapes=[
            pltpu.VMEM((plan.blocks, LANE), jnp.bfloat16),
            pltpu.VMEM((2 * plan.half, LANE), jnp.float32),
            pltpu.SMEM((plan.lists, LANE), jnp.int32),
            pltpu.SemaphoreType.DMA((FETCHES,)),
            pltpu.SemaphoreType.DMA,
            pltpu.SemaphoreType.DMA((2, len(shapes))),
        ],
        compiler_params=pltpu.CompilerParams(vmem_limit_bytes=58 * MIB),
        name="place_gradients",
    )(owners, norm_grads, grads)
    return dict(zip(plan.order(), outs)), outs[-1]


def owned_kernel(plan, place_ref, owner_ref, weights_ref, owned_ref, natural_ref, held, listed, order, sem_in, sem_order):
    fetch = pltpu.make_async_copy(weights_ref, held, sem_in)
    fetch.start()
    lists = plan.lists
    me = plan.index(place_ref[0], place_ref[1], place_ref[2])
    flags = (owner_ref[...] == me).astype(jnp.float32).astype(jnp.bfloat16)
    lane_in = lax.broadcasted_iota(jnp.int32, (LANE, LANE), 0)
    lane_out = lax.broadcasted_iota(jnp.int32, (LANE, LANE), 1)
    upto = (lane_in <= lane_out).astype(jnp.float32).astype(jnp.bfloat16)
    inner = jnp.dot(flags, upto, preferred_element_type=jnp.float32).astype(jnp.bfloat16)
    totals = lax.dot_general(
        jnp.ones((8, LANE), jnp.bfloat16), flags, (((1,), (1,)), ((), ())), preferred_element_type=jnp.float32
    )
    row_in = lax.broadcasted_iota(jnp.int32, (lists, lists), 0)
    row_out = lax.broadcasted_iota(jnp.int32, (lists, lists), 1)
    upto = (row_in <= row_out).astype(jnp.float32).astype(jnp.bfloat16)
    ends = jnp.dot(totals.astype(jnp.bfloat16), upto, preferred_element_type=jnp.float32)[0:1, :]
    place_of = lax.broadcasted_iota(jnp.int32, (LANE, lists), 1).astype(jnp.float32)
    rank_of = lax.broadcasted_iota(jnp.int32, (LANE, 1), 0)
    for step in range(listed.shape[0]):
        if step * LANE >= plan.own:
            break
        rank = (rank_of + step * LANE).astype(jnp.float32)
        passed = ends <= rank
        line = jnp.sum(passed.astype(jnp.float32), axis=1, keepdims=True)
        before = jnp.max(jnp.where(passed, ends, 0.0), axis=1, keepdims=True)
        chosen = (place_of == line).astype(jnp.float32).astype(jnp.bfloat16)
        counts = jnp.dot(chosen, inner, preferred_element_type=jnp.float32)
        column = jnp.sum((counts <= rank - before).astype(jnp.float32), axis=1, keepdims=True)
        block = jnp.broadcast_to((line * LANE + column).astype(jnp.int32), (LANE, LANE))
        natural_ref[step * LANE : (step + 1) * LANE, :] = block
        listed[step : step + 1, :] = jnp.sum(jnp.where(lane_in == lane_out, block, 0), axis=0, keepdims=True)
    to_scalar = pltpu.make_async_copy(listed, order, sem_order)
    to_scalar.start()
    to_scalar.wait()
    fetch.wait()

    def pick(line, count):
        for u in range(count):
            owned_ref[pl.ds(line * LANE + u, 1), :] = held[pl.ds(order[line, u], 1), :]

    @pl.loop(0, plan.own // LANE)
    def _(line):
        pick(line, LANE)

    if plan.own % LANE:
        pick(plan.own // LANE, plan.own % LANE)


def owned(plan, my_place, owners, weights):
    high_rows = -(-plan.own // (8 * LANE)) * 8
    ranks = -(-plan.own // LANE) * LANE
    vmem = pl.BlockSpec(memory_space=pltpu.VMEM)
    return pl.pallas_call(
        functools.partial(owned_kernel, plan),
        out_shape=[
            jax.ShapeDtypeStruct((plan.own, LANE), jnp.float32),
            jax.ShapeDtypeStruct((ranks, LANE), jnp.int32),
        ],
        in_specs=[pl.BlockSpec(memory_space=pltpu.SMEM), vmem, pl.BlockSpec(memory_space=pl.ANY)],
        out_specs=[vmem] * 2,
        scratch_shapes=[
            pltpu.VMEM((plan.blocks, LANE), jnp.float32),
            pltpu.VMEM((high_rows, LANE), jnp.int32),
            pltpu.SMEM((high_rows, LANE), jnp.int32),
            pltpu.SemaphoreType.DMA,
            pltpu.SemaphoreType.DMA,
        ],
        compiler_params=pltpu.CompilerParams(vmem_limit_bytes=58 * MIB),
        cost_estimate=pl.CostEstimate(flops=0, bytes_accessed=20 * MIB, transcendentals=0),
        name="owned_weights",
    )(my_place, owners, weights)


def update_kernel(plan, terms, *refs):
    parts, refs = refs[:terms], refs[terms:]
    first_ref, second_ref, weight_ref, natural_ref = refs[:4]
    new_first_ref, new_second_ref, block_ref = refs[4:]
    gradient = parts[0][: plan.block, :]
    for part in parts[1:]:
        gradient = gradient + part[: plan.block, :]
    tail, gradient = gradient[plan.own :, :], gradient[: plan.own, :]
    moment_one = beta_one * first_ref[...] + (1.0 - beta_one) * gradient
    moment_two = beta_two * second_ref[...] + (1.0 - beta_two) * gradient * gradient
    new_first_ref[...] = moment_one
    new_second_ref[...] = moment_two
    step = moment_one / bias_one / (jnp.sqrt(moment_two / bias_two) + epsilon)
    block_ref[: plan.own, :] = step
    weight = weight_ref[...]
    direction = step + decay_rate * weight
    natural = natural_ref[: plan.own, :]
    limits = (0,) + plan.bounds + (plan.blocks,)
    lane = lax.broadcasted_iota(jnp.int32, (8, LANE), 1)
    rank = lax.broadcasted_iota(jnp.int32, (8, LANE), 0)
    stats = jnp.zeros((8, LANE), jnp.float32)
    for column, squares in enumerate((weight * weight, direction * direction)):
        for k in range(matrices):
            inside = (natural >= limits[k]) & (natural < limits[k + 1])
            kept = jnp.where(inside, squares, 0.0).reshape(plan.own // 8, 8, LANE)
            total = jnp.sum(jnp.sum(kept, axis=0))
            stats = jnp.where((rank == plan.norm_each + k) & (lane == column), total, stats)
    block_ref[plan.own :, :] = tail + stats


def update(plan, parts, first, second, weight, natural):
    vmem = pl.BlockSpec(memory_space=pltpu.VMEM)
    shapes = [(plan.own, LANE), (plan.own, LANE), (plan.block, LANE)]
    return pl.pallas_call(
        functools.partial(update_kernel, plan, len(parts)),
        out_shape=[jax.ShapeDtypeStruct(s, jnp.float32) for s in shapes],
        in_specs=[vmem] * (len(parts) + 4),
        out_specs=[vmem] * len(shapes),
        compiler_params=pltpu.CompilerParams(vmem_limit_bytes=20 * MIB),
        name="moments",
    )(*parts, first, second, weight, natural)


def adam_rows(gradient, moment_one, moment_two, weight):
    moment_one = beta_one * moment_one + (1.0 - beta_one) * gradient
    moment_two = beta_two * moment_two + (1.0 - beta_two) * gradient * gradient
    step = moment_one / bias_one / (jnp.sqrt(moment_two / bias_two) + epsilon) + decay_rate * weight
    return (moment_one, moment_two, step)


def finish_kernel(plan, tile, slots, place_ref, position_ref, total_ref, norm_ref, weights_ref, *refs):
    pieces, refs = refs[: len(slots)], refs[len(slots) :]
    out_ref, new_norm_ref, trust_ref, held, norms, rates = refs
    now = pl.program_id(0)

    @pl.when(now == 0)
    def _():
        for piece, parts in zip(pieces, slots):
            for i, slot in enumerate(parts):
                held[pl.ds(plan.start(*slot), plan.block), :] = piece[i * plan.block : (i + 1) * plan.block, :]
        total = total_ref[...]
        for z in range(plan.nz):
            for x in range(plan.nx):
                for c in range(2):
                    start = plan.start(place_ref[0] ^ z, place_ref[1] ^ x, place_ref[2] ^ c) + plan.own
                    tail = held[pl.ds(pl.multiple_of(start, 8), plan.tail), :]
                    first = plan.index(z, x, c) * plan.norm_each
                    for row in range(first, min(first + plan.norm_each, plan.norm_rows)):
                        norms[row : row + 1, :] = tail[row - first : row - first + 1, :]
        for k in range(matrices):
            row = plan.norm_each + k
            weight_square, direction_square = total[row : row + 1, 0:1], total[row : row + 1, 1:2]
            ratio = jnp.sqrt(weight_square) / (jnp.sqrt(direction_square) + epsilon)
            rates[k : k + 1, :] = jnp.broadcast_to(learning * ratio, (1, LANE))
            trust_ref[k] = jnp.sum(ratio)
        each = plan.norm_rows // 2
        for i in range(2):
            gains, first, second = (
                jnp.concatenate([norm_ref[j, i : i + 1, row * LANE : (row + 1) * LANE] for row in range(each)], 0)
                for j in range(3)
            )
            one, two, step = adam_rows(norms[i * each : (i + 1) * each, :], first, second, gains)
            gain_square = jnp.sum(jnp.sum(gains * gains, axis=1, keepdims=True), axis=0, keepdims=True)
            step_square = jnp.sum(jnp.sum(step * step, axis=1, keepdims=True), axis=0, keepdims=True)
            ratio = jnp.sqrt(gain_square) / (jnp.sqrt(step_square) + epsilon)
            trust_ref[matrices + i] = jnp.sum(ratio)
            for j, value in enumerate((gains - learning * ratio * step, one, two)):
                for row in range(each):
                    new_norm_ref[j, i : i + 1, row * LANE : (row + 1) * LANE] = value[row : row + 1, :]

    lines = tile // LANE

    @pl.loop(0, lines)
    def _(line):
        matrix = jnp.int32(0)
        for bound in plan.bounds:
            matrix = matrix + (now * lines + line >= bound // LANE).astype(jnp.int32)
        rate = jnp.broadcast_to(rates[pl.ds(matrix, 1), :], (8, LANE))
        for group in range(0, LANE, 8):
            rows = [held[pl.ds(position_ref[now * lines + line, group + u], 1), :] for u in range(8)]
            here = pl.ds(pl.multiple_of(line * LANE + group, 8), 8)
            weight = weights_ref[pl.ds(pl.multiple_of((now * lines + line) * LANE + group, 8), 8), :]
            direction = jnp.concatenate(rows, 0) + decay_rate * weight
            out_ref[here, :] = weight - rate * direction


def finish(plan, my_place, position, total, norm_state, weights, pieces, slots):
    assert all(bound % LANE == 0 for bound in plan.bounds + (plan.blocks,))
    tile = plan.blocks // next(n for n in (TILES, 4, 2, 1) if plan.blocks // LANE % n == 0)
    smem = pl.BlockSpec(memory_space=pltpu.SMEM)
    vmem = pl.BlockSpec(memory_space=pltpu.VMEM)
    return pl.pallas_call(
        functools.partial(finish_kernel, plan, tile, slots),
        grid=(plan.blocks // tile,),
        out_shape=[
            jax.ShapeDtypeStruct((plan.blocks, LANE), jnp.float32),
            jax.ShapeDtypeStruct(norm_state.shape, jnp.float32),
            jax.ShapeDtypeStruct((matrices + 2,), jnp.float32),
        ],
        in_specs=[smem, smem, vmem, vmem, vmem]
        + [vmem] * len(pieces),
        out_specs=[pl.BlockSpec((tile, LANE), lambda i: (i, 0)), vmem, smem],
        scratch_shapes=[
            pltpu.VMEM((2 * plan.half, LANE), jnp.float32),
            pltpu.VMEM((plan.norm_rows, LANE), jnp.float32),
            pltpu.VMEM((8, LANE), jnp.float32),
        ],
        compiler_params=pltpu.CompilerParams(vmem_limit_bytes=20 * MIB),
        name="new_weights",
    )(my_place, position, total, norm_state, weights, *pieces)


def local(gradients, weights, first_moment, second_moment, owner_list, norm_grads, norm_state):
    plan = Plan(lax.axis_size("dp"), lax.axis_size("mp"), weights.shape[0])
    me = lax.axis_index("dp").astype(jnp.int32)
    my_place = jnp.stack([me // (2 * plan.nx), (me // 2) % plan.nx, me % 2]).astype(jnp.int32)
    owners = jnp.pad(owner_list[0], (0, plan.lists * LANE - plan.blocks), constant_values=-1)
    owners = owners.reshape(plan.lists, LANE)
    placed, position = place(plan, owners, norm_grads[0], gradients[0])
    weight_own, natural = owned(plan, my_place, owners, weights)

    mine, theirs = [None] * plan.nz, [None] * plan.nz
    for z in reversed(range(plan.nz)):
        both = [None] * plan.nx
        for x in reversed(range(plan.nx)):
            both[x] = placed[z, x, 0] + plan.swap(placed[z, x, 1])
            if (z, x) == (3, plan.nx - 1):
                later = [slot for slot in plan.order() if slot[2] and slot[:2] != (z, x)]
                both[x], *values = together(both[x], *(placed[slot] for slot in later))
                placed.update(zip(later, values))
        mine[z], theirs[z] = both[0], both[1:]
    if plan.nz == 4:
        parts = reduce(plan, mine, theirs, (weight_own, natural))
        parts, (weight_own, natural) = parts[:-2], parts[-2:]
    else:
        near = []
        for z in reversed(range(plan.nz)):
            terms = line_reduce(plan, "x", [mine[z]] + theirs[z])
            near.insert(0, sum(terms[1:], terms[0]) if z else None)
        parts = terms + line_reduce(plan, "z", near)[1:]
    new_first, new_second, block = update(
        plan, parts, first_moment[0], second_moment[0], weight_own, natural
    )

    found, total = gather(plan, my_place, block)
    pieces, slots = [piece for piece, _ in found], [parts for _, parts in found]
    new_weights, new_state, trust_ratios = finish(
        plan, my_place, position, total, norm_state, weights, pieces, slots
    )
    return (new_weights, new_first[None], new_second[None], new_state, trust_ratios)


def solution(mesh):
    in_specs = (
        P("dp", "mp", None),
        P("mp", None),
        P("mp", "dp", None),
        P("mp", "dp", None),
        P("mp", None),
        P("dp", None, None),
        P(),
    )
    out_specs = (P("mp", None), P("mp", "dp", None), P("mp", "dp", None), P(), P())
    return jax.shard_map(local, mesh=mesh, in_specs=in_specs, out_specs=out_specs, check_vma=False)
```
